32 devices in a mesh: seq: 4 (over y, core), fsdp: 8 (over z, x).
Axes of the slice: x: 2, y: 2, z: 4, core: 2. Of those that a mesh axis runs over, the one named last changes fastest.
Arguments:
- tokens: bfloat16 [8, 4096, 768], P('fsdp', 'seq'), may hold values from -6 to 6
- lengths: int32 [8], P('fsdp'), may hold values from 3073 to 4096
- attn_gain: bfloat16 [768], P('fsdp'), may hold values from 0.5 to 1.5
- qkv_weight: bfloat16 [768, 2304], P('fsdp'), may hold values from -0.21875 to 0.21875
- proj_weight: bfloat16 [768, 768], P('fsdp'), may hold values from -6 to 6
- ffn_gain: bfloat16 [768], P('fsdp'), may hold values from 0.5 to 1.5
- in_weight: bfloat16 [768, 2304], P('fsdp'), may hold values from -0.21875 to 0.21875
- out_weight: bfloat16 [1152, 768], P('fsdp'), may hold values from -0.1875 to 0.1875
- out_grad: bfloat16 [8, 4096, 768], P('fsdp', 'seq'), may hold values from -6 to 6
Outputs:
- block_out: bfloat16 [8, 4096, 768], P('fsdp', 'seq')
- tokens_grad: float32 [8, 4096, 768], P('fsdp', 'seq')
- attn_gain_grad: float32 [768], P('fsdp')
- qkv_weight_grad: float32 [768, 2304], P('fsdp')
- proj_weight_grad: float32 [768, 768], P('fsdp')
- ffn_gain_grad: float32 [768], P('fsdp')
- in_weight_grad: float32 [768, 2304], P('fsdp')
- out_weight_grad: float32 [1152, 768], P('fsdp')
The draws below stay inside these ranges and needn't reach their ends.
Inputs may be any that keep to these rules, and one draw needn't show every extreme that they name: `lengths`: positions at or beyond a sequence's length are padding, which no query attends to.
All inputs are finite; a program needn't handle non-finite values.
Results may differ from the reference program's by a relative error of at most 0.017.
Values may be sent and summed in bfloat16 or wider, within the bound.
No kernel may reach another device: no remote copies, remote signals or barrier semaphores. Data moves between devices by JAX's collectives and lax.ppermute only.
A program may use at most 192 MiB of HBM per device.

```python
import jax
import jax.numpy as jnp
from jax import lax

D = 768
HEADS = 12
FF = 1152
SEQ_LEN = 4096
SEQS = 8


def touch_ends(array, rng, low, high):
    longest = array.shape.index(max(array.shape))
    spots = []
    for shift in (0, 1):
        where = [jax.random.randint(jax.random.fold_in(rng, axis), (), 0, length) for axis, length in enumerate(array.shape)]
        where[longest] = (where[longest] + shift) % array.shape[longest]
        spots.append(tuple(where))
    return array.at[spots[0]].set(low).at[spots[1]].set(high)


def raised(entries, stream_key, source, target, shards_of, factor):
    def block_of(position):
        return (jnp.arange(entries.shape[position]) // (entries.shape[position] // shards_of)).reshape((-1,) + (1,) * (entries.ndim - 1 - position))

    near = jax.random.permutation(stream_key, shards_of)[block_of(target)]
    far = (block_of(target) + shards_of // 2) % shards_of
    return jnp.where((block_of(source) == near) | (block_of(source) == far), factor * entries, entries)


def block_scale(key, dims, split, smallest, top_value):
    factor_of = 1.0
    for axis_at, shards_of in split:
        heights = jax.random.uniform(jax.random.fold_in(jax.random.fold_in(key, 6), axis_at), (shards_of,), jnp.float32, smallest / len(split), top_value / len(split))
        factor_of = factor_of * jnp.repeat(jnp.exp(heights), dims[axis_at] // shards_of).reshape((-1,) + (1,) * (len(dims) - 1 - axis_at))
    return factor_of


def scatter_about(stream_key, shape, scale, reach, pieces=(), kind=jnp.bfloat16):
    values = jax.random.normal(stream_key, shape, jnp.float32) * scale
    if len(pieces) > 0:
        values = block_scale(stream_key, shape, pieces, -0.22, 0.18) * values
    return jnp.clip(values, min=-reach, max=reach).astype(kind)


def noise_with(own_key, dims, width, limit, shards, heavy, kind=jnp.bfloat16):
    array = width * jax.random.normal(own_key, dims, jnp.float32)
    if shards:
        array = array * block_scale(own_key, dims, shards, -0.22, 0.18)
    return jnp.clip(raised(array, jax.random.fold_in(own_key, 3), *heavy), -limit, limit).astype(kind)


def setup_inputs(seed: int = 0) -> dict:
    arg_keys = jax.random.split(jax.random.key(seed), 10)
    tokens = noise_with(arg_keys[0], (SEQS, SEQ_LEN, D), 1.0, 6.0, ((0, 8), (1, 4)), (0, 2, 8, 2.0))
    lengths = touch_ends(jax.random.randint(arg_keys[1], (SEQS,), 3 * SEQ_LEN // 4 + 1, SEQ_LEN + 1), jax.random.fold_in(arg_keys[1], 1), 3 * SEQ_LEN // 4 + 1, SEQ_LEN).astype(jnp.int32)
    attn_gain = jnp.clip(1.0 + 0.1 * jax.random.normal(arg_keys[2], (D,), jnp.float32), 0.5, 1.5).astype(jnp.bfloat16)
    qkv_weight = scatter_about(arg_keys[3], (D, 3 * D), D ** -0.5, 0.21875, ((0, 8),))
    proj_weight = scatter_about(arg_keys[4], (D, D), (max(1, 3 * D // SEQ_LEN)) ** -0.5, 6.0, ((0, 8),))
    ffn_gain = jnp.clip(1.0 + 0.1 * jax.random.normal(arg_keys[5], (D,), jnp.float32), 0.5, 1.5).astype(jnp.bfloat16)
    in_weight = scatter_about(arg_keys[6], (D, 2 * FF), D ** -0.5, 0.21875, ((0, 8),))
    out_weight = scatter_about(arg_keys[7], (FF, D), FF ** -0.5, 0.1875, ((0, 8),))
    out_grad = scatter_about(arg_keys[8], (SEQS, SEQ_LEN, D), 1.0, 6.0, ((0, 8), (1, 4)))
    return dict(tokens=tokens, lengths=lengths, attn_gain=attn_gain, qkv_weight=qkv_weight, proj_weight=proj_weight, ffn_gain=ffn_gain, in_weight=in_weight, out_weight=out_weight, out_grad=out_grad)


epsilon = 1e-05
rope_base = 160000.0
masked_score = -1e+30
highest = lax.Precision.HIGHEST

@jax.custom_vjp
def low(v):
    return lax.optimization_barrier(v.astype(jnp.bfloat16)).astype(jnp.float32)

@jax.custom_vjp
def low_back(v):
    return v

def low_keep(v):
    return (low(v), None)

def low_pass(kept, grad):
    return (grad,)

def back_keep(v):
    return (v, None)

def back_low(kept, grad):
    return (low(grad),)
low.defvjp(low_keep, low_pass)
low_back.defvjp(back_keep, back_low)

def layer_norm(activation, gain_row):
    centred = activation - lax.optimization_barrier(jnp.mean(activation, axis=-1, keepdims=True))
    inverse = lax.rsqrt(lax.optimization_barrier(jnp.mean(centred * centred, axis=-1, keepdims=True)) + epsilon)
    return centred * inverse * gain_row

def rope_tables(length, head_dim):
    half_dim = head_dim // 2
    frequency = rope_base ** (-(jnp.arange(half_dim, dtype=jnp.float32) * 2.0) / head_dim)
    angles = jnp.arange(length, dtype=jnp.float32)[:, None] * frequency[None, :]
    angles = jnp.concatenate([angles, angles], axis=1)
    return (jnp.cos(angles), jnp.sin(angles))

def rotate(activation, cosine, sine_table):
    half_dim = activation.shape[-1] // 2
    turned = jnp.concatenate([-activation[..., half_dim:], activation[..., :half_dim]], axis=-1)
    return activation * cosine[:, None, :] + turned * sine_table[:, None, :]

def attend(queries, key_rows, values, valid_keys):
    length, heads_here, head_dim = queries.shape
    score_scale = head_dim ** (-0.5)
    block_rows = min(512, length)
    query_blocks = queries.reshape(length // block_rows, block_rows, heads_here, head_dim)

    def one_block(query_block):
        scores = jnp.einsum('qhd,khd->hqk', query_block, key_rows, precision=highest) * score_scale
        scores = low_back(jnp.where(valid_keys[None, None, :], scores, masked_score))
        weights = low(jax.nn.softmax(scores, axis=-1))
        return jnp.einsum('hqk,khd->qhd', weights, values, precision=highest)
    mixed_heads = lax.map(jax.checkpoint(one_block), query_blocks)
    return mixed_heads.reshape(length, heads_here * head_dim)

def forward(tokens, valid_keys, attn_gain, qkv_weight, proj_weight, ffn_gain, in_weight, out_weight):
    length = tokens.shape[0]
    head_dim = D // HEADS
    normed = low(layer_norm(tokens, attn_gain))
    packed = low_back(jnp.dot(normed, qkv_weight, precision=highest))
    packed = packed.reshape(length, 3, HEADS, head_dim)
    cosine, sine_table = rope_tables(length, head_dim)
    queries = low(low_back(rotate(packed[:, 0], cosine, sine_table)))
    key_rows = low(low_back(rotate(packed[:, 1], cosine, sine_table)))
    values = low(low_back(packed[:, 2]))
    mixed_heads = low(low_back(attend(queries, key_rows, values, valid_keys)))
    hidden = tokens + low_back(jnp.dot(mixed_heads, proj_weight, precision=highest))
    second = low(layer_norm(hidden, ffn_gain))
    gate_up = low_back(jnp.dot(second, in_weight, precision=highest))
    inner_low = low(jax.nn.gelu(gate_up[:, :FF], approximate=False) * gate_up[:, FF:])
    return hidden + low_back(jnp.dot(inner_low, out_weight, precision=highest))

def reference(tokens, lengths, attn_gain, qkv_weight, proj_weight, ffn_gain, in_weight, out_weight, out_grad):
    params = tuple((weight_arg.astype(jnp.float32) for weight_arg in (attn_gain, qkv_weight, proj_weight, ffn_gain, in_weight, out_weight)))
    positions = jnp.arange(SEQ_LEN, dtype=jnp.int32)

    def one_sequence(totals, inputs):
        sequence, length, cotangent = inputs
        valid_keys = positions < length

        def apply_layer(sequence_in, *weights):
            return forward(sequence_in, valid_keys, *weights)
        result, pullback = jax.vjp(apply_layer, sequence.astype(jnp.float32), *params)
        gradients = pullback(cotangent.astype(jnp.float32))
        totals = tuple((running + update for running, update in zip(totals, gradients[1:])))
        return (totals, (result.astype(jnp.bfloat16), gradients[0]))
    zero_grads = tuple((jnp.zeros(weight_arg.shape, jnp.float32) for weight_arg in params))
    totals, (outputs, tokens_grad) = lax.scan(one_sequence, zero_grads, (tokens, lengths, out_grad))
    return (outputs, tokens_grad, totals[0], totals[1], totals[2], totals[3], totals[4], totals[5])
```

```python
import functools

import jax
import jax.numpy as jnp
from jax import lax
from jax.experimental import pallas as pl
from jax.experimental.pallas import tpu as pltpu
from jax.sharding import PartitionSpec as P

D = 768
HEADS = 12
HD = 64

epsilon = 1e-05
rope_base = 160000.0
masked_score = -1e30
LOG2E = 1.4426950408889634
LN2 = 0.6931471805599453

bf = jnp.bfloat16
f32 = jnp.float32
NN = ((1,), (0,))
NT = ((1,), (1,))
TN = ((0,), (0,))


def dg(a, b, dims):
    return lax.dot_general(a, b, (dims, ((), ())), preferred_element_type=f32)


def unit_rows_of(x):
    centred = x - jnp.mean(x, axis=-1, keepdims=True)
    inverse = lax.rsqrt(jnp.mean(centred * centred, axis=-1, keepdims=True) + epsilon)
    return centred * inverse, inverse


def qkv_kernel(heads, info_ref, x_ref, gain_ref, w_ref, cs_ref, *refs):
    n_ref, k_ref, v_ref, qt_ref, kt_ref, vt_ref = refs[-6:]
    rb = x_ref.shape[0]
    unit, _ = unit_rows_of(x_ref[...].astype(f32))
    normed = (unit * gain_ref[...]).astype(bf)
    n_ref[...] = normed
    cs = cs_ref[...]
    lane = lax.broadcasted_iota(jnp.int32, (rb, 128), 1)
    row = lax.broadcasted_iota(jnp.int32, (rb, 128), 0)
    position = info_ref[0] + pl.program_id(0) * rb + row
    bias = jnp.where(position < info_ref[1], 0.0, masked_score)
    key_tail = jnp.where(lane == HD, bias, 0.0)
    query_tail = jnp.where(lane == HD, 1.0, 0.0)
    value_tail = jnp.where(lane < HD + 2, -1.0, 0.0)
    head_lane = lane < HD
    for h in range(heads):
        y = dg(normed, w_ref[:, h * 384 : (h + 1) * 384], NN)
        q = y[:, :128] * cs
        q = q + pltpu.roll(q, HD, 1)
        k = y[:, 128:256] * cs
        k = k + pltpu.roll(k, HD, 1)
        v = y[:, 256:]
        qe = jnp.where(head_lane, q * (HD**-0.5 * LOG2E), query_tail)
        qt_ref[h] = qe.T.astype(bf)
        ke = jnp.where(head_lane, k, key_tail)
        k_ref[h] = ke.astype(bf)
        kt_ref[h] = ke.T[:HD].astype(bf)
        v_ref[h] = jnp.where(head_lane, v, value_tail).astype(bf)
        ve = jnp.where(head_lane, v, query_tail)
        vt_ref[h] = ve.T[:80].astype(bf)


def qkv_call(block, blocks, info, x, gain, w, cs, carried):
    rows = x.shape[0]
    S = rows * blocks
    heads = w.shape[1] // 384
    rb = min(256, rows)
    steps = rows // rb
    at = lambda i: block * steps + i
    outs = (
        jax.ShapeDtypeStruct((S, D), bf),
        jax.ShapeDtypeStruct((heads, S, 128), bf),
        jax.ShapeDtypeStruct((heads, S, 128), bf),
        jax.ShapeDtypeStruct((heads, 128, S), bf),
        jax.ShapeDtypeStruct((heads, HD, S), bf),
        jax.ShapeDtypeStruct((heads, 80, S), bf),
    )
    in_specs = [
        pl.BlockSpec(memory_space=pltpu.SMEM),
        pl.BlockSpec((rb, D), lambda i: (i, 0)),
        pl.BlockSpec((1, D), lambda i: (0, 0)),
        pl.BlockSpec(w.shape, lambda i: (0, 0)),
        pl.BlockSpec((rb, 128), lambda i: (at(i), 0)),
    ]
    aliases = {}
    if carried is not None:
        in_specs += [pl.BlockSpec(memory_space=pl.ANY)] * 6
        aliases = {5 + n: n for n in range(6)}
    return pl.pallas_call(
        functools.partial(qkv_kernel, heads),
        grid=(steps,),
        out_shape=outs,
        in_specs=in_specs,
        out_specs=(
            pl.BlockSpec((rb, D), lambda i: (at(i), 0)),
            pl.BlockSpec((heads, rb, 128), lambda i: (0, at(i), 0)),
            pl.BlockSpec((heads, rb, 128), lambda i: (0, at(i), 0)),
            pl.BlockSpec((heads, 128, rb), lambda i: (0, 0, at(i))),
            pl.BlockSpec((heads, HD, rb), lambda i: (0, 0, at(i))),
            pl.BlockSpec((heads, 80, rb), lambda i: (0, 0, at(i))),
        ),
        input_output_aliases=aliases,
        compiler_params=pltpu.CompilerParams(vmem_limit_bytes=48 * 2**20),
        cost_estimate=pl.CostEstimate(
            flops=4 * rows * D * w.shape[1], bytes_accessed=rows * 8192, transcendentals=0
        ),
        name="qkv",
    )(info, x, gain, w, cs, *(carried or ()))


def attend_kernel(kc, k_ref, q_ref, v_ref, p_ref, o_ref, ob_ref, linv_ref, s_ref):
    rows = k_ref.shape[1]
    bq = q_ref.shape[2]
    q = q_ref[0]
    m = jnp.full((8, bq), -jnp.inf, f32)
    for c in range(rows // kc):
        at = slice(c * kc, (c + 1) * kc)
        s = dg(k_ref[0, at, :], q, NN)
        s_ref[at, :] = s
        m = jnp.maximum(m, jnp.max(s.reshape(kc // 8, 8, bq), axis=0))
    m = jnp.max(m, axis=0, keepdims=True)
    acc = jnp.zeros((v_ref.shape[1], bq), f32)
    for c in range(rows // kc):
        at = slice(c * kc, (c + 1) * kc)
        p = jnp.exp2(s_ref[at, :] - m).astype(bf)
        p_ref[0, at, :] = p
        acc = acc + dg(v_ref[0, :, at], p, NN)
    linv = 1.0 / acc[HD : HD + 1, :]
    o = acc[:HD, :] * linv
    o_ref[...] = o
    ob_ref[0] = o.astype(bf)
    linv_ref[0] = linv


def attend(h, k, qt, vt, groups, bq=512, kc=512):
    S = k.shape[1]
    nq = S // bq
    per = nq // groups
    return pl.pallas_call(
        functools.partial(attend_kernel, kc),
        grid=(nq,),
        out_shape=(
            jax.ShapeDtypeStruct((nq, S, bq), bf),
            jax.ShapeDtypeStruct((HD, S), f32),
            jax.ShapeDtypeStruct((groups, HD, S // groups), bf),
            jax.ShapeDtypeStruct((nq, 1, bq), f32),
        ),
        in_specs=[
            pl.BlockSpec((1, S, 128), lambda i: (h, 0, 0)),
            pl.BlockSpec((1, 128, bq), lambda i: (h, 0, i)),
            pl.BlockSpec((1, 80, S), lambda i: (h, 0, 0)),
        ],
        out_specs=(
            pl.BlockSpec((1, S, bq), lambda i: (i, 0, 0)),
            pl.BlockSpec((HD, bq), lambda i: (0, i)),
            pl.BlockSpec((1, HD, bq), lambda i: (i // per, 0, i % per)),
            pl.BlockSpec((1, 1, bq), lambda i: (i, 0, 0)),
        ),
        scratch_shapes=[pltpu.VMEM((S, bq), f32)],
        compiler_params=pltpu.CompilerParams(vmem_limit_bytes=48 * 2**20),
        cost_estimate=pl.CostEstimate(
            flops=16 * HD * S * S, bytes_accessed=2 * S * S, transcendentals=S * S
        ),
        name="attend",
    )(k, qt, vt)


def attend_back_kernel(
    kc, nq, per, v_ref, kt_ref, q_ref, do_ref, o_ref, linv_ref, p_ref, cos_ref, sin_ref, out_ref, acc_ref
):
    i = pl.program_id(0)
    rows = v_ref.shape[1]
    bq = q_ref.shape[2]

    @pl.when(i == 0)
    def _():
        acc_ref[...] = jnp.zeros_like(acc_ref)

    dop = (do_ref[0].astype(f32) * linv_ref[0]).astype(bf)
    delta = jnp.sum(dop.astype(f32) * o_ref[...], axis=0, keepdims=True)
    high = delta.astype(bf).astype(f32)
    r = lax.broadcasted_iota(jnp.int32, (16, bq), 0)
    tail = jnp.where(r == 0, high, jnp.where(r == 1, delta - high, 0.0)).astype(bf)
    doe = jnp.concatenate([dop, tail, jnp.zeros((128 - HD - 16, bq), bf)], axis=0)
    zero = jnp.zeros((HD, bq), bf)
    right_v = jnp.concatenate([dop, zero], axis=0)
    right_k = jnp.concatenate([zero, q_ref[0, :HD, :]], axis=0)
    dq = jnp.zeros((HD, bq), f32)
    for c in range(rows // kc):
        at = slice(c * kc, (c + 1) * kc)
        p = p_ref[0, at, :]
        ds = p * dg(v_ref[0, at, :], doe, NN).astype(bf)
        acc_ref[at, :] = acc_ref[at, :] + dg(p, right_v, NT) + dg(ds, right_k, NT)
        dq = dq + dg(kt_ref[0, :, at], ds, NN)
    dq = dq * HD**-0.5
    turned = jnp.concatenate([dq[HD // 2 :], -dq[: HD // 2]], axis=0)
    here = pl.ds(pl.multiple_of(i * bq, bq), bq)
    dq = dq * cos_ref[:, here] + turned * sin_ref[:, here]
    out_ref[i // per, :HD, pl.ds(pl.multiple_of((i % per) * bq, bq), bq)] = dq.astype(bf)

    @pl.when(i == nq - 1)
    def _():
        groups = out_ref.shape[0]
        width = rows // groups
        for j in range(groups):
            at = slice(j * width, (j + 1) * width)
            t = acc_ref[at, :].T
            dk = t[HD:] * LN2
            turned_k = jnp.concatenate([dk[HD // 2 :], -dk[: HD // 2]], axis=0)
            dk = dk * cos_ref[:, at] + turned_k * sin_ref[:, at]
            out_ref[j, HD : 2 * HD] = dk.astype(bf)
            out_ref[j, 2 * HD :] = t[:HD].astype(bf)


def attend_back(h, v, kt, qt, do, o, linv, p, cos, sin, groups, bq=512, kc=512):
    S = v.shape[1]
    nq = S // bq
    per = nq // groups
    return pl.pallas_call(
        functools.partial(attend_back_kernel, kc, nq, per),
        grid=(nq,),
        out_shape=jax.ShapeDtypeStruct((groups, 3 * HD, S // groups), bf),
        in_specs=[
            pl.BlockSpec((1, S, 128), lambda i: (h, 0, 0)),
            pl.BlockSpec((1, HD, S), lambda i: (h, 0, 0)),
            pl.BlockSpec((1, 128, bq), lambda i: (h, 0, i)),
            pl.BlockSpec((1, HD, bq), lambda i: (i // per, 0, i % per)),
            pl.BlockSpec((HD, bq), lambda i: (0, i)),
            pl.BlockSpec((1, 1, bq), lambda i: (i, 0, 0)),
            pl.BlockSpec((1, S, bq), lambda i: (i, 0, 0)),
            pl.BlockSpec((HD, S), lambda i: (0, 0)),
            pl.BlockSpec((HD, S), lambda i: (0, 0)),
        ],
        out_specs=pl.BlockSpec((groups, 3 * HD, S // groups), lambda i: (0, 0, 0)),
        scratch_shapes=[pltpu.VMEM((S, 128), f32)],
        compiler_params=pltpu.CompilerParams(vmem_limit_bytes=48 * 2**20),
        cost_estimate=pl.CostEstimate(
            flops=24 * HD * S * S, bytes_accessed=2 * S * S, transcendentals=0
        ),
        name="attend_back",
    )(v, kt, qt, do, o, linv, p, cos, sin)


def normalize_back(gradient, unit_rows, inverse, gain_row):
    scaled = gradient * gain_row
    gain_grad = jnp.sum(gradient * unit_rows, axis=0)
    input_grad = inverse * (
        scaled
        - jnp.mean(scaled, axis=-1, keepdims=True)
        - unit_rows * jnp.mean(scaled * unit_rows, axis=-1, keepdims=True)
    )
    return (input_grad, gain_grad)


def body(
    tokens, lengths, attn_gain, qkv_weight, proj_weight, ffn_gain, in_weight, out_weight, out_grad
):
    rows = tokens.shape[1]
    groups = lax.axis_size("seq")
    S = rows * groups
    heads = HEADS // groups
    me = lax.axis_index("seq")

    def swap(array, j):
        return lax.ppermute(array, "seq", [(i, i ^ j) for i in range(groups)])

    def exchange(chunks):
        return [chunks[0]] + [swap(chunks[j], j) for j in range(1, groups)]

    def relative(array, axis):
        return [lax.dynamic_index_in_dim(array, me ^ j, axis, False) for j in range(groups)]

    def gather(array):
        return lax.all_gather(array, "fsdp", axis=0, tiled=True)

    x0 = tokens[0]
    blocks = [x0]
    step = 1
    while step < groups:
        blocks = blocks + [swap(b, step) for b in blocks]
        step *= 2

    own_columns = lax.dynamic_index_in_dim(
        qkv_weight.reshape(-1, 3, groups, heads * HD), me, 2, False
    ).reshape(-1, 3 * heads * HD)
    first = gather(jnp.concatenate([own_columns, attn_gain[:, None]], axis=1))
    own_full = first[:, : 3 * heads * HD].reshape(D, 3, heads, HD)
    gain_one = first[:, 3 * heads * HD].astype(f32)[None, :]
    turned = jnp.concatenate([-own_full[..., HD // 2 :], own_full[..., : HD // 2]], axis=-1)
    turned = jnp.concatenate([turned[:, :2], jnp.zeros_like(turned[:, :1])], axis=1)
    w_ext = (
        jnp.concatenate([own_full, turned], axis=-1).transpose(0, 2, 1, 3).reshape(D, heads * 384)
    )

    half = HD // 2
    frequency = rope_base ** (-(lax.iota(f32, half) * 2.0) / HD)
    starts = [(me ^ j) * rows for j in range(groups)]
    positions = jnp.concatenate([s + lax.iota(jnp.int32, rows) for s in starts]).astype(f32)
    angles = frequency[:, None] * positions[None, :]
    cosine, sine = jnp.cos(angles), jnp.sin(angles)
    cos_t = jnp.concatenate([cosine, cosine], axis=0)
    sin_t = jnp.concatenate([sine, sine], axis=0)
    cs = jnp.concatenate([cos_t, sin_t], axis=0).T

    carried = None
    for j in range(groups):
        info = jnp.stack([starts[j], lengths[0]]).astype(jnp.int32)
        carried = qkv_call(j, groups, info, blocks[j], gain_one, w_ext, cs, carried)
    normed, k, v, qt, kt, vt = carried

    proj_full = gather(proj_weight)
    gain_two = gather(ffn_gain).astype(f32)[None, :]
    in_full = gather(in_weight)
    out_full = gather(out_weight)
    qkv_full = gather(qkv_weight)

    kept = []
    mixed_parts = []
    for h in range(heads):
        p, o, ob, linv = attend(h, k, qt, vt, groups)
        kept.append((p, o, linv))
        mixed_parts += exchange([ob[j] for j in range(groups)])
    mixed_t = jnp.concatenate(mixed_parts, axis=0)
    proj_rel = jnp.stack(
        relative(proj_full.reshape(groups, heads, HD, D), 0), axis=1
    ).reshape(D, D)

    x = x0.astype(f32)
    hidden = x + dg(mixed_t, proj_rel, TN)
    unit_two, inverse_two = unit_rows_of(hidden)
    second_low = (unit_two * gain_two).astype(bf)
    gate_up = dg(second_low, in_full, NN)
    ff = gate_up.shape[1] // 2
    gate, up = gate_up[:, :ff], gate_up[:, ff:]
    bell = 0.5 * (1.0 + lax.erf(gate * 0.7071067811865476))
    gelu = gate * bell
    inner_low = (gelu * up).astype(bf)
    result = hidden + dg(inner_low, out_full, NN)
    dy_low = out_grad[0]
    cotangent = dy_low.astype(f32)
    d_inner = dg(dy_low, out_full, NT)
    slope = bell + gate * (jnp.exp(-0.5 * gate * gate) * 0.3989422804014327)
    d_gate_up = jnp.concatenate([d_inner * up * slope, d_inner * gelu], axis=1).astype(bf)
    d_second = dg(d_gate_up, in_full, NT)
    d_norm_two, grad_ffn_gain = normalize_back(d_second, unit_two, inverse_two, gain_two)
    d_hidden = cotangent + d_norm_two
    d_branch = d_hidden.astype(bf)
    d_heads = dg(proj_rel, d_branch, NT).astype(bf).reshape(heads, groups, HD, rows)
    d_mixed = [jnp.stack(exchange([d_heads[h, j] for j in range(groups)])) for h in range(heads)]

    grad_out = dg(inner_low, dy_low, TN)
    grad_in = dg(second_low, d_gate_up, TN)
    grad_proj = dg(mixed_t, d_branch, NN).reshape(heads, groups, HD, D)
    grad_proj = jnp.stack(relative(grad_proj, 1), axis=0).reshape(D, D)

    def over_seq(array):
        parts = array.astype(bf).reshape(array.shape[0], groups, -1)
        mine = relative(parts, 1)
        total = mine[0].astype(f32)
        for j in range(1, groups):
            total = total + swap(mine[j], j).astype(f32)
        return total.astype(bf)

    def to_owner(array):
        return lax.psum_scatter(array, "fsdp", scatter_dimension=0, tiled=True)

    wide = to_owner(over_seq(jnp.concatenate([grad_in, grad_proj], axis=1)))
    tall = to_owner(over_seq(grad_out))
    wide = lax.all_gather(wide, "seq", axis=1, tiled=True).astype(f32)
    out_weight_grad = lax.all_gather(tall, "seq", axis=1, tiled=True).astype(f32)
    in_weight_grad, proj_weight_grad = wide[:, : 2 * ff], wide[:, 2 * ff :]

    wt = qkv_full.T.reshape(3, groups, heads, HD, D)
    wt = jnp.stack(relative(wt, 1), axis=0)
    normed_blocks = normed.reshape(groups, rows, D)
    d_normed = jnp.zeros((rows, D), f32)
    qkv_parts = []
    for h in range(heads):
        p, o, linv = kept[h]
        d_own = attend_back(h, v, kt, qt, d_mixed[h], o, linv, p, cos_t, sin_t, groups)
        received = jnp.concatenate(exchange([d_own[j] for j in range(groups)]), axis=0)
        d_normed = d_normed + dg(received, wt[:, :, h].reshape(3 * groups * HD, D), TN)
        grad = jnp.einsum("jdp,jpf->fd", d_own, normed_blocks, preferred_element_type=f32)
        qkv_parts.append(to_owner(grad.astype(bf)))
    qkv_own = jnp.stack(qkv_parts)
    qkv_all = lax.all_gather(qkv_own, "seq", axis=0)
    qkv_weight_grad = (
        qkv_all.reshape(groups, heads, -1, 3, HD)
        .transpose(2, 3, 0, 1, 4)
        .reshape(-1, 3 * D)
        .astype(f32)
    )
    unit_one, inverse_one = unit_rows_of(x)
    d_norm_one, grad_attn_gain = normalize_back(d_normed, unit_one, inverse_one, gain_one)
    tokens_grad = d_hidden + d_norm_one
    gains = lax.psum(jnp.stack([grad_attn_gain, grad_ffn_gain]), ("seq", "fsdp"))
    shard = D // lax.axis_size("fsdp")
    gains = lax.dynamic_slice_in_dim(gains, lax.axis_index("fsdp") * shard, shard, 1)
    return (
        result.astype(bf)[None],
        tokens_grad[None],
        gains[0],
        qkv_weight_grad,
        proj_weight_grad,
        gains[1],
        in_weight_grad,
        out_weight_grad,
    )


def solution(mesh):
    in_specs = (
        P("fsdp", "seq", None),
        P("fsdp"),
        P("fsdp"),
        P("fsdp", None),
        P("fsdp", None),
        P("fsdp"),
        P("fsdp", None),
        P("fsdp", None),
        P("fsdp", "seq", None),
    )
    out_specs = (
        P("fsdp", "seq", None),
        P("fsdp", "seq", None),
        P("fsdp"),
        P("fsdp", None),
        P("fsdp", None),
        P("fsdp"),
        P("fsdp", None),
        P("fsdp", None),
    )
    return jax.shard_map(body, mesh=mesh, in_specs=in_specs, out_specs=out_specs, check_vma=False)
```

```python
import functools

import jax
import jax.numpy as jnp
from jax import lax
from jax.experimental import pallas as pl
from jax.experimental.pallas import tpu as pltpu
from jax.sharding import PartitionSpec as P

D = 768
HEADS = 12
HD = 64

epsilon = 1e-05
rope_base = 160000.0
masked_score = -1e30
LOG2E = 1.4426950408889634
LN2 = 0.6931471805599453

bf = jnp.bfloat16
f32 = jnp.float32
NN = ((1,), (0,))
NT = ((1,), (1,))
TN = ((0,), (0,))


def dg(a, b, dims):
    return lax.dot_general(a, b, (dims, ((), ())), preferred_element_type=f32)


def unit_rows_of(x):
    centred = x - jnp.mean(x, axis=-1, keepdims=True)
    inverse = lax.rsqrt(jnp.mean(centred * centred, axis=-1, keepdims=True) + epsilon)
    return centred * inverse, inverse


def qkv_kernel(heads, count, info_ref, x_ref, cos_ref, sin_ref, *refs):
    parts = refs[:count]
    n_ref, k_ref, v_ref, qt_ref, kt_ref, vt_ref, w_ref, g_ref = refs[-8:]
    rb = x_ref.shape[0]
    value_at = heads * 128

    @pl.when(pl.program_id(0) == 0)
    def _():
        shard = parts[0].shape[0]
        for j in range(count):
            start = pl.multiple_of((info_ref[2] ^ j) * shard, shard) if count > 1 else 0
            w_ref[pl.ds(start, shard), :] = parts[j][...]
        last = w_ref[:, w_ref.shape[1] - 128 :].astype(f32).T
        g_ref[...] = last[HD : HD + 8]

    unit, _ = unit_rows_of(x_ref[...].astype(f32))
    normed = (unit * g_ref[:1]).astype(bf)
    n_ref[...] = normed
    lane = lax.broadcasted_iota(jnp.int32, (rb, 128), 1)
    row = lax.broadcasted_iota(jnp.int32, (rb, 128), 0)
    position = info_ref[0] + pl.program_id(0) * rb + row
    bias = jnp.where(position < info_ref[1], 0.0, masked_score)
    key_tail = jnp.where(lane == HD, bias, 0.0)
    value_tail = jnp.where(lane < HD + 2, -1.0, 0.0)
    head_lane = lane < HD
    lower = (lane & (HD - 1)) < HD // 2
    one_row = jnp.where(lax.broadcasted_iota(jnp.int32, (HD, rb), 0) == 0, 1.0, 0.0).astype(bf)
    y = dg(normed, w_ref[...], NN)
    for h in range(heads):
        t = y[:, h * 128 : (h + 1) * 128]
        turned = jnp.where(lower, pltpu.roll(t, 128 - HD // 2, 1), pltpu.roll(t, HD // 2, 1))
        t = t * cos_ref[...] + turned * sin_ref[...]
        k_ref[h] = jnp.where(head_lane, pltpu.roll(t, HD, 1), key_tail).astype(bf)
        t = t.T.astype(bf)
        qt_ref[h, :HD] = t[:HD]
        qt_ref[h, HD:] = one_row
        kt_ref[h] = t[HD:]
    for h in range(heads):
        at = value_at + h // 2 * 128
        t = y[:, at : at + 128]
        turned = t if h % 2 == 0 else pltpu.roll(t, HD, 1)
        v_ref[h] = jnp.where(head_lane, turned, value_tail).astype(bf)
        if h % 2 == 0:
            t_rows = t.T.astype(bf)
        vt_ref[h, :HD] = t_rows[:HD] if h % 2 == 0 else t_rows[HD:]
        vt_ref[h, HD:] = one_row[:16]


def qkv_call(block, blocks, heads, info, x, cos, sin, parts, carried):
    rows = x.shape[0]
    S = rows * blocks
    rb = min(256, rows)
    steps = rows // rb
    width = parts[0].shape[1]
    at = lambda i: block * steps + i
    outs = (
        jax.ShapeDtypeStruct((S, D), bf),
        jax.ShapeDtypeStruct((heads, S, 128), bf),
        jax.ShapeDtypeStruct((heads, S, 128), bf),
        jax.ShapeDtypeStruct((heads, 128, S), bf),
        jax.ShapeDtypeStruct((heads, HD, S), bf),
        jax.ShapeDtypeStruct((heads, 80, S), bf),
    )
    in_specs = [
        pl.BlockSpec(memory_space=pltpu.SMEM),
        pl.BlockSpec((rb, D), lambda i: (i, 0)),
        pl.BlockSpec((rb, 128), lambda i: (at(i), 0)),
        pl.BlockSpec((rb, 128), lambda i: (at(i), 0)),
    ] + [pl.BlockSpec(part.shape, lambda i: (0, 0)) for part in parts]
    aliases = {}
    if carried is not None:
        first = len(in_specs)
        in_specs += [pl.BlockSpec(memory_space=pl.ANY)] * 6
        aliases = {first + n: n for n in range(6)}
    return pl.pallas_call(
        functools.partial(qkv_kernel, heads, len(parts)),
        grid=(steps,),
        out_shape=outs,
        in_specs=in_specs,
        out_specs=(
            pl.BlockSpec((rb, D), lambda i: (at(i), 0)),
            pl.BlockSpec((heads, rb, 128), lambda i: (0, at(i), 0)),
            pl.BlockSpec((heads, rb, 128), lambda i: (0, at(i), 0)),
            pl.BlockSpec((heads, 128, rb), lambda i: (0, 0, at(i))),
            pl.BlockSpec((heads, HD, rb), lambda i: (0, 0, at(i))),
            pl.BlockSpec((heads, 80, rb), lambda i: (0, 0, at(i))),
        ),
        scratch_shapes=[pltpu.VMEM((D, width), bf), pltpu.VMEM((8, D), f32)],
        input_output_aliases=aliases,
        compiler_params=pltpu.CompilerParams(vmem_limit_bytes=48 * 2**20),
        cost_estimate=pl.CostEstimate(
            flops=4 * rows * D * width, bytes_accessed=rows * 8192, transcendentals=0
        ),
        name="qkv",
    )(info, x, cos, sin, *parts, *(carried or ()))


def attend_kernel(kc, k_ref, q_ref, v_ref, p_ref, o_ref, ob_ref, linv_ref, s_ref):
    rows = k_ref.shape[1]
    bq = q_ref.shape[2]
    q = q_ref[0]
    m = jnp.full((8, bq), -jnp.inf, f32)
    for c in range(rows // kc):
        at = slice(c * kc, (c + 1) * kc)
        s = dg(k_ref[0, at, :], q, NN)
        s_ref[at, :] = s
        m = jnp.maximum(m, jnp.max(s.reshape(kc // 8, 8, bq), axis=0))
    m = jnp.max(m, axis=0, keepdims=True)
    acc = jnp.zeros((v_ref.shape[1], bq), f32)
    for c in range(rows // kc):
        at = slice(c * kc, (c + 1) * kc)
        p = jnp.exp2(s_ref[at, :] - m).astype(bf)
        p_ref[0, at, :] = p
        acc = acc + dg(v_ref[0, :, at], p, NN)
    linv = 1.0 / acc[HD : HD + 1, :]
    o = acc[:HD, :] * linv
    o_ref[...] = o
    ob_ref[0] = o.astype(bf)
    linv_ref[0] = linv


def attend(h, k, qt, vt, groups, bq=512, kc=512):
    S = k.shape[1]
    nq = S // bq
    per = nq // groups
    return pl.pallas_call(
        functools.partial(attend_kernel, kc),
        grid=(nq,),
        out_shape=(
            jax.ShapeDtypeStruct((nq, S, bq), bf),
            jax.ShapeDtypeStruct((HD, S), f32),
            jax.ShapeDtypeStruct((groups, HD, S // groups), bf),
            jax.ShapeDtypeStruct((nq, 1, bq), f32),
        ),
        in_specs=[
            pl.BlockSpec((1, S, 128), lambda i: (h, 0, 0)),
            pl.BlockSpec((1, 128, bq), lambda i: (h, 0, i)),
            pl.BlockSpec((1, 80, S), lambda i: (h, 0, 0)),
        ],
        out_specs=(
            pl.BlockSpec((1, S, bq), lambda i: (i, 0, 0)),
            pl.BlockSpec((HD, bq), lambda i: (0, i)),
            pl.BlockSpec((1, HD, bq), lambda i: (i // per, 0, i % per)),
            pl.BlockSpec((1, 1, bq), lambda i: (i, 0, 0)),
        ),
        scratch_shapes=[pltpu.VMEM((S, bq), f32)],
        compiler_params=pltpu.CompilerParams(vmem_limit_bytes=48 * 2**20),
        cost_estimate=pl.CostEstimate(
            flops=16 * HD * S * S, bytes_accessed=2 * S * S, transcendentals=S * S
        ),
        name="attend",
    )(k, qt, vt)


def attend_back_kernel(
    kc, nq, per, v_ref, kt_ref, q_ref, o_ref, linv_ref, p_ref, cos_ref, sin_ref, *refs
):
    out_ref, acc_ref, do_ref = refs[-3:]
    i = pl.program_id(0)
    rows = v_ref.shape[1]
    bq = q_ref.shape[2]

    @pl.when(i == 0)
    def _():
        acc_ref[...] = jnp.zeros_like(acc_ref)
        for j in range(len(refs) - 3):
            do_ref[j] = refs[j][...]

    do = do_ref[i // per, :, pl.ds(pl.multiple_of((i % per) * bq, bq), bq)]
    dop = (do.astype(f32) * linv_ref[0]).astype(bf)
    delta = jnp.sum(dop.astype(f32) * o_ref[...], axis=0, keepdims=True)
    high = delta.astype(bf).astype(f32)
    r = lax.broadcasted_iota(jnp.int32, (16, bq), 0)
    tail = jnp.where(r == 0, high, jnp.where(r == 1, delta - high, 0.0)).astype(bf)
    doe = jnp.concatenate([dop, tail, jnp.zeros((128 - HD - 16, bq), bf)], axis=0)
    zero = jnp.zeros((HD, bq), bf)
    right_v = jnp.concatenate([dop, zero], axis=0)
    right_k = jnp.concatenate([zero, q_ref[0, :HD, :]], axis=0)
    dq = jnp.zeros((HD, bq), f32)
    for c in range(rows // kc):
        at = slice(c * kc, (c + 1) * kc)
        p = p_ref[0, at, :]
        ds = p * dg(v_ref[0, at, :], doe, NN).astype(bf)
        acc_ref[at, :] = acc_ref[at, :] + dg(p, right_v, NT) + dg(ds, right_k, NT)
        dq = dq + dg(kt_ref[0, :, at], ds, NN)
    dq = dq * HD**-0.5
    turned = jnp.concatenate([dq[HD // 2 :], -dq[: HD // 2]], axis=0)
    here = pl.ds(pl.multiple_of(i * bq, bq), bq)
    dq = dq * cos_ref[:, here] + turned * sin_ref[:, here]
    out_ref[i // per, :HD, pl.ds(pl.multiple_of((i % per) * bq, bq), bq)] = dq.astype(bf)

    @pl.when(i == nq - 1)
    def _():
        groups = out_ref.shape[0]
        width = rows // groups
        for j in range(groups):
            at = slice(j * width, (j + 1) * width)
            t = acc_ref[at, :].T
            dk = t[HD:] * LN2
            turned_k = jnp.concatenate([dk[HD // 2 :], -dk[: HD // 2]], axis=0)
            dk = dk * cos_ref[:, at] + turned_k * sin_ref[:, at]
            out_ref[j, HD : 2 * HD] = dk.astype(bf)
            out_ref[j, 2 * HD :] = t[:HD].astype(bf)


def attend_back(h, v, kt, qt, do, o, linv, p, cos, sin, groups, bq=512, kc=512):
    S = v.shape[1]
    nq = S // bq
    per = nq // groups
    return pl.pallas_call(
        functools.partial(attend_back_kernel, kc, nq, per),
        grid=(nq,),
        out_shape=jax.ShapeDtypeStruct((groups, 3 * HD, S // groups), bf),
        in_specs=[
            pl.BlockSpec((1, S, 128), lambda i: (h, 0, 0)),
            pl.BlockSpec((1, HD, S), lambda i: (h, 0, 0)),
            pl.BlockSpec((1, 128, bq), lambda i: (h, 0, i)),
            pl.BlockSpec((HD, bq), lambda i: (0, i)),
            pl.BlockSpec((1, 1, bq), lambda i: (i, 0, 0)),
            pl.BlockSpec((1, S, bq), lambda i: (i, 0, 0)),
            pl.BlockSpec((HD, S), lambda i: (0, 0)),
            pl.BlockSpec((HD, S), lambda i: (0, 0)),
        ]
        + [pl.BlockSpec((HD, S // groups), lambda i: (0, 0))] * groups,
        out_specs=pl.BlockSpec((groups, 3 * HD, S // groups), lambda i: (0, 0, 0)),
        scratch_shapes=[pltpu.VMEM((S, 128), f32), pltpu.VMEM((groups, HD, S // groups), bf)],
        compiler_params=pltpu.CompilerParams(vmem_limit_bytes=48 * 2**20),
        cost_estimate=pl.CostEstimate(
            flops=24 * HD * S * S, bytes_accessed=2 * S * S, transcendentals=0
        ),
        name="attend_back",
    )(v, kt, qt, o, linv, p, cos, sin, *do)


def normalize_back(gradient, unit_rows, inverse, gain_row):
    scaled = gradient * gain_row
    return inverse * (
        scaled
        - jnp.mean(scaled, axis=-1, keepdims=True)
        - unit_rows * jnp.mean(scaled * unit_rows, axis=-1, keepdims=True)
    )


def middle_kernel(
    groups, heads, ff, info_ref, x_ref, dy_ref, w_ref, out_w_ref, *refs
):
    count = groups * heads
    chunks = refs[:count]
    (result_ref, dh_ref, dheads_ref, mixed_ref, second_ref, dgu_ref, inner_ref, branch_ref,
     g_ref, t_ref) = refs[count:]
    width = heads * HD
    me = info_ref[0]

    @pl.when(pl.program_id(0) == 0)
    def _():
        g_ref[...] = w_ref[:, 2 * ff + D :].astype(f32).T[:8]

    for h in range(heads):
        for j in range(groups):
            start = pl.multiple_of((me ^ j) * width + h * HD, HD)
            mixed_ref[pl.ds(start, HD), :] = chunks[h * groups + j][...]
    gain = g_ref[:1]
    proj = w_ref[:, 2 * ff : 2 * ff + D]
    hidden = x_ref[...].astype(f32) + dg(mixed_ref[...], proj, TN)
    unit, inverse = unit_rows_of(hidden)
    second = (unit * gain).astype(bf)
    second_ref[...] = second
    dy = dy_ref[...]
    result = hidden
    d_second = jnp.zeros_like(hidden)
    step = 384
    for c in range(ff // step):
        a = slice(c * step, (c + 1) * step)
        b = slice(ff + c * step, ff + (c + 1) * step)
        gate = dg(second, w_ref[:, a], NN)
        up = dg(second, w_ref[:, b], NN)
        d_inner = dg(dy, out_w_ref[a, :], NT)
        bell = 0.5 + 0.5 * lax.erf(gate * 0.7071067811865476)
        gelu = gate * bell
        inner = (gelu * up).astype(bf)
        inner_ref[:, a] = inner
        result = result + dg(inner, out_w_ref[a, :], NN)
        slope = bell + gate * (jnp.exp(-0.5 * gate * gate) * 0.3989422804014327)
        d_gate = (d_inner * up * slope).astype(bf)
        d_up = (d_inner * gelu).astype(bf)
        dgu_ref[:, a] = d_gate
        dgu_ref[:, b] = d_up
        d_second = d_second + dg(d_gate, w_ref[:, a], NT) + dg(d_up, w_ref[:, b], NT)
    result_ref[...] = result.astype(bf)
    d_hidden = dy.astype(f32) + normalize_back(d_second, unit, inverse, gain)
    dh_ref[...] = d_hidden
    branch = d_hidden.astype(bf)
    branch_ref[...] = branch
    t_ref[...] = dg(proj, branch, NT).astype(bf)
    for h in range(heads):
        for j in range(groups):
            start = pl.multiple_of((me ^ j) * width + h * HD, HD)
            dheads_ref[h, j] = t_ref[pl.ds(start, HD), :]


def middle(groups, heads, info, x, dy, wide, out_w, chunks):
    rows = x.shape[0]
    ff = out_w.shape[0]
    rb = min(256, rows)
    by_row = lambda i: (i, 0)
    by_column = lambda i: (0, i)
    whole = lambda i: (0, 0)
    return pl.pallas_call(
        functools.partial(middle_kernel, groups, heads, ff),
        grid=(rows // rb,),
        out_shape=(
            jax.ShapeDtypeStruct((rows, D), bf),
            jax.ShapeDtypeStruct((rows, D), f32),
            jax.ShapeDtypeStruct((heads, groups, HD, rows), bf),
            jax.ShapeDtypeStruct((D, rows), bf),
            jax.ShapeDtypeStruct((rows, D), bf),
            jax.ShapeDtypeStruct((rows, 2 * ff), bf),
            jax.ShapeDtypeStruct((rows, ff), bf),
            jax.ShapeDtypeStruct((rows, D), bf),
        ),
        in_specs=[
            pl.BlockSpec(memory_space=pltpu.SMEM),
            pl.BlockSpec((rb, D), by_row),
            pl.BlockSpec((rb, D), by_row),
            pl.BlockSpec(wide.shape, whole, pipeline_mode=pl.Buffered(1)),
            pl.BlockSpec(out_w.shape, whole, pipeline_mode=pl.Buffered(1)),
        ]
        + [pl.BlockSpec((HD, rb), by_column)] * (groups * heads),
        out_specs=(
            pl.BlockSpec((rb, D), by_row),
            pl.BlockSpec((rb, D), by_row),
            pl.BlockSpec((heads, groups, HD, rb), lambda i: (0, 0, 0, i)),
            pl.BlockSpec((D, rb), by_column),
            pl.BlockSpec((rb, D), by_row),
            pl.BlockSpec((rb, 2 * ff), by_row),
            pl.BlockSpec((rb, ff), by_row),
            pl.BlockSpec((rb, D), by_row),
        ),
        scratch_shapes=[pltpu.VMEM((8, D), f32), pltpu.VMEM((D, rb), bf)],
        compiler_params=pltpu.CompilerParams(vmem_limit_bytes=48 * 2**20),
        cost_estimate=pl.CostEstimate(
            flops=rows * D * (14 * ff + 4 * D), bytes_accessed=30 * 2**20, transcendentals=rows * ff
        ),
        name="middle",
    )(info, x, dy, wide, out_w, *chunks)


def last_kernel(groups, heads, info_ref, x_ref, dh_ref, w_ref, *refs):
    count = groups * heads
    out_ref, dp_ref, g_ref = refs[count:]
    me = info_ref[0]

    @pl.when(pl.program_id(0) == 0)
    def _():
        g_ref[...] = w_ref[:, 3 * D :].astype(f32).T[:8]

    width = heads * HD
    for h in range(heads):
        for j in range(groups):
            for t in range(3):
                start = pl.multiple_of(t * D + (me ^ j) * width + h * HD, HD)
                dp_ref[pl.ds(start, HD), :] = refs[h * groups + j][t * HD : (t + 1) * HD, :]
    d_normed = dg(w_ref[:, : 3 * D], dp_ref[...], NN).T
    unit, inverse = unit_rows_of(x_ref[...].astype(f32))
    out_ref[...] = dh_ref[...] + normalize_back(d_normed, unit, inverse, g_ref[:1])


def last(groups, heads, info, x, d_hidden, w, chunks):
    rows = x.shape[0]
    rb = min(256, rows)
    by_row = lambda i: (i, 0)
    whole = lambda i: (0, 0)
    return pl.pallas_call(
        functools.partial(last_kernel, groups, heads),
        grid=(rows // rb,),
        out_shape=jax.ShapeDtypeStruct((rows, D), f32),
        in_specs=[
            pl.BlockSpec(memory_space=pltpu.SMEM),
            pl.BlockSpec((rb, D), by_row),
            pl.BlockSpec((rb, D), by_row),
            pl.BlockSpec(w.shape, whole, pipeline_mode=pl.Buffered(1)),
        ]
        + [pl.BlockSpec((3 * HD, rb), lambda i: (0, i))] * (groups * heads),
        out_specs=pl.BlockSpec((rb, D), by_row),
        scratch_shapes=[pltpu.VMEM((3 * D, rb), bf), pltpu.VMEM((8, D), f32)],
        compiler_params=pltpu.CompilerParams(vmem_limit_bytes=48 * 2**20),
        cost_estimate=pl.CostEstimate(
            flops=6 * rows * D * D, bytes_accessed=16 * 2**20, transcendentals=0
        ),
        name="last",
    )(info, x, d_hidden, w, *chunks)


def body(
    tokens, lengths, attn_gain, qkv_weight, proj_weight, ffn_gain, in_weight, out_weight, out_grad
):
    rows = tokens.shape[1]
    groups = lax.axis_size("seq")
    shards = lax.axis_size("fsdp")
    heads = HEADS // groups
    shard = D // shards
    me = lax.axis_index("seq")
    owner = lax.axis_index("fsdp")

    def swap(array, j, axis="seq"):
        size = lax.axis_size(axis)
        return lax.ppermute(array, axis, [(i, i ^ j) for i in range(size)])

    def exchange(chunks):
        return [chunks[0]] + [swap(chunks[j], j) for j in range(1, groups)]

    def relative(array, axis):
        return [lax.dynamic_index_in_dim(array, me ^ j, axis, False) for j in range(groups)]

    def gather(array):
        return lax.all_gather(array, "fsdp", axis=0, tiled=True)

    own = lax.dynamic_index_in_dim(
        qkv_weight.reshape(shard, 3, groups, heads, HD), me, 2, False
    )
    pieces = []
    for h in range(heads):
        pieces += [own[:, 0, h], own[:, 1, h]]
    pieces += [own[:, 2, h] for h in range(heads)] + [attn_gain[:, None]]
    used = 3 * heads * HD + 1
    pieces.append(jnp.zeros((shard, -used % 128), bf))
    own = jnp.concatenate(pieces, axis=1)
    if shards <= 8:
        parts = [own] + [swap(own, j, "fsdp") for j in range(1, shards)]
    else:
        parts = [gather(own)]

    x0 = tokens[0]
    blocks = [x0]
    step = 1
    while step < groups:
        blocks = blocks + [swap(b, step) for b in blocks]
        step *= 2

    half = HD // 2
    frequency = rope_base ** (-(lax.iota(f32, half) * 2.0) / HD)
    starts = [(me ^ j) * rows for j in range(groups)]
    positions = jnp.concatenate([s + lax.iota(jnp.int32, rows) for s in starts]).astype(f32)
    angles = frequency[:, None] * positions[None, :]
    cosine, sine = jnp.cos(angles), jnp.sin(angles)
    cos_t = jnp.concatenate([cosine, cosine], axis=0)
    sin_t = jnp.concatenate([sine, sine], axis=0)
    scale = HD**-0.5 * LOG2E
    cos_rows = jnp.concatenate([cos_t * scale, cos_t], axis=0).T
    signed = jnp.concatenate([-sine, sine], axis=0)
    sin_rows = jnp.concatenate([signed * scale, signed], axis=0).T

    carried = None
    for j in range(groups):
        info = jnp.stack([starts[j], lengths[0], owner]).astype(jnp.int32)
        carried = qkv_call(j, groups, heads, info, blocks[j], cos_rows, sin_rows, parts, carried)
    normed, k, v, qt, kt, vt = carried

    ff2 = in_weight.shape[1]
    wide_shard = jnp.concatenate(
        [in_weight, proj_weight, ffn_gain[:, None], jnp.zeros((shard, 127), bf)], axis=1
    )
    wide_shard, out_shard, qkv_shard, gain_shard, _ = lax.optimization_barrier(
        (wide_shard, out_weight, qkv_weight, attn_gain, parts[-1])
    )
    wide = gather(wide_shard)
    out_full = gather(out_shard)
    qkv_full = gather(jnp.concatenate([qkv_shard, jnp.tile(gain_shard[:, None], (1, 128))], axis=1))

    kept = []
    chunks = []
    for h in range(heads):
        p, o, ob, linv = attend(h, k, qt, vt, groups)
        kept.append((p, o, linv))
        chunks += exchange([ob[j] for j in range(groups)])

    place = jnp.stack([me]).astype(jnp.int32)
    dy = out_grad[0]
    result, d_hidden, d_heads, mixed_t, second, d_gate_up, inner, branch = middle(
        groups, heads, place, x0, dy, wide, out_full, chunks
    )
    d_mixed = [exchange([d_heads[h, j] for j in range(groups)]) for h in range(heads)]

    def over_seq(array):
        parts = array.astype(bf).reshape(array.shape[0], groups, -1)
        mine = relative(parts, 1)
        total = mine[0].astype(f32)
        for j in range(1, groups):
            total = total + swap(mine[j], j).astype(f32)
        return total.astype(bf)

    def to_owner(array):
        parts = array.reshape(shards, array.shape[0] // shards, -1)
        parts = lax.all_to_all(parts, "fsdp", split_axis=0, concat_axis=0, tiled=True)
        return jnp.sum(parts.astype(f32), axis=0).astype(bf)

    def from_seq(array):
        parts = jnp.stack([array] + [swap(array, j) for j in range(1, groups)])
        return relative(parts, 0)

    grad_out = dg(inner, dy, TN)
    grad_in = dg(second, d_gate_up, TN)
    grad_proj = dg(mixed_t, branch, NN)
    part_in = to_owner(over_seq(jnp.concatenate([grad_in, grad_proj], axis=1)))
    part_out = to_owner(over_seq(grad_out))
    wide_grad = jnp.concatenate(from_seq(part_in), axis=1).astype(f32)
    out_weight_grad = jnp.concatenate(from_seq(part_out), axis=1).astype(f32)
    in_weight_grad, proj_weight_grad = wide_grad[:, :ff2], wide_grad[:, ff2:]

    normed_blocks = normed.reshape(groups, rows, D)
    received = []
    qkv_parts = []
    for h in range(heads):
        p, o, linv = kept[h]
        d_own = attend_back(h, v, kt, qt, d_mixed[h], o, linv, p, cos_t, sin_t, groups)
        received += exchange([d_own[j] for j in range(groups)])
        grad = jnp.einsum("jdp,jpf->fd", d_own, normed_blocks, preferred_element_type=f32)
        qkv_parts.append(to_owner(grad.astype(bf)))
    qkv_all = jnp.stack(from_seq(jnp.stack(qkv_parts)))
    qkv_weight_grad = (
        qkv_all.reshape(groups, heads, shard, 3, HD)
        .transpose(2, 3, 0, 1, 4)
        .reshape(shard, 3 * D)
        .astype(f32)
    )
    tokens_grad = last(groups, heads, place, x0, d_hidden, qkv_full, received)

    def gain_grad(weight, grad, gain):
        return jnp.sum(weight.astype(f32) * grad, axis=1) / gain.astype(f32)

    return (
        result[None],
        tokens_grad[None],
        gain_grad(qkv_weight, qkv_weight_grad, attn_gain),
        qkv_weight_grad,
        proj_weight_grad,
        gain_grad(in_weight, in_weight_grad, ffn_gain),
        in_weight_grad,
        out_weight_grad,
    )


def solution(mesh):
    in_specs = (
        P("fsdp", "seq", None),
        P("fsdp"),
        P("fsdp"),
        P("fsdp", None),
        P("fsdp", None),
        P("fsdp"),
        P("fsdp", None),
        P("fsdp", None),
        P("fsdp", "seq", None),
    )
    out_specs = (
        P("fsdp", "seq", None),
        P("fsdp", "seq", None),
        P("fsdp"),
        P("fsdp", None),
        P("fsdp", None),
        P("fsdp"),
        P("fsdp", None),
        P("fsdp", None),
    )
    return jax.shard_map(body, mesh=mesh, in_specs=in_specs, out_specs=out_specs, check_vma=False)
```

```python
import functools

import jax
import jax.numpy as jnp
from jax import lax
from jax.experimental import pallas as pl
from jax.experimental.pallas import tpu as pltpu
from jax.sharding import PartitionSpec as P

D = 768
HEADS = 12
HD = 64

epsilon = 1e-05
rope_base = 160000.0
masked_score = -1e30
LOG2E = 1.4426950408889634
LN2 = 0.6931471805599453

bf = jnp.bfloat16
f32 = jnp.float32
NN = ((1,), (0,))
NT = ((1,), (1,))
TN = ((0,), (0,))


def dg(a, b, dims):
    return lax.dot_general(a, b, (dims, ((), ())), preferred_element_type=f32)


def unit_rows_of(x):
    centred = x - jnp.mean(x, axis=-1, keepdims=True)
    inverse = lax.rsqrt(jnp.mean(centred * centred, axis=-1, keepdims=True) + epsilon)
    return centred * inverse, inverse


def qkv_kernel(heads, count, info_ref, x_ref, cos_ref, sin_ref, *refs):
    parts = refs[:count]
    n_ref, k_ref, v_ref, qt_ref, kt_ref, vt_ref, w_ref, g_ref = refs[-8:]
    rb = x_ref.shape[0]
    value_at = heads * 128

    @pl.when(pl.program_id(0) == 0)
    def _():
        shard = parts[0].shape[0]
        for j in range(count):
            start = pl.multiple_of((info_ref[2] ^ j) * shard, shard) if count > 1 else 0
            w_ref[pl.ds(start, shard), :] = parts[j][...]
        last = w_ref[:, w_ref.shape[1] - 128 :].astype(f32).T
        g_ref[...] = last[HD : HD + 8]

    unit, _ = unit_rows_of(x_ref[...].astype(f32))
    normed = (unit * g_ref[:1]).astype(bf)
    n_ref[...] = normed
    lane = lax.broadcasted_iota(jnp.int32, (rb, 128), 1)
    row = lax.broadcasted_iota(jnp.int32, (rb, 128), 0)
    position = info_ref[0] + pl.program_id(0) * rb + row
    bias = jnp.where(position < info_ref[1], 0.0, masked_score)
    key_tail = jnp.where(lane == HD, bias, 0.0)
    value_tail = jnp.where(lane < HD + 2, -1.0, 0.0)
    head_lane = lane < HD
    lower = (lane & (HD - 1)) < HD // 2
    one_row = jnp.where(lax.broadcasted_iota(jnp.int32, (HD, rb), 0) == 0, 1.0, 0.0).astype(bf)
    y = dg(normed, w_ref[...], NN)
    for h in range(heads):
        t = y[:, h * 128 : (h + 1) * 128]
        turned = jnp.where(lower, pltpu.roll(t, 128 - HD // 2, 1), pltpu.roll(t, HD // 2, 1))
        t = t * cos_ref[...] + turned * sin_ref[...]
        k_ref[h] = jnp.where(head_lane, pltpu.roll(t, HD, 1), key_tail).astype(bf)
        t = t.T.astype(bf)
        qt_ref[h, :HD] = t[:HD]
        qt_ref[h, HD:] = one_row
        kt_ref[h] = t[HD:]
    for h in range(heads):
        at = value_at + h // 2 * 128
        t = y[:, at : at + 128]
        turned = t if h % 2 == 0 else pltpu.roll(t, HD, 1)
        v_ref[h] = jnp.where(head_lane, turned, value_tail).astype(bf)
        if h % 2 == 0:
            t_rows = t.T.astype(bf)
        vt_ref[h, :HD] = t_rows[:HD] if h % 2 == 0 else t_rows[HD:]
        vt_ref[h, HD:] = one_row[:16]


def qkv_call(block, blocks, heads, info, x, cos, sin, parts, carried):
    rows = x.shape[0]
    S = rows * blocks
    rb = min(256, rows)
    steps = rows // rb
    width = parts[0].shape[1]
    at = lambda i: block * steps + i
    outs = (
        jax.ShapeDtypeStruct((S, D), bf),
        jax.ShapeDtypeStruct((heads, S, 128), bf),
        jax.ShapeDtypeStruct((heads, S, 128), bf),
        jax.ShapeDtypeStruct((heads, 128, S), bf),
        jax.ShapeDtypeStruct((heads, HD, S), bf),
        jax.ShapeDtypeStruct((heads, 80, S), bf),
    )
    in_specs = [
        pl.BlockSpec(memory_space=pltpu.SMEM),
        pl.BlockSpec((rb, D), lambda i: (i, 0)),
        pl.BlockSpec((rb, 128), lambda i: (at(i), 0)),
        pl.BlockSpec((rb, 128), lambda i: (at(i), 0)),
    ] + [pl.BlockSpec(part.shape, lambda i: (0, 0)) for part in parts]
    aliases = {}
    if carried is not None:
        first = len(in_specs)
        in_specs += [pl.BlockSpec(memory_space=pl.ANY)] * 6
        aliases = {first + n: n for n in range(6)}
    return pl.pallas_call(
        functools.partial(qkv_kernel, heads, len(parts)),
        grid=(steps,),
        out_shape=outs,
        in_specs=in_specs,
        out_specs=(
            pl.BlockSpec((rb, D), lambda i: (at(i), 0)),
            pl.BlockSpec((heads, rb, 128), lambda i: (0, at(i), 0)),
            pl.BlockSpec((heads, rb, 128), lambda i: (0, at(i), 0)),
            pl.BlockSpec((heads, 128, rb), lambda i: (0, 0, at(i))),
            pl.BlockSpec((heads, HD, rb), lambda i: (0, 0, at(i))),
            pl.BlockSpec((heads, 80, rb), lambda i: (0, 0, at(i))),
        ),
        scratch_shapes=[pltpu.VMEM((D, width), bf), pltpu.VMEM((8, D), f32)],
        input_output_aliases=aliases,
        compiler_params=pltpu.CompilerParams(vmem_limit_bytes=48 * 2**20),
        cost_estimate=pl.CostEstimate(
            flops=4 * rows * D * width, bytes_accessed=rows * 8192, transcendentals=0
        ),
        name="qkv",
    )(info, x, cos, sin, *parts, *(carried or ()))


def attend_kernel(kc, k_ref, q_ref, v_ref, p_ref, o_ref, ob_ref, linv_ref, s_ref):
    rows = k_ref.shape[1]
    bq = q_ref.shape[2]
    q = q_ref[0]
    m = jnp.full((8, bq), -jnp.inf, f32)
    for c in range(rows // kc):
        at = slice(c * kc, (c + 1) * kc)
        s = dg(k_ref[0, at, :], q, NN)
        s_ref[at, :] = s
        m = jnp.maximum(m, jnp.max(s.reshape(kc // 8, 8, bq), axis=0))
    m = jnp.max(m, axis=0, keepdims=True)
    acc = jnp.zeros((v_ref.shape[1], bq), f32)
    for c in range(rows // kc):
        at = slice(c * kc, (c + 1) * kc)
        p = jnp.exp2(s_ref[at, :] - m).astype(bf)
        p_ref[0, at, :] = p
        acc = acc + dg(v_ref[0, :, at], p, NN)
    linv = 1.0 / acc[HD : HD + 1, :]
    o = acc[:HD, :] * linv
    o_ref[...] = o
    ob_ref[0] = o.astype(bf)
    linv_ref[0] = linv


def attend(h, k, qt, vt, groups, bq=512, kc=512):
    S = k.shape[1]
    nq = S // bq
    per = nq // groups
    return pl.pallas_call(
        functools.partial(attend_kernel, kc),
        grid=(nq,),
        out_shape=(
            jax.ShapeDtypeStruct((nq, S, bq), bf),
            jax.ShapeDtypeStruct((HD, S), f32),
            jax.ShapeDtypeStruct((groups, HD, S // groups), bf),
            jax.ShapeDtypeStruct((nq, 1, bq), f32),
        ),
        in_specs=[
            pl.BlockSpec((1, S, 128), lambda i: (h, 0, 0)),
            pl.BlockSpec((1, 128, bq), lambda i: (h, 0, i)),
            pl.BlockSpec((1, 80, S), lambda i: (h, 0, 0)),
        ],
        out_specs=(
            pl.BlockSpec((1, S, bq), lambda i: (i, 0, 0)),
            pl.BlockSpec((HD, bq), lambda i: (0, i)),
            pl.BlockSpec((1, HD, bq), lambda i: (i // per, 0, i % per)),
            pl.BlockSpec((1, 1, bq), lambda i: (i, 0, 0)),
        ),
        scratch_shapes=[pltpu.VMEM((S, bq), f32)],
        compiler_params=pltpu.CompilerParams(vmem_limit_bytes=58 * 2**20),
        cost_estimate=pl.CostEstimate(
            flops=16 * HD * S * S, bytes_accessed=2 * S * S, transcendentals=S * S
        ),
        name="attend",
    )(k, qt, vt)


def attend_back_kernel(
    kc, nq, per, v_ref, kt_ref, q_ref, o_ref, linv_ref, p_ref, cos_ref, sin_ref, n_ref, *refs
):
    out_ref, grad_ref, acc_ref, do_ref, held_ref, sem = refs[-6:]
    i = pl.program_id(0)
    rows = v_ref.shape[1]
    bq = q_ref.shape[2]
    groups = out_ref.shape[0]
    fetch = pltpu.make_async_copy(n_ref, held_ref, sem)

    @pl.when(i == 0)
    def _():
        fetch.start()
        acc_ref[...] = jnp.zeros_like(acc_ref)
        for j in range(groups):
            do_ref[j] = refs[j][...]

    do = do_ref[i // per, :, pl.ds(pl.multiple_of((i % per) * bq, bq), bq)]
    dop = (do.astype(f32) * linv_ref[0]).astype(bf)
    delta = jnp.sum(dop.astype(f32) * o_ref[...], axis=0, keepdims=True)
    high = delta.astype(bf).astype(f32)
    r = lax.broadcasted_iota(jnp.int32, (16, bq), 0)
    tail = jnp.where(r == 0, high, jnp.where(r == 1, delta - high, 0.0)).astype(bf)
    doe = jnp.concatenate([dop, tail, jnp.zeros((128 - HD - 16, bq), bf)], axis=0)
    zero = jnp.zeros((HD, bq), bf)
    right_v = jnp.concatenate([dop, zero], axis=0)
    right_k = jnp.concatenate([zero, q_ref[0, :HD, :]], axis=0)
    dq = jnp.zeros((HD, bq), f32)
    for c in range(rows // kc):
        at = slice(c * kc, (c + 1) * kc)
        p = p_ref[0, at, :]
        ds = p * dg(v_ref[0, at, :], doe, NN).astype(bf)
        acc_ref[at, :] = acc_ref[at, :] + dg(p, right_v, NT) + dg(ds, right_k, NT)
        dq = dq + dg(kt_ref[0, :, at], ds, NN)
    dq = dq * HD**-0.5
    turned = jnp.concatenate([dq[HD // 2 :], -dq[: HD // 2]], axis=0)
    here = pl.ds(pl.multiple_of(i * bq, bq), bq)
    dq = dq * cos_ref[:, here] + turned * sin_ref[:, here]
    out_ref[i // per, :HD, pl.ds(pl.multiple_of((i % per) * bq, bq), bq)] = dq.astype(bf)

    @pl.when(i == nq - 1)
    def _():
        fetch.wait()
        width = rows // groups
        grad = jnp.zeros((3 * HD, D), f32)
        for j in range(groups):
            at = slice(j * width, (j + 1) * width)
            t = acc_ref[at, :].T
            dk = t[HD:] * LN2
            turned_k = jnp.concatenate([dk[HD // 2 :], -dk[: HD // 2]], axis=0)
            dk = dk * cos_ref[:, at] + turned_k * sin_ref[:, at]
            out_ref[j, HD : 2 * HD] = dk.astype(bf)
            out_ref[j, 2 * HD :] = t[:HD].astype(bf)
            grad = grad + dg(out_ref[j], held_ref[at, :], NN)
        grad_ref[:, : 3 * HD] = grad.T.astype(bf)
        grad_ref[:, 3 * HD :] = jnp.zeros((D, HD), bf)


def attend_back(h, v, kt, qt, do, o, linv, p, cos, sin, normed, groups, place, after, bq=512, kc=512):
    S = v.shape[1]
    nq = S // bq
    per = nq // groups
    columns, column, earlier = place
    extra = list(after) if earlier is None else [earlier] + list(after)
    return pl.pallas_call(
        functools.partial(attend_back_kernel, kc, nq, per),
        grid=(nq,),
        out_shape=(
            jax.ShapeDtypeStruct((groups, 3 * HD, S // groups), bf),
            jax.ShapeDtypeStruct((D, columns), bf),
        ),
        in_specs=[
            pl.BlockSpec((1, S, 128), lambda i: (h, 0, 0)),
            pl.BlockSpec((1, HD, S), lambda i: (h, 0, 0)),
            pl.BlockSpec((1, 128, bq), lambda i: (h, 0, i)),
            pl.BlockSpec((HD, bq), lambda i: (0, i)),
            pl.BlockSpec((1, 1, bq), lambda i: (i, 0, 0)),
            pl.BlockSpec((1, S, bq), lambda i: (i, 0, 0)),
            pl.BlockSpec((HD, S), lambda i: (0, 0)),
            pl.BlockSpec((HD, S), lambda i: (0, 0)),
            pl.BlockSpec(memory_space=pl.ANY),
        ]
        + [pl.BlockSpec((HD, S // groups), lambda i: (0, 0))] * groups
        + [pl.BlockSpec(memory_space=pl.ANY)] * len(extra),
        out_specs=(
            pl.BlockSpec((groups, 3 * HD, S // groups), lambda i: (0, 0, 0)),
            pl.BlockSpec((D, 256), lambda i: (0, column)),
        ),
        scratch_shapes=[
            pltpu.VMEM((S, 128), f32),
            pltpu.VMEM((groups, HD, S // groups), bf),
            pltpu.VMEM((S, D), bf),
            pltpu.SemaphoreType.DMA,
        ],
        input_output_aliases={} if earlier is None else {9 + groups: 1},
        compiler_params=pltpu.CompilerParams(vmem_limit_bytes=58 * 2**20),
        cost_estimate=pl.CostEstimate(
            flops=24 * HD * S * S, bytes_accessed=2 * S * S, transcendentals=0
        ),
        name="attend_back",
    )(v, kt, qt, o, linv, p, cos, sin, normed, *do, *extra)


def normalize_back(gradient, unit_rows, inverse, gain_row):
    scaled = gradient * gain_row
    return inverse * (
        scaled
        - jnp.mean(scaled, axis=-1, keepdims=True)
        - unit_rows * jnp.mean(scaled * unit_rows, axis=-1, keepdims=True)
    )


def middle_kernel(
    groups, heads, ff, info_ref, x_ref, dy_ref, w_ref, out_w_ref, *refs
):
    count = groups * heads
    chunks = refs[:count]
    (result_ref, dh_ref, dheads_ref, mixed_ref, second_ref, dgu_ref, inner_ref, branch_ref,
     g_ref, t_ref) = refs[count:]
    width = heads * HD
    me = info_ref[0]

    @pl.when(pl.program_id(0) == 0)
    def _():
        g_ref[...] = w_ref[:, 2 * ff + D :].astype(f32).T[:8]

    for h in range(heads):
        for j in range(groups):
            start = pl.multiple_of((me ^ j) * width + h * HD, HD)
            mixed_ref[pl.ds(start, HD), :] = chunks[h * groups + j][...]
    gain = g_ref[:1]
    proj = w_ref[:, 2 * ff : 2 * ff + D]
    hidden = x_ref[...].astype(f32) + dg(mixed_ref[...], proj, TN)
    unit, inverse = unit_rows_of(hidden)
    second = (unit * gain).astype(bf)
    second_ref[...] = second
    dy = dy_ref[...]
    result = hidden
    d_second = jnp.zeros_like(hidden)
    step = 384
    for c in range(ff // step):
        a = slice(c * step, (c + 1) * step)
        b = slice(ff + c * step, ff + (c + 1) * step)
        gate = dg(second, w_ref[:, a], NN)
        up = dg(second, w_ref[:, b], NN)
        d_inner = dg(dy, out_w_ref[a, :], NT)
        bell = 0.5 + 0.5 * lax.erf(gate * 0.7071067811865476)
        gelu = gate * bell
        inner = (gelu * up).astype(bf)
        inner_ref[:, a] = inner
        result = result + dg(inner, out_w_ref[a, :], NN)
        slope = bell + gate * (jnp.exp(-0.5 * gate * gate) * 0.3989422804014327)
        d_gate = (d_inner * up * slope).astype(bf)
        d_up = (d_inner * gelu).astype(bf)
        dgu_ref[:, a] = d_gate
        dgu_ref[:, b] = d_up
        d_second = d_second + dg(d_gate, w_ref[:, a], NT) + dg(d_up, w_ref[:, b], NT)
    result_ref[...] = result.astype(bf)
    d_hidden = dy.astype(f32) + normalize_back(d_second, unit, inverse, gain)
    dh_ref[...] = d_hidden
    branch = d_hidden.astype(bf)
    branch_ref[...] = branch
    t_ref[...] = dg(proj, branch, NT).astype(bf)
    for h in range(heads):
        for j in range(groups):
            start = pl.multiple_of((me ^ j) * width + h * HD, HD)
            dheads_ref[h, j] = t_ref[pl.ds(start, HD), :]


def middle(groups, heads, info, x, dy, wide, out_w, chunks):
    rows = x.shape[0]
    ff = out_w.shape[0]
    rb = min(256, rows)
    by_row = lambda i: (i, 0)
    by_column = lambda i: (0, i)
    whole = lambda i: (0, 0)
    return pl.pallas_call(
        functools.partial(middle_kernel, groups, heads, ff),
        grid=(rows // rb,),
        out_shape=(
            jax.ShapeDtypeStruct((rows, D), bf),
            jax.ShapeDtypeStruct((rows, D), f32),
            jax.ShapeDtypeStruct((heads, groups, HD, rows), bf),
            jax.ShapeDtypeStruct((D, rows), bf),
            jax.ShapeDtypeStruct((rows, D), bf),
            jax.ShapeDtypeStruct((rows, 2 * ff), bf),
            jax.ShapeDtypeStruct((rows, ff), bf),
            jax.ShapeDtypeStruct((rows, D), bf),
        ),
        in_specs=[
            pl.BlockSpec(memory_space=pltpu.SMEM),
            pl.BlockSpec((rb, D), by_row),
            pl.BlockSpec((rb, D), by_row),
            pl.BlockSpec(wide.shape, whole, pipeline_mode=pl.Buffered(1)),
            pl.BlockSpec(out_w.shape, whole, pipeline_mode=pl.Buffered(1)),
        ]
        + [pl.BlockSpec((HD, rb), by_column)] * (groups * heads),
        out_specs=(
            pl.BlockSpec((rb, D), by_row),
            pl.BlockSpec((rb, D), by_row),
            pl.BlockSpec((heads, groups, HD, rb), lambda i: (0, 0, 0, i)),
            pl.BlockSpec((D, rb), by_column),
            pl.BlockSpec((rb, D), by_row),
            pl.BlockSpec((rb, 2 * ff), by_row),
            pl.BlockSpec((rb, ff), by_row),
            pl.BlockSpec((rb, D), by_row),
        ),
        scratch_shapes=[pltpu.VMEM((8, D), f32), pltpu.VMEM((D, rb), bf)],
        compiler_params=pltpu.CompilerParams(vmem_limit_bytes=48 * 2**20),
        cost_estimate=pl.CostEstimate(
            flops=rows * D * (14 * ff + 4 * D), bytes_accessed=30 * 2**20, transcendentals=rows * ff
        ),
        name="middle",
    )(info, x, dy, wide, out_w, *chunks)


def last_kernel(groups, heads, info_ref, x_ref, dh_ref, w_ref, *refs):
    count = groups * heads
    out_ref, dp_ref, g_ref = refs[count:]
    me = info_ref[0]

    @pl.when(pl.program_id(0) == 0)
    def _():
        g_ref[...] = w_ref[:, 3 * D :].astype(f32).T[:8]

    width = heads * HD
    for h in range(heads):
        for j in range(groups):
            for t in range(3):
                start = pl.multiple_of(t * D + (me ^ j) * width + h * HD, HD)
                dp_ref[pl.ds(start, HD), :] = refs[h * groups + j][t * HD : (t + 1) * HD, :]
    d_normed = dg(w_ref[:, : 3 * D], dp_ref[...], NN).T
    unit, inverse = unit_rows_of(x_ref[...].astype(f32))
    out_ref[...] = dh_ref[...] + normalize_back(d_normed, unit, inverse, g_ref[:1])


def last(groups, heads, info, x, d_hidden, w, chunks):
    rows = x.shape[0]
    rb = min(256, rows)
    by_row = lambda i: (i, 0)
    whole = lambda i: (0, 0)
    return pl.pallas_call(
        functools.partial(last_kernel, groups, heads),
        grid=(rows // rb,),
        out_shape=jax.ShapeDtypeStruct((rows, D), f32),
        in_specs=[
            pl.BlockSpec(memory_space=pltpu.SMEM),
            pl.BlockSpec((rb, D), by_row),
            pl.BlockSpec((rb, D), by_row),
            pl.BlockSpec(w.shape, whole, pipeline_mode=pl.Buffered(1)),
        ]
        + [pl.BlockSpec((3 * HD, rb), lambda i: (0, i))] * (groups * heads),
        out_specs=pl.BlockSpec((rb, D), by_row),
        scratch_shapes=[pltpu.VMEM((3 * D, rb), bf), pltpu.VMEM((8, D), f32)],
        compiler_params=pltpu.CompilerParams(vmem_limit_bytes=48 * 2**20),
        cost_estimate=pl.CostEstimate(
            flops=6 * rows * D * D, bytes_accessed=16 * 2**20, transcendentals=0
        ),
        name="last",
    )(info, x, d_hidden, w, *chunks)


def own_kernel(groups, heads, info_ref, w_ref, gain_ref, out_ref):
    for g in range(groups):

        @pl.when(info_ref[0] == g)
        def _():
            def piece(t, h):
                start = t * D + (g * heads + h) * HD
                return w_ref[:, start : start + HD]

            pieces = []
            for h in range(heads):
                pieces += [piece(0, h), piece(1, h)]
            pieces += [piece(2, h) for h in range(heads)] + [gain_ref[...]]
            missing = out_ref.shape[1] - 3 * heads * HD - 1
            pieces.append(jnp.zeros((w_ref.shape[0], missing), bf))
            out_ref[...] = jnp.concatenate(pieces, axis=1)


def own_columns(groups, heads, info, w, gain):
    width = (3 * heads * HD + 128) // 128 * 128
    return pl.pallas_call(
        functools.partial(own_kernel, groups, heads),
        out_shape=jax.ShapeDtypeStruct((w.shape[0], width), bf),
        in_specs=[
            pl.BlockSpec(memory_space=pltpu.SMEM),
            pl.BlockSpec(memory_space=pltpu.VMEM),
            pl.BlockSpec(memory_space=pltpu.VMEM),
        ],
        out_specs=pl.BlockSpec(memory_space=pltpu.VMEM),
        name="own_columns",
    )(info, w, gain)


def tables_kernel(cos_ref, sin_ref, cos_rows_ref, sin_rows_ref, cos_t_ref, sin_t_ref):
    c, s = cos_ref[...], sin_ref[...]
    cos_t_ref[...] = jnp.concatenate([c, c], axis=0)
    sin_t_ref[...] = jnp.concatenate([s, s], axis=0)
    scale = HD**-0.5 * LOG2E
    cos_rows_ref[...] = jnp.concatenate([c * scale, c * scale, c, c], axis=0).T
    sin_rows_ref[...] = jnp.concatenate([s * -scale, s * scale, -s, s], axis=0).T


def tables(cosine, sine):
    half, S = cosine.shape
    rb = min(1024, S)
    return pl.pallas_call(
        tables_kernel,
        grid=(S // rb,),
        out_shape=(jax.ShapeDtypeStruct((S, 4 * half), f32),) * 2
        + (jax.ShapeDtypeStruct((2 * half, S), f32),) * 2,
        in_specs=[pl.BlockSpec((half, rb), lambda i: (0, i))] * 2,
        out_specs=(pl.BlockSpec((rb, 4 * half), lambda i: (i, 0)),) * 2
        + (pl.BlockSpec((2 * half, rb), lambda i: (0, i)),) * 2,
        name="tables",
    )(cosine, sine)


def grads_kernel(place_ref, second_ref, dgu_ref, mixed_ref, branch_ref, inner_ref, dy_ref, wide_ref, tall_ref):
    g = pl.program_id(0)
    end = pl.num_programs(0) - 1

    @pl.when(g < end)
    def _():
        wide_ref[0] = dg(second_ref[...], dgu_ref[...], TN).astype(bf)
        tall_ref[...] = dg(inner_ref[...], dy_ref[...], TN).astype(bf)

    @pl.when(g == end)
    def _():
        wide_ref[0] = dg(mixed_ref[...], branch_ref[...], NN).astype(bf)


def grads(place, second, d_gate_up, mixed_t, branch, inner, dy):
    rows = second.shape[0]
    ff = inner.shape[1]
    steps = 2 * ff // D
    whole = lambda i, p: (0, 0)
    column = lambda i, p: (0, jnp.minimum(i, steps - 1))
    return pl.pallas_call(
        grads_kernel,
        grid_spec=pltpu.PrefetchScalarGridSpec(
            num_scalar_prefetch=1,
            grid=(steps + 1,),
            in_specs=[
                pl.BlockSpec((rows, D), whole),
                pl.BlockSpec((rows, D), column),
                pl.BlockSpec((D, rows), whole),
                pl.BlockSpec((rows, D), whole),
                pl.BlockSpec((rows, ff // steps), column),
                pl.BlockSpec((rows, D), whole),
            ],
            out_specs=(
                pl.BlockSpec((1, D, D), lambda i, p: (i ^ p[0], 0, 0)),
                pl.BlockSpec((ff // steps, D), lambda i, p: (jnp.minimum(i, steps - 1), 0)),
            ),
        ),
        out_shape=(
            jax.ShapeDtypeStruct((steps + 1, D, D), bf),
            jax.ShapeDtypeStruct((ff, D), bf),
        ),
        compiler_params=pltpu.CompilerParams(vmem_limit_bytes=48 * 2**20),
        cost_estimate=pl.CostEstimate(
            flops=2 * rows * D * (3 * ff + D), bytes_accessed=20 * 2**20, transcendentals=0
        ),
        name="grads",
    )(place, second, d_gate_up, mixed_t, branch, inner, dy)


def add_kernel(count, *refs):
    total = None
    for ref in refs[:count]:
        for j in range(ref.shape[0]):
            term = ref[j].astype(f32)
            total = term if total is None else total + term
    out_ref = refs[-1]
    out_ref[...] = total.astype(out_ref.dtype)


def add_up(arrays, after, dtype=bf, leading=None):
    arrays = [a if a.ndim == 3 else a[None] for a in arrays]
    rows, columns = arrays[0].shape[1:]
    rb = 256 if rows % 256 == 0 else rows
    first = arrays[0].shape[0] if leading is None else leading
    lead = [first] + [a.shape[0] for a in arrays[1:]]
    return pl.pallas_call(
        functools.partial(add_kernel, len(arrays)),
        grid=(rows // rb,),
        out_shape=jax.ShapeDtypeStruct((rows, columns), dtype),
        in_specs=[pl.BlockSpec((n, rb, columns), lambda i: (0, i, 0)) for n in lead]
        + [pl.BlockSpec(memory_space=pl.ANY)] * len(after),
        out_specs=pl.BlockSpec((rb, columns), lambda i: (i, 0)),
        compiler_params=pltpu.CompilerParams(vmem_limit_bytes=48 * 2**20),
        name="add_up",
    )(*arrays, *after)


def finish_wide_kernel(groups, info_ref, w_ref, gain_ref, *refs):
    in_ref, proj_ref, dgain_ref, held_ref = refs[groups : groups + 4]
    for j in range(groups):
        held_ref[info_ref[0] ^ j] = refs[j][...]
    total = 0.0
    for g in range(groups - 1):
        at = slice(g * D, (g + 1) * D)
        grad = held_ref[g].astype(f32)
        in_ref[:, at] = grad
        total = total + jnp.sum(w_ref[:, at].astype(f32) * grad, axis=1, keepdims=True)
    proj_ref[...] = held_ref[groups - 1].astype(f32)
    dgain_ref[...] = total / gain_ref[...].astype(f32)


def finish_qkv_kernel(groups, heads, info_ref, w_ref, gain_ref, *refs):
    out_ref, dgain_ref, held_ref = refs[groups : groups + 3]
    for j in range(groups):
        held_ref[info_ref[0] ^ j] = refs[j][...]
    pieces = []
    for t in range(3):
        for g in range(groups):
            for h in range(heads):
                start = h * 256 + t * HD
                pieces.append(held_ref[g, :, start : start + HD].astype(f32))
    grad = jnp.concatenate(pieces, axis=1)
    out_ref[...] = grad
    total = jnp.sum(w_ref[...].astype(f32) * grad, axis=1, keepdims=True)
    dgain_ref[...] = total / gain_ref[...].astype(f32)


def finish(kernel, groups, info, w, gain, parts, widths, name):
    shard = w.shape[0]
    vmem = pl.BlockSpec(memory_space=pltpu.VMEM)
    return pl.pallas_call(
        kernel,
        out_shape=tuple(jax.ShapeDtypeStruct((shard, n), f32) for n in widths),
        in_specs=[pl.BlockSpec(memory_space=pltpu.SMEM)] + [vmem] * (2 + groups),
        out_specs=(vmem,) * len(widths),
        scratch_shapes=[pltpu.VMEM((groups,) + parts[0].shape, bf)],
        compiler_params=pltpu.CompilerParams(vmem_limit_bytes=48 * 2**20),
        name=name,
    )(info, w, gain, *parts)


def body(
    tokens, lengths, attn_gain, qkv_weight, proj_weight, ffn_gain, in_weight, out_weight, out_grad
):
    rows = tokens.shape[1]
    groups = lax.axis_size("seq")
    shards = lax.axis_size("fsdp")
    heads = HEADS // groups
    shard = D // shards
    me = lax.axis_index("seq")
    owner = lax.axis_index("fsdp")

    def swap(array, j, axis="seq"):
        size = lax.axis_size(axis)
        return lax.ppermute(array, axis, [(i, i ^ j) for i in range(size)])

    def exchange(chunks):
        return [chunks[0]] + [swap(chunks[j], j) for j in range(1, groups)]

    def gather(array):
        return lax.all_gather(array, "fsdp", axis=0, tiled=True)

    place = jnp.stack([me]).astype(jnp.int32)
    x0 = tokens[0]
    across = swap(x0, 2)
    near = swap(x0, 1)
    own = own_columns(groups, heads, place, qkv_weight, attn_gain[:, None])
    if shards <= 8:
        parts = [own] + [swap(own, j, "fsdp") for j in range(1, shards)]
    else:
        parts = [gather(own)]
    blocks = [x0, near, across, swap(across, 1)]

    half = HD // 2
    frequency = rope_base ** (-(lax.iota(f32, half) * 2.0) / HD)
    starts = [(me ^ j) * rows for j in range(groups)]
    positions = jnp.concatenate([s + lax.iota(jnp.int32, rows) for s in starts]).astype(f32)
    angles = frequency[:, None] * positions[None, :]
    cos_rows, sin_rows, cos_t, sin_t = tables(jnp.cos(angles), jnp.sin(angles))

    carried = None
    for j in range(groups):
        info = jnp.stack([starts[j], lengths[0], owner]).astype(jnp.int32)
        carried = qkv_call(j, groups, heads, info, blocks[j], cos_rows, sin_rows, parts, carried)
    normed, k, v, qt, kt, vt = carried

    ff2 = in_weight.shape[1]
    wide_shard = jnp.concatenate(
        [in_weight, proj_weight, ffn_gain[:, None], jnp.zeros((shard, 127), bf)], axis=1
    )
    wide_shard, out_shard, qkv_shard, gain_shard, _ = lax.optimization_barrier(
        (wide_shard, out_weight, qkv_weight, attn_gain, parts[-1])
    )
    wide = gather(wide_shard)
    out_full = gather(out_shard)
    qkv_full = gather(jnp.concatenate([qkv_shard, jnp.tile(gain_shard[:, None], (1, 128))], axis=1))

    kept = []
    chunks = []
    for h in range(heads):
        p, o, ob, linv = attend(h, k, qt, vt, groups)
        kept.append((p, o, linv))
        chunks += exchange([ob[j] for j in range(groups)])

    dy = out_grad[0]
    result, d_hidden, d_heads, mixed_t, second, d_gate_up, inner, branch = middle(
        groups, heads, place, x0, dy, wide, out_full, chunks
    )
    d_mixed = [exchange([d_heads[h, j] for j in range(groups)]) for h in range(heads)]

    def to_owner(array):
        parts = array.reshape(shards, array.shape[0] // shards, -1)
        return lax.all_to_all(parts, "fsdp", split_axis=0, concat_axis=0, tiled=True)

    def from_peers(array):
        return [array] + [swap(array, j) for j in range(1, groups)]

    wide_grad, tall_grad = grads(place, second, d_gate_up, mixed_t, branch, inner, dy)
    wide_sent = [swap(wide_grad[j], j) for j in range(1, groups)]
    tall_parts = to_owner(tall_grad)

    def back(h, grad_place, after):
        p, o, linv = kept[h]
        own, grad = attend_back(
            h, v, kt, qt, d_mixed[h], o, linv, p, cos_t, sin_t, normed, groups, grad_place, after
        )
        return exchange([own[j] for j in range(groups)]), grad

    received, qkv_first = back(0, (512, 0, None), [tall_grad])
    wide_sum = add_up([wide_grad] + wide_sent, [qkv_first], leading=1)
    wide_parts = to_owner(wide_sum)
    tall_sum = add_up([tall_parts], [qkv_first])
    tall_peers = from_peers(tall_sum)
    more, qkv_first = back(1, (512, 1, qkv_first), [wide_sum, tall_sum])
    received += more
    qkv_parts = to_owner(qkv_first)
    wide_owned = add_up([wide_parts], [qkv_first])
    wide_peers = from_peers(wide_owned)
    out_weight_grad = add_up(tall_peers, [qkv_first], dtype=f32)
    more, qkv_second = back(2, (256, 0, None), [wide_owned, out_weight_grad])
    received += more
    qkv_second_parts = to_owner(qkv_second)

    in_weight_grad, proj_weight_grad, ffn_gain_grad = finish(
        functools.partial(finish_wide_kernel, groups),
        groups, place, in_weight, ffn_gain[:, None], wide_peers, (ff2, D, 1), "finish_wide",
    )
    first_sum = add_up([qkv_parts], [qkv_second])
    second_sum = add_up([qkv_second_parts], [])
    qkv_peers = from_peers(jnp.concatenate([first_sum, second_sum], axis=1))
    tokens_grad = last(groups, heads, place, x0, d_hidden, qkv_full, received)
    qkv_weight_grad, attn_gain_grad = finish(
        functools.partial(finish_qkv_kernel, groups, heads),
        groups, place, qkv_weight, attn_gain[:, None], qkv_peers, (3 * D, 1), "finish_qkv",
    )
    return (
        result[None],
        tokens_grad[None],
        attn_gain_grad[:, 0],
        qkv_weight_grad,
        proj_weight_grad,
        ffn_gain_grad[:, 0],
        in_weight_grad,
        out_weight_grad,
    )


def solution(mesh):
    in_specs = (
        P("fsdp", "seq", None),
        P("fsdp"),
        P("fsdp"),
        P("fsdp", None),
        P("fsdp", None),
        P("fsdp"),
        P("fsdp", None),
        P("fsdp", None),
        P("fsdp", "seq", None),
    )
    out_specs = (
        P("fsdp", "seq", None),
        P("fsdp", "seq", None),
        P("fsdp"),
        P("fsdp", None),
        P("fsdp", None),
        P("fsdp"),
        P("fsdp", None),
        P("fsdp", None),
    )
    return jax.shard_map(body, mesh=mesh, in_specs=in_specs, out_specs=out_specs, check_vma=False)
```

```python
import functools

import jax
import jax.numpy as jnp
from jax import lax
from jax.experimental import pallas as pl
from jax.experimental.pallas import tpu as pltpu
from jax.sharding import PartitionSpec as P

D = 768
HEADS = 12
HD = 64

epsilon = 1e-05
rope_base = 160000.0
masked_score = -1e30
LOG2E = 1.4426950408889634
LN2 = 0.6931471805599453

bf = jnp.bfloat16
f32 = jnp.float32
NN = ((1,), (0,))
NT = ((1,), (1,))
TN = ((0,), (0,))


def dg(a, b, dims):
    return lax.dot_general(a, b, (dims, ((), ())), preferred_element_type=f32)


def unit_rows_of(x):
    centred = x - jnp.mean(x, axis=-1, keepdims=True)
    inverse = lax.rsqrt(jnp.mean(centred * centred, axis=-1, keepdims=True) + epsilon)
    return centred * inverse, inverse


def qkv_kernel(heads, info_ref, x_ref, cos_ref, sin_ref, w_ref, *refs):
    n_ref, k_ref, v_ref, qt_ref, kt_ref, vt_ref, g_ref = refs[-7:]
    rb = x_ref.shape[0]
    value_at = heads * 128

    @pl.when(pl.program_id(0) == 0)
    def _():
        last = w_ref[:, w_ref.shape[1] - 128 :].astype(f32).T
        g_ref[...] = last[HD : HD + 8]

    unit, _ = unit_rows_of(x_ref[...].astype(f32))
    normed = (unit * g_ref[:1]).astype(bf)
    n_ref[...] = normed
    lane = lax.broadcasted_iota(jnp.int32, (rb, 128), 1)
    row = lax.broadcasted_iota(jnp.int32, (rb, 128), 0)
    position = info_ref[0] + pl.program_id(0) * rb + row
    bias = jnp.where(position < info_ref[1], 0.0, masked_score)
    key_tail = jnp.where(lane == HD, bias, 0.0)
    value_tail = jnp.where(lane < HD + 2, -1.0, 0.0)
    head_lane = lane < HD
    lower = (lane & (HD - 1)) < HD // 2
    one_row = jnp.where(lax.broadcasted_iota(jnp.int32, (HD, rb), 0) == 0, 1.0, 0.0).astype(bf)
    y = dg(normed, w_ref[...], NN)
    for h in range(heads):
        t = y[:, h * 128 : (h + 1) * 128]
        turned = jnp.where(lower, pltpu.roll(t, 128 - HD // 2, 1), pltpu.roll(t, HD // 2, 1))
        t = t * cos_ref[...] + turned * sin_ref[...]
        k_ref[h] = jnp.where(head_lane, pltpu.roll(t, HD, 1), key_tail).astype(bf)
        t = t.T.astype(bf)
        qt_ref[h, :HD] = t[:HD]
        qt_ref[h, HD:] = one_row
        kt_ref[h] = t[HD:]
    for h in range(heads):
        at = value_at + h // 2 * 128
        t = y[:, at : at + 128]
        turned = t if h % 2 == 0 else pltpu.roll(t, HD, 1)
        v_ref[h] = jnp.where(head_lane, turned, value_tail).astype(bf)
        if h % 2 == 0:
            t_rows = t.T.astype(bf)
        vt_ref[h, :HD] = t_rows[:HD] if h % 2 == 0 else t_rows[HD:]
        vt_ref[h, HD:] = one_row[:16]


def qkv_call(block, blocks, heads, info, x, cos, sin, w, carried):
    rows = x.shape[0]
    S = rows * blocks
    rb = min(256, rows)
    steps = rows // rb
    width = w.shape[1]
    at = lambda i: block * steps + i
    outs = (
        jax.ShapeDtypeStruct((S, D), bf),
        jax.ShapeDtypeStruct((heads, S, 128), bf),
        jax.ShapeDtypeStruct((heads, S, 128), bf),
        jax.ShapeDtypeStruct((heads, 128, S), bf),
        jax.ShapeDtypeStruct((heads, HD, S), bf),
        jax.ShapeDtypeStruct((heads, 80, S), bf),
    )
    in_specs = [
        pl.BlockSpec(memory_space=pltpu.SMEM),
        pl.BlockSpec((rb, D), lambda i: (i, 0)),
        pl.BlockSpec((rb, 128), lambda i: (at(i), 0)),
        pl.BlockSpec((rb, 128), lambda i: (at(i), 0)),
        pl.BlockSpec((D, width), lambda i: (0, 0)),
    ]
    aliases = {}
    if carried is not None:
        first = len(in_specs)
        in_specs += [pl.BlockSpec(memory_space=pl.ANY)] * 6
        aliases = {first + n: n for n in range(6)}
    return pl.pallas_call(
        functools.partial(qkv_kernel, heads),
        grid=(steps,),
        out_shape=outs,
        in_specs=in_specs,
        out_specs=(
            pl.BlockSpec((rb, D), lambda i: (at(i), 0)),
            pl.BlockSpec((heads, rb, 128), lambda i: (0, at(i), 0)),
            pl.BlockSpec((heads, rb, 128), lambda i: (0, at(i), 0)),
            pl.BlockSpec((heads, 128, rb), lambda i: (0, 0, at(i))),
            pl.BlockSpec((heads, HD, rb), lambda i: (0, 0, at(i))),
            pl.BlockSpec((heads, 80, rb), lambda i: (0, 0, at(i))),
        ),
        scratch_shapes=[pltpu.VMEM((8, D), f32)],
        input_output_aliases=aliases,
        compiler_params=pltpu.CompilerParams(vmem_limit_bytes=48 * 2**20),
        cost_estimate=pl.CostEstimate(
            flops=4 * rows * D * width, bytes_accessed=rows * 8192, transcendentals=0
        ),
        name="qkv",
    )(info, x, cos, sin, w, *(carried or ()))


def attend_kernel(kc, half, k_ref, qa_ref, qb_ref, v_ref, *refs):
    pa_ref, pb_ref, oa_ref, ob_ref, la_ref, lb_ref = refs[:6]
    chunks = refs[6 : 6 + half]
    sa_ref, sb_ref, m_ref = refs[6 + half :]
    i = pl.program_id(0)
    rows = k_ref.shape[1]
    bq = qa_ref.shape[2]

    def stage(new, old):
        if new is not None:
            q_ref, s_new, new_slot = new
            q = q_ref[0]
            m = jnp.full((8, bq), -jnp.inf, f32)
        if old is not None:
            s_old, old_slot, p_ref, o_ref, l_ref, block = old
            top = jnp.max(m_ref[old_slot], axis=0, keepdims=True)
            acc = jnp.zeros((v_ref.shape[1], bq), f32)
        for c in range(rows // kc):
            at = slice(c * kc, (c + 1) * kc)
            if new is not None:
                s = dg(k_ref[0, at, :], q, NN)
                s_new[at, :] = s
                m = jnp.maximum(m, jnp.max(s.reshape(kc // 8, 8, bq), axis=0))
            if old is not None:
                p = jnp.exp2(s_old[at, :] - top).astype(bf)
                p_ref[0, at, :] = p
                acc = acc + dg(v_ref[0, :, at], p, NN)
        if new is not None:
            m_ref[new_slot] = m
        if old is not None:
            linv = 1.0 / acc[HD : HD + 1, :]
            o = acc[:HD, :] * linv
            o_ref[...] = o
            l_ref[0] = linv
            low = o.astype(bf)
            for j in range(half):

                @pl.when(block // 2 == j)
                def _():
                    chunks[j][:, old_slot * bq : (old_slot + 1) * bq] = low

    first = (qa_ref, sa_ref, 0)
    odd = (sb_ref, 1, pb_ref, ob_ref, lb_ref, 2 * i - 1)

    @pl.when(i == 0)
    def _():
        stage(first, None)

    @pl.when((i > 0) & (i < half))
    def _():
        stage(first, odd)

    @pl.when(i == half)
    def _():
        stage(None, odd)

    @pl.when(i < half)
    def _():
        stage((qb_ref, sb_ref, 1), (sa_ref, 0, pa_ref, oa_ref, la_ref, 2 * i))


def attend(h, k, qt, vt, groups, kc=256):
    S = k.shape[1]
    bq = S // groups // 2
    a = lambda i: jnp.minimum(i, groups - 1)
    b = lambda i: jnp.maximum(i - 1, 0)
    outs = pl.pallas_call(
        functools.partial(attend_kernel, kc, groups),
        grid=(groups + 1,),
        out_shape=(jax.ShapeDtypeStruct((groups, S, bq), bf),) * 2
        + (jax.ShapeDtypeStruct((HD, S // 2), f32),) * 2
        + (jax.ShapeDtypeStruct((groups, 1, bq), f32),) * 2
        + (jax.ShapeDtypeStruct((HD, 2 * bq), bf),) * groups,
        in_specs=[
            pl.BlockSpec((1, S, 128), lambda i: (h, 0, 0)),
            pl.BlockSpec((1, 128, bq), lambda i: (h, 0, 2 * a(i))),
            pl.BlockSpec((1, 128, bq), lambda i: (h, 0, 2 * a(i) + 1)),
            pl.BlockSpec((1, 80, S), lambda i: (h, 0, 0)),
        ],
        out_specs=(
            pl.BlockSpec((1, S, bq), lambda i: (a(i), 0, 0)),
            pl.BlockSpec((1, S, bq), lambda i: (b(i), 0, 0)),
            pl.BlockSpec((HD, bq), lambda i: (0, a(i))),
            pl.BlockSpec((HD, bq), lambda i: (0, b(i))),
            pl.BlockSpec((1, 1, bq), lambda i: (a(i), 0, 0)),
            pl.BlockSpec((1, 1, bq), lambda i: (b(i), 0, 0)),
        )
        + (pl.BlockSpec((HD, 2 * bq), lambda i: (0, 0)),) * groups,
        scratch_shapes=[
            pltpu.VMEM((S, bq), f32),
            pltpu.VMEM((S, bq), f32),
            pltpu.VMEM((2, 8, bq), f32),
        ],
        compiler_params=pltpu.CompilerParams(vmem_limit_bytes=58 * 2**20),
        cost_estimate=pl.CostEstimate(
            flops=16 * HD * S * S, bytes_accessed=2 * S * S, transcendentals=S * S
        ),
        name="attend",
    )(k, qt, qt, vt)
    return outs[:6], list(outs[6:])


def attend_back_kernel(kc, groups, v_ref, kt_ref, q_ref, *refs):
    oa_ref, ob_ref, la_ref, lb_ref, pa_ref, pb_ref, cos_ref, sin_ref, n_ref = refs[:9]
    do_refs = refs[9 : 9 + groups]
    outs = refs[-5 - groups : -5]
    grad_ref, acc_ref, do_ref, held_ref, sem = refs[-5:]
    i = pl.program_id(0)
    rows = v_ref.shape[1]
    width = q_ref.shape[2]
    bq = width // 2
    fetch = pltpu.make_async_copy(n_ref, held_ref, sem)

    @pl.when(i == 0)
    def _():
        fetch.start()
        acc_ref[...] = jnp.zeros_like(acc_ref)

    for j in range(groups):

        @pl.when(i == j)
        def _():
            do_ref[...] = do_refs[j][...]

    zero = jnp.zeros((HD, bq), bf)
    r = lax.broadcasted_iota(jnp.int32, (16, bq), 0)
    sides = []
    for n, (o_ref, l_ref, p_ref) in enumerate(((oa_ref, la_ref, pa_ref), (ob_ref, lb_ref, pb_ref))):
        at = slice(n * bq, (n + 1) * bq)
        dop = (do_ref[:, at].astype(f32) * l_ref[0]).astype(bf)
        delta = jnp.sum(dop.astype(f32) * o_ref[...], axis=0, keepdims=True)
        high = delta.astype(bf).astype(f32)
        tail = jnp.where(r == 0, high, jnp.where(r == 1, delta - high, 0.0)).astype(bf)
        doe = jnp.concatenate([dop, tail, jnp.zeros((128 - HD - 16, bq), bf)], axis=0)
        right_v = jnp.concatenate([dop, zero], axis=0)
        right_k = jnp.concatenate([zero, q_ref[0, :HD, at]], axis=0)
        sides.append((p_ref, doe, right_v, right_k))
    dq = [jnp.zeros((HD, bq), f32), jnp.zeros((HD, bq), f32)]
    for c in range(rows // kc):
        at = slice(c * kc, (c + 1) * kc)
        total = acc_ref[at, :]
        for n, (p_ref, doe, right_v, right_k) in enumerate(sides):
            p = p_ref[0, at, :]
            ds = p * dg(v_ref[0, at, :], doe, NN).astype(bf)
            total = total + dg(p, right_v, NT) + dg(ds, right_k, NT)
            dq[n] = dq[n] + dg(kt_ref[0, :, at], ds, NN)
        acc_ref[at, :] = total
    dq = jnp.concatenate(dq, axis=1) * HD**-0.5
    turned = jnp.concatenate([dq[HD // 2 :], -dq[: HD // 2]], axis=0)
    here = pl.ds(pl.multiple_of(i * width, width), width)
    dq = (dq * cos_ref[:, here] + turned * sin_ref[:, here]).astype(bf)
    for j in range(groups):

        @pl.when(i == j)
        def _():
            outs[j][:HD] = dq

    @pl.when(i == groups - 1)
    def _():
        fetch.wait()
        grad = jnp.zeros((3 * HD, D), f32)
        for j in range(groups):
            at = slice(j * width, (j + 1) * width)
            t = acc_ref[at, :].T
            dk = t[HD:] * LN2
            turned_k = jnp.concatenate([dk[HD // 2 :], -dk[: HD // 2]], axis=0)
            dk = dk * cos_ref[:, at] + turned_k * sin_ref[:, at]
            outs[j][HD : 2 * HD] = dk.astype(bf)
            outs[j][2 * HD :] = t[:HD].astype(bf)
            grad = grad + dg(outs[j][...], held_ref[at, :], NN)
        grad_ref[:, : 3 * HD] = grad.T.astype(bf)
        grad_ref[:, 3 * HD :] = jnp.zeros((D, HD), bf)


def attend_back(h, v, kt, qt, do, kept, cos, sin, normed, groups, place, after, kc=512):
    S = v.shape[1]
    width = S // groups
    bq = width // 2
    pa, pb, oa, ob, la, lb = kept
    columns, column, earlier = place
    extra = list(after) if earlier is None else [earlier] + list(after)
    whole = lambda i: (0, 0)
    by_block = lambda i: (i, 0, 0)
    outs = pl.pallas_call(
        functools.partial(attend_back_kernel, kc, groups),
        grid=(groups,),
        out_shape=(jax.ShapeDtypeStruct((3 * HD, width), bf),) * groups
        + (jax.ShapeDtypeStruct((D, columns), bf),),
        in_specs=[
            pl.BlockSpec((1, S, 128), lambda i: (h, 0, 0)),
            pl.BlockSpec((1, HD, S), lambda i: (h, 0, 0)),
            pl.BlockSpec((1, 128, width), lambda i: (h, 0, i)),
            pl.BlockSpec((HD, bq), lambda i: (0, i)),
            pl.BlockSpec((HD, bq), lambda i: (0, i)),
            pl.BlockSpec((1, 1, bq), by_block),
            pl.BlockSpec((1, 1, bq), by_block),
            pl.BlockSpec((1, S, bq), by_block),
            pl.BlockSpec((1, S, bq), by_block),
            pl.BlockSpec((HD, S), whole),
            pl.BlockSpec((HD, S), whole),
            pl.BlockSpec(memory_space=pl.ANY),
        ]
        + [pl.BlockSpec((HD, width), lambda i: (h, 0))] * groups
        + [pl.BlockSpec(memory_space=pl.ANY)] * len(extra),
        out_specs=(pl.BlockSpec((3 * HD, width), whole),) * groups
        + (pl.BlockSpec((D, 256), lambda i: (0, column)),),
        scratch_shapes=[
            pltpu.VMEM((S, 128), f32),
            pltpu.VMEM((HD, width), bf),
            pltpu.VMEM((S, D), bf),
            pltpu.SemaphoreType.DMA,
        ],
        input_output_aliases={} if earlier is None else {12 + groups: groups},
        compiler_params=pltpu.CompilerParams(vmem_limit_bytes=58 * 2**20),
        cost_estimate=pl.CostEstimate(
            flops=24 * HD * S * S, bytes_accessed=2 * S * S, transcendentals=0
        ),
        name="attend_back",
    )(v, kt, qt, oa, ob, la, lb, pa, pb, cos, sin, normed, *do, *extra)
    return list(outs[:groups]), outs[groups]


def normalize_back(gradient, unit_rows, inverse, gain_row):
    scaled = gradient * gain_row
    return inverse * (
        scaled
        - jnp.mean(scaled, axis=-1, keepdims=True)
        - unit_rows * jnp.mean(scaled * unit_rows, axis=-1, keepdims=True)
    )


def middle_kernel(groups, heads, ff, shards, info_ref, x_ref, dy_ref, w_ref, *refs):
    count = groups * heads
    given = len(refs) - count - groups - 10
    out_given = refs[:given]
    chunks = refs[given : given + count]
    d_chunks = refs[given + count : given + count + groups]
    (result_ref, dh_ref, mixed_ref, second_ref, dgu_ref, inner_ref, branch_ref,
     g_ref, t_ref, out_w_ref) = refs[given + count + groups :]
    width = heads * HD
    me = info_ref[0]

    @pl.when(pl.program_id(0) == 0)
    def _():
        g_ref[...] = w_ref[:, 2 * ff + D : 2 * ff + D + 128].astype(f32).T[:8]
        if given:
            out_w_ref[...] = out_given[0][...]
        else:
            tall, short = ff // shards, D // shards
            rest = tall - short
            one = 2 * ff + D + 128
            two, three = one + D, one + D + D // 2
            for f in range(shards):
                src = slice(f * short, (f + 1) * short)
                out_w_ref[f * tall : f * tall + short, :] = w_ref[src, one:two]
                dst = slice(f * tall + short, (f + 1) * tall)
                src = slice(f * short, f * short + rest)
                out_w_ref[dst, : D // 2] = w_ref[src, two:three]
                src = slice(f * short + rest, f * short + 2 * rest)
                out_w_ref[dst, D // 2 :] = w_ref[src, two:three]

    for h in range(heads):
        for j in range(groups):
            start = pl.multiple_of((me ^ j) * width + h * HD, HD)
            mixed_ref[pl.ds(start, HD), :] = chunks[h * groups + j][...]
    gain = g_ref[:1]
    proj = w_ref[:, 2 * ff : 2 * ff + D]
    hidden = x_ref[...].astype(f32) + dg(mixed_ref[...], proj, TN)
    unit, inverse = unit_rows_of(hidden)
    second = (unit * gain).astype(bf)
    second_ref[...] = second
    dy = dy_ref[...]
    result = hidden
    d_second = jnp.zeros_like(hidden)
    step = 384
    for c in range(ff // step):
        a = slice(c * step, (c + 1) * step)
        b = slice(ff + c * step, ff + (c + 1) * step)
        gate = dg(second, w_ref[:, a], NN)
        up = dg(second, w_ref[:, b], NN)
        d_inner = dg(dy, out_w_ref[a, :], NT)
        bell = 0.5 + 0.5 * lax.erf(gate * 0.7071067811865476)
        gelu = gate * bell
        inner = (gelu * up).astype(bf)
        inner_ref[:, a] = inner
        result = result + dg(inner, out_w_ref[a, :], NN)
        slope = bell + gate * (jnp.exp(-0.5 * gate * gate) * 0.3989422804014327)
        d_gate = (d_inner * up * slope).astype(bf)
        d_up = (d_inner * gelu).astype(bf)
        dgu_ref[:, a] = d_gate
        dgu_ref[:, b] = d_up
        d_second = d_second + dg(d_gate, w_ref[:, a], NT) + dg(d_up, w_ref[:, b], NT)
    result_ref[...] = result.astype(bf)
    d_hidden = dy.astype(f32) + normalize_back(d_second, unit, inverse, gain)
    dh_ref[...] = d_hidden
    branch = d_hidden.astype(bf)
    branch_ref[...] = branch
    t_ref[...] = dg(proj, branch, NT).astype(bf)
    for j in range(groups):
        start = pl.multiple_of((me ^ j) * width, HD)
        d_chunks[j][...] = t_ref[pl.ds(start, width), :]


def middle(groups, heads, shards, ff, info, x, dy, wide, out_w, chunks):
    rows = x.shape[0]
    rb = min(256, rows)
    by_row = lambda i: (i, 0)
    by_column = lambda i: (0, i)
    whole = lambda i: (0, 0)
    outs = pl.pallas_call(
        functools.partial(middle_kernel, groups, heads, ff, shards),
        grid=(rows // rb,),
        out_shape=(jax.ShapeDtypeStruct((heads * HD, rows), bf),) * groups
        + (
            jax.ShapeDtypeStruct((rows, D), bf),
            jax.ShapeDtypeStruct((rows, D), f32),
            jax.ShapeDtypeStruct((D, rows), bf),
            jax.ShapeDtypeStruct((rows, D), bf),
            jax.ShapeDtypeStruct((rows, 2 * ff), bf),
            jax.ShapeDtypeStruct((rows, ff), bf),
            jax.ShapeDtypeStruct((rows, D), bf),
        ),
        in_specs=[
            pl.BlockSpec(memory_space=pltpu.SMEM),
            pl.BlockSpec((rb, D), by_row),
            pl.BlockSpec((rb, D), by_row),
            pl.BlockSpec(wide.shape, whole, pipeline_mode=pl.Buffered(1)),
        ]
        + [pl.BlockSpec(w.shape, whole, pipeline_mode=pl.Buffered(1)) for w in out_w]
        + [pl.BlockSpec((HD, rb), by_column)] * (groups * heads),
        out_specs=(pl.BlockSpec((heads * HD, rb), by_column),) * groups
        + (
            pl.BlockSpec((rb, D), by_row),
            pl.BlockSpec((rb, D), by_row),
            pl.BlockSpec((D, rb), by_column),
            pl.BlockSpec((rb, D), by_row),
            pl.BlockSpec((rb, 2 * ff), by_row),
            pl.BlockSpec((rb, ff), by_row),
            pl.BlockSpec((rb, D), by_row),
        ),
        scratch_shapes=[
            pltpu.VMEM((8, D), f32),
            pltpu.VMEM((D, rb), bf),
            pltpu.VMEM((ff, D), bf),
        ],
        compiler_params=pltpu.CompilerParams(vmem_limit_bytes=58 * 2**20),
        cost_estimate=pl.CostEstimate(
            flops=rows * D * (14 * ff + 4 * D), bytes_accessed=30 * 2**20, transcendentals=rows * ff
        ),
        name="middle",
    )(info, x, dy, wide, *out_w, *chunks)
    return list(outs[:groups]), outs[groups:]


def last_kernel(groups, heads, chosen, final, info_ref, w_ref, *refs):
    count = groups * len(chosen)
    chunks = refs[:count]
    rest = refs[count:]
    dp_ref, wh_ref = rest[-2:]
    me = info_ref[0]
    width = heads * HD

    @pl.when(pl.program_id(0) == 0)
    def _():
        for n, h in enumerate(chosen):
            pieces = []
            for g in range(groups):
                for t in range(3):
                    start = t * D + g * width + h * HD
                    pieces.append(w_ref[:, start : start + HD])
            wh_ref[:, n * D : (n + 1) * D] = jnp.concatenate(pieces, axis=1)

    for n in range(len(chosen)):
        for j in range(groups):
            start = pl.multiple_of(n * D + (me ^ j) * 3 * HD, 3 * HD)
            dp_ref[pl.ds(start, 3 * HD), :] = chunks[n * groups + j][...]
    d_normed = dg(wh_ref[...], dp_ref[...], NN).T
    if not final:
        rest[0][...] = d_normed
        return
    base_ref, x_ref, dh_ref, gain_ref, out_ref = rest[:5]
    gain = gain_ref[...].astype(f32).T[:1]
    d_normed = d_normed + base_ref[...]
    unit, inverse = unit_rows_of(x_ref[...].astype(f32))
    out_ref[...] = dh_ref[...] + normalize_back(d_normed, unit, inverse, gain)


def last(groups, heads, chosen, info, w, chunks, others, after):
    rows = chunks[0].shape[1]
    rb = min(256, rows)
    by_row = lambda i: (i, 0)
    whole = lambda i: (0, 0)
    others = list(others)
    specs = [pl.BlockSpec((rb, D), by_row)] * len(others)
    if others:
        others.append(w)
        specs.append(pl.BlockSpec((D, 128), lambda i: (0, 3 * D // 128)))

    def kernel(*refs):
        skip = 2 + len(chunks) + len(others)
        last_kernel(
            groups, heads, chosen, bool(others), *refs[:skip], *refs[skip + len(after) :]
        )

    return pl.pallas_call(
        kernel,
        grid=(rows // rb,),
        out_shape=jax.ShapeDtypeStruct((rows, D), f32),
        in_specs=[
            pl.BlockSpec(memory_space=pltpu.SMEM),
            pl.BlockSpec((D, 3 * D), whole, pipeline_mode=pl.Buffered(1)),
        ]
        + [pl.BlockSpec((3 * HD, rb), lambda i: (0, i))] * len(chunks)
        + specs
        + [pl.BlockSpec(memory_space=pl.ANY)] * len(after),
        out_specs=pl.BlockSpec((rb, D), by_row),
        scratch_shapes=[
            pltpu.VMEM((len(chosen) * D, rb), bf),
            pltpu.VMEM((D, len(chosen) * D), bf),
        ],
        compiler_params=pltpu.CompilerParams(vmem_limit_bytes=58 * 2**20),
        cost_estimate=pl.CostEstimate(
            flops=2 * len(chosen) * rows * D * D, bytes_accessed=12 * 2**20, transcendentals=0
        ),
        name="last",
    )(info, w, *chunks, *others, *after)


def pass_on(arrays, after):
    vmem = pl.BlockSpec(memory_space=pltpu.VMEM)
    count = len(arrays)

    def kernel(*refs):
        for source, target in zip(refs[:count], refs[-count:]):
            target[...] = source[...]

    return pl.pallas_call(
        kernel,
        out_shape=tuple(jax.ShapeDtypeStruct(a.shape, a.dtype) for a in arrays),
        in_specs=[vmem] * count + [pl.BlockSpec(memory_space=pl.ANY)] * len(after),
        out_specs=(vmem,) * count,
        compiler_params=pltpu.CompilerParams(vmem_limit_bytes=58 * 2**20),
        name="pass_on",
    )(*arrays, *after)


def own_kernel(groups, heads, info_ref, w_ref, gain_ref, out_ref):
    for g in range(groups):

        @pl.when(info_ref[0] == g)
        def _():
            def piece(t, h):
                start = t * D + (g * heads + h) * HD
                return w_ref[:, start : start + HD]

            pieces = []
            for h in range(heads):
                pieces += [piece(0, h), piece(1, h)]
            pieces += [piece(2, h) for h in range(heads)] + [gain_ref[...]]
            missing = out_ref.shape[2] - 3 * heads * HD - 1
            pieces.append(jnp.zeros((w_ref.shape[0], missing), bf))
            own = jnp.concatenate(pieces, axis=1)
            for f in range(out_ref.shape[0]):
                out_ref[f] = own


def own_columns(groups, heads, shards, info, w, gain):
    width = (3 * heads * HD + 128) // 128 * 128
    return pl.pallas_call(
        functools.partial(own_kernel, groups, heads),
        out_shape=jax.ShapeDtypeStruct((shards, w.shape[0], width), bf),
        in_specs=[
            pl.BlockSpec(memory_space=pltpu.SMEM),
            pl.BlockSpec(memory_space=pltpu.VMEM),
            pl.BlockSpec(memory_space=pltpu.VMEM),
        ],
        out_specs=pl.BlockSpec(memory_space=pltpu.VMEM),
        name="own_columns",
    )(info, w, gain)


def tables_kernel(cos_ref, sin_ref, cos_rows_ref, sin_rows_ref, cos_t_ref, sin_t_ref):
    c, s = cos_ref[...], sin_ref[...]
    cos_t_ref[...] = jnp.concatenate([c, c], axis=0)
    sin_t_ref[...] = jnp.concatenate([s, s], axis=0)
    scale = HD**-0.5 * LOG2E
    cos_rows_ref[...] = jnp.concatenate([c * scale, c * scale, c, c], axis=0).T
    sin_rows_ref[...] = jnp.concatenate([s * -scale, s * scale, -s, s], axis=0).T


def tables(cosine, sine):
    half, S = cosine.shape
    rb = min(1024, S)
    return pl.pallas_call(
        tables_kernel,
        grid=(S // rb,),
        out_shape=(jax.ShapeDtypeStruct((S, 4 * half), f32),) * 2
        + (jax.ShapeDtypeStruct((2 * half, S), f32),) * 2,
        in_specs=[pl.BlockSpec((half, rb), lambda i: (0, i))] * 2,
        out_specs=(pl.BlockSpec((rb, 4 * half), lambda i: (i, 0)),) * 2
        + (pl.BlockSpec((2 * half, rb), lambda i: (0, i)),) * 2,
        name="tables",
    )(cosine, sine)


def grads_kernel(place_ref, second_ref, dgu_ref, mixed_ref, branch_ref, inner_ref, dy_ref, wide_ref, tall_ref):
    g = pl.program_id(0)
    end = pl.num_programs(0) - 1

    @pl.when(g < end)
    def _():
        wide_ref[0] = dg(second_ref[...], dgu_ref[...], TN).astype(bf)
        tall_ref[...] = dg(inner_ref[...], dy_ref[...], TN).astype(bf)

    @pl.when(g == end)
    def _():
        wide_ref[0] = dg(mixed_ref[...], branch_ref[...], NN).astype(bf)


def grads(place, second, d_gate_up, mixed_t, branch, inner, dy):
    rows = second.shape[0]
    ff = inner.shape[1]
    steps = 2 * ff // D
    whole = lambda i, p: (0, 0)
    column = lambda i, p: (0, jnp.minimum(i, steps - 1))
    return pl.pallas_call(
        grads_kernel,
        grid_spec=pltpu.PrefetchScalarGridSpec(
            num_scalar_prefetch=1,
            grid=(steps + 1,),
            in_specs=[
                pl.BlockSpec((rows, D), whole),
                pl.BlockSpec((rows, D), column),
                pl.BlockSpec((D, rows), whole),
                pl.BlockSpec((rows, D), whole),
                pl.BlockSpec((rows, ff // steps), column),
                pl.BlockSpec((rows, D), whole),
            ],
            out_specs=(
                pl.BlockSpec((1, D, D), lambda i, p: (i ^ p[0], 0, 0)),
                pl.BlockSpec((ff // steps, D), lambda i, p: (jnp.minimum(i, steps - 1), 0)),
            ),
        ),
        out_shape=(
            jax.ShapeDtypeStruct((steps + 1, D, D), bf),
            jax.ShapeDtypeStruct((ff, D), bf),
        ),
        compiler_params=pltpu.CompilerParams(vmem_limit_bytes=58 * 2**20),
        cost_estimate=pl.CostEstimate(
            flops=2 * rows * D * (3 * ff + D), bytes_accessed=20 * 2**20, transcendentals=0
        ),
        name="grads",
    )(place, second, d_gate_up, mixed_t, branch, inner, dy)


def add_kernel(count, *refs):
    total = None
    for ref in refs[:count]:
        for j in range(ref.shape[0]):
            term = ref[j].astype(f32)
            total = term if total is None else total + term
    out_ref = refs[-1]
    out_ref[...] = total.astype(out_ref.dtype)


def add_up(arrays, after, dtype=bf, leading=None):
    arrays = [a if a.ndim == 3 else a[None] for a in arrays]
    rows, columns = arrays[0].shape[1:]
    rb = 256 if rows % 256 == 0 else rows
    first = arrays[0].shape[0] if leading is None else leading
    lead = [first] + [a.shape[0] for a in arrays[1:]]
    return pl.pallas_call(
        functools.partial(add_kernel, len(arrays)),
        grid=(rows // rb,),
        out_shape=jax.ShapeDtypeStruct((rows, columns), dtype),
        in_specs=[pl.BlockSpec((n, rb, columns), lambda i: (0, i, 0)) for n in lead]
        + [pl.BlockSpec(memory_space=pl.ANY)] * len(after),
        out_specs=pl.BlockSpec((rb, columns), lambda i: (i, 0)),
        compiler_params=pltpu.CompilerParams(vmem_limit_bytes=58 * 2**20),
        name="add_up",
    )(*arrays, *after)


def up16(n):
    return -(-n // 16) * 16


def owned_kernel(wide_ref, tall_ref, *refs):
    out_ref = refs[-1]
    start = 0
    for ref in (wide_ref, tall_ref):
        total = ref[0].astype(f32)
        for f in range(1, ref.shape[0]):
            total = total + ref[f].astype(f32)
        out_ref[start : start + ref.shape[1], :] = total.astype(bf)
        start += up16(ref.shape[1])


def owned(wide, tall, after):
    vmem = pl.BlockSpec(memory_space=pltpu.VMEM)
    return pl.pallas_call(
        owned_kernel,
        out_shape=jax.ShapeDtypeStruct((up16(wide.shape[1]) + up16(tall.shape[1]), D), bf),
        in_specs=[vmem, vmem] + [pl.BlockSpec(memory_space=pl.ANY)] * len(after),
        out_specs=vmem,
        compiler_params=pltpu.CompilerParams(vmem_limit_bytes=58 * 2**20),
        name="owned",
    )(wide, tall, *after)


def finish_wide_kernel(groups, info_ref, w_ref, gain_ref, *refs):
    in_ref, proj_ref, dgain_ref, out_ref, held_ref = refs[groups:]
    shard = w_ref.shape[0]
    start = up16(shard)
    tall = 0.0
    for j in range(groups):
        held_ref[info_ref[0] ^ j] = refs[j][...]
        tall = tall + refs[j][start : start + out_ref.shape[0], :].astype(f32)
    out_ref[...] = tall
    total = 0.0
    for g in range(groups - 1):
        at = slice(g * D, (g + 1) * D)
        grad = held_ref[g, :shard, :].astype(f32)
        in_ref[:, at] = grad
        total = total + jnp.sum(w_ref[:, at].astype(f32) * grad, axis=1, keepdims=True)
    proj_ref[...] = held_ref[groups - 1, :shard, :].astype(f32)
    dgain_ref[...] = total / gain_ref[...].astype(f32)


def finish_qkv_kernel(groups, heads, info_ref, w_ref, gain_ref, *refs):
    out_ref, dgain_ref, held_ref = refs[groups : groups + 3]
    for j in range(groups):
        held_ref[info_ref[0] ^ j] = refs[j][...]
    pieces = []
    for t in range(3):
        for g in range(groups):
            for h in range(heads):
                start = h * 256 + t * HD
                pieces.append(held_ref[g, :, start : start + HD].astype(f32))
    grad = jnp.concatenate(pieces, axis=1)
    out_ref[...] = grad
    total = jnp.sum(w_ref[...].astype(f32) * grad, axis=1, keepdims=True)
    dgain_ref[...] = total / gain_ref[...].astype(f32)


def finish(kernel, groups, info, w, gain, parts, shapes, name):
    vmem = pl.BlockSpec(memory_space=pltpu.VMEM)
    return pl.pallas_call(
        kernel,
        out_shape=tuple(jax.ShapeDtypeStruct(shape, f32) for shape in shapes),
        in_specs=[pl.BlockSpec(memory_space=pltpu.SMEM)] + [vmem] * (2 + groups),
        out_specs=(vmem,) * len(shapes),
        scratch_shapes=[pltpu.VMEM((groups,) + parts[0].shape, bf)],
        compiler_params=pltpu.CompilerParams(vmem_limit_bytes=58 * 2**20),
        name=name,
    )(info, w, gain, *parts)


def body(
    tokens, lengths, attn_gain, qkv_weight, proj_weight, ffn_gain, in_weight, out_weight, out_grad
):
    rows = tokens.shape[1]
    groups = lax.axis_size("seq")
    shards = lax.axis_size("fsdp")
    heads = HEADS // groups
    shard = D // shards
    me = lax.axis_index("seq")

    def swap(array, j, axis="seq"):
        size = lax.axis_size(axis)
        return lax.ppermute(array, axis, [(i, i ^ j) for i in range(size)])

    def exchange(chunks):
        return [chunks[0]] + [swap(chunks[j], j) for j in range(1, groups)]

    def gather(array):
        return lax.all_gather(array, "fsdp", axis=0, tiled=True)

    place = jnp.stack([me]).astype(jnp.int32)
    x0 = tokens[0]
    across = swap(x0, 2)
    near = swap(x0, 1)
    own = own_columns(groups, heads, shards, place, qkv_weight, attn_gain[:, None])
    own = lax.all_to_all(own, "fsdp", split_axis=0, concat_axis=0, tiled=True).reshape(D, -1)
    blocks = [x0, near, across, swap(across, 1)]

    half = HD // 2
    frequency = rope_base ** (-(lax.iota(f32, half) * 2.0) / HD)
    starts = [(me ^ j) * rows for j in range(groups)]
    positions = jnp.concatenate([s + lax.iota(jnp.int32, rows) for s in starts]).astype(f32)
    angles = frequency[:, None] * positions[None, :]
    cos_rows, sin_rows, cos_t, sin_t = tables(jnp.cos(angles), jnp.sin(angles))

    carried = None
    for j in range(groups):
        info = jnp.stack([starts[j], lengths[0]]).astype(jnp.int32)
        carried = qkv_call(j, groups, heads, info, blocks[j], cos_rows, sin_rows, own, carried)
    normed, k, v, qt, kt, vt = carried

    ff = in_weight.shape[1] // 2
    tall = out_weight.shape[0]
    pieces = [in_weight, proj_weight, ffn_gain[:, None], jnp.zeros((shard, 127), bf)]
    if shards <= 8:
        rest = out_weight[shard:]
        pieces += [
            out_weight[:shard],
            jnp.concatenate([rest[:, : D // 2], rest[:, D // 2 :]], axis=0),
        ]
        out_full = []
    else:
        out_full = [gather(out_weight)]
    wide = gather(jnp.concatenate(pieces, axis=1))
    qkv_full = gather(jnp.concatenate([qkv_weight, jnp.tile(attn_gain[:, None], (1, 128))], axis=1))

    kept = []
    chunks = []
    for h in range(heads):
        saved, mixed = attend(h, k, qt, vt, groups)
        kept.append(saved)
        chunks += exchange(mixed)

    dy = out_grad[0]
    d_mixed, (result, d_hidden, mixed_t, second, d_gate_up, inner, branch) = middle(
        groups, heads, shards, ff, place, x0, dy, wide, out_full, chunks
    )
    d_mixed = exchange(d_mixed)

    def to_owner(array):
        parts = array.reshape(shards, array.shape[0] // shards, -1)
        return lax.all_to_all(parts, "fsdp", split_axis=0, concat_axis=0, tiled=True)

    def from_peers(array):
        return [array] + [swap(array, j) for j in range(1, groups)]

    wide_grad, tall_grad = grads(place, second, d_gate_up, mixed_t, branch, inner, dy)
    wide_sent = [swap(wide_grad[j], j) for j in range(1, groups)]
    tall_parts = to_owner(tall_grad)

    def back(h, grad_place, after):
        return attend_back(
            h, v, kt, qt, d_mixed, kept[h], cos_t, sin_t, normed, groups, grad_place, after
        )

    sent_0, qkv_first = back(0, (512, 0, None), [tall_grad])
    wide_sum = add_up([wide_grad] + wide_sent, [qkv_first], leading=1)
    wide_parts = to_owner(wide_sum)
    received_0 = exchange(sent_0)

    sent_1, qkv_first = back(1, (512, 1, qkv_first), [wide_sum, qkv_full])
    both = owned(wide_parts, tall_parts, [qkv_first] + received_0[1:])
    both_peers = from_peers(both)
    received_1 = exchange(sent_1)
    qkv_parts = to_owner(qkv_first)

    sent_2, qkv_second = back(2, (256, 0, None), [both])
    *sent_2, qkv_second = pass_on(sent_2 + [qkv_second], received_1[1:] + [qkv_parts])
    received_2 = exchange(sent_2)
    qkv_second_parts = to_owner(qkv_second)

    base = last(groups, heads, (0, 1), place, qkv_full, received_0 + received_1, [], [qkv_second])
    first_sum = add_up([qkv_parts], [qkv_second])
    in_weight_grad, proj_weight_grad, ffn_gain_grad, out_weight_grad = finish(
        functools.partial(finish_wide_kernel, groups),
        groups, place, in_weight, ffn_gain[:, None], both_peers,
        ((shard, 2 * ff), (shard, D), (shard, 1), (tall, D)), "finish_wide",
    )
    second_sum = add_up([qkv_second_parts], [])
    qkv_peers = from_peers(jnp.concatenate([first_sum, second_sum], axis=1))
    tokens_grad = last(
        groups, heads, (2,), place, qkv_full, received_2, [base, x0, d_hidden], []
    )
    qkv_weight_grad, attn_gain_grad = finish(
        functools.partial(finish_qkv_kernel, groups, heads),
        groups, place, qkv_weight, attn_gain[:, None], qkv_peers,
        ((shard, 3 * D), (shard, 1)), "finish_qkv",
    )
    return (
        result[None],
        tokens_grad[None],
        attn_gain_grad[:, 0],
        qkv_weight_grad,
        proj_weight_grad,
        ffn_gain_grad[:, 0],
        in_weight_grad,
        out_weight_grad,
    )


def solution(mesh):
    in_specs = (
        P("fsdp", "seq", None),
        P("fsdp"),
        P("fsdp"),
        P("fsdp", None),
        P("fsdp", None),
        P("fsdp"),
        P("fsdp", None),
        P("fsdp", None),
        P("fsdp", "seq", None),
    )
    out_specs = (
        P("fsdp", "seq", None),
        P("fsdp", "seq", None),
        P("fsdp"),
        P("fsdp", None),
        P("fsdp", None),
        P("fsdp"),
        P("fsdp", None),
        P("fsdp", None),
    )
    return jax.shard_map(body, mesh=mesh, in_specs=in_specs, out_specs=out_specs, check_vma=False)
```

```python
import functools

import jax
import jax.numpy as jnp
from jax import lax
from jax.experimental import pallas as pl
from jax.experimental.pallas import tpu as pltpu
from jax.sharding import PartitionSpec as P

D = 768
HEADS = 12
HD = 64

epsilon = 1e-05
rope_base = 160000.0
masked_score = -1e30
LOG2E = 1.4426950408889634
LN2 = 0.6931471805599453

bf = jnp.bfloat16
f32 = jnp.float32
NN = ((1,), (0,))
NT = ((1,), (1,))
TN = ((0,), (0,))


def dg(a, b, dims):
    return lax.dot_general(a, b, (dims, ((), ())), preferred_element_type=f32)


def unit_rows_of(x):
    centred = x - jnp.mean(x, axis=-1, keepdims=True)
    inverse = lax.rsqrt(jnp.mean(centred * centred, axis=-1, keepdims=True) + epsilon)
    return centred * inverse, inverse


def qkv_kernel(heads, info_ref, x_ref, cos_ref, sin_ref, w_ref, *refs):
    n_ref, k_ref, v_ref, qt_ref, kt_ref, vt_ref, g_ref = refs[-7:]
    rb = x_ref.shape[0]
    value_at = heads * 128

    @pl.when(pl.program_id(0) == 0)
    def _():
        last = w_ref[:, w_ref.shape[1] - 128 :].astype(f32).T
        g_ref[...] = last[HD : HD + 8]

    unit, _ = unit_rows_of(x_ref[...].astype(f32))
    normed = (unit * g_ref[:1]).astype(bf)
    n_ref[...] = normed
    lane = lax.broadcasted_iota(jnp.int32, (rb, 128), 1)
    row = lax.broadcasted_iota(jnp.int32, (rb, 128), 0)
    position = info_ref[0] + pl.program_id(0) * rb + row
    bias = jnp.where(position < info_ref[1], 0.0, masked_score)
    key_tail = jnp.where(lane == HD, bias, 0.0)
    value_tail = jnp.where(lane < HD + 2, -1.0, 0.0)
    head_lane = lane < HD
    lower = (lane & (HD - 1)) < HD // 2
    one_row = jnp.where(lax.broadcasted_iota(jnp.int32, (HD, rb), 0) == 0, 1.0, 0.0).astype(bf)
    y = dg(normed, w_ref[...], NN)
    for h in range(heads):
        t = y[:, h * 128 : (h + 1) * 128]
        turned = jnp.where(lower, pltpu.roll(t, 128 - HD // 2, 1), pltpu.roll(t, HD // 2, 1))
        t = t * cos_ref[...] + turned * sin_ref[...]
        k_ref[h] = jnp.where(head_lane, pltpu.roll(t, HD, 1), key_tail).astype(bf)
        t = t.T.astype(bf)
        qt_ref[h, :HD] = t[:HD]
        qt_ref[h, HD:] = one_row
        kt_ref[h] = t[HD:]
    for h in range(heads):
        at = value_at + h // 2 * 128
        t = y[:, at : at + 128]
        turned = t if h % 2 == 0 else pltpu.roll(t, HD, 1)
        v_ref[h] = jnp.where(head_lane, turned, value_tail).astype(bf)
        if h % 2 == 0:
            t_rows = t.T.astype(bf)
        vt_ref[h, :HD] = t_rows[:HD] if h % 2 == 0 else t_rows[HD:]
        vt_ref[h, HD:] = one_row[:16]


def qkv_call(block, blocks, heads, info, x, cos, sin, w, carried):
    rows = x.shape[0]
    S = rows * blocks
    rb = min(256, rows)
    steps = rows // rb
    width = w.shape[1]
    at = lambda i: block * steps + i
    outs = (
        jax.ShapeDtypeStruct((S, D), bf),
        jax.ShapeDtypeStruct((heads, S, 128), bf),
        jax.ShapeDtypeStruct((heads, S, 128), bf),
        jax.ShapeDtypeStruct((heads, 128, S), bf),
        jax.ShapeDtypeStruct((heads, HD, S), bf),
        jax.ShapeDtypeStruct((heads, 80, S), bf),
    )
    in_specs = [
        pl.BlockSpec(memory_space=pltpu.SMEM),
        pl.BlockSpec((rb, D), lambda i: (i, 0)),
        pl.BlockSpec((rb, 128), lambda i: (at(i), 0)),
        pl.BlockSpec((rb, 128), lambda i: (at(i), 0)),
        pl.BlockSpec((D, width), lambda i: (0, 0)),
    ]
    aliases = {}
    if carried is not None:
        first = len(in_specs)
        in_specs += [pl.BlockSpec(memory_space=pl.ANY)] * 6
        aliases = {first + n: n for n in range(6)}
    return pl.pallas_call(
        functools.partial(qkv_kernel, heads),
        grid=(steps,),
        out_shape=outs,
        in_specs=in_specs,
        out_specs=(
            pl.BlockSpec((rb, D), lambda i: (at(i), 0)),
            pl.BlockSpec((heads, rb, 128), lambda i: (0, at(i), 0)),
            pl.BlockSpec((heads, rb, 128), lambda i: (0, at(i), 0)),
            pl.BlockSpec((heads, 128, rb), lambda i: (0, 0, at(i))),
            pl.BlockSpec((heads, HD, rb), lambda i: (0, 0, at(i))),
            pl.BlockSpec((heads, 80, rb), lambda i: (0, 0, at(i))),
        ),
        scratch_shapes=[pltpu.VMEM((8, D), f32)],
        input_output_aliases=aliases,
        compiler_params=pltpu.CompilerParams(vmem_limit_bytes=48 * 2**20),
        cost_estimate=pl.CostEstimate(
            flops=4 * rows * D * width, bytes_accessed=rows * 8192, transcendentals=0
        ),
        name="qkv",
    )(info, x, cos, sin, w, *(carried or ()))


def attend_kernel(kc, half, count, k_ref, qa_ref, qb_ref, v_ref, *refs):
    refs = refs[count:]
    pa_ref, pb_ref, oa_ref, ob_ref, la_ref, lb_ref = refs[:6]
    chunks = refs[6 : 6 + half]
    sa_ref, sb_ref, m_ref = refs[6 + half :]
    i = pl.program_id(0)
    rows = k_ref.shape[1]
    bq = qa_ref.shape[2]

    def stage(new, old):
        if new is not None:
            q_ref, s_new, new_slot = new
            q = q_ref[0]
            m = jnp.full((8, bq), -jnp.inf, f32)
        if old is not None:
            s_old, old_slot, p_ref, o_ref, l_ref, block = old
            top = jnp.max(m_ref[old_slot], axis=0, keepdims=True)
            acc = jnp.zeros((v_ref.shape[1], bq), f32)
        for c in range(rows // kc):
            at = slice(c * kc, (c + 1) * kc)
            if new is not None:
                s = dg(k_ref[0, at, :], q, NN)
                s_new[at, :] = s
                m = jnp.maximum(m, jnp.max(s.reshape(kc // 8, 8, bq), axis=0))
            if old is not None:
                p = jnp.exp2(s_old[at, :] - top).astype(bf)
                p_ref[0, at, :] = p
                acc = acc + dg(v_ref[0, :, at], p, NN)
        if new is not None:
            m_ref[new_slot] = m
        if old is not None:
            linv = 1.0 / acc[HD : HD + 1, :]
            o = acc[:HD, :] * linv
            o_ref[...] = o
            l_ref[0] = linv
            low = o.astype(bf)
            for j in range(half):

                @pl.when(block // 2 == j)
                def _():
                    chunks[j][:, old_slot * bq : (old_slot + 1) * bq] = low

    first = (qa_ref, sa_ref, 0)
    odd = (sb_ref, 1, pb_ref, ob_ref, lb_ref, 2 * i - 1)

    @pl.when(i == 0)
    def _():
        stage(first, None)

    @pl.when((i > 0) & (i < half))
    def _():
        stage(first, odd)

    @pl.when(i == half)
    def _():
        stage(None, odd)

    @pl.when(i < half)
    def _():
        stage((qb_ref, sb_ref, 1), (sa_ref, 0, pa_ref, oa_ref, la_ref, 2 * i))


def attend(h, k, qt, vt, groups, after, kc=256):
    S = k.shape[1]
    bq = S // groups // 2
    a = lambda i: jnp.minimum(i, groups - 1)
    b = lambda i: jnp.maximum(i - 1, 0)
    outs = pl.pallas_call(
        functools.partial(attend_kernel, kc, groups, len(after)),
        grid=(groups + 1,),
        out_shape=(jax.ShapeDtypeStruct((groups, S, bq), bf),) * 2
        + (jax.ShapeDtypeStruct((HD, S // 2), f32),) * 2
        + (jax.ShapeDtypeStruct((groups, 1, bq), f32),) * 2
        + (jax.ShapeDtypeStruct((HD, 2 * bq), bf),) * groups,
        in_specs=[
            pl.BlockSpec((1, S, 128), lambda i: (h, 0, 0)),
            pl.BlockSpec((1, 128, bq), lambda i: (h, 0, 2 * a(i))),
            pl.BlockSpec((1, 128, bq), lambda i: (h, 0, 2 * a(i) + 1)),
            pl.BlockSpec((1, 80, S), lambda i: (h, 0, 0)),
        ]
        + [pl.BlockSpec(memory_space=pl.ANY)] * len(after),
        out_specs=(
            pl.BlockSpec((1, S, bq), lambda i: (a(i), 0, 0)),
            pl.BlockSpec((1, S, bq), lambda i: (b(i), 0, 0)),
            pl.BlockSpec((HD, bq), lambda i: (0, a(i))),
            pl.BlockSpec((HD, bq), lambda i: (0, b(i))),
            pl.BlockSpec((1, 1, bq), lambda i: (a(i), 0, 0)),
            pl.BlockSpec((1, 1, bq), lambda i: (b(i), 0, 0)),
        )
        + (pl.BlockSpec((HD, 2 * bq), lambda i: (0, 0)),) * groups,
        scratch_shapes=[
            pltpu.VMEM((S, bq), f32),
            pltpu.VMEM((S, bq), f32),
            pltpu.VMEM((2, 8, bq), f32),
        ],
        compiler_params=pltpu.CompilerParams(vmem_limit_bytes=58 * 2**20),
        cost_estimate=pl.CostEstimate(
            flops=16 * HD * S * S, bytes_accessed=2 * S * S, transcendentals=S * S
        ),
        name="attend",
    )(k, qt, qt, vt, *after)
    return outs[:6], list(outs[6:])


def attend_back_kernel(kc, groups, v_ref, kt_ref, q_ref, *refs):
    oa_ref, ob_ref, la_ref, lb_ref, pa_ref, pb_ref, cos_ref, sin_ref, n_ref = refs[:9]
    do_refs = refs[9 : 9 + groups]
    outs = refs[-5 - groups : -5]
    grad_ref, acc_ref, do_ref, held_ref, sem = refs[-5:]
    i = pl.program_id(0)
    rows = v_ref.shape[1]
    width = q_ref.shape[2]
    bq = width // 2
    fetch = pltpu.make_async_copy(n_ref, held_ref, sem)

    @pl.when(i == 0)
    def _():
        fetch.start()
        acc_ref[...] = jnp.zeros_like(acc_ref)

    for j in range(groups):

        @pl.when(i == j)
        def _():
            do_ref[...] = do_refs[j][...]

    zero = jnp.zeros((HD, bq), bf)
    r = lax.broadcasted_iota(jnp.int32, (16, bq), 0)
    sides = []
    for n, (o_ref, l_ref, p_ref) in enumerate(((oa_ref, la_ref, pa_ref), (ob_ref, lb_ref, pb_ref))):
        at = slice(n * bq, (n + 1) * bq)
        dop = (do_ref[:, at].astype(f32) * l_ref[0]).astype(bf)
        delta = jnp.sum(dop.astype(f32) * o_ref[...], axis=0, keepdims=True)
        high = delta.astype(bf).astype(f32)
        tail = jnp.where(r == 0, high, jnp.where(r == 1, delta - high, 0.0)).astype(bf)
        doe = jnp.concatenate([dop, tail, jnp.zeros((128 - HD - 16, bq), bf)], axis=0)
        right_v = jnp.concatenate([dop, zero], axis=0)
        right_k = jnp.concatenate([zero, q_ref[0, :HD, at]], axis=0)
        sides.append((p_ref, doe, right_v, right_k))
    dq = [jnp.zeros((HD, bq), f32), jnp.zeros((HD, bq), f32)]
    for n, (p_ref, doe, right_v, right_k) in enumerate(sides):
        for c in range(rows // kc):
            at = slice(c * kc, (c + 1) * kc)
            p = p_ref[0, at, :]
            ds = p * dg(v_ref[0, at, :], doe, NN).astype(bf)
            acc_ref[at, :] = acc_ref[at, :] + dg(p, right_v, NT) + dg(ds, right_k, NT)
            dq[n] = dq[n] + dg(kt_ref[0, :, at], ds, NN)
    dq = jnp.concatenate(dq, axis=1) * HD**-0.5
    turned = jnp.concatenate([dq[HD // 2 :], -dq[: HD // 2]], axis=0)
    here = pl.ds(pl.multiple_of(i * width, width), width)
    dq = (dq * cos_ref[:, here] + turned * sin_ref[:, here]).astype(bf)
    for j in range(groups):

        @pl.when(i == j)
        def _():
            outs[j][:HD] = dq

    @pl.when(i == groups - 1)
    def _():
        fetch.wait()
        grad = jnp.zeros((3 * HD, D), f32)
        for j in range(groups):
            at = slice(j * width, (j + 1) * width)
            t = acc_ref[at, :].T
            dk = t[HD:] * LN2
            turned_k = jnp.concatenate([dk[HD // 2 :], -dk[: HD // 2]], axis=0)
            dk = dk * cos_ref[:, at] + turned_k * sin_ref[:, at]
            outs[j][HD : 2 * HD] = dk.astype(bf)
            outs[j][2 * HD :] = t[:HD].astype(bf)
            grad = grad + dg(outs[j][...], held_ref[at, :], NN)
        grad_ref[:, : 3 * HD] = grad.T.astype(bf)
        grad_ref[:, 3 * HD :] = jnp.zeros((D, HD), bf)


def attend_back(h, v, kt, qt, do, kept, cos, sin, normed, groups, place, after, kc=512):
    S = v.shape[1]
    width = S // groups
    bq = width // 2
    pa, pb, oa, ob, la, lb = kept
    columns, column, earlier = place
    extra = list(after) if earlier is None else [earlier] + list(after)
    whole = lambda i: (0, 0)
    by_block = lambda i: (i, 0, 0)
    outs = pl.pallas_call(
        functools.partial(attend_back_kernel, kc, groups),
        grid=(groups,),
        out_shape=(jax.ShapeDtypeStruct((3 * HD, width), bf),) * groups
        + (jax.ShapeDtypeStruct((D, columns), bf),),
        in_specs=[
            pl.BlockSpec((1, S, 128), lambda i: (h, 0, 0)),
            pl.BlockSpec((1, HD, S), lambda i: (h, 0, 0)),
            pl.BlockSpec((1, 128, width), lambda i: (h, 0, i)),
            pl.BlockSpec((HD, bq), lambda i: (0, i)),
            pl.BlockSpec((HD, bq), lambda i: (0, i)),
            pl.BlockSpec((1, 1, bq), by_block),
            pl.BlockSpec((1, 1, bq), by_block),
            pl.BlockSpec((1, S, bq), by_block),
            pl.BlockSpec((1, S, bq), by_block),
            pl.BlockSpec((HD, S), whole),
            pl.BlockSpec((HD, S), whole),
            pl.BlockSpec(memory_space=pl.ANY),
        ]
        + [pl.BlockSpec((HD, width), lambda i: (max(h - 1, 0), 0))] * groups
        + [pl.BlockSpec(memory_space=pl.ANY)] * len(extra),
        out_specs=(pl.BlockSpec((3 * HD, width), whole),) * groups
        + (pl.BlockSpec((D, 256), lambda i: (0, column)),),
        scratch_shapes=[
            pltpu.VMEM((S, 128), f32),
            pltpu.VMEM((HD, width), bf),
            pltpu.VMEM((S, D), bf),
            pltpu.SemaphoreType.DMA,
        ],
        input_output_aliases={} if earlier is None else {12 + groups: groups},
        compiler_params=pltpu.CompilerParams(vmem_limit_bytes=58 * 2**20),
        cost_estimate=pl.CostEstimate(
            flops=24 * HD * S * S, bytes_accessed=2 * S * S, transcendentals=0
        ),
        name="attend_back",
    )(v, kt, qt, oa, ob, la, lb, pa, pb, cos, sin, normed, *do, *extra)
    return list(outs[:groups]), outs[groups]


def normalize_back(gradient, unit_rows, inverse, gain_row):
    scaled = gradient * gain_row
    return inverse * (
        scaled
        - jnp.mean(scaled, axis=-1, keepdims=True)
        - unit_rows * jnp.mean(scaled * unit_rows, axis=-1, keepdims=True)
    )


def column(row_ref):
    row = row_ref[...].astype(f32)
    return jnp.broadcast_to(row, (8, row.shape[1])).T[:, :1]


def row_of(total):
    return jnp.broadcast_to(total, (total.shape[0], 128)).T[:1]


def half_kernel(packed, info_ref, in_ref, proj_ref, gain_ref, out_w_ref, *refs):
    half_ref = refs[-1]
    side = info_ref[0] & 1

    @pl.when(side == 0)
    def _():
        half_ref[...] = in_ref[...]

    @pl.when(side == 1)
    def _():
        short = in_ref.shape[0]
        half_ref[:, :D] = proj_ref[...]
        gain = jnp.broadcast_to(column(gain_ref), (short, 128)).astype(bf)
        half_ref[:, D : D + 128] = gain
        if packed:
            one, two, three = D + 128, 2 * D + 128, 2 * D + D // 2 + 128
            tall = out_w_ref.shape[0]
            half_ref[:, one:two] = out_w_ref[:short, :]
            half_ref[: tall - short, two:three] = out_w_ref[short:, : D // 2]
            half_ref[tall - short :, two:three] = out_w_ref[short:, D // 2 :]


def own_half(packed, info, in_w, proj_w, gain, out_w, after):
    vmem = pl.BlockSpec(memory_space=pltpu.VMEM)
    return pl.pallas_call(
        functools.partial(half_kernel, packed),
        out_shape=jax.ShapeDtypeStruct(in_w.shape, bf),
        in_specs=[pl.BlockSpec(memory_space=pltpu.SMEM)]
        + [vmem] * 4
        + [pl.BlockSpec(memory_space=pl.ANY)] * len(after),
        out_specs=vmem,
        name="own_half",
    )(info, in_w, proj_w, gain, out_w, *after)


def hold(array, after):
    def kernel(*refs):
        pass

    return pl.pallas_call(
        kernel,
        out_shape=jax.ShapeDtypeStruct(array.shape, array.dtype),
        in_specs=[pl.BlockSpec(memory_space=pl.ANY)] * (1 + len(after)),
        out_specs=pl.BlockSpec(memory_space=pl.ANY),
        input_output_aliases={0: 0},
        name="hold",
    )(array, *after)


def middle_kernel(groups, heads, ff, shards, info_ref, x_ref, dy_ref, mine_ref, other_ref, *refs):
    count = groups * heads
    given = len(refs) - count - 2 * groups - 13
    out_given = refs[:given]
    chunks = refs[given : given + count]
    d_first = refs[given + count : given + count + groups]
    d_rest = refs[given + count + groups : given + count + 2 * groups]
    (result_ref, dh_ref, mixed_ref, second_ref, dgu_ref, inner_ref, branch_ref,
     g_ref, t_ref, out_w_ref, w_ref, rest_ref, sems) = refs[given + count + 2 * groups :]
    width = heads * HD
    me = info_ref[0]

    @pl.when(pl.program_id(0) == 0)
    def _():
        def fetch(first, second):
            copies = [
                pltpu.make_async_copy(first, w_ref, sems.at[0]),
                pltpu.make_async_copy(second, rest_ref, sems.at[1]),
            ]
            for copy in copies:
                copy.start()
            for copy in copies:
                copy.wait()

        @pl.when((me & 1) == 0)
        def _():
            fetch(mine_ref, other_ref)

        @pl.when((me & 1) == 1)
        def _():
            fetch(other_ref, mine_ref)

        g_ref[...] = rest_ref[:, D : D + 128].astype(f32).T[:8]
        if given:
            out_w_ref[...] = out_given[0][...]
        else:
            tall, short = ff // shards, D // shards
            rest = tall - short
            one, two, three = D + 128, 2 * D + 128, 2 * D + D // 2 + 128
            for f in range(shards):
                src = slice(f * short, (f + 1) * short)
                out_w_ref[f * tall : f * tall + short, :] = rest_ref[src, one:two]
                dst = slice(f * tall + short, (f + 1) * tall)
                src = slice(f * short, f * short + rest)
                out_w_ref[dst, : D // 2] = rest_ref[src, two:three]
                src = slice(f * short + rest, f * short + 2 * rest)
                out_w_ref[dst, D // 2 :] = rest_ref[src, two:three]

    for h in range(heads):
        for j in range(groups):
            start = pl.multiple_of((me ^ j) * width + h * HD, HD)
            mixed_ref[pl.ds(start, HD), :] = chunks[h * groups + j][...]
    gain = g_ref[:1]
    proj = rest_ref[:, :D]
    hidden = x_ref[...].astype(f32) + dg(mixed_ref[...], proj, TN)
    unit, inverse = unit_rows_of(hidden)
    second = (unit * gain).astype(bf)
    second_ref[...] = second
    dy = dy_ref[...]
    result = hidden
    d_second = jnp.zeros_like(hidden)
    step = 384
    for c in range(ff // step):
        a = slice(c * step, (c + 1) * step)
        b = slice(ff + c * step, ff + (c + 1) * step)
        gate = dg(second, w_ref[:, a], NN)
        up = dg(second, w_ref[:, b], NN)
        d_inner = dg(dy, out_w_ref[a, :], NT)
        bell = 0.5 + 0.5 * lax.erf(gate * 0.7071067811865476)
        gelu = gate * bell
        inner = (gelu * up).astype(bf)
        inner_ref[:, a] = inner
        result = result + dg(inner, out_w_ref[a, :], NN)
        slope = bell + gate * (jnp.exp(-0.5 * gate * gate) * 0.3989422804014327)
        d_gate = (d_inner * up * slope).astype(bf)
        d_up = (d_inner * gelu).astype(bf)
        dgu_ref[:, a] = d_gate
        dgu_ref[:, b] = d_up
        d_second = d_second + dg(d_gate, w_ref[:, a], NT) + dg(d_up, w_ref[:, b], NT)
    result_ref[...] = result.astype(bf)
    d_hidden = dy.astype(f32) + normalize_back(d_second, unit, inverse, gain)
    dh_ref[...] = d_hidden
    branch = d_hidden.astype(bf)
    branch_ref[...] = branch
    t_ref[...] = dg(proj, branch, NT).astype(bf)
    for j in range(groups):
        start = pl.multiple_of((me ^ j) * width, HD)
        d_first[j][...] = t_ref[pl.ds(start, HD), :]
        d_rest[j][...] = t_ref[pl.ds(start + HD, width - HD), :]


def middle(groups, heads, shards, ff, info, x, dy, mine, other, out_w, chunks):
    rows = x.shape[0]
    rb = min(256, rows)
    by_row = lambda i: (i, 0)
    by_column = lambda i: (0, i)
    whole = lambda i: (0, 0)
    outs = pl.pallas_call(
        functools.partial(middle_kernel, groups, heads, ff, shards),
        grid=(rows // rb,),
        out_shape=(jax.ShapeDtypeStruct((HD, rows), bf),) * groups
        + (jax.ShapeDtypeStruct(((heads - 1) * HD, rows), bf),) * groups
        + (
            jax.ShapeDtypeStruct((rows, D), bf),
            jax.ShapeDtypeStruct((rows, D), f32),
            jax.ShapeDtypeStruct((D, rows), bf),
            jax.ShapeDtypeStruct((rows, D), bf),
            jax.ShapeDtypeStruct((rows, 2 * ff), bf),
            jax.ShapeDtypeStruct((rows, ff), bf),
            jax.ShapeDtypeStruct((rows, D), bf),
        ),
        in_specs=[
            pl.BlockSpec(memory_space=pltpu.SMEM),
            pl.BlockSpec((rb, D), by_row),
            pl.BlockSpec((rb, D), by_row),
            pl.BlockSpec(memory_space=pl.ANY),
            pl.BlockSpec(memory_space=pl.ANY),
        ]
        + [pl.BlockSpec(w.shape, whole, pipeline_mode=pl.Buffered(1)) for w in out_w]
        + [pl.BlockSpec((HD, rb), by_column)] * (groups * heads),
        out_specs=(pl.BlockSpec((HD, rb), by_column),) * groups
        + (pl.BlockSpec(((heads - 1) * HD, rb), by_column),) * groups
        + (
            pl.BlockSpec((rb, D), by_row),
            pl.BlockSpec((rb, D), by_row),
            pl.BlockSpec((D, rb), by_column),
            pl.BlockSpec((rb, D), by_row),
            pl.BlockSpec((rb, 2 * ff), by_row),
            pl.BlockSpec((rb, ff), by_row),
            pl.BlockSpec((rb, D), by_row),
        ),
        scratch_shapes=[
            pltpu.VMEM((8, D), f32),
            pltpu.VMEM((D, rb), bf),
            pltpu.VMEM((ff, D), bf),
            pltpu.VMEM(mine.shape, bf),
            pltpu.VMEM(mine.shape, bf),
            pltpu.SemaphoreType.DMA((2,)),
        ],
        compiler_params=pltpu.CompilerParams(vmem_limit_bytes=58 * 2**20),
        cost_estimate=pl.CostEstimate(
            flops=rows * D * (14 * ff + 4 * D), bytes_accessed=30 * 2**20, transcendentals=rows * ff
        ),
        name="middle",
    )(info, x, dy, mine, other, *out_w, *chunks)
    return list(outs[:groups]), list(outs[groups : 2 * groups]), outs[2 * groups :]


def last_kernel(groups, chosen, x_ref, base_ref, gain_ref, *refs):
    count = groups * len(chosen)
    chunks = refs[:count]
    pairs = refs[count : 2 * count]
    value_refs = refs[2 * count : 3 * count]
    out_ref, dp_ref, wh_ref, g_ref = refs[-4:]
    both = groups * 2 * HD

    @pl.when(pl.program_id(0) == 0)
    def _():
        g_ref[...] = gain_ref[...].astype(f32).T[HD : HD + 8]
        for n, h in enumerate(chosen):
            side = (h & 1) * HD
            pieces = [ref[...] for ref in pairs[n * groups : (n + 1) * groups]]
            pieces += [ref[:, side : side + HD] for ref in value_refs[n * groups : (n + 1) * groups]]
            wh_ref[:, n * D : (n + 1) * D] = jnp.concatenate(pieces, axis=1)

    for n in range(len(chosen)):
        for j in range(groups):
            chunk = chunks[n * groups + j]
            start = n * D + j * 2 * HD
            dp_ref[start : start + 2 * HD, :] = chunk[: 2 * HD, :]
            start = n * D + both + j * HD
            dp_ref[start : start + HD, :] = chunk[2 * HD :, :]
    d_normed = dg(wh_ref[...], dp_ref[...], NN).T
    unit, inverse = unit_rows_of(x_ref[...].astype(f32))
    out_ref[...] = base_ref[...] + normalize_back(d_normed, unit, inverse, g_ref[:1])


def last(groups, heads, chosen, x, base, peers, chunks, after):
    rows = chunks[0].shape[1]
    rb = min(256, rows)
    by_row = lambda i: (i, 0)

    def tile(n):
        return pl.BlockSpec((D, 128), lambda i: (0, n), pipeline_mode=pl.Buffered(1))

    pairs = [tile(h) for h in chosen for _ in peers]
    value_tiles = [tile(heads + h // 2) for h in chosen for _ in peers]
    return pl.pallas_call(
        functools.partial(last_kernel, groups, chosen),
        grid=(rows // rb,),
        out_shape=jax.ShapeDtypeStruct((rows, D), f32),
        in_specs=[
            pl.BlockSpec((rb, D), by_row),
            pl.BlockSpec((rb, D), by_row),
            tile(peers[0].shape[1] // 128 - 1),
        ]
        + [pl.BlockSpec((3 * HD, rb), lambda i: (0, i))] * len(chunks)
        + pairs
        + value_tiles
        + [pl.BlockSpec(memory_space=pl.ANY)] * len(after),
        out_specs=pl.BlockSpec((rb, D), by_row),
        scratch_shapes=[
            pltpu.VMEM((len(chosen) * D, rb), bf),
            pltpu.VMEM((D, len(chosen) * D), bf),
            pltpu.VMEM((8, D), f32),
        ],
        compiler_params=pltpu.CompilerParams(vmem_limit_bytes=58 * 2**20),
        cost_estimate=pl.CostEstimate(
            flops=2 * len(chosen) * rows * D * D, bytes_accessed=12 * 2**20, transcendentals=0
        ),
        name="last",
    )(x, base, peers[0], *chunks, *(list(peers) * (2 * len(chosen))), *after)


def pass_on(arrays, after):
    vmem = pl.BlockSpec(memory_space=pltpu.VMEM)
    count = len(arrays)

    def kernel(*refs):
        for source, target in zip(refs[:count], refs[-count:]):
            target[...] = source[...]

    return pl.pallas_call(
        kernel,
        out_shape=tuple(jax.ShapeDtypeStruct(a.shape, a.dtype) for a in arrays),
        in_specs=[vmem] * count + [pl.BlockSpec(memory_space=pl.ANY)] * len(after),
        out_specs=(vmem,) * count,
        compiler_params=pltpu.CompilerParams(vmem_limit_bytes=58 * 2**20),
        name="pass_on",
    )(*arrays, *after)


def own_kernel(groups, heads, info_ref, w_ref, gain_ref, out_ref):
    for g in range(groups):

        @pl.when(info_ref[0] == g)
        def _():
            def piece(t, h):
                start = t * D + (g * heads + h) * HD
                return w_ref[:, start : start + HD]

            pieces = []
            for h in range(heads):
                pieces += [piece(0, h), piece(1, h)]
            pieces += [piece(2, h) for h in range(heads)] + [column(gain_ref).astype(bf)]
            missing = out_ref.shape[2] - 3 * heads * HD - 1
            pieces.append(jnp.zeros((w_ref.shape[0], missing), bf))
            own = jnp.concatenate(pieces, axis=1)
            for f in range(out_ref.shape[0]):
                out_ref[f] = own


def own_columns(groups, heads, shards, info, w, gain):
    width = (3 * heads * HD + 128) // 128 * 128
    return pl.pallas_call(
        functools.partial(own_kernel, groups, heads),
        out_shape=jax.ShapeDtypeStruct((shards, w.shape[0], width), bf),
        in_specs=[
            pl.BlockSpec(memory_space=pltpu.SMEM),
            pl.BlockSpec(memory_space=pltpu.VMEM),
            pl.BlockSpec(memory_space=pltpu.VMEM),
        ],
        out_specs=pl.BlockSpec(memory_space=pltpu.VMEM),
        name="own_columns",
    )(info, w, gain)


def tables_kernel(cos_ref, sin_ref, cos_rows_ref, sin_rows_ref, cos_t_ref, sin_t_ref):
    c, s = cos_ref[...], sin_ref[...]
    cos_t_ref[...] = jnp.concatenate([c, c], axis=0)
    sin_t_ref[...] = jnp.concatenate([s, s], axis=0)
    scale = HD**-0.5 * LOG2E
    cos_rows_ref[...] = jnp.concatenate([c * scale, c * scale, c, c], axis=0).T
    sin_rows_ref[...] = jnp.concatenate([s * -scale, s * scale, -s, s], axis=0).T


def tables(cosine, sine):
    half, S = cosine.shape
    rb = min(1024, S)
    return pl.pallas_call(
        tables_kernel,
        grid=(S // rb,),
        out_shape=(jax.ShapeDtypeStruct((S, 4 * half), f32),) * 2
        + (jax.ShapeDtypeStruct((2 * half, S), f32),) * 2,
        in_specs=[pl.BlockSpec((half, rb), lambda i: (0, i))] * 2,
        out_specs=(pl.BlockSpec((rb, 4 * half), lambda i: (i, 0)),) * 2
        + (pl.BlockSpec((2 * half, rb), lambda i: (0, i)),) * 2,
        name="tables",
    )(cosine, sine)


def wide_kernel(second_ref, dgu_ref, mixed_ref, branch_ref, out_ref):
    g = pl.program_id(0)
    end = pl.num_programs(0) - 1

    @pl.when(g < end)
    def _():
        out_ref[0] = dg(second_ref[...], dgu_ref[...], TN).astype(bf)

    @pl.when(g == end)
    def _():
        out_ref[0] = dg(mixed_ref[...], branch_ref[...], NN).astype(bf)


def wide_grads(second, d_gate_up, mixed_t, branch):
    rows = second.shape[0]
    steps = d_gate_up.shape[1] // D
    whole = lambda i: (0, 0)
    return pl.pallas_call(
        wide_kernel,
        grid=(steps + 1,),
        in_specs=[
            pl.BlockSpec((rows, D), whole),
            pl.BlockSpec((rows, D), lambda i: (0, jnp.minimum(i, steps - 1))),
            pl.BlockSpec((D, rows), whole),
            pl.BlockSpec((rows, D), whole),
        ],
        out_specs=pl.BlockSpec((1, D, D), lambda i: (i, 0, 0)),
        out_shape=jax.ShapeDtypeStruct((steps + 1, D, D), bf),
        compiler_params=pltpu.CompilerParams(vmem_limit_bytes=58 * 2**20),
        cost_estimate=pl.CostEstimate(
            flops=2 * rows * D * D * (steps + 1), bytes_accessed=16 * 2**20, transcendentals=0
        ),
        name="wide_grads",
    )(second, d_gate_up, mixed_t, branch)


def tall_kernel(inner_ref, dy_ref, *refs):
    refs[-1][...] = dg(inner_ref[...], dy_ref[...], TN).astype(bf)


def tall_grads(inner, dy, after):
    rows, ff = inner.shape
    step = ff // 3
    return pl.pallas_call(
        tall_kernel,
        grid=(3,),
        in_specs=[
            pl.BlockSpec((rows, step), lambda i: (0, i)),
            pl.BlockSpec((rows, D), lambda i: (0, 0)),
        ]
        + [pl.BlockSpec(memory_space=pl.ANY)] * len(after),
        out_specs=pl.BlockSpec((step, D), lambda i: (i, 0)),
        out_shape=jax.ShapeDtypeStruct((ff, D), bf),
        compiler_params=pltpu.CompilerParams(vmem_limit_bytes=58 * 2**20),
        cost_estimate=pl.CostEstimate(
            flops=2 * rows * D * ff, bytes_accessed=6 * 2**20, transcendentals=0
        ),
        name="tall_grads",
    )(inner, dy, *after)


def add_kernel(count, *refs):
    total = None
    for ref in refs[:count]:
        for j in range(ref.shape[0]):
            term = ref[j].astype(f32)
            total = term if total is None else total + term
    out_ref = refs[-1]
    out_ref[...] = total.astype(out_ref.dtype)


def add_up(arrays, after, dtype=bf):
    arrays = [a if a.ndim == 3 else a[None] for a in arrays]
    rows, columns = arrays[0].shape[1:]
    rb = 256 if rows % 256 == 0 else rows
    return pl.pallas_call(
        functools.partial(add_kernel, len(arrays)),
        grid=(rows // rb,),
        out_shape=jax.ShapeDtypeStruct((rows, columns), dtype),
        in_specs=[pl.BlockSpec((n, rb, columns), lambda i: (0, i, 0)) for n in [a.shape[0] for a in arrays]]
        + [pl.BlockSpec(memory_space=pl.ANY)] * len(after),
        out_specs=pl.BlockSpec((rb, columns), lambda i: (i, 0)),
        compiler_params=pltpu.CompilerParams(vmem_limit_bytes=58 * 2**20),
        name="add_up",
    )(*arrays, *after)


def up16(n):
    return -(-n // 16) * 16


def owned_kernel(wide_ref, tall_ref, *refs):
    out_ref = refs[-1]
    start = 0
    for ref in (wide_ref, tall_ref):
        total = ref[0].astype(f32)
        for f in range(1, ref.shape[0]):
            total = total + ref[f].astype(f32)
        out_ref[start : start + ref.shape[1], :] = total.astype(bf)
        start += up16(ref.shape[1])


def owned(wide, tall, after):
    vmem = pl.BlockSpec(memory_space=pltpu.VMEM)
    return pl.pallas_call(
        owned_kernel,
        out_shape=jax.ShapeDtypeStruct((up16(wide.shape[1]) + up16(tall.shape[1]), D), bf),
        in_specs=[vmem, vmem] + [pl.BlockSpec(memory_space=pl.ANY)] * len(after),
        out_specs=vmem,
        compiler_params=pltpu.CompilerParams(vmem_limit_bytes=58 * 2**20),
        name="owned",
    )(wide, tall, *after)


def finish_wide_kernel(groups, info_ref, w_ref, gain_ref, *refs):
    in_ref, proj_ref, dgain_ref, out_ref, held_ref = refs[groups:]
    shard = w_ref.shape[0]
    start = up16(shard)
    tall = 0.0
    for j in range(groups):
        held_ref[info_ref[0] ^ j] = refs[j][...]
        tall = tall + refs[j][start : start + out_ref.shape[0], :].astype(f32)
    out_ref[...] = tall
    total = 0.0
    for g in range(groups - 1):
        at = slice(g * D, (g + 1) * D)
        grad = held_ref[g, :shard, :].astype(f32)
        in_ref[:, at] = grad
        total = total + jnp.sum(w_ref[:, at].astype(f32) * grad, axis=1, keepdims=True)
    proj_ref[...] = held_ref[groups - 1, :shard, :].astype(f32)
    dgain_ref[...] = row_of(total / column(gain_ref))


def finish_qkv_kernel(groups, heads, info_ref, w_ref, gain_ref, *refs):
    out_ref, dgain_ref, held_ref = refs[groups : groups + 3]
    for j in range(groups):
        held_ref[info_ref[0] ^ j] = refs[j][...]
    pieces = []
    for t in range(3):
        for g in range(groups):
            for h in range(heads):
                start = h * 256 + t * HD
                pieces.append(held_ref[g, :, start : start + HD].astype(f32))
    grad = jnp.concatenate(pieces, axis=1)
    out_ref[...] = grad
    total = jnp.sum(w_ref[...].astype(f32) * grad, axis=1, keepdims=True)
    dgain_ref[...] = row_of(total / column(gain_ref))


def finish(kernel, groups, info, w, gain, parts, shapes, name):
    vmem = pl.BlockSpec(memory_space=pltpu.VMEM)
    return pl.pallas_call(
        kernel,
        out_shape=tuple(jax.ShapeDtypeStruct(shape, f32) for shape in shapes),
        in_specs=[pl.BlockSpec(memory_space=pltpu.SMEM)] + [vmem] * (2 + groups),
        out_specs=(vmem,) * len(shapes),
        scratch_shapes=[pltpu.VMEM((groups,) + parts[0].shape, bf)],
        compiler_params=pltpu.CompilerParams(vmem_limit_bytes=58 * 2**20),
        name=name,
    )(info, w, gain, *parts)


def body(
    tokens, lengths, attn_gain, qkv_weight, proj_weight, ffn_gain, in_weight, out_weight, out_grad
):
    rows = tokens.shape[1]
    groups = lax.axis_size("seq")
    shards = lax.axis_size("fsdp")
    heads = HEADS // groups
    shard = D // shards
    me = lax.axis_index("seq")

    def swap(array, j, axis="seq"):
        size = lax.axis_size(axis)
        return lax.ppermute(array, axis, [(i, i ^ j) for i in range(size)])

    def exchange(chunks):
        return [chunks[0]] + [swap(chunks[j], j) for j in range(1, groups)]

    def gather(array):
        return lax.all_gather(array, "fsdp", axis=0, tiled=True)

    place = jnp.stack([me]).astype(jnp.int32)
    x0 = tokens[0]
    across = swap(x0, 2)
    near = swap(x0, 1)
    attn_row = attn_gain[None, :]
    ffn_row = ffn_gain[None, :]
    own = own_columns(groups, heads, shards, place, qkv_weight, attn_row)
    own = lax.all_to_all(own, "fsdp", split_axis=0, concat_axis=0, tiled=True).reshape(D, -1)

    half = HD // 2
    frequency = rope_base ** (-(lax.iota(f32, half) * 2.0) / HD)
    starts = [(me ^ j) * rows for j in range(groups)]
    positions = jnp.concatenate([s + lax.iota(jnp.int32, rows) for s in starts]).astype(f32)
    angles = frequency[:, None] * positions[None, :]
    cos_rows, sin_rows, cos_t, sin_t = tables(jnp.cos(angles), jnp.sin(angles))

    def project(j, block, carried):
        info = jnp.stack([starts[j], lengths[0]]).astype(jnp.int32)
        return qkv_call(j, groups, heads, info, block, cos_rows, sin_rows, own, carried)

    carried = project(0, x0, None)
    carried = project(1, near, carried)
    across = hold(across, [carried[0]])
    diagonal = swap(across, 1)
    carried = project(2, across, carried)
    normed, k, v, qt, kt, vt = project(3, diagonal, carried)

    ff = in_weight.shape[1] // 2
    tall = out_weight.shape[0]
    packed = shards <= 8
    mine = gather(own_half(packed, place, in_weight, proj_weight, ffn_row, out_weight, [own]))
    other = swap(mine, 1)
    out_full = [] if packed else [gather(out_weight)]

    own_near, own_across = swap(own, 1), swap(own, 2)
    own_diagonal = swap(own_across, 1)
    peers = [own, own_near, own_across, own_diagonal]

    kept = []
    chunks = []
    orders = [[], [own_near, own_across], [own_diagonal]]
    for h in range(heads):
        saved, mixed = attend(h, k, qt, vt, groups, orders[h])
        kept.append(saved)
        chunks += exchange(mixed)

    dy = out_grad[0]
    d_first, d_rest, (result, d_hidden, mixed_t, second, d_gate_up, inner, branch) = middle(
        groups, heads, shards, ff, place, x0, dy, mine, other, out_full, chunks
    )
    d_first = exchange(d_first)
    d_rest = exchange(d_rest)

    def to_owner(array):
        parts = array.reshape(shards, array.shape[0] // shards, -1)
        return lax.all_to_all(parts, "fsdp", split_axis=0, concat_axis=0, tiled=True)

    def from_peers(array):
        return [array] + [swap(array, j) for j in range(1, groups)]

    wide_grad = wide_grads(second, d_gate_up, mixed_t, branch)
    tall_grad = tall_grads(inner, dy, [wide_grad] + d_first[1:])
    wide_sent = lax.all_to_all(wide_grad, "seq", split_axis=0, concat_axis=0, tiled=True)
    tall_parts = to_owner(tall_grad)

    def back(h, grad_place, after):
        d_mixed = d_first if h == 0 else d_rest
        return attend_back(
            h, v, kt, qt, d_mixed, kept[h], cos_t, sin_t, normed, groups, grad_place, after
        )

    sent_0, qkv_first = back(0, (512, 0, None), [tall_grad])
    wide_sum = add_up([wide_sent], [qkv_first])
    wide_parts = to_owner(wide_sum)
    received_0 = exchange(sent_0)

    sent_1, qkv_first = back(1, (512, 1, qkv_first), [wide_sum])
    both = owned(wide_parts, tall_parts, [qkv_first] + received_0[1:])
    both_peers = from_peers(both)
    received_1 = exchange(sent_1)
    qkv_parts = to_owner(qkv_first)

    sent_2, qkv_second = back(2, (256, 0, None), [both])
    *others, qkv_second = pass_on(sent_2[1:] + [qkv_second], received_1[1:] + [qkv_parts])
    sent_2 = sent_2[:1] + others
    received_2 = exchange(sent_2)
    qkv_second_parts = to_owner(qkv_second)

    base = last(
        groups, heads, (0, 1), x0, d_hidden, peers, received_0 + received_1, [qkv_second]
    )
    first_sum = add_up([qkv_parts], [qkv_second])
    in_weight_grad, proj_weight_grad, ffn_gain_grad, out_weight_grad = finish(
        functools.partial(finish_wide_kernel, groups),
        groups, place, in_weight, ffn_row, both_peers,
        ((shard, 2 * ff), (shard, D), (1, shard), (tall, D)), "finish_wide",
    )
    second_sum = add_up([qkv_second_parts], [])
    qkv_peers = from_peers(jnp.concatenate([first_sum, second_sum], axis=1))
    tokens_grad = last(groups, heads, (2,), x0, base, peers, received_2, [])
    qkv_weight_grad, attn_gain_grad = finish(
        functools.partial(finish_qkv_kernel, groups, heads),
        groups, place, qkv_weight, attn_row, qkv_peers,
        ((shard, 3 * D), (1, shard)), "finish_qkv",
    )
    return (
        result[None],
        tokens_grad[None],
        attn_gain_grad[0],
        qkv_weight_grad,
        proj_weight_grad,
        ffn_gain_grad[0],
        in_weight_grad,
        out_weight_grad,
    )


def solution(mesh):
    in_specs = (
        P("fsdp", "seq", None),
        P("fsdp"),
        P("fsdp"),
        P("fsdp", None),
        P("fsdp", None),
        P("fsdp"),
        P("fsdp", None),
        P("fsdp", None),
        P("fsdp", "seq", None),
    )
    out_specs = (
        P("fsdp", "seq", None),
        P("fsdp", "seq", None),
        P("fsdp"),
        P("fsdp", None),
        P("fsdp", None),
        P("fsdp"),
        P("fsdp", None),
        P("fsdp", None),
    )
    return jax.shard_map(body, mesh=mesh, in_specs=in_specs, out_specs=out_specs, check_vma=False)
```

```python
import functools

import jax
import jax.numpy as jnp
from jax import lax
from jax.experimental import pallas as pl
from jax.experimental.pallas import tpu as pltpu
from jax.sharding import PartitionSpec as P

D = 768
HEADS = 12
HD = 64

epsilon = 1e-05
rope_base = 160000.0
masked_score = -1e30
LOG2E = 1.4426950408889634
LN2 = 0.6931471805599453

bf = jnp.bfloat16
f32 = jnp.float32
NN = ((1,), (0,))
NT = ((1,), (1,))
TN = ((0,), (0,))


def dg(a, b, dims):
    return lax.dot_general(a, b, (dims, ((), ())), preferred_element_type=f32)


def unit_rows_of(x):
    centred = x - jnp.mean(x, axis=-1, keepdims=True)
    inverse = lax.rsqrt(jnp.mean(centred * centred, axis=-1, keepdims=True) + epsilon)
    return centred * inverse, inverse


def qkv_kernel(heads, info_ref, x_ref, cos_ref, sin_ref, w_ref, *refs):
    n_ref, k_ref, v_ref, qt_ref, kt_ref, vt_ref, g_ref = refs[-7:]
    rb = x_ref.shape[0]
    value_at = heads * 128

    @pl.when(pl.program_id(0) == 0)
    def _():
        last = w_ref[:, w_ref.shape[1] - 128 :].astype(f32).T
        g_ref[...] = last[HD : HD + 8]

    unit, _ = unit_rows_of(x_ref[...].astype(f32))
    normed = (unit * g_ref[:1]).astype(bf)
    n_ref[...] = normed
    lane = lax.broadcasted_iota(jnp.int32, (rb, 128), 1)
    row = lax.broadcasted_iota(jnp.int32, (rb, 128), 0)
    position = info_ref[0] + pl.program_id(0) * rb + row
    bias = jnp.where(position < info_ref[1], 0.0, masked_score)
    key_tail = jnp.where(lane == HD, bias, 0.0)
    value_tail = jnp.where(lane < HD + 2, -1.0, 0.0)
    head_lane = lane < HD
    lower = (lane & (HD - 1)) < HD // 2
    one_row = jnp.where(lax.broadcasted_iota(jnp.int32, (HD, rb), 0) == 0, 1.0, 0.0).astype(bf)
    y = dg(normed, w_ref[...], NN)
    for h in range(heads):
        t = y[:, h * 128 : (h + 1) * 128]
        turned = jnp.where(lower, pltpu.roll(t, 128 - HD // 2, 1), pltpu.roll(t, HD // 2, 1))
        t = t * cos_ref[...] + turned * sin_ref[...]
        k_ref[h] = jnp.where(head_lane, pltpu.roll(t, HD, 1), key_tail).astype(bf)
        t = t.T.astype(bf)
        qt_ref[h, :HD] = t[:HD]
        qt_ref[h, HD:] = one_row
        kt_ref[h] = t[HD:]
    for h in range(heads):
        at = value_at + h // 2 * 128
        t = y[:, at : at + 128]
        turned = t if h % 2 == 0 else pltpu.roll(t, HD, 1)
        v_ref[h] = jnp.where(head_lane, turned, value_tail).astype(bf)
        if h % 2 == 0:
            t_rows = t.T.astype(bf)
        vt_ref[h, :HD] = t_rows[:HD] if h % 2 == 0 else t_rows[HD:]
        vt_ref[h, HD:] = one_row[:16]


def qkv_call(block, blocks, heads, info, x, cos, sin, w, carried):
    rows = x.shape[0]
    S = rows * blocks
    rb = min(256, rows)
    steps = rows // rb
    width = w.shape[1]
    at = lambda i: block * steps + i
    outs = (
        jax.ShapeDtypeStruct((S, D), bf),
        jax.ShapeDtypeStruct((heads, S, 128), bf),
        jax.ShapeDtypeStruct((heads, S, 128), bf),
        jax.ShapeDtypeStruct((heads, 128, S), bf),
        jax.ShapeDtypeStruct((heads, HD, S), bf),
        jax.ShapeDtypeStruct((heads, 80, S), bf),
    )
    in_specs = [
        pl.BlockSpec(memory_space=pltpu.SMEM),
        pl.BlockSpec((rb, D), lambda i: (i, 0)),
        pl.BlockSpec((rb, 128), lambda i: (at(i), 0)),
        pl.BlockSpec((rb, 128), lambda i: (at(i), 0)),
        pl.BlockSpec((D, width), lambda i: (0, 0)),
    ]
    aliases = {}
    if carried is not None:
        first = len(in_specs)
        in_specs += [pl.BlockSpec(memory_space=pl.ANY)] * 6
        aliases = {first + n: n for n in range(6)}
    return pl.pallas_call(
        functools.partial(qkv_kernel, heads),
        grid=(steps,),
        out_shape=outs,
        in_specs=in_specs,
        out_specs=(
            pl.BlockSpec((rb, D), lambda i: (at(i), 0)),
            pl.BlockSpec((heads, rb, 128), lambda i: (0, at(i), 0)),
            pl.BlockSpec((heads, rb, 128), lambda i: (0, at(i), 0)),
            pl.BlockSpec((heads, 128, rb), lambda i: (0, 0, at(i))),
            pl.BlockSpec((heads, HD, rb), lambda i: (0, 0, at(i))),
            pl.BlockSpec((heads, 80, rb), lambda i: (0, 0, at(i))),
        ),
        scratch_shapes=[pltpu.VMEM((8, D), f32)],
        input_output_aliases=aliases,
        compiler_params=pltpu.CompilerParams(vmem_limit_bytes=48 * 2**20),
        cost_estimate=pl.CostEstimate(
            flops=4 * rows * D * width, bytes_accessed=rows * 8192, transcendentals=0
        ),
        name="qkv",
    )(info, x, cos, sin, w, *(carried or ()))


def attend_kernel(kc, half, count, k_ref, qa_ref, qb_ref, v_ref, *refs):
    refs = refs[count:]
    pa_ref, pb_ref, oa_ref, ob_ref, la_ref, lb_ref = refs[:6]
    chunks = refs[6 : 6 + half]
    sa_ref, sb_ref, m_ref = refs[6 + half :]
    i = pl.program_id(0)
    rows = k_ref.shape[1]
    bq = qa_ref.shape[2]

    def stage(new, old):
        if new is not None:
            q_ref, s_new, new_slot = new
            q = q_ref[0]
            m = jnp.full((8, bq), -jnp.inf, f32)
        if old is not None:
            s_old, old_slot, p_ref, o_ref, l_ref, block = old
            top = jnp.max(m_ref[old_slot], axis=0, keepdims=True)
            acc = jnp.zeros((v_ref.shape[1], bq), f32)
        for c in range(rows // kc):
            at = slice(c * kc, (c + 1) * kc)
            if new is not None:
                s = dg(k_ref[0, at, :], q, NN)
                s_new[at, :] = s
                m = jnp.maximum(m, jnp.max(s.reshape(kc // 8, 8, bq), axis=0))
            if old is not None:
                p = jnp.exp2(s_old[at, :] - top).astype(bf)
                p_ref[0, at, :] = p
                acc = acc + dg(v_ref[0, :, at], p, NN)
        if new is not None:
            m_ref[new_slot] = m
        if old is not None:
            linv = 1.0 / acc[HD : HD + 1, :]
            o = acc[:HD, :] * linv
            o_ref[...] = o
            l_ref[0] = linv
            low = o.astype(bf)
            for j in range(half):

                @pl.when(block // 2 == j)
                def _():
                    chunks[j][:, old_slot * bq : (old_slot + 1) * bq] = low

    first = (qa_ref, sa_ref, 0)
    odd = (sb_ref, 1, pb_ref, ob_ref, lb_ref, 2 * i - 1)

    @pl.when(i == 0)
    def _():
        stage(first, None)

    @pl.when((i > 0) & (i < half))
    def _():
        stage(first, odd)

    @pl.when(i == half)
    def _():
        stage(None, odd)

    @pl.when(i < half)
    def _():
        stage((qb_ref, sb_ref, 1), (sa_ref, 0, pa_ref, oa_ref, la_ref, 2 * i))


def attend(h, k, qt, vt, groups, after, kc=256):
    S = k.shape[1]
    bq = S // groups // 2
    a = lambda i: jnp.minimum(i, groups - 1)
    b = lambda i: jnp.maximum(i - 1, 0)
    outs = pl.pallas_call(
        functools.partial(attend_kernel, kc, groups, len(after)),
        grid=(groups + 1,),
        out_shape=(jax.ShapeDtypeStruct((groups, S, bq), bf),) * 2
        + (jax.ShapeDtypeStruct((HD, S // 2), f32),) * 2
        + (jax.ShapeDtypeStruct((groups, 1, bq), f32),) * 2
        + (jax.ShapeDtypeStruct((HD, 2 * bq), bf),) * groups,
        in_specs=[
            pl.BlockSpec((1, S, 128), lambda i: (h, 0, 0)),
            pl.BlockSpec((1, 128, bq), lambda i: (h, 0, 2 * a(i))),
            pl.BlockSpec((1, 128, bq), lambda i: (h, 0, 2 * a(i) + 1)),
            pl.BlockSpec((1, 80, S), lambda i: (h, 0, 0)),
        ]
        + [pl.BlockSpec(memory_space=pl.ANY)] * len(after),
        out_specs=(
            pl.BlockSpec((1, S, bq), lambda i: (a(i), 0, 0)),
            pl.BlockSpec((1, S, bq), lambda i: (b(i), 0, 0)),
            pl.BlockSpec((HD, bq), lambda i: (0, a(i))),
            pl.BlockSpec((HD, bq), lambda i: (0, b(i))),
            pl.BlockSpec((1, 1, bq), lambda i: (a(i), 0, 0)),
            pl.BlockSpec((1, 1, bq), lambda i: (b(i), 0, 0)),
        )
        + (pl.BlockSpec((HD, 2 * bq), lambda i: (0, 0)),) * groups,
        scratch_shapes=[
            pltpu.VMEM((S, bq), f32),
            pltpu.VMEM((S, bq), f32),
            pltpu.VMEM((2, 8, bq), f32),
        ],
        compiler_params=pltpu.CompilerParams(vmem_limit_bytes=58 * 2**20),
        cost_estimate=pl.CostEstimate(
            flops=16 * HD * S * S, bytes_accessed=2 * S * S, transcendentals=S * S
        ),
        name="attend",
    )(k, qt, qt, vt, *after)
    return outs[:6], list(outs[6:])


def attend_back_kernel(kc, groups, v_ref, kt_ref, q_ref, *refs):
    oa_ref, ob_ref, la_ref, lb_ref, pa_ref, pb_ref, cos_ref, sin_ref, n_ref = refs[:9]
    do_refs = refs[9 : 9 + groups]
    outs = refs[-5 - groups : -5]
    grad_ref, acc_ref, do_ref, held_ref, sem = refs[-5:]
    i = pl.program_id(0)
    rows = v_ref.shape[1]
    width = q_ref.shape[2]
    bq = width // 2
    fetch = pltpu.make_async_copy(n_ref, held_ref, sem)

    @pl.when(i == 0)
    def _():
        fetch.start()
        acc_ref[...] = jnp.zeros_like(acc_ref)

    for j in range(groups):

        @pl.when(i == j)
        def _():
            do_ref[...] = do_refs[j][...]

    zero = jnp.zeros((HD, bq), bf)
    r = lax.broadcasted_iota(jnp.int32, (16, bq), 0)
    sides = []
    for n, (o_ref, l_ref, p_ref) in enumerate(((oa_ref, la_ref, pa_ref), (ob_ref, lb_ref, pb_ref))):
        at = slice(n * bq, (n + 1) * bq)
        dop = (do_ref[:, at].astype(f32) * l_ref[0]).astype(bf)
        delta = jnp.sum(dop.astype(f32) * o_ref[...], axis=0, keepdims=True)
        high = delta.astype(bf).astype(f32)
        tail = jnp.where(r == 0, high, jnp.where(r == 1, delta - high, 0.0)).astype(bf)
        doe = jnp.concatenate([dop, tail, jnp.zeros((128 - HD - 16, bq), bf)], axis=0)
        right_v = jnp.concatenate([dop, zero], axis=0)
        right_k = jnp.concatenate([zero, q_ref[0, :HD, at]], axis=0)
        sides.append((p_ref, doe, right_v, right_k))
    dq = [jnp.zeros((HD, bq), f32), jnp.zeros((HD, bq), f32)]
    for n, (p_ref, doe, right_v, right_k) in enumerate(sides):
        for c in range(rows // kc):
            at = slice(c * kc, (c + 1) * kc)
            p = p_ref[0, at, :]
            ds = p * dg(v_ref[0, at, :], doe, NN).astype(bf)
            acc_ref[at, :] = acc_ref[at, :] + dg(p, right_v, NT) + dg(ds, right_k, NT)
            dq[n] = dq[n] + dg(kt_ref[0, :, at], ds, NN)
    dq = jnp.concatenate(dq, axis=1) * HD**-0.5
    turned = jnp.concatenate([dq[HD // 2 :], -dq[: HD // 2]], axis=0)
    here = pl.ds(pl.multiple_of(i * width, width), width)
    dq = (dq * cos_ref[:, here] + turned * sin_ref[:, here]).astype(bf)
    for j in range(groups):

        @pl.when(i == j)
        def _():
            outs[j][:HD] = dq

    @pl.when(i == groups - 1)
    def _():
        fetch.wait()
        grad = jnp.zeros((3 * HD, D), f32)
        for j in range(groups):
            at = slice(j * width, (j + 1) * width)
            t = acc_ref[at, :].T
            dk = t[HD:] * LN2
            turned_k = jnp.concatenate([dk[HD // 2 :], -dk[: HD // 2]], axis=0)
            dk = dk * cos_ref[:, at] + turned_k * sin_ref[:, at]
            outs[j][HD : 2 * HD] = dk.astype(bf)
            outs[j][2 * HD :] = t[:HD].astype(bf)
            grad = grad + dg(outs[j][...], held_ref[at, :], NN)
        grad_ref[:, : 3 * HD] = grad.T.astype(bf)
        grad_ref[:, 3 * HD :] = jnp.zeros((D, HD), bf)


def attend_back(h, v, kt, qt, do, kept, cos, sin, normed, groups, place, after, kc=512):
    S = v.shape[1]
    width = S // groups
    bq = width // 2
    pa, pb, oa, ob, la, lb = kept
    columns, column, earlier = place
    extra = list(after) if earlier is None else [earlier] + list(after)
    whole = lambda i: (0, 0)
    by_block = lambda i: (i, 0, 0)
    outs = pl.pallas_call(
        functools.partial(attend_back_kernel, kc, groups),
        grid=(groups,),
        out_shape=(jax.ShapeDtypeStruct((3 * HD, width), bf),) * groups
        + (jax.ShapeDtypeStruct((D, columns), bf),),
        in_specs=[
            pl.BlockSpec((1, S, 128), lambda i: (h, 0, 0)),
            pl.BlockSpec((1, HD, S), lambda i: (h, 0, 0)),
            pl.BlockSpec((1, 128, width), lambda i: (h, 0, i)),
            pl.BlockSpec((HD, bq), lambda i: (0, i)),
            pl.BlockSpec((HD, bq), lambda i: (0, i)),
            pl.BlockSpec((1, 1, bq), by_block),
            pl.BlockSpec((1, 1, bq), by_block),
            pl.BlockSpec((1, S, bq), by_block),
            pl.BlockSpec((1, S, bq), by_block),
            pl.BlockSpec((HD, S), whole),
            pl.BlockSpec((HD, S), whole),
            pl.BlockSpec(memory_space=pl.ANY),
        ]
        + [pl.BlockSpec((HD, width), lambda i: (h, 0))] * groups
        + [pl.BlockSpec(memory_space=pl.ANY)] * len(extra),
        out_specs=(pl.BlockSpec((3 * HD, width), whole),) * groups
        + (pl.BlockSpec((D, 256), lambda i: (0, column)),),
        scratch_shapes=[
            pltpu.VMEM((S, 128), f32),
            pltpu.VMEM((HD, width), bf),
            pltpu.VMEM((S, D), bf),
            pltpu.SemaphoreType.DMA,
        ],
        input_output_aliases={} if earlier is None else {12 + groups: groups},
        compiler_params=pltpu.CompilerParams(vmem_limit_bytes=58 * 2**20),
        cost_estimate=pl.CostEstimate(
            flops=24 * HD * S * S, bytes_accessed=2 * S * S, transcendentals=0
        ),
        name="attend_back",
    )(v, kt, qt, oa, ob, la, lb, pa, pb, cos, sin, normed, *do, *extra)
    return list(outs[:groups]), outs[groups]


def normalize_back(gradient, unit_rows, inverse, gain_row):
    scaled = gradient * gain_row
    return inverse * (
        scaled
        - jnp.mean(scaled, axis=-1, keepdims=True)
        - unit_rows * jnp.mean(scaled * unit_rows, axis=-1, keepdims=True)
    )


def column(row_ref):
    row = row_ref[...].astype(f32)
    return jnp.broadcast_to(row, (8, row.shape[1])).T[:, :1]


def row_of(total):
    return jnp.broadcast_to(total, (total.shape[0], 128)).T[:1]


def half_kernel(packed, info_ref, in_ref, proj_ref, gain_ref, out_w_ref, *refs):
    half_ref = refs[-1]
    side = info_ref[0] & 1

    @pl.when(side == 0)
    def _():
        half_ref[...] = in_ref[...]

    @pl.when(side == 1)
    def _():
        short = in_ref.shape[0]
        half_ref[:, :D] = proj_ref[...]
        gain = jnp.broadcast_to(column(gain_ref), (short, 128)).astype(bf)
        half_ref[:, D : D + 128] = gain
        if packed:
            one, two, three = D + 128, 2 * D + 128, 2 * D + D // 2 + 128
            tall = out_w_ref.shape[0]
            half_ref[:, one:two] = out_w_ref[:short, :]
            half_ref[: tall - short, two:three] = out_w_ref[short:, : D // 2]
            half_ref[tall - short :, two:three] = out_w_ref[short:, D // 2 :]


def own_half(packed, info, in_w, proj_w, gain, out_w, after):
    vmem = pl.BlockSpec(memory_space=pltpu.VMEM)
    return pl.pallas_call(
        functools.partial(half_kernel, packed),
        out_shape=jax.ShapeDtypeStruct(in_w.shape, bf),
        in_specs=[pl.BlockSpec(memory_space=pltpu.SMEM)]
        + [vmem] * 4
        + [pl.BlockSpec(memory_space=pl.ANY)] * len(after),
        out_specs=vmem,
        name="own_half",
    )(info, in_w, proj_w, gain, out_w, *after)


def hold(array, after):
    def kernel(*refs):
        pass

    return pl.pallas_call(
        kernel,
        out_shape=jax.ShapeDtypeStruct(array.shape, array.dtype),
        in_specs=[pl.BlockSpec(memory_space=pl.ANY)] * (1 + len(after)),
        out_specs=pl.BlockSpec(memory_space=pl.ANY),
        input_output_aliases={0: 0},
        name="hold",
    )(array, *after)


def middle_kernel(groups, heads, ff, shards, info_ref, x_ref, dy_ref, mine_ref, other_ref, *refs):
    count = groups * heads
    given = len(refs) - count - groups - 13
    out_given = refs[:given]
    chunks = refs[given : given + count]
    d_chunks = refs[given + count : given + count + groups]
    (result_ref, dh_ref, mixed_ref, second_ref, dgu_ref, inner_ref, branch_ref,
     g_ref, t_ref, out_w_ref, w_ref, rest_ref, sems) = refs[given + count + groups :]
    width = heads * HD
    me = info_ref[0]

    @pl.when(pl.program_id(0) == 0)
    def _():
        def fetch(first, second):
            copies = [
                pltpu.make_async_copy(first, w_ref, sems.at[0]),
                pltpu.make_async_copy(second, rest_ref, sems.at[1]),
            ]
            for copy in copies:
                copy.start()
            for copy in copies:
                copy.wait()

        @pl.when((me & 1) == 0)
        def _():
            fetch(mine_ref, other_ref)

        @pl.when((me & 1) == 1)
        def _():
            fetch(other_ref, mine_ref)

        g_ref[...] = rest_ref[:, D : D + 128].astype(f32).T[:8]
        if given:
            out_w_ref[...] = out_given[0][...]
        else:
            tall, short = ff // shards, D // shards
            rest = tall - short
            one, two, three = D + 128, 2 * D + 128, 2 * D + D // 2 + 128
            for f in range(shards):
                src = slice(f * short, (f + 1) * short)
                out_w_ref[f * tall : f * tall + short, :] = rest_ref[src, one:two]
                dst = slice(f * tall + short, (f + 1) * tall)
                src = slice(f * short, f * short + rest)
                out_w_ref[dst, : D // 2] = rest_ref[src, two:three]
                src = slice(f * short + rest, f * short + 2 * rest)
                out_w_ref[dst, D // 2 :] = rest_ref[src, two:three]

    for h in range(heads):
        for j in range(groups):
            start = pl.multiple_of((me ^ j) * width + h * HD, HD)
            mixed_ref[pl.ds(start, HD), :] = chunks[h * groups + j][...]
    gain = g_ref[:1]
    proj = rest_ref[:, :D]
    hidden = x_ref[...].astype(f32) + dg(mixed_ref[...], proj, TN)
    unit, inverse = unit_rows_of(hidden)
    second = (unit * gain).astype(bf)
    second_ref[...] = second
    dy = dy_ref[...]
    result = hidden
    d_second = jnp.zeros_like(hidden)
    step = 384
    for c in range(ff // step):
        a = slice(c * step, (c + 1) * step)
        b = slice(ff + c * step, ff + (c + 1) * step)
        gate = dg(second, w_ref[:, a], NN)
        up = dg(second, w_ref[:, b], NN)
        d_inner = dg(dy, out_w_ref[a, :], NT)
        bell = 0.5 + 0.5 * lax.erf(gate * 0.7071067811865476)
        gelu = gate * bell
        inner = (gelu * up).astype(bf)
        inner_ref[:, a] = inner
        result = result + dg(inner, out_w_ref[a, :], NN)
        slope = bell + gate * (jnp.exp(-0.5 * gate * gate) * 0.3989422804014327)
        d_gate = (d_inner * up * slope).astype(bf)
        d_up = (d_inner * gelu).astype(bf)
        dgu_ref[:, a] = d_gate
        dgu_ref[:, b] = d_up
        d_second = d_second + dg(d_gate, w_ref[:, a], NT) + dg(d_up, w_ref[:, b], NT)
    result_ref[...] = result.astype(bf)
    d_hidden = dy.astype(f32) + normalize_back(d_second, unit, inverse, gain)
    dh_ref[...] = d_hidden
    branch = d_hidden.astype(bf)
    branch_ref[...] = branch
    t_ref[...] = dg(proj, branch, NT).astype(bf)
    for j in range(groups):
        start = pl.multiple_of((me ^ j) * width, HD)
        d_chunks[j][...] = t_ref[pl.ds(start, width), :]


def middle(groups, heads, shards, ff, info, x, dy, mine, other, out_w, chunks):
    rows = x.shape[0]
    rb = min(256, rows)
    by_row = lambda i: (i, 0)
    by_column = lambda i: (0, i)
    whole = lambda i: (0, 0)
    outs = pl.pallas_call(
        functools.partial(middle_kernel, groups, heads, ff, shards),
        grid=(rows // rb,),
        out_shape=(jax.ShapeDtypeStruct((heads * HD, rows), bf),) * groups
        + (
            jax.ShapeDtypeStruct((rows, D), bf),
            jax.ShapeDtypeStruct((rows, D), f32),
            jax.ShapeDtypeStruct((D, rows), bf),
            jax.ShapeDtypeStruct((rows, D), bf),
            jax.ShapeDtypeStruct((rows, 2 * ff), bf),
            jax.ShapeDtypeStruct((rows, ff), bf),
            jax.ShapeDtypeStruct((rows, D), bf),
        ),
        in_specs=[
            pl.BlockSpec(memory_space=pltpu.SMEM),
            pl.BlockSpec((rb, D), by_row),
            pl.BlockSpec((rb, D), by_row),
            pl.BlockSpec(memory_space=pl.ANY),
            pl.BlockSpec(memory_space=pl.ANY),
        ]
        + [pl.BlockSpec(w.shape, whole, pipeline_mode=pl.Buffered(1)) for w in out_w]
        + [pl.BlockSpec((HD, rb), by_column)] * (groups * heads),
        out_specs=(pl.BlockSpec((heads * HD, rb), by_column),) * groups
        + (
            pl.BlockSpec((rb, D), by_row),
            pl.BlockSpec((rb, D), by_row),
            pl.BlockSpec((D, rb), by_column),
            pl.BlockSpec((rb, D), by_row),
            pl.BlockSpec((rb, 2 * ff), by_row),
            pl.BlockSpec((rb, ff), by_row),
            pl.BlockSpec((rb, D), by_row),
        ),
        scratch_shapes=[
            pltpu.VMEM((8, D), f32),
            pltpu.VMEM((D, rb), bf),
            pltpu.VMEM((ff, D), bf),
            pltpu.VMEM(mine.shape, bf),
            pltpu.VMEM(mine.shape, bf),
            pltpu.SemaphoreType.DMA((2,)),
        ],
        compiler_params=pltpu.CompilerParams(vmem_limit_bytes=58 * 2**20),
        cost_estimate=pl.CostEstimate(
            flops=rows * D * (14 * ff + 4 * D), bytes_accessed=30 * 2**20, transcendentals=rows * ff
        ),
        name="middle",
    )(info, x, dy, mine, other, *out_w, *chunks)
    return list(outs[:groups]), outs[groups:]


def last_kernel(groups, chosen, x_ref, base_ref, gain_ref, *refs):
    count = groups * len(chosen)
    chunks = refs[:count]
    pairs = refs[count : 2 * count]
    value_refs = refs[2 * count : 3 * count]
    out_ref, dp_ref, wh_ref, g_ref = refs[-4:]
    both = groups * 2 * HD

    @pl.when(pl.program_id(0) == 0)
    def _():
        g_ref[...] = gain_ref[...].astype(f32).T[HD : HD + 8]
        for n, h in enumerate(chosen):
            side = (h & 1) * HD
            pieces = [ref[...] for ref in pairs[n * groups : (n + 1) * groups]]
            pieces += [ref[:, side : side + HD] for ref in value_refs[n * groups : (n + 1) * groups]]
            wh_ref[:, n * D : (n + 1) * D] = jnp.concatenate(pieces, axis=1)

    for n in range(len(chosen)):
        for j in range(groups):
            chunk = chunks[n * groups + j]
            start = n * D + j * 2 * HD
            dp_ref[start : start + 2 * HD, :] = chunk[: 2 * HD, :]
            start = n * D + both + j * HD
            dp_ref[start : start + HD, :] = chunk[2 * HD :, :]
    d_normed = dg(wh_ref[...], dp_ref[...], NN).T
    unit, inverse = unit_rows_of(x_ref[...].astype(f32))
    out_ref[...] = base_ref[...] + normalize_back(d_normed, unit, inverse, g_ref[:1])


def last(groups, heads, chosen, x, base, peers, chunks, after):
    rows = chunks[0].shape[1]
    rb = min(256, rows)
    by_row = lambda i: (i, 0)

    def tile(n):
        return pl.BlockSpec((D, 128), lambda i: (0, n), pipeline_mode=pl.Buffered(1))

    pairs = [tile(h) for h in chosen for _ in peers]
    value_tiles = [tile(heads + h // 2) for h in chosen for _ in peers]
    return pl.pallas_call(
        functools.partial(last_kernel, groups, chosen),
        grid=(rows // rb,),
        out_shape=jax.ShapeDtypeStruct((rows, D), f32),
        in_specs=[
            pl.BlockSpec((rb, D), by_row),
            pl.BlockSpec((rb, D), by_row),
            tile(peers[0].shape[1] // 128 - 1),
        ]
        + [pl.BlockSpec((3 * HD, rb), lambda i: (0, i))] * len(chunks)
        + pairs
        + value_tiles
        + [pl.BlockSpec(memory_space=pl.ANY)] * len(after),
        out_specs=pl.BlockSpec((rb, D), by_row),
        scratch_shapes=[
            pltpu.VMEM((len(chosen) * D, rb), bf),
            pltpu.VMEM((D, len(chosen) * D), bf),
            pltpu.VMEM((8, D), f32),
        ],
        compiler_params=pltpu.CompilerParams(vmem_limit_bytes=58 * 2**20),
        cost_estimate=pl.CostEstimate(
            flops=2 * len(chosen) * rows * D * D, bytes_accessed=12 * 2**20, transcendentals=0
        ),
        name="last",
    )(x, base, peers[0], *chunks, *(list(peers) * (2 * len(chosen))), *after)


def pass_on(arrays, after):
    vmem = pl.BlockSpec(memory_space=pltpu.VMEM)
    count = len(arrays)

    def kernel(*refs):
        for source, target in zip(refs[:count], refs[-count:]):
            target[...] = source[...]

    return pl.pallas_call(
        kernel,
        out_shape=tuple(jax.ShapeDtypeStruct(a.shape, a.dtype) for a in arrays),
        in_specs=[vmem] * count + [pl.BlockSpec(memory_space=pl.ANY)] * len(after),
        out_specs=(vmem,) * count,
        compiler_params=pltpu.CompilerParams(vmem_limit_bytes=58 * 2**20),
        name="pass_on",
    )(*arrays, *after)


def own_kernel(groups, heads, info_ref, w_ref, gain_ref, out_ref):
    for g in range(groups):

        @pl.when(info_ref[0] == g)
        def _():
            def piece(t, h):
                start = t * D + (g * heads + h) * HD
                return w_ref[:, start : start + HD]

            pieces = []
            for h in range(heads):
                pieces += [piece(0, h), piece(1, h)]
            pieces += [piece(2, h) for h in range(heads)] + [column(gain_ref).astype(bf)]
            missing = out_ref.shape[2] - 3 * heads * HD - 1
            pieces.append(jnp.zeros((w_ref.shape[0], missing), bf))
            own = jnp.concatenate(pieces, axis=1)
            for f in range(out_ref.shape[0]):
                out_ref[f] = own


def own_columns(groups, heads, shards, info, w, gain):
    width = (3 * heads * HD + 128) // 128 * 128
    return pl.pallas_call(
        functools.partial(own_kernel, groups, heads),
        out_shape=jax.ShapeDtypeStruct((shards, w.shape[0], width), bf),
        in_specs=[
            pl.BlockSpec(memory_space=pltpu.SMEM),
            pl.BlockSpec(memory_space=pltpu.VMEM),
            pl.BlockSpec(memory_space=pltpu.VMEM),
        ],
        out_specs=pl.BlockSpec(memory_space=pltpu.VMEM),
        name="own_columns",
    )(info, w, gain)


def tables_kernel(cos_ref, sin_ref, cos_rows_ref, sin_rows_ref, cos_t_ref, sin_t_ref):
    c, s = cos_ref[...], sin_ref[...]
    cos_t_ref[...] = jnp.concatenate([c, c], axis=0)
    sin_t_ref[...] = jnp.concatenate([s, s], axis=0)
    scale = HD**-0.5 * LOG2E
    cos_rows_ref[...] = jnp.concatenate([c * scale, c * scale, c, c], axis=0).T
    sin_rows_ref[...] = jnp.concatenate([s * -scale, s * scale, -s, s], axis=0).T


def tables(cosine, sine):
    half, S = cosine.shape
    rb = min(1024, S)
    return pl.pallas_call(
        tables_kernel,
        grid=(S // rb,),
        out_shape=(jax.ShapeDtypeStruct((S, 4 * half), f32),) * 2
        + (jax.ShapeDtypeStruct((2 * half, S), f32),) * 2,
        in_specs=[pl.BlockSpec((half, rb), lambda i: (0, i))] * 2,
        out_specs=(pl.BlockSpec((rb, 4 * half), lambda i: (i, 0)),) * 2
        + (pl.BlockSpec((2 * half, rb), lambda i: (0, i)),) * 2,
        name="tables",
    )(cosine, sine)


def wide_kernel(second_ref, dgu_ref, mixed_ref, branch_ref, out_ref):
    g = pl.program_id(0)
    end = pl.num_programs(0) - 1

    @pl.when(g < end)
    def _():
        out_ref[0] = dg(second_ref[...], dgu_ref[...], TN).astype(bf)

    @pl.when(g == end)
    def _():
        out_ref[0] = dg(mixed_ref[...], branch_ref[...], NN).astype(bf)


def wide_grads(second, d_gate_up, mixed_t, branch):
    rows = second.shape[0]
    steps = d_gate_up.shape[1] // D
    whole = lambda i: (0, 0)
    return pl.pallas_call(
        wide_kernel,
        grid=(steps + 1,),
        in_specs=[
            pl.BlockSpec((rows, D), whole),
            pl.BlockSpec((rows, D), lambda i: (0, jnp.minimum(i, steps - 1))),
            pl.BlockSpec((D, rows), whole),
            pl.BlockSpec((rows, D), whole),
        ],
        out_specs=pl.BlockSpec((1, D, D), lambda i: (i, 0, 0)),
        out_shape=jax.ShapeDtypeStruct((steps + 1, D, D), bf),
        compiler_params=pltpu.CompilerParams(vmem_limit_bytes=58 * 2**20),
        cost_estimate=pl.CostEstimate(
            flops=2 * rows * D * D * (steps + 1), bytes_accessed=16 * 2**20, transcendentals=0
        ),
        name="wide_grads",
    )(second, d_gate_up, mixed_t, branch)


def tall_kernel(inner_ref, dy_ref, *refs):
    refs[-2][...] = dg(inner_ref[...], dy_ref[...], TN).astype(bf)


def tall_grads(inner, dy, wide, after):
    rows, ff = inner.shape
    step = ff // 3
    return pl.pallas_call(
        tall_kernel,
        grid=(3,),
        in_specs=[
            pl.BlockSpec((rows, step), lambda i: (0, i)),
            pl.BlockSpec((rows, D), lambda i: (0, 0)),
        ]
        + [pl.BlockSpec(memory_space=pl.ANY)] * (1 + len(after)),
        out_specs=(
            pl.BlockSpec((step, D), lambda i: (i, 0)),
            pl.BlockSpec(memory_space=pl.ANY),
        ),
        out_shape=(
            jax.ShapeDtypeStruct((ff, D), bf),
            jax.ShapeDtypeStruct(wide.shape, bf),
        ),
        input_output_aliases={2: 1},
        compiler_params=pltpu.CompilerParams(vmem_limit_bytes=58 * 2**20),
        cost_estimate=pl.CostEstimate(
            flops=2 * rows * D * ff, bytes_accessed=6 * 2**20, transcendentals=0
        ),
        name="tall_grads",
    )(inner, dy, wide, *after)


def add_kernel(count, *refs):
    total = None
    for ref in refs[:count]:
        for j in range(ref.shape[0]):
            term = ref[j].astype(f32)
            total = term if total is None else total + term
    out_ref = refs[-1]
    out_ref[...] = total.astype(out_ref.dtype)


def add_up(arrays, after, dtype=bf):
    arrays = [a if a.ndim == 3 else a[None] for a in arrays]
    rows, columns = arrays[0].shape[1:]
    rb = 256 if rows % 256 == 0 else rows
    return pl.pallas_call(
        functools.partial(add_kernel, len(arrays)),
        grid=(rows // rb,),
        out_shape=jax.ShapeDtypeStruct((rows, columns), dtype),
        in_specs=[pl.BlockSpec((n, rb, columns), lambda i: (0, i, 0)) for n in [a.shape[0] for a in arrays]]
        + [pl.BlockSpec(memory_space=pl.ANY)] * len(after),
        out_specs=pl.BlockSpec((rb, columns), lambda i: (i, 0)),
        compiler_params=pltpu.CompilerParams(vmem_limit_bytes=58 * 2**20),
        name="add_up",
    )(*arrays, *after)


def up16(n):
    return -(-n // 16) * 16


def owned_kernel(wide_ref, tall_ref, *refs):
    out_ref = refs[-1]
    start = 0
    for ref in (wide_ref, tall_ref):
        total = ref[0].astype(f32)
        for f in range(1, ref.shape[0]):
            total = total + ref[f].astype(f32)
        out_ref[start : start + ref.shape[1], :] = total.astype(bf)
        start += up16(ref.shape[1])


def owned(wide, tall, after):
    vmem = pl.BlockSpec(memory_space=pltpu.VMEM)
    return pl.pallas_call(
        owned_kernel,
        out_shape=jax.ShapeDtypeStruct((up16(wide.shape[1]) + up16(tall.shape[1]), D), bf),
        in_specs=[vmem, vmem] + [pl.BlockSpec(memory_space=pl.ANY)] * len(after),
        out_specs=vmem,
        compiler_params=pltpu.CompilerParams(vmem_limit_bytes=58 * 2**20),
        name="owned",
    )(wide, tall, *after)


def finish_wide_kernel(groups, info_ref, w_ref, gain_ref, *refs):
    in_ref, proj_ref, dgain_ref, out_ref, held_ref = refs[groups:]
    shard = w_ref.shape[0]
    start = up16(shard)
    tall = 0.0
    for j in range(groups):
        held_ref[info_ref[0] ^ j] = refs[j][...]
        tall = tall + refs[j][start : start + out_ref.shape[0], :].astype(f32)
    out_ref[...] = tall
    total = 0.0
    for g in range(groups - 1):
        at = slice(g * D, (g + 1) * D)
        grad = held_ref[g, :shard, :].astype(f32)
        in_ref[:, at] = grad
        total = total + jnp.sum(w_ref[:, at].astype(f32) * grad, axis=1, keepdims=True)
    proj_ref[...] = held_ref[groups - 1, :shard, :].astype(f32)
    dgain_ref[...] = row_of(total / column(gain_ref))


def finish_qkv_kernel(groups, heads, info_ref, w_ref, gain_ref, *refs):
    out_ref, dgain_ref, held_ref = refs[groups : groups + 3]
    for j in range(groups):
        held_ref[info_ref[0] ^ j] = refs[j][...]
    pieces = []
    for t in range(3):
        for g in range(groups):
            for h in range(heads):
                start = h * 256 + t * HD
                pieces.append(held_ref[g, :, start : start + HD].astype(f32))
    grad = jnp.concatenate(pieces, axis=1)
    out_ref[...] = grad
    total = jnp.sum(w_ref[...].astype(f32) * grad, axis=1, keepdims=True)
    dgain_ref[...] = row_of(total / column(gain_ref))


def finish(kernel, groups, info, w, gain, parts, shapes, name):
    vmem = pl.BlockSpec(memory_space=pltpu.VMEM)
    return pl.pallas_call(
        kernel,
        out_shape=tuple(jax.ShapeDtypeStruct(shape, f32) for shape in shapes),
        in_specs=[pl.BlockSpec(memory_space=pltpu.SMEM)] + [vmem] * (2 + groups),
        out_specs=(vmem,) * len(shapes),
        scratch_shapes=[pltpu.VMEM((groups,) + parts[0].shape, bf)],
        compiler_params=pltpu.CompilerParams(vmem_limit_bytes=58 * 2**20),
        name=name,
    )(info, w, gain, *parts)


def body(
    tokens, lengths, attn_gain, qkv_weight, proj_weight, ffn_gain, in_weight, out_weight, out_grad
):
    rows = tokens.shape[1]
    groups = lax.axis_size("seq")
    shards = lax.axis_size("fsdp")
    heads = HEADS // groups
    shard = D // shards
    me = lax.axis_index("seq")

    def swap(array, j, axis="seq"):
        size = lax.axis_size(axis)
        return lax.ppermute(array, axis, [(i, i ^ j) for i in range(size)])

    def exchange(chunks):
        return [chunks[0]] + [swap(chunks[j], j) for j in range(1, groups)]

    def gather(array):
        return lax.all_gather(array, "fsdp", axis=0, tiled=True)

    place = jnp.stack([me]).astype(jnp.int32)
    x0 = tokens[0]
    across = swap(x0, 2)
    near = swap(x0, 1)
    attn_row = attn_gain[None, :]
    ffn_row = ffn_gain[None, :]
    own = own_columns(groups, heads, shards, place, qkv_weight, attn_row)
    own = lax.all_to_all(own, "fsdp", split_axis=0, concat_axis=0, tiled=True).reshape(D, -1)

    half = HD // 2
    frequency = rope_base ** (-(lax.iota(f32, half) * 2.0) / HD)
    starts = [(me ^ j) * rows for j in range(groups)]
    positions = jnp.concatenate([s + lax.iota(jnp.int32, rows) for s in starts]).astype(f32)
    angles = frequency[:, None] * positions[None, :]
    cos_rows, sin_rows, cos_t, sin_t = tables(jnp.cos(angles), jnp.sin(angles))

    def project(j, block, carried):
        info = jnp.stack([starts[j], lengths[0]]).astype(jnp.int32)
        return qkv_call(j, groups, heads, info, block, cos_rows, sin_rows, own, carried)

    diagonal = swap(across, 1)
    carried = project(2, across, None)
    carried = project(0, x0, carried)
    carried = project(1, near, carried)
    normed, k, v, qt, kt, vt = project(3, diagonal, carried)

    ff = in_weight.shape[1] // 2
    tall = out_weight.shape[0]
    packed = shards <= 8
    mine = gather(own_half(packed, place, in_weight, proj_weight, ffn_row, out_weight, [own, cos_t]))
    out_full = [] if packed else [gather(out_weight)]

    own = hold(own, [normed])
    own_near, own_across = swap(own, 1), swap(own, 2)
    own_diagonal = swap(own_across, 1)
    peers = [own, own_near, own_across, own_diagonal]

    kept = []
    chunks = []
    orders = [[], [own_near, own_across], [own_diagonal]]
    for h in range(heads):
        before = [kept[-1][2]] if kept else []
        if h == 2:
            before += chunks[1:groups]
        saved, mixed = attend(h, k, qt, vt, groups, orders[h] + before)
        kept.append(saved)
        chunks += exchange(mixed)
        if h == heads - 2:
            mine = hold(mine, [saved[2]])
            other = swap(mine, 1)

    dy = out_grad[0]
    d_mixed, (result, d_hidden, mixed_t, second, d_gate_up, inner, branch) = middle(
        groups, heads, shards, ff, place, x0, dy, mine, other, out_full, chunks
    )
    d_mixed = exchange(d_mixed)

    def to_owner(array):
        parts = array.reshape(shards, array.shape[0] // shards, -1)
        return lax.all_to_all(parts, "fsdp", split_axis=0, concat_axis=0, tiled=True)

    def from_peers(array):
        return [array] + [swap(array, j) for j in range(1, groups)]

    wide_grad = wide_grads(second, d_gate_up, mixed_t, branch)
    tall_grad, wide_grad = tall_grads(inner, dy, wide_grad, d_mixed[1:])
    wide_sent = lax.all_to_all(wide_grad, "seq", split_axis=0, concat_axis=0, tiled=True)
    tall_parts = to_owner(tall_grad)

    def back(h, grad_place, after):
        return attend_back(
            h, v, kt, qt, d_mixed, kept[h], cos_t, sin_t, normed, groups, grad_place, after
        )

    sent_0, qkv_first = back(0, (512, 0, None), [tall_grad])
    wide_sum = add_up([wide_sent], [qkv_first])
    wide_parts = to_owner(wide_sum)
    received_0 = exchange(sent_0)

    sent_1, qkv_first = back(1, (512, 1, qkv_first), [wide_sum])
    both = owned(wide_parts, tall_parts, [qkv_first] + received_0[1:])
    both_peers = from_peers(both)
    received_1 = exchange(sent_1)
    qkv_parts = to_owner(qkv_first)

    sent_2, qkv_second = back(2, (256, 0, None), [both])
    *others, qkv_second = pass_on(sent_2[1:] + [qkv_second], received_1[1:] + both_peers[1:] + [qkv_parts])
    sent_2 = sent_2[:1] + others
    received_2 = exchange(sent_2)
    qkv_second_parts = to_owner(qkv_second)

    base = last(
        groups, heads, (0, 1), x0, d_hidden, peers, received_0 + received_1, [qkv_second]
    )
    first_sum = add_up([qkv_parts], [qkv_second])
    in_weight_grad, proj_weight_grad, ffn_gain_grad, out_weight_grad = finish(
        functools.partial(finish_wide_kernel, groups),
        groups, place, in_weight, ffn_row, both_peers,
        ((shard, 2 * ff), (shard, D), (1, shard), (tall, D)), "finish_wide",
    )
    second_sum = add_up([qkv_second_parts], [])
    qkv_peers = from_peers(jnp.concatenate([first_sum, second_sum], axis=1))
    tokens_grad = last(groups, heads, (2,), x0, base, peers, received_2, [])
    qkv_weight_grad, attn_gain_grad = finish(
        functools.partial(finish_qkv_kernel, groups, heads),
        groups, place, qkv_weight, attn_row, qkv_peers,
        ((shard, 3 * D), (1, shard)), "finish_qkv",
    )
    return (
        result[None],
        tokens_grad[None],
        attn_gain_grad[0],
        qkv_weight_grad,
        proj_weight_grad,
        ffn_gain_grad[0],
        in_weight_grad,
        out_weight_grad,
    )


def solution(mesh):
    in_specs = (
        P("fsdp", "seq", None),
        P("fsdp"),
        P("fsdp"),
        P("fsdp", None),
        P("fsdp", None),
        P("fsdp"),
        P("fsdp", None),
        P("fsdp", None),
        P("fsdp", "seq", None),
    )
    out_specs = (
        P("fsdp", "seq", None),
        P("fsdp", "seq", None),
        P("fsdp"),
        P("fsdp", None),
        P("fsdp", None),
        P("fsdp"),
        P("fsdp", None),
        P("fsdp", None),
    )
    return jax.shard_map(body, mesh=mesh, in_specs=in_specs, out_specs=out_specs, check_vma=False)
```

```python
import functools

import jax
import jax.numpy as jnp
from jax import lax
from jax.experimental import pallas as pl
from jax.experimental.pallas import tpu as pltpu
from jax.sharding import PartitionSpec as P

D = 768
HEADS = 12
HD = 64

epsilon = 1e-05
rope_base = 160000.0
masked_score = -1e30
LOG2E = 1.4426950408889634
LN2 = 0.6931471805599453

bf = jnp.bfloat16
f32 = jnp.float32
NN = ((1,), (0,))
NT = ((1,), (1,))
TN = ((0,), (0,))


def dg(a, b, dims):
    return lax.dot_general(a, b, (dims, ((), ())), preferred_element_type=f32)


def unit_rows_of(x):
    centred = x - jnp.mean(x, axis=-1, keepdims=True)
    inverse = lax.rsqrt(jnp.mean(centred * centred, axis=-1, keepdims=True) + epsilon)
    return centred * inverse, inverse


def qkv_kernel(heads, info_ref, x_ref, cos_ref, sin_ref, w_ref, *refs):
    n_ref, k_ref, v_ref, qt_ref, kt_ref, vt_ref, g_ref = refs[-7:]
    rb = x_ref.shape[0]
    value_at = heads * 128

    @pl.when(pl.program_id(0) == 0)
    def _():
        last = w_ref[:, w_ref.shape[1] - 128 :].astype(f32).T
        g_ref[...] = last[HD : HD + 8]

    unit, _ = unit_rows_of(x_ref[...].astype(f32))
    normed = (unit * g_ref[:1]).astype(bf)
    n_ref[...] = normed
    lane = lax.broadcasted_iota(jnp.int32, (rb, 128), 1)
    row = lax.broadcasted_iota(jnp.int32, (rb, 128), 0)
    position = info_ref[0] + pl.program_id(0) * rb + row
    bias = jnp.where(position < info_ref[1], 0.0, masked_score)
    key_tail = jnp.where(lane == HD, bias, 0.0)
    value_tail = jnp.where(lane < HD + 2, -1.0, 0.0)
    head_lane = lane < HD
    lower = (lane & (HD - 1)) < HD // 2
    one_row = jnp.where(lax.broadcasted_iota(jnp.int32, (HD, rb), 0) == 0, 1.0, 0.0).astype(bf)
    y = dg(normed, w_ref[...], NN)
    for h in range(heads):
        t = y[:, h * 128 : (h + 1) * 128]
        turned = jnp.where(lower, pltpu.roll(t, 128 - HD // 2, 1), pltpu.roll(t, HD // 2, 1))
        t = t * cos_ref[...] + turned * sin_ref[...]
        k_ref[h] = jnp.where(head_lane, pltpu.roll(t, HD, 1), key_tail).astype(bf)
        t = t.T.astype(bf)
        qt_ref[h, :HD] = t[:HD]
        qt_ref[h, HD:] = one_row
        kt_ref[h] = t[HD:]
    for h in range(heads):
        at = value_at + h // 2 * 128
        t = y[:, at : at + 128]
        turned = t if h % 2 == 0 else pltpu.roll(t, HD, 1)
        v_ref[h] = jnp.where(head_lane, turned, value_tail).astype(bf)
        if h % 2 == 0:
            t_rows = t.T.astype(bf)
        vt_ref[h, :HD] = t_rows[:HD] if h % 2 == 0 else t_rows[HD:]
        vt_ref[h, HD:] = one_row[:16]


def qkv_call(block, blocks, heads, info, x, cos, sin, w, carried):
    rows = x.shape[0]
    S = rows * blocks
    rb = min(256, rows)
    steps = rows // rb
    width = w.shape[1]
    at = lambda i: block * steps + i
    outs = (
        jax.ShapeDtypeStruct((S, D), bf),
        jax.ShapeDtypeStruct((heads, S, 128), bf),
        jax.ShapeDtypeStruct((heads, S, 128), bf),
        jax.ShapeDtypeStruct((heads, 128, S), bf),
        jax.ShapeDtypeStruct((heads, HD, S), bf),
        jax.ShapeDtypeStruct((heads, 80, S), bf),
    )
    in_specs = [
        pl.BlockSpec(memory_space=pltpu.SMEM),
        pl.BlockSpec((rb, D), lambda i: (i, 0)),
        pl.BlockSpec((rb, 128), lambda i: (at(i), 0)),
        pl.BlockSpec((rb, 128), lambda i: (at(i), 0)),
        pl.BlockSpec((D, width), lambda i: (0, 0)),
    ]
    aliases = {}
    if carried is not None:
        first = len(in_specs)
        in_specs += [pl.BlockSpec(memory_space=pl.ANY)] * 6
        aliases = {first + n: n for n in range(6)}
    return pl.pallas_call(
        functools.partial(qkv_kernel, heads),
        grid=(steps,),
        out_shape=outs,
        in_specs=in_specs,
        out_specs=(
            pl.BlockSpec((rb, D), lambda i: (at(i), 0)),
            pl.BlockSpec((heads, rb, 128), lambda i: (0, at(i), 0)),
            pl.BlockSpec((heads, rb, 128), lambda i: (0, at(i), 0)),
            pl.BlockSpec((heads, 128, rb), lambda i: (0, 0, at(i))),
            pl.BlockSpec((heads, HD, rb), lambda i: (0, 0, at(i))),
            pl.BlockSpec((heads, 80, rb), lambda i: (0, 0, at(i))),
        ),
        scratch_shapes=[pltpu.VMEM((8, D), f32)],
        input_output_aliases=aliases,
        compiler_params=pltpu.CompilerParams(vmem_limit_bytes=48 * 2**20),
        cost_estimate=pl.CostEstimate(
            flops=4 * rows * D * width, bytes_accessed=rows * 8192, transcendentals=0
        ),
        name="qkv",
    )(info, x, cos, sin, w, *(carried or ()))


def attend_kernel(kc, half, count, k_ref, qa_ref, qb_ref, v_ref, *refs):
    refs = refs[count:]
    pa_ref, pb_ref, oa_ref, ob_ref, la_ref, lb_ref = refs[:6]
    chunks = refs[6 : 6 + half]
    sa_ref, sb_ref, m_ref = refs[6 + half :]
    i = pl.program_id(0)
    rows = k_ref.shape[1]
    bq = qa_ref.shape[2]

    def stage(new, old):
        if new is not None:
            q_ref, s_new, new_slot = new
            q = q_ref[0]
            m = jnp.full((8, bq), -jnp.inf, f32)
        if old is not None:
            s_old, old_slot, p_ref, o_ref, l_ref, block = old
            top = jnp.max(m_ref[old_slot], axis=0, keepdims=True)
            acc = jnp.zeros((v_ref.shape[1], bq), f32)
        for c in range(rows // kc):
            at = slice(c * kc, (c + 1) * kc)
            if new is not None:
                s = dg(k_ref[0, at, :], q, NN)
                s_new[at, :] = s
                m = jnp.maximum(m, jnp.max(s.reshape(kc // 8, 8, bq), axis=0))
            if old is not None:
                p = jnp.exp2(s_old[at, :] - top).astype(bf)
                p_ref[0, at, :] = p
                acc = acc + dg(v_ref[0, :, at], p, NN)
        if new is not None:
            m_ref[new_slot] = m
        if old is not None:
            linv = 1.0 / acc[HD : HD + 1, :]
            o = acc[:HD, :] * linv
            o_ref[...] = o
            l_ref[0] = linv
            low = o.astype(bf)
            for j in range(half):

                @pl.when(block // 2 == j)
                def _():
                    chunks[j][:, old_slot * bq : (old_slot + 1) * bq] = low

    first = (qa_ref, sa_ref, 0)
    odd = (sb_ref, 1, pb_ref, ob_ref, lb_ref, 2 * i - 1)

    @pl.when(i == 0)
    def _():
        stage(first, None)

    @pl.when((i > 0) & (i < half))
    def _():
        stage(first, odd)

    @pl.when(i == half)
    def _():
        stage(None, odd)

    @pl.when(i < half)
    def _():
        stage((qb_ref, sb_ref, 1), (sa_ref, 0, pa_ref, oa_ref, la_ref, 2 * i))


def attend(h, k, qt, vt, groups, after, kc=256):
    S = k.shape[1]
    bq = S // groups // 2
    a = lambda i: jnp.minimum(i, groups - 1)
    b = lambda i: jnp.maximum(i - 1, 0)
    outs = pl.pallas_call(
        functools.partial(attend_kernel, kc, groups, len(after)),
        grid=(groups + 1,),
        out_shape=(jax.ShapeDtypeStruct((groups, S, bq), bf),) * 2
        + (jax.ShapeDtypeStruct((HD, S // 2), f32),) * 2
        + (jax.ShapeDtypeStruct((groups, 1, bq), f32),) * 2
        + (jax.ShapeDtypeStruct((HD, 2 * bq), bf),) * groups,
        in_specs=[
            pl.BlockSpec((1, S, 128), lambda i: (h, 0, 0)),
            pl.BlockSpec((1, 128, bq), lambda i: (h, 0, 2 * a(i))),
            pl.BlockSpec((1, 128, bq), lambda i: (h, 0, 2 * a(i) + 1)),
            pl.BlockSpec((1, 80, S), lambda i: (h, 0, 0)),
        ]
        + [pl.BlockSpec(memory_space=pl.ANY)] * len(after),
        out_specs=(
            pl.BlockSpec((1, S, bq), lambda i: (a(i), 0, 0)),
            pl.BlockSpec((1, S, bq), lambda i: (b(i), 0, 0)),
            pl.BlockSpec((HD, bq), lambda i: (0, a(i))),
            pl.BlockSpec((HD, bq), lambda i: (0, b(i))),
            pl.BlockSpec((1, 1, bq), lambda i: (a(i), 0, 0)),
            pl.BlockSpec((1, 1, bq), lambda i: (b(i), 0, 0)),
        )
        + (pl.BlockSpec((HD, 2 * bq), lambda i: (0, 0)),) * groups,
        scratch_shapes=[
            pltpu.VMEM((S, bq), f32),
            pltpu.VMEM((S, bq), f32),
            pltpu.VMEM((2, 8, bq), f32),
        ],
        compiler_params=pltpu.CompilerParams(vmem_limit_bytes=58 * 2**20),
        cost_estimate=pl.CostEstimate(
            flops=16 * HD * S * S, bytes_accessed=2 * S * S, transcendentals=S * S
        ),
        name="attend",
    )(k, qt, qt, vt, *after)
    return outs[:6], list(outs[6:])


def attend_back_kernel(kc, groups, v_ref, kt_ref, q_ref, *refs):
    oa_ref, ob_ref, la_ref, lb_ref, pa_ref, pb_ref, cos_ref, sin_ref, n_ref = refs[:9]
    do_refs = refs[9 : 9 + groups]
    outs = refs[-5 - groups : -5]
    grad_ref, acc_ref, do_ref, held_ref, sem = refs[-5:]
    i = pl.program_id(0)
    rows = v_ref.shape[1]
    width = q_ref.shape[2]
    bq = width // 2
    fetch = pltpu.make_async_copy(n_ref, held_ref, sem)

    @pl.when(i == 0)
    def _():
        fetch.start()
        acc_ref[...] = jnp.zeros_like(acc_ref)

    for j in range(groups):

        @pl.when(i == j)
        def _():
            do_ref[...] = do_refs[j][...]

    zero = jnp.zeros((HD, bq), bf)
    r = lax.broadcasted_iota(jnp.int32, (16, bq), 0)
    sides = []
    for n, (o_ref, l_ref, p_ref) in enumerate(((oa_ref, la_ref, pa_ref), (ob_ref, lb_ref, pb_ref))):
        at = slice(n * bq, (n + 1) * bq)
        dop = (do_ref[:, at].astype(f32) * l_ref[0]).astype(bf)
        delta = jnp.sum(dop.astype(f32) * o_ref[...], axis=0, keepdims=True)
        high = delta.astype(bf).astype(f32)
        tail = jnp.where(r == 0, high, jnp.where(r == 1, delta - high, 0.0)).astype(bf)
        doe = jnp.concatenate([dop, tail, jnp.zeros((128 - HD - 16, bq), bf)], axis=0)
        right_v = jnp.concatenate([dop, zero], axis=0).T
        right_k = jnp.concatenate([zero, q_ref[0, :HD, at]], axis=0).T
        sides.append((p_ref, doe, jnp.concatenate([right_v, right_k], axis=0)))
    dq = [jnp.zeros((HD, bq), f32), jnp.zeros((HD, bq), f32)]
    for n, (p_ref, doe, right) in enumerate(sides):
        for c in range(rows // kc):
            at = slice(c * kc, (c + 1) * kc)
            p = p_ref[0, at, :]
            ds = p * dg(v_ref[0, at, :], doe, NN).astype(bf)
            acc_ref[at, :] = acc_ref[at, :] + dg(jnp.concatenate([p, ds], axis=1), right, NN)
            dq[n] = dq[n] + dg(kt_ref[0, :, at], ds, NN)
    dq = jnp.concatenate(dq, axis=1) * HD**-0.5
    turned = jnp.concatenate([dq[HD // 2 :], -dq[: HD // 2]], axis=0)
    here = pl.ds(pl.multiple_of(i * width, width), width)
    dq = (dq * cos_ref[:, here] + turned * sin_ref[:, here]).astype(bf)
    for j in range(groups):

        @pl.when(i == j)
        def _():
            outs[j][:HD] = dq

    @pl.when(i == groups - 1)
    def _():
        fetch.wait()
        grad = jnp.zeros((3 * HD, D), f32)
        for j in range(groups):
            at = slice(j * width, (j + 1) * width)
            t = acc_ref[at, :].T
            dk = t[HD:] * LN2
            turned_k = jnp.concatenate([dk[HD // 2 :], -dk[: HD // 2]], axis=0)
            dk = dk * cos_ref[:, at] + turned_k * sin_ref[:, at]
            outs[j][HD : 2 * HD] = dk.astype(bf)
            outs[j][2 * HD :] = t[:HD].astype(bf)
            grad = grad + dg(outs[j][...], held_ref[at, :], NN)
        grad_ref[:, : 3 * HD] = grad.T.astype(bf)
        grad_ref[:, 3 * HD :] = jnp.zeros((D, HD), bf)


def attend_back(h, v, kt, qt, do, kept, cos, sin, normed, groups, place, after, kc=256):
    S = v.shape[1]
    width = S // groups
    bq = width // 2
    pa, pb, oa, ob, la, lb = kept
    columns, column, earlier = place
    extra = list(after) if earlier is None else [earlier] + list(after)
    whole = lambda i: (0, 0)
    by_block = lambda i: (i, 0, 0)
    outs = pl.pallas_call(
        functools.partial(attend_back_kernel, kc, groups),
        grid=(groups,),
        out_shape=(jax.ShapeDtypeStruct((3 * HD, width), bf),) * groups
        + (jax.ShapeDtypeStruct((D, columns), bf),),
        in_specs=[
            pl.BlockSpec((1, S, 128), lambda i: (h, 0, 0)),
            pl.BlockSpec((1, HD, S), lambda i: (h, 0, 0)),
            pl.BlockSpec((1, 128, width), lambda i: (h, 0, i)),
            pl.BlockSpec((HD, bq), lambda i: (0, i)),
            pl.BlockSpec((HD, bq), lambda i: (0, i)),
            pl.BlockSpec((1, 1, bq), by_block),
            pl.BlockSpec((1, 1, bq), by_block),
            pl.BlockSpec((1, S, bq), by_block),
            pl.BlockSpec((1, S, bq), by_block),
            pl.BlockSpec((HD, S), whole),
            pl.BlockSpec((HD, S), whole),
            pl.BlockSpec(memory_space=pl.ANY),
        ]
        + [pl.BlockSpec((HD, width), lambda i: (h, 0))] * groups
        + [pl.BlockSpec(memory_space=pl.ANY)] * len(extra),
        out_specs=(pl.BlockSpec((3 * HD, width), whole),) * groups
        + (pl.BlockSpec((D, 256), lambda i: (0, column)),),
        scratch_shapes=[
            pltpu.VMEM((S, 128), f32),
            pltpu.VMEM((HD, width), bf),
            pltpu.VMEM((S, D), bf),
            pltpu.SemaphoreType.DMA,
        ],
        input_output_aliases={} if earlier is None else {12 + groups: groups},
        compiler_params=pltpu.CompilerParams(vmem_limit_bytes=58 * 2**20),
        cost_estimate=pl.CostEstimate(
            flops=24 * HD * S * S, bytes_accessed=2 * S * S, transcendentals=0
        ),
        name="attend_back",
    )(v, kt, qt, oa, ob, la, lb, pa, pb, cos, sin, normed, *do, *extra)
    return list(outs[:groups]), outs[groups]


def normalize_back(gradient, unit_rows, inverse, gain_row):
    scaled = gradient * gain_row
    return inverse * (
        scaled
        - jnp.mean(scaled, axis=-1, keepdims=True)
        - unit_rows * jnp.mean(scaled * unit_rows, axis=-1, keepdims=True)
    )


def column(row_ref):
    row = row_ref[...].astype(f32)
    return jnp.broadcast_to(row, (8, row.shape[1])).T[:, :1]


def row_of(total):
    return jnp.broadcast_to(total, (total.shape[0], 128)).T[:1]


def half_kernel(packed, info_ref, in_ref, proj_ref, gain_ref, out_w_ref, *refs):
    half_ref = refs[-1]
    side = info_ref[0] & 1

    @pl.when(side == 0)
    def _():
        half_ref[...] = in_ref[...]

    @pl.when(side == 1)
    def _():
        short = in_ref.shape[0]
        half_ref[:, :D] = proj_ref[...]
        gain = jnp.broadcast_to(column(gain_ref), (short, 128)).astype(bf)
        half_ref[:, D : D + 128] = gain
        if packed:
            one, two, three = D + 128, 2 * D + 128, 2 * D + D // 2 + 128
            tall = out_w_ref.shape[0]
            half_ref[:, one:two] = out_w_ref[:short, :]
            half_ref[: tall - short, two:three] = out_w_ref[short:, : D // 2]
            half_ref[tall - short :, two:three] = out_w_ref[short:, D // 2 :]


def own_half(packed, info, in_w, proj_w, gain, out_w, after):
    vmem = pl.BlockSpec(memory_space=pltpu.VMEM)
    return pl.pallas_call(
        functools.partial(half_kernel, packed),
        out_shape=jax.ShapeDtypeStruct(in_w.shape, bf),
        in_specs=[pl.BlockSpec(memory_space=pltpu.SMEM)]
        + [vmem] * 4
        + [pl.BlockSpec(memory_space=pl.ANY)] * len(after),
        out_specs=vmem,
        name="own_half",
    )(info, in_w, proj_w, gain, out_w, *after)


def hold(array, after):
    def kernel(*refs):
        pass

    return pl.pallas_call(
        kernel,
        out_shape=jax.ShapeDtypeStruct(array.shape, array.dtype),
        in_specs=[pl.BlockSpec(memory_space=pl.ANY)] * (1 + len(after)),
        out_specs=pl.BlockSpec(memory_space=pl.ANY),
        input_output_aliases={0: 0},
        name="hold",
    )(array, *after)


def middle_kernel(groups, heads, ff, shards, info_ref, x_ref, dy_ref, mine_ref, other_ref, *refs):
    count = groups * heads
    given = len(refs) - count - groups - 13
    out_given = refs[:given]
    chunks = refs[given : given + count]
    d_chunks = refs[given + count : given + count + groups]
    (result_ref, dh_ref, mixed_ref, second_ref, dgu_ref, inner_ref, branch_ref,
     g_ref, t_ref, out_w_ref, w_ref, rest_ref, sems) = refs[given + count + groups :]
    width = heads * HD
    me = info_ref[0]

    @pl.when(pl.program_id(0) == 0)
    def _():
        def fetch(first, second):
            copies = [
                pltpu.make_async_copy(first, w_ref, sems.at[0]),
                pltpu.make_async_copy(second, rest_ref, sems.at[1]),
            ]
            for copy in copies:
                copy.start()
            for copy in copies:
                copy.wait()

        @pl.when((me & 1) == 0)
        def _():
            fetch(mine_ref, other_ref)

        @pl.when((me & 1) == 1)
        def _():
            fetch(other_ref, mine_ref)

        g_ref[...] = rest_ref[:, D : D + 128].astype(f32).T[:8]
        if given:
            out_w_ref[...] = out_given[0][...]
        else:
            tall, short = ff // shards, D // shards
            rest = tall - short
            one, two, three = D + 128, 2 * D + 128, 2 * D + D // 2 + 128
            for f in range(shards):
                src = slice(f * short, (f + 1) * short)
                out_w_ref[f * tall : f * tall + short, :] = rest_ref[src, one:two]
                dst = slice(f * tall + short, (f + 1) * tall)
                src = slice(f * short, f * short + rest)
                out_w_ref[dst, : D // 2] = rest_ref[src, two:three]
                src = slice(f * short + rest, f * short + 2 * rest)
                out_w_ref[dst, D // 2 :] = rest_ref[src, two:three]

    for h in range(heads):
        for j in range(groups):
            start = pl.multiple_of((me ^ j) * width + h * HD, HD)
            mixed_ref[pl.ds(start, HD), :] = chunks[h * groups + j][...]
    gain = g_ref[:1]
    proj = rest_ref[:, :D]
    hidden = x_ref[...].astype(f32) + dg(mixed_ref[...], proj, TN)
    unit, inverse = unit_rows_of(hidden)
    second = (unit * gain).astype(bf)
    second_ref[...] = second
    dy = dy_ref[...]
    result = hidden
    d_second = jnp.zeros_like(hidden)
    step = 384
    for c in range(ff // step):
        a = slice(c * step, (c + 1) * step)
        b = slice(ff + c * step, ff + (c + 1) * step)
        gate = dg(second, w_ref[:, a], NN)
        up = dg(second, w_ref[:, b], NN)
        d_inner = dg(dy, out_w_ref[a, :], NT)
        bell = 0.5 + 0.5 * lax.erf(gate * 0.7071067811865476)
        gelu = gate * bell
        inner = (gelu * up).astype(bf)
        inner_ref[:, a] = inner
        result = result + dg(inner, out_w_ref[a, :], NN)
        slope = bell + gate * (jnp.exp(-0.5 * gate * gate) * 0.3989422804014327)
        d_gate = (d_inner * up * slope).astype(bf)
        d_up = (d_inner * gelu).astype(bf)
        dgu_ref[:, a] = d_gate
        dgu_ref[:, b] = d_up
        d_second = d_second + dg(d_gate, w_ref[:, a], NT) + dg(d_up, w_ref[:, b], NT)
    result_ref[...] = result.astype(bf)
    d_hidden = dy.astype(f32) + normalize_back(d_second, unit, inverse, gain)
    dh_ref[...] = d_hidden
    branch = d_hidden.astype(bf)
    branch_ref[...] = branch
    t_ref[...] = dg(proj, branch, NT).astype(bf)
    for j in range(groups):
        start = pl.multiple_of((me ^ j) * width, HD)
        d_chunks[j][...] = t_ref[pl.ds(start, width), :]


def middle(groups, heads, shards, ff, info, x, dy, mine, other, out_w, chunks):
    rows = x.shape[0]
    rb = min(256, rows)
    by_row = lambda i: (i, 0)
    by_column = lambda i: (0, i)
    whole = lambda i: (0, 0)
    outs = pl.pallas_call(
        functools.partial(middle_kernel, groups, heads, ff, shards),
        grid=(rows // rb,),
        out_shape=(jax.ShapeDtypeStruct((heads * HD, rows), bf),) * groups
        + (
            jax.ShapeDtypeStruct((rows, D), bf),
            jax.ShapeDtypeStruct((rows, D), f32),
            jax.ShapeDtypeStruct((D, rows), bf),
            jax.ShapeDtypeStruct((rows, D), bf),
            jax.ShapeDtypeStruct((rows, 2 * ff), bf),
            jax.ShapeDtypeStruct((rows, ff), bf),
            jax.ShapeDtypeStruct((rows, D), bf),
        ),
        in_specs=[
            pl.BlockSpec(memory_space=pltpu.SMEM),
            pl.BlockSpec((rb, D), by_row),
            pl.BlockSpec((rb, D), by_row),
            pl.BlockSpec(memory_space=pl.ANY),
            pl.BlockSpec(memory_space=pl.ANY),
        ]
        + [pl.BlockSpec(w.shape, whole, pipeline_mode=pl.Buffered(1)) for w in out_w]
        + [pl.BlockSpec((HD, rb), by_column)] * (groups * heads),
        out_specs=(pl.BlockSpec((heads * HD, rb), by_column),) * groups
        + (
            pl.BlockSpec((rb, D), by_row),
            pl.BlockSpec((rb, D), by_row),
            pl.BlockSpec((D, rb), by_column),
            pl.BlockSpec((rb, D), by_row),
            pl.BlockSpec((rb, 2 * ff), by_row),
            pl.BlockSpec((rb, ff), by_row),
            pl.BlockSpec((rb, D), by_row),
        ),
        scratch_shapes=[
            pltpu.VMEM((8, D), f32),
            pltpu.VMEM((D, rb), bf),
            pltpu.VMEM((ff, D), bf),
            pltpu.VMEM(mine.shape, bf),
            pltpu.VMEM(mine.shape, bf),
            pltpu.SemaphoreType.DMA((2,)),
        ],
        compiler_params=pltpu.CompilerParams(vmem_limit_bytes=58 * 2**20),
        cost_estimate=pl.CostEstimate(
            flops=rows * D * (14 * ff + 4 * D), bytes_accessed=30 * 2**20, transcendentals=rows * ff
        ),
        name="middle",
    )(info, x, dy, mine, other, *out_w, *chunks)
    return list(outs[:groups]), outs[groups:]


def last_kernel(groups, chosen, x_ref, base_ref, gain_ref, *refs):
    count = groups * len(chosen)
    chunks = refs[:count]
    pairs = refs[count : 2 * count]
    value_refs = refs[2 * count : 3 * count]
    out_ref, dp_ref, wh_ref, g_ref = refs[-4:]
    both = groups * 2 * HD

    @pl.when(pl.program_id(0) == 0)
    def _():
        g_ref[...] = gain_ref[...].astype(f32).T[HD : HD + 8]
        for n, h in enumerate(chosen):
            side = (h & 1) * HD
            pieces = [ref[...] for ref in pairs[n * groups : (n + 1) * groups]]
            pieces += [ref[:, side : side + HD] for ref in value_refs[n * groups : (n + 1) * groups]]
            wh_ref[:, n * D : (n + 1) * D] = jnp.concatenate(pieces, axis=1)

    for n in range(len(chosen)):
        for j in range(groups):
            chunk = chunks[n * groups + j]
            start = n * D + j * 2 * HD
            dp_ref[start : start + 2 * HD, :] = chunk[: 2 * HD, :]
            start = n * D + both + j * HD
            dp_ref[start : start + HD, :] = chunk[2 * HD :, :]
    d_normed = dg(wh_ref[...], dp_ref[...], NN).T
    unit, inverse = unit_rows_of(x_ref[...].astype(f32))
    out_ref[...] = base_ref[...] + normalize_back(d_normed, unit, inverse, g_ref[:1])


def last(groups, heads, chosen, x, base, peers, chunks, after):
    rows = chunks[0].shape[1]
    rb = min(256, rows)
    by_row = lambda i: (i, 0)

    def tile(n):
        return pl.BlockSpec((D, 128), lambda i: (0, n), pipeline_mode=pl.Buffered(1))

    pairs = [tile(h) for h in chosen for _ in peers]
    value_tiles = [tile(heads + h // 2) for h in chosen for _ in peers]
    return pl.pallas_call(
        functools.partial(last_kernel, groups, chosen),
        grid=(rows // rb,),
        out_shape=jax.ShapeDtypeStruct((rows, D), f32),
        in_specs=[
            pl.BlockSpec((rb, D), by_row),
            pl.BlockSpec((rb, D), by_row),
            tile(peers[0].shape[1] // 128 - 1),
        ]
        + [pl.BlockSpec((3 * HD, rb), lambda i: (0, i))] * len(chunks)
        + pairs
        + value_tiles
        + [pl.BlockSpec(memory_space=pl.ANY)] * len(after),
        out_specs=pl.BlockSpec((rb, D), by_row),
        scratch_shapes=[
            pltpu.VMEM((len(chosen) * D, rb), bf),
            pltpu.VMEM((D, len(chosen) * D), bf),
            pltpu.VMEM((8, D), f32),
        ],
        compiler_params=pltpu.CompilerParams(vmem_limit_bytes=58 * 2**20),
        cost_estimate=pl.CostEstimate(
            flops=2 * len(chosen) * rows * D * D, bytes_accessed=12 * 2**20, transcendentals=0
        ),
        name="last",
    )(x, base, peers[0], *chunks, *(list(peers) * (2 * len(chosen))), *after)


def own_kernel(groups, heads, info_ref, w_ref, gain_ref, out_ref):
    for g in range(groups):

        @pl.when(info_ref[0] == g)
        def _():
            def piece(t, h):
                start = t * D + (g * heads + h) * HD
                return w_ref[:, start : start + HD]

            pieces = []
            for h in range(heads):
                pieces += [piece(0, h), piece(1, h)]
            pieces += [piece(2, h) for h in range(heads)] + [column(gain_ref).astype(bf)]
            missing = out_ref.shape[2] - 3 * heads * HD - 1
            pieces.append(jnp.zeros((w_ref.shape[0], missing), bf))
            own = jnp.concatenate(pieces, axis=1)
            for f in range(out_ref.shape[0]):
                out_ref[f] = own


def own_columns(groups, heads, shards, info, w, gain):
    width = (3 * heads * HD + 128) // 128 * 128
    return pl.pallas_call(
        functools.partial(own_kernel, groups, heads),
        out_shape=jax.ShapeDtypeStruct((shards, w.shape[0], width), bf),
        in_specs=[
            pl.BlockSpec(memory_space=pltpu.SMEM),
            pl.BlockSpec(memory_space=pltpu.VMEM),
            pl.BlockSpec(memory_space=pltpu.VMEM),
        ],
        out_specs=pl.BlockSpec(memory_space=pltpu.VMEM),
        name="own_columns",
    )(info, w, gain)


def tables_kernel(cos_ref, sin_ref, cos_rows_ref, sin_rows_ref, cos_t_ref, sin_t_ref):
    c, s = cos_ref[...], sin_ref[...]
    cos_t_ref[...] = jnp.concatenate([c, c], axis=0)
    sin_t_ref[...] = jnp.concatenate([s, s], axis=0)
    scale = HD**-0.5 * LOG2E
    cos_rows_ref[...] = jnp.concatenate([c * scale, c * scale, c, c], axis=0).T
    sin_rows_ref[...] = jnp.concatenate([s * -scale, s * scale, -s, s], axis=0).T


def tables(cosine, sine):
    half, S = cosine.shape
    rb = min(1024, S)
    return pl.pallas_call(
        tables_kernel,
        grid=(S // rb,),
        out_shape=(jax.ShapeDtypeStruct((S, 4 * half), f32),) * 2
        + (jax.ShapeDtypeStruct((2 * half, S), f32),) * 2,
        in_specs=[pl.BlockSpec((half, rb), lambda i: (0, i))] * 2,
        out_specs=(pl.BlockSpec((rb, 4 * half), lambda i: (i, 0)),) * 2
        + (pl.BlockSpec((2 * half, rb), lambda i: (0, i)),) * 2,
        name="tables",
    )(cosine, sine)


def wide_kernel(place_ref, second_ref, dgu_ref, mixed_ref, branch_ref, *refs):
    outs, held_ref = refs[:-1], refs[-1]
    i = pl.program_id(0)
    group = i ^ place_ref[0]
    end = pl.num_programs(0) - 1

    @pl.when(group < end)
    def _():
        held_ref[...] = dg(second_ref[...], dgu_ref[...], TN).astype(bf)

    @pl.when(group == end)
    def _():
        held_ref[...] = dg(mixed_ref[...], branch_ref[...], NN).astype(bf)

    for j in range(len(outs)):

        @pl.when(i == j)
        def _():
            outs[j][...] = held_ref[...]


def wide_grads(place, second, d_gate_up, mixed_t, branch):
    rows = second.shape[0]
    steps = d_gate_up.shape[1] // D
    whole = lambda i, p: (0, 0)
    return pl.pallas_call(
        wide_kernel,
        grid_spec=pltpu.PrefetchScalarGridSpec(
            num_scalar_prefetch=1,
            grid=(steps + 1,),
            in_specs=[
                pl.BlockSpec((rows, D), whole),
                pl.BlockSpec((rows, D), lambda i, p: (0, jnp.minimum(i ^ p[0], steps - 1))),
                pl.BlockSpec((D, rows), whole),
                pl.BlockSpec((rows, D), whole),
            ],
            out_specs=(pl.BlockSpec((D, D), whole),) * (steps + 1),
            scratch_shapes=[pltpu.VMEM((D, D), bf)],
        ),
        out_shape=(jax.ShapeDtypeStruct((D, D), bf),) * (steps + 1),
        compiler_params=pltpu.CompilerParams(vmem_limit_bytes=58 * 2**20),
        cost_estimate=pl.CostEstimate(
            flops=2 * rows * D * D * (steps + 1), bytes_accessed=16 * 2**20, transcendentals=0
        ),
        name="wide_grads",
    )(place, second, d_gate_up, mixed_t, branch)


def tall_grads(inner, dy, wide, after):
    rows, ff = inner.shape
    step = ff // 3
    many = len(wide)

    def kernel(inner_ref, dy_ref, *refs):
        refs[many + len(after)][...] = dg(inner_ref[...], dy_ref[...], TN).astype(bf)

    anywhere = pl.BlockSpec(memory_space=pl.ANY)
    outs = pl.pallas_call(
        kernel,
        grid=(3,),
        in_specs=[
            pl.BlockSpec((rows, step), lambda i: (0, i)),
            pl.BlockSpec((rows, D), lambda i: (0, 0)),
        ]
        + [anywhere] * (many + len(after)),
        out_specs=(pl.BlockSpec((step, D), lambda i: (i, 0)),) + (anywhere,) * many,
        out_shape=(jax.ShapeDtypeStruct((ff, D), bf),)
        + tuple(jax.ShapeDtypeStruct(w.shape, bf) for w in wide),
        input_output_aliases={2 + n: 1 + n for n in range(many)},
        compiler_params=pltpu.CompilerParams(vmem_limit_bytes=58 * 2**20),
        cost_estimate=pl.CostEstimate(
            flops=2 * rows * D * ff, bytes_accessed=6 * 2**20, transcendentals=0
        ),
        name="tall_grads",
    )(inner, dy, *wide, *after)
    return outs[0], list(outs[1:])


def ordered(kernel, arrays, after, carry, out_shape, in_specs, out_specs, name, grid=()):
    first = len(arrays) + len(after)
    own = len(out_shape)
    anywhere = pl.BlockSpec(memory_space=pl.ANY)

    def call(*refs):
        outs = refs[first + len(carry) :]
        kernel(*refs[: len(arrays)], *outs[:own])

    outs = pl.pallas_call(
        call,
        grid=grid,
        out_shape=tuple(out_shape) + tuple(jax.ShapeDtypeStruct(a.shape, a.dtype) for a in carry),
        in_specs=list(in_specs) + [anywhere] * (len(after) + len(carry)),
        out_specs=tuple(out_specs) + (anywhere,) * len(carry),
        input_output_aliases={first + n: own + n for n in range(len(carry))},
        compiler_params=pltpu.CompilerParams(vmem_limit_bytes=58 * 2**20),
        name=name,
    )(*arrays, *after, *carry)
    return list(outs[:own]), list(outs[own:])


def add_kernel(*refs):
    total = refs[0][...].astype(f32)
    for ref in refs[1:-1]:
        total = total + ref[...].astype(f32)
    refs[-1][...] = total.astype(bf)


def add_up(arrays, after, carry):
    rows, columns = arrays[0].shape
    rb = 256
    spec = pl.BlockSpec((rb, columns), lambda i: (i, 0))
    (total,), carried = ordered(
        add_kernel, arrays, after, carry, [jax.ShapeDtypeStruct((rows, columns), bf)],
        [spec] * len(arrays), [spec], "add_up", grid=(rows // rb,),
    )
    return total, carried


def up16(n):
    return -(-n // 16) * 16


def beside_kernel(first_ref, second_ref, *refs):
    out_ref = refs[-1]
    start = 0
    for ref in (first_ref, second_ref):
        total = ref[0].astype(f32)
        for f in range(1, ref.shape[0]):
            total = total + ref[f].astype(f32)
        out_ref[:, start : start + ref.shape[2]] = total.astype(bf)
        start += ref.shape[2]


def beside(first, second, after):
    vmem = pl.BlockSpec(memory_space=pltpu.VMEM)
    return pl.pallas_call(
        beside_kernel,
        out_shape=jax.ShapeDtypeStruct((first.shape[1], first.shape[2] + second.shape[2]), bf),
        in_specs=[vmem, vmem] + [pl.BlockSpec(memory_space=pl.ANY)] * len(after),
        out_specs=vmem,
        compiler_params=pltpu.CompilerParams(vmem_limit_bytes=58 * 2**20),
        name="beside",
    )(first, second, *after)


def owned_kernel(wide_ref, tall_ref, *refs):
    out_ref = refs[-1]
    start = 0
    for ref in (wide_ref, tall_ref):
        total = ref[0].astype(f32)
        for f in range(1, ref.shape[0]):
            total = total + ref[f].astype(f32)
        out_ref[start : start + ref.shape[1], :] = total.astype(bf)
        start += up16(ref.shape[1])


def owned(wide, tall, after, carry):
    vmem = pl.BlockSpec(memory_space=pltpu.VMEM)
    shape = (up16(wide.shape[1]) + up16(tall.shape[1]), D)
    (total,), carried = ordered(
        owned_kernel, [wide, tall], after, carry, [jax.ShapeDtypeStruct(shape, bf)],
        [vmem] * 2, [vmem], "owned",
    )
    return total, carried


def finish_wide_kernel(groups, info_ref, w_ref, gain_ref, *refs):
    in_ref, proj_ref, dgain_ref, out_ref, held_ref = refs[groups:]
    shard = w_ref.shape[0]
    start = up16(shard)
    tall = 0.0
    for j in range(groups):
        held_ref[info_ref[0] ^ j] = refs[j][...]
        tall = tall + refs[j][start : start + out_ref.shape[0], :].astype(f32)
    out_ref[...] = tall
    total = 0.0
    for g in range(groups - 1):
        at = slice(g * D, (g + 1) * D)
        grad = held_ref[g, :shard, :].astype(f32)
        in_ref[:, at] = grad
        total = total + jnp.sum(w_ref[:, at].astype(f32) * grad, axis=1, keepdims=True)
    proj_ref[...] = held_ref[groups - 1, :shard, :].astype(f32)
    dgain_ref[...] = row_of(total / column(gain_ref))


def finish_qkv_kernel(groups, heads, info_ref, w_ref, gain_ref, *refs):
    out_ref, dgain_ref, held_ref = refs[groups : groups + 3]
    for j in range(groups):
        held_ref[info_ref[0] ^ j] = refs[j][...]
    pieces = []
    for t in range(3):
        for g in range(groups):
            for h in range(heads):
                start = h * 256 + t * HD
                pieces.append(held_ref[g, :, start : start + HD].astype(f32))
    grad = jnp.concatenate(pieces, axis=1)
    out_ref[...] = grad
    total = jnp.sum(w_ref[...].astype(f32) * grad, axis=1, keepdims=True)
    dgain_ref[...] = row_of(total / column(gain_ref))


def finish(kernel, groups, info, w, gain, parts, shapes, name, after=()):
    vmem = pl.BlockSpec(memory_space=pltpu.VMEM)
    first = 3 + groups

    def call(*refs):
        kernel(*refs[:first], *refs[first + len(after) :])

    return pl.pallas_call(
        call,
        out_shape=tuple(jax.ShapeDtypeStruct(shape, f32) for shape in shapes),
        in_specs=[pl.BlockSpec(memory_space=pltpu.SMEM)]
        + [vmem] * (2 + groups)
        + [pl.BlockSpec(memory_space=pl.ANY)] * len(after),
        out_specs=(vmem,) * len(shapes),
        scratch_shapes=[pltpu.VMEM((groups,) + parts[0].shape, bf)],
        compiler_params=pltpu.CompilerParams(vmem_limit_bytes=58 * 2**20),
        name=name,
    )(info, w, gain, *parts, *after)


def body(
    tokens, lengths, attn_gain, qkv_weight, proj_weight, ffn_gain, in_weight, out_weight, out_grad
):
    rows = tokens.shape[1]
    groups = lax.axis_size("seq")
    shards = lax.axis_size("fsdp")
    heads = HEADS // groups
    shard = D // shards
    me = lax.axis_index("seq")

    def swap(array, j, axis="seq"):
        size = lax.axis_size(axis)
        return lax.ppermute(array, axis, [(i, i ^ j) for i in range(size)])

    def exchange(chunks):
        return [chunks[0]] + [swap(chunks[j], j) for j in range(1, groups)]

    def gather(array):
        return lax.all_gather(array, "fsdp", axis=0, tiled=True)

    place = jnp.stack([me]).astype(jnp.int32)
    x0 = tokens[0]
    across = swap(x0, 2)
    near = swap(x0, 1)
    attn_row = attn_gain[None, :]
    ffn_row = ffn_gain[None, :]
    own = own_columns(groups, heads, shards, place, qkv_weight, attn_row)
    own = lax.all_to_all(own, "fsdp", split_axis=0, concat_axis=0, tiled=True).reshape(D, -1)

    half = HD // 2
    frequency = rope_base ** (-(lax.iota(f32, half) * 2.0) / HD)
    starts = [(me ^ j) * rows for j in range(groups)]
    positions = jnp.concatenate([s + lax.iota(jnp.int32, rows) for s in starts]).astype(f32)
    angles = frequency[:, None] * positions[None, :]
    cos_rows, sin_rows, cos_t, sin_t = tables(jnp.cos(angles), jnp.sin(angles))

    def project(j, block, carried):
        info = jnp.stack([starts[j], lengths[0]]).astype(jnp.int32)
        return qkv_call(j, groups, heads, info, block, cos_rows, sin_rows, own, carried)

    diagonal = swap(across, 1)
    carried = project(2, across, None)
    carried = project(0, x0, carried)
    carried = project(1, near, carried)
    normed, k, v, qt, kt, vt = project(3, diagonal, carried)

    ff = in_weight.shape[1] // 2
    tall = out_weight.shape[0]
    packed = shards <= 8
    mine = gather(own_half(packed, place, in_weight, proj_weight, ffn_row, out_weight, [own, cos_t]))
    out_full = [] if packed else [gather(out_weight)]

    own = hold(own, [normed])
    own_near, own_across = swap(own, 1), swap(own, 2)
    own_diagonal = swap(own_across, 1)
    peers = [own, own_near, own_across, own_diagonal]

    kept = []
    chunks = []
    orders = [[], [own_near, own_across], [own_diagonal]]
    for h in range(heads):
        before = [kept[-1][2]] if kept else []
        if h == 2:
            before += chunks[1:groups]
        saved, mixed = attend(h, k, qt, vt, groups, orders[h] + before)
        kept.append(saved)
        chunks += exchange(mixed)
        if h == heads - 2:
            mine = hold(mine, [saved[2]])
            other = swap(mine, 1)

    dy = out_grad[0]
    d_mixed, (result, d_hidden, mixed_t, second, d_gate_up, inner, branch) = middle(
        groups, heads, shards, ff, place, x0, dy, mine, other, out_full, chunks
    )
    d_mixed = exchange(d_mixed)

    def to_owner(array):
        parts = array.reshape(shards, array.shape[0] // shards, -1)
        return lax.all_to_all(parts, "fsdp", split_axis=0, concat_axis=0, tiled=True)

    def from_peers(array):
        return [array] + [swap(array, j) for j in range(1, groups)]

    wide_own, *wide_rest = wide_grads(place, second, d_gate_up, mixed_t, branch)
    tall_grad, wide_rest = tall_grads(inner, dy, wide_rest, d_mixed[1:])
    wide_all = exchange([wide_own] + wide_rest)
    tall_parts = to_owner(tall_grad)

    def back(h, grad_place, after):
        return attend_back(
            h, v, kt, qt, d_mixed, kept[h], cos_t, sin_t, normed, groups, grad_place, after
        )

    sent_0, qkv_first = back(0, (512, 0, None), [tall_grad])
    wide_sum, others = add_up(wide_all, [qkv_first, tall_parts], sent_0[1:])
    wide_parts = to_owner(wide_sum)
    received_0 = exchange(sent_0[:1] + others)

    sent_1, qkv_first = back(1, (512, 1, qkv_first), [wide_sum])
    both, carried = owned(wide_parts, tall_parts, received_0[1:], sent_1[1:] + [qkv_first])
    received_1 = exchange(sent_1[:1] + carried[:-1])
    both_far = [swap(both, j) for j in range(2, groups)]
    qkv_parts = to_owner(carried[-1])

    sent_2, qkv_second = back(2, (256, 0, None), [both])
    _, carried = ordered(
        lambda: None, [], received_1[1:] + both_far + [qkv_parts],
        sent_2[1:] + [qkv_second, both], [], [], [], "pass_on",
    )
    qkv_second, both = carried[-2:]
    received_2 = exchange(sent_2[:1] + carried[:-2])
    both_peers = [both, swap(both, 1)] + both_far
    qkv_second_parts = to_owner(qkv_second)

    base = last(
        groups, heads, (0, 1), x0, d_hidden, peers, received_0 + received_1, [qkv_second]
    )
    in_weight_grad, proj_weight_grad, ffn_gain_grad, out_weight_grad = finish(
        functools.partial(finish_wide_kernel, groups),
        groups, place, in_weight, ffn_row, both_peers,
        ((shard, 2 * ff), (shard, D), (1, shard), (tall, D)), "finish_wide",
    )
    qkv_peers = from_peers(beside(qkv_parts, qkv_second_parts, [base] + received_2[1:]))
    tokens_grad = last(groups, heads, (2,), x0, base, peers, received_2, [])
    qkv_weight_grad, attn_gain_grad = finish(
        functools.partial(finish_qkv_kernel, groups, heads),
        groups, place, qkv_weight, attn_row, qkv_peers,
        ((shard, 3 * D), (1, shard)), "finish_qkv", [tokens_grad],
    )
    return (
        result[None],
        tokens_grad[None],
        attn_gain_grad[0],
        qkv_weight_grad,
        proj_weight_grad,
        ffn_gain_grad[0],
        in_weight_grad,
        out_weight_grad,
    )


def solution(mesh):
    in_specs = (
        P("fsdp", "seq", None),
        P("fsdp"),
        P("fsdp"),
        P("fsdp", None),
        P("fsdp", None),
        P("fsdp"),
        P("fsdp", None),
        P("fsdp", None),
        P("fsdp", "seq", None),
    )
    out_specs = (
        P("fsdp", "seq", None),
        P("fsdp", "seq", None),
        P("fsdp"),
        P("fsdp", None),
        P("fsdp", None),
        P("fsdp"),
        P("fsdp", None),
        P("fsdp", None),
    )
    return jax.shard_map(body, mesh=mesh, in_specs=in_specs, out_specs=out_specs, check_vma=False)
```

```python
import functools

import jax
import jax.numpy as jnp
from jax import lax
from jax.experimental import pallas as pl
from jax.experimental.pallas import tpu as pltpu
from jax.sharding import PartitionSpec as P

D = 768
HEADS = 12
HD = 64

epsilon = 1e-05
rope_base = 160000.0
masked_score = -1e30
LOG2E = 1.4426950408889634
LN2 = 0.6931471805599453

bf = jnp.bfloat16
f32 = jnp.float32
NN = ((1,), (0,))
NT = ((1,), (1,))
TN = ((0,), (0,))


def dg(a, b, dims):
    return lax.dot_general(a, b, (dims, ((), ())), preferred_element_type=f32)


def unit_rows_of(x):
    centred = x - jnp.mean(x, axis=-1, keepdims=True)
    inverse = lax.rsqrt(jnp.mean(centred * centred, axis=-1, keepdims=True) + epsilon)
    return centred * inverse, inverse


def qkv_kernel(heads, info_ref, x_ref, cos_ref, sin_ref, w_ref, *refs):
    n_ref, k_ref, v_ref, qt_ref, kt_ref, vt_ref, g_ref = refs[-7:]
    rb = x_ref.shape[0]
    value_at = heads * 128

    @pl.when(pl.program_id(0) == 0)
    def _():
        last = w_ref[:, w_ref.shape[1] - 128 :].astype(f32).T
        g_ref[...] = last[HD : HD + 8]

    unit, _ = unit_rows_of(x_ref[...].astype(f32))
    normed = (unit * g_ref[:1]).astype(bf)
    n_ref[...] = normed
    lane = lax.broadcasted_iota(jnp.int32, (rb, 128), 1)
    row = lax.broadcasted_iota(jnp.int32, (rb, 128), 0)
    position = info_ref[0] + pl.program_id(0) * rb + row
    bias = jnp.where(position < info_ref[1], 0.0, masked_score)
    key_tail = jnp.where(lane == HD, bias, 0.0)
    value_tail = jnp.where(lane < HD + 2, -1.0, 0.0)
    head_lane = lane < HD
    lower = (lane & (HD - 1)) < HD // 2
    one_row = jnp.where(lax.broadcasted_iota(jnp.int32, (HD, rb), 0) == 0, 1.0, 0.0).astype(bf)
    y = dg(normed, w_ref[...], NN)
    for h in range(heads):
        t = y[:, h * 128 : (h + 1) * 128]
        turned = jnp.where(lower, pltpu.roll(t, 128 - HD // 2, 1), pltpu.roll(t, HD // 2, 1))
        t = t * cos_ref[...] + turned * sin_ref[...]
        k_ref[h] = jnp.where(head_lane, pltpu.roll(t, HD, 1), key_tail).astype(bf)
        t = t.T.astype(bf)
        qt_ref[h, :HD] = t[:HD]
        qt_ref[h, HD:] = one_row
        kt_ref[h] = t[HD:]
    for h in range(heads):
        at = value_at + h // 2 * 128
        t = y[:, at : at + 128]
        turned = t if h % 2 == 0 else pltpu.roll(t, HD, 1)
        v_ref[h] = jnp.where(head_lane, turned, value_tail).astype(bf)
        if h % 2 == 0:
            t_rows = t.T.astype(bf)
        vt_ref[h, :HD] = t_rows[:HD] if h % 2 == 0 else t_rows[HD:]
        vt_ref[h, HD:] = one_row[:16]


def qkv_call(block, blocks, heads, info, x, cos, sin, w, carried):
    rows = x.shape[0]
    S = rows * blocks
    rb = min(256, rows)
    steps = rows // rb
    width = w.shape[1]
    at = lambda i: block * steps + i
    outs = (
        jax.ShapeDtypeStruct((S, D), bf),
        jax.ShapeDtypeStruct((heads, S, 128), bf),
        jax.ShapeDtypeStruct((heads, S, 128), bf),
        jax.ShapeDtypeStruct((heads, 128, S), bf),
        jax.ShapeDtypeStruct((heads, HD, S), bf),
        jax.ShapeDtypeStruct((heads, 80, S), bf),
    )
    in_specs = [
        pl.BlockSpec(memory_space=pltpu.SMEM),
        pl.BlockSpec((rb, D), lambda i: (i, 0)),
        pl.BlockSpec((rb, 128), lambda i: (at(i), 0)),
        pl.BlockSpec((rb, 128), lambda i: (at(i), 0)),
        pl.BlockSpec((D, width), lambda i: (0, 0)),
    ]
    aliases = {}
    if carried is not None:
        first = len(in_specs)
        in_specs += [pl.BlockSpec(memory_space=pl.ANY)] * 6
        aliases = {first + n: n for n in range(6)}
    return pl.pallas_call(
        functools.partial(qkv_kernel, heads),
        grid=(steps,),
        out_shape=outs,
        in_specs=in_specs,
        out_specs=(
            pl.BlockSpec((rb, D), lambda i: (at(i), 0)),
            pl.BlockSpec((heads, rb, 128), lambda i: (0, at(i), 0)),
            pl.BlockSpec((heads, rb, 128), lambda i: (0, at(i), 0)),
            pl.BlockSpec((heads, 128, rb), lambda i: (0, 0, at(i))),
            pl.BlockSpec((heads, HD, rb), lambda i: (0, 0, at(i))),
            pl.BlockSpec((heads, 80, rb), lambda i: (0, 0, at(i))),
        ),
        scratch_shapes=[pltpu.VMEM((8, D), f32)],
        input_output_aliases=aliases,
        compiler_params=pltpu.CompilerParams(vmem_limit_bytes=48 * 2**20),
        cost_estimate=pl.CostEstimate(
            flops=4 * rows * D * width, bytes_accessed=rows * 8192, transcendentals=0
        ),
        name="qkv",
    )(info, x, cos, sin, w, *(carried or ()))


def attend_kernel(kc, half, count, k_ref, qa_ref, qb_ref, v_ref, *refs):
    refs = refs[count:]
    pa_ref, pb_ref, oa_ref, ob_ref, la_ref, lb_ref = refs[:6]
    chunks = refs[6 : 6 + half]
    sa_ref, sb_ref, m_ref = refs[6 + half :]
    i = pl.program_id(0)
    rows = k_ref.shape[1]
    bq = qa_ref.shape[2]

    def stage(new, old):
        if new is not None:
            q_ref, s_new, new_slot = new
            q = q_ref[0]
            m = jnp.full((8, bq), -jnp.inf, f32)
        if old is not None:
            s_old, old_slot, p_ref, o_ref, l_ref, block = old
            top = jnp.max(m_ref[old_slot], axis=0, keepdims=True)
            acc = jnp.zeros((v_ref.shape[1], bq), f32)
        for c in range(rows // kc):
            at = slice(c * kc, (c + 1) * kc)
            if new is not None:
                s = dg(k_ref[0, at, :], q, NN)
                s_new[at, :] = s
                m = jnp.maximum(m, jnp.max(s.reshape(kc // 8, 8, bq), axis=0))
            if old is not None:
                p = jnp.exp2(s_old[at, :] - top).astype(bf)
                p_ref[0, at, :] = p
                acc = acc + dg(v_ref[0, :, at], p, NN)
        if new is not None:
            m_ref[new_slot] = m
        if old is not None:
            linv = 1.0 / acc[HD : HD + 1, :]
            o = acc[:HD, :] * linv
            o_ref[...] = o
            l_ref[0] = linv
            low = o.astype(bf)
            for j in range(half):

                @pl.when(block // 2 == j)
                def _():
                    chunks[j][:, old_slot * bq : (old_slot + 1) * bq] = low

    first = (qa_ref, sa_ref, 0)
    odd = (sb_ref, 1, pb_ref, ob_ref, lb_ref, 2 * i - 1)

    @pl.when(i == 0)
    def _():
        stage(first, None)

    @pl.when((i > 0) & (i < half))
    def _():
        stage(first, odd)

    @pl.when(i == half)
    def _():
        stage(None, odd)

    @pl.when(i < half)
    def _():
        stage((qb_ref, sb_ref, 1), (sa_ref, 0, pa_ref, oa_ref, la_ref, 2 * i))


def attend(h, k, qt, vt, groups, after, kc=256):
    S = k.shape[1]
    bq = S // groups // 2
    a = lambda i: jnp.minimum(i, groups - 1)
    b = lambda i: jnp.maximum(i - 1, 0)
    outs = pl.pallas_call(
        functools.partial(attend_kernel, kc, groups, len(after)),
        grid=(groups + 1,),
        out_shape=(jax.ShapeDtypeStruct((groups, S, bq), bf),) * 2
        + (jax.ShapeDtypeStruct((HD, S // 2), f32),) * 2
        + (jax.ShapeDtypeStruct((groups, 1, bq), f32),) * 2
        + (jax.ShapeDtypeStruct((HD, 2 * bq), bf),) * groups,
        in_specs=[
            pl.BlockSpec((1, S, 128), lambda i: (h, 0, 0)),
            pl.BlockSpec((1, 128, bq), lambda i: (h, 0, 2 * a(i))),
            pl.BlockSpec((1, 128, bq), lambda i: (h, 0, 2 * a(i) + 1)),
            pl.BlockSpec((1, 80, S), lambda i: (h, 0, 0)),
        ]
        + [pl.BlockSpec(memory_space=pl.ANY)] * len(after),
        out_specs=(
            pl.BlockSpec((1, S, bq), lambda i: (a(i), 0, 0)),
            pl.BlockSpec((1, S, bq), lambda i: (b(i), 0, 0)),
            pl.BlockSpec((HD, bq), lambda i: (0, a(i))),
            pl.BlockSpec((HD, bq), lambda i: (0, b(i))),
            pl.BlockSpec((1, 1, bq), lambda i: (a(i), 0, 0)),
            pl.BlockSpec((1, 1, bq), lambda i: (b(i), 0, 0)),
        )
        + (pl.BlockSpec((HD, 2 * bq), lambda i: (0, 0)),) * groups,
        scratch_shapes=[
            pltpu.VMEM((S, bq), f32),
            pltpu.VMEM((S, bq), f32),
            pltpu.VMEM((2, 8, bq), f32),
        ],
        compiler_params=pltpu.CompilerParams(vmem_limit_bytes=58 * 2**20),
        cost_estimate=pl.CostEstimate(
            flops=16 * HD * S * S, bytes_accessed=2 * S * S, transcendentals=S * S
        ),
        name="attend",
    )(k, qt, qt, vt, *after)
    return outs[:6], list(outs[6:])


def attend_back_kernel(kc, groups, v_ref, kt_ref, q_ref, *refs):
    oa_ref, ob_ref, la_ref, lb_ref, pa_ref, pb_ref, cos_ref, sin_ref, n_ref = refs[:9]
    do_refs = refs[9 : 9 + groups]
    outs = refs[-5 - groups : -5]
    grad_ref, acc_ref, do_ref, held_ref, sem = refs[-5:]
    i = pl.program_id(0)
    rows = v_ref.shape[1]
    width = q_ref.shape[2]
    bq = width // 2
    fetch = pltpu.make_async_copy(n_ref, held_ref, sem)

    @pl.when(i == 0)
    def _():
        fetch.start()
        acc_ref[...] = jnp.zeros_like(acc_ref)

    for j in range(groups):

        @pl.when(i == j)
        def _():
            do_ref[...] = do_refs[j][...]

    zero = jnp.zeros((HD, bq), bf)
    r = lax.broadcasted_iota(jnp.int32, (16, bq), 0)
    sides = []
    for n, (o_ref, l_ref, p_ref) in enumerate(((oa_ref, la_ref, pa_ref), (ob_ref, lb_ref, pb_ref))):
        at = slice(n * bq, (n + 1) * bq)
        dop = (do_ref[:, at].astype(f32) * l_ref[0]).astype(bf)
        delta = jnp.sum(dop.astype(f32) * o_ref[...], axis=0, keepdims=True)
        high = delta.astype(bf).astype(f32)
        tail = jnp.where(r == 0, high, jnp.where(r == 1, delta - high, 0.0)).astype(bf)
        doe = jnp.concatenate([dop, tail, jnp.zeros((128 - HD - 16, bq), bf)], axis=0)
        right_v = jnp.concatenate([dop, zero], axis=0).T
        right_k = jnp.concatenate([zero, q_ref[0, :HD, at]], axis=0).T
        sides.append((p_ref, doe, jnp.concatenate([right_v, right_k], axis=0)))
    dq = [jnp.zeros((HD, bq), f32), jnp.zeros((HD, bq), f32)]
    for n, (p_ref, doe, right) in enumerate(sides):
        for c in range(rows // kc):
            at = slice(c * kc, (c + 1) * kc)
            p = p_ref[0, at, :]
            ds = p * dg(v_ref[0, at, :], doe, NN).astype(bf)
            acc_ref[at, :] = acc_ref[at, :] + dg(jnp.concatenate([p, ds], axis=1), right, NN)
            dq[n] = dq[n] + dg(kt_ref[0, :, at], ds, NN)
    dq = jnp.concatenate(dq, axis=1) * HD**-0.5
    turned = jnp.concatenate([dq[HD // 2 :], -dq[: HD // 2]], axis=0)
    here = pl.ds(pl.multiple_of(i * width, width), width)
    dq = (dq * cos_ref[:, here] + turned * sin_ref[:, here]).astype(bf)
    for j in range(groups):

        @pl.when(i == j)
        def _():
            outs[j][:HD] = dq

    @pl.when(i == groups - 1)
    def _():
        fetch.wait()
        grad = jnp.zeros((3 * HD, D), f32)
        for j in range(groups):
            at = slice(j * width, (j + 1) * width)
            t = acc_ref[at, :].T
            dk = t[HD:] * LN2
            turned_k = jnp.concatenate([dk[HD // 2 :], -dk[: HD // 2]], axis=0)
            dk = dk * cos_ref[:, at] + turned_k * sin_ref[:, at]
            outs[j][HD : 2 * HD] = dk.astype(bf)
            outs[j][2 * HD :] = t[:HD].astype(bf)
            grad = grad + dg(outs[j][...], held_ref[at, :], NN)
        grad_ref[:, : 3 * HD] = grad.T.astype(bf)
        grad_ref[:, 3 * HD :] = jnp.zeros((D, HD), bf)


def attend_back(h, v, kt, qt, do, kept, cos, sin, normed, groups, place, after, kc=256):
    S = v.shape[1]
    width = S // groups
    bq = width // 2
    pa, pb, oa, ob, la, lb = kept
    columns, column, earlier = place
    extra = list(after) if earlier is None else [earlier] + list(after)
    whole = lambda i: (0, 0)
    by_block = lambda i: (i, 0, 0)
    outs = pl.pallas_call(
        functools.partial(attend_back_kernel, kc, groups),
        grid=(groups,),
        out_shape=(jax.ShapeDtypeStruct((3 * HD, width), bf),) * groups
        + (jax.ShapeDtypeStruct((D, columns), bf),),
        in_specs=[
            pl.BlockSpec((1, S, 128), lambda i: (h, 0, 0)),
            pl.BlockSpec((1, HD, S), lambda i: (h, 0, 0)),
            pl.BlockSpec((1, 128, width), lambda i: (h, 0, i)),
            pl.BlockSpec((HD, bq), lambda i: (0, i)),
            pl.BlockSpec((HD, bq), lambda i: (0, i)),
            pl.BlockSpec((1, 1, bq), by_block),
            pl.BlockSpec((1, 1, bq), by_block),
            pl.BlockSpec((1, S, bq), by_block),
            pl.BlockSpec((1, S, bq), by_block),
            pl.BlockSpec((HD, S), whole),
            pl.BlockSpec((HD, S), whole),
            pl.BlockSpec(memory_space=pl.ANY),
        ]
        + [pl.BlockSpec((HD, width), lambda i: (h, 0))] * groups
        + [pl.BlockSpec(memory_space=pl.ANY)] * len(extra),
        out_specs=(pl.BlockSpec((3 * HD, width), whole),) * groups
        + (pl.BlockSpec((D, 256), lambda i: (0, column)),),
        scratch_shapes=[
            pltpu.VMEM((S, 128), f32),
            pltpu.VMEM((HD, width), bf),
            pltpu.VMEM((S, D), bf),
            pltpu.SemaphoreType.DMA,
        ],
        input_output_aliases={} if earlier is None else {12 + groups: groups},
        compiler_params=pltpu.CompilerParams(vmem_limit_bytes=58 * 2**20),
        cost_estimate=pl.CostEstimate(
            flops=24 * HD * S * S, bytes_accessed=2 * S * S, transcendentals=0
        ),
        name="attend_back",
    )(v, kt, qt, oa, ob, la, lb, pa, pb, cos, sin, normed, *do, *extra)
    return list(outs[:groups]), outs[groups]


def normalize_back(gradient, unit_rows, inverse, gain_row):
    scaled = gradient * gain_row
    return inverse * (
        scaled
        - jnp.mean(scaled, axis=-1, keepdims=True)
        - unit_rows * jnp.mean(scaled * unit_rows, axis=-1, keepdims=True)
    )


def column(row_ref):
    row = row_ref[...].astype(f32)
    return jnp.broadcast_to(row, (8, row.shape[1])).T[:, :1]


def row_of(total):
    return jnp.broadcast_to(total, (total.shape[0], 128)).T[:1]


def half_kernel(packed, info_ref, in_ref, proj_ref, gain_ref, out_w_ref, *refs):
    half_ref = refs[-1]
    side = info_ref[0] & 1

    @pl.when(side == 0)
    def _():
        half_ref[...] = in_ref[...]

    @pl.when(side == 1)
    def _():
        short = in_ref.shape[0]
        half_ref[:, :D] = proj_ref[...]
        gain = jnp.broadcast_to(column(gain_ref), (short, 128)).astype(bf)
        half_ref[:, D : D + 128] = gain
        if packed:
            one, two, three = D + 128, 2 * D + 128, 2 * D + D // 2 + 128
            tall = out_w_ref.shape[0]
            half_ref[:, one:two] = out_w_ref[:short, :]
            half_ref[: tall - short, two:three] = out_w_ref[short:, : D // 2]
            half_ref[tall - short :, two:three] = out_w_ref[short:, D // 2 :]


def own_half(packed, info, in_w, proj_w, gain, out_w, after):
    vmem = pl.BlockSpec(memory_space=pltpu.VMEM)
    return pl.pallas_call(
        functools.partial(half_kernel, packed),
        out_shape=jax.ShapeDtypeStruct(in_w.shape, bf),
        in_specs=[pl.BlockSpec(memory_space=pltpu.SMEM)]
        + [vmem] * 4
        + [pl.BlockSpec(memory_space=pl.ANY)] * len(after),
        out_specs=vmem,
        name="own_half",
    )(info, in_w, proj_w, gain, out_w, *after)


def hold(array, after):
    def kernel(*refs):
        pass

    return pl.pallas_call(
        kernel,
        out_shape=jax.ShapeDtypeStruct(array.shape, array.dtype),
        in_specs=[pl.BlockSpec(memory_space=pl.ANY)] * (1 + len(after)),
        out_specs=pl.BlockSpec(memory_space=pl.ANY),
        input_output_aliases={0: 0},
        name="hold",
    )(array, *after)


def middle_kernel(groups, heads, ff, shards, info_ref, x_ref, dy_ref, mine_ref, other_ref, *refs):
    count = groups * heads
    given = len(refs) - count - groups - 13
    out_given = refs[:given]
    chunks = refs[given : given + count]
    d_chunks = refs[given + count : given + count + groups]
    (result_ref, dh_ref, mixed_ref, second_ref, dgu_ref, inner_ref, branch_ref,
     g_ref, t_ref, out_w_ref, w_ref, rest_ref, sems) = refs[given + count + groups :]
    width = heads * HD
    me = info_ref[0]

    @pl.when(pl.program_id(0) == 0)
    def _():
        def fetch(first, second):
            copies = [
                pltpu.make_async_copy(first, w_ref, sems.at[0]),
                pltpu.make_async_copy(second, rest_ref, sems.at[1]),
            ]
            for copy in copies:
                copy.start()
            for copy in copies:
                copy.wait()

        @pl.when((me & 1) == 0)
        def _():
            fetch(mine_ref, other_ref)

        @pl.when((me & 1) == 1)
        def _():
            fetch(other_ref, mine_ref)

        g_ref[...] = rest_ref[:, D : D + 128].astype(f32).T[:8]
        if given:
            out_w_ref[...] = out_given[0][...]
        else:
            tall, short = ff // shards, D // shards
            rest = tall - short
            one, two, three = D + 128, 2 * D + 128, 2 * D + D // 2 + 128
            for f in range(shards):
                src = slice(f * short, (f + 1) * short)
                out_w_ref[f * tall : f * tall + short, :] = rest_ref[src, one:two]
                dst = slice(f * tall + short, (f + 1) * tall)
                src = slice(f * short, f * short + rest)
                out_w_ref[dst, : D // 2] = rest_ref[src, two:three]
                src = slice(f * short + rest, f * short + 2 * rest)
                out_w_ref[dst, D // 2 :] = rest_ref[src, two:three]

    for h in range(heads):
        for j in range(groups):
            start = pl.multiple_of((me ^ j) * width + h * HD, HD)
            mixed_ref[pl.ds(start, HD), :] = chunks[h * groups + j][...]
    gain = g_ref[:1]
    proj = rest_ref[:, :D]
    hidden = x_ref[...].astype(f32) + dg(mixed_ref[...], proj, TN)
    unit, inverse = unit_rows_of(hidden)
    second = (unit * gain).astype(bf)
    second_ref[...] = second
    dy = dy_ref[...]
    result = hidden
    d_second = jnp.zeros_like(hidden)
    step = 384
    for c in range(ff // step):
        a = slice(c * step, (c + 1) * step)
        b = slice(ff + c * step, ff + (c + 1) * step)
        gate = dg(second, w_ref[:, a], NN)
        up = dg(second, w_ref[:, b], NN)
        d_inner = dg(dy, out_w_ref[a, :], NT)
        bell = 0.5 + 0.5 * lax.erf(gate * 0.7071067811865476)
        gelu = gate * bell
        inner = (gelu * up).astype(bf)
        inner_ref[:, a] = inner
        result = result + dg(inner, out_w_ref[a, :], NN)
        slope = bell + gate * (jnp.exp(-0.5 * gate * gate) * 0.3989422804014327)
        d_gate = (d_inner * up * slope).astype(bf)
        d_up = (d_inner * gelu).astype(bf)
        dgu_ref[:, a] = d_gate
        dgu_ref[:, b] = d_up
        d_second = d_second + dg(d_gate, w_ref[:, a], NT) + dg(d_up, w_ref[:, b], NT)
    result_ref[...] = result.astype(bf)
    d_hidden = dy.astype(f32) + normalize_back(d_second, unit, inverse, gain)
    dh_ref[...] = d_hidden
    branch = d_hidden.astype(bf)
    branch_ref[...] = branch
    t_ref[...] = dg(proj, branch, NT).astype(bf)
    for j in range(groups):
        start = pl.multiple_of((me ^ j) * width, HD)
        d_chunks[j][...] = t_ref[pl.ds(start, width), :]


def middle(groups, heads, shards, ff, info, x, dy, mine, other, out_w, chunks):
    rows = x.shape[0]
    rb = min(256, rows)
    by_row = lambda i: (i, 0)
    by_column = lambda i: (0, i)
    whole = lambda i: (0, 0)
    outs = pl.pallas_call(
        functools.partial(middle_kernel, groups, heads, ff, shards),
        grid=(rows // rb,),
        out_shape=(jax.ShapeDtypeStruct((heads * HD, rows), bf),) * groups
        + (
            jax.ShapeDtypeStruct((rows, D), bf),
            jax.ShapeDtypeStruct((rows, D), f32),
            jax.ShapeDtypeStruct((D, rows), bf),
            jax.ShapeDtypeStruct((rows, D), bf),
            jax.ShapeDtypeStruct((rows, 2 * ff), bf),
            jax.ShapeDtypeStruct((rows, ff), bf),
            jax.ShapeDtypeStruct((rows, D), bf),
        ),
        in_specs=[
            pl.BlockSpec(memory_space=pltpu.SMEM),
            pl.BlockSpec((rb, D), by_row),
            pl.BlockSpec((rb, D), by_row),
            pl.BlockSpec(memory_space=pl.ANY),
            pl.BlockSpec(memory_space=pl.ANY),
        ]
        + [pl.BlockSpec(w.shape, whole, pipeline_mode=pl.Buffered(1)) for w in out_w]
        + [pl.BlockSpec((HD, rb), by_column)] * (groups * heads),
        out_specs=(pl.BlockSpec((heads * HD, rb), by_column),) * groups
        + (
            pl.BlockSpec((rb, D), by_row),
            pl.BlockSpec((rb, D), by_row),
            pl.BlockSpec((D, rb), by_column),
            pl.BlockSpec((rb, D), by_row),
            pl.BlockSpec((rb, 2 * ff), by_row),
            pl.BlockSpec((rb, ff), by_row),
            pl.BlockSpec((rb, D), by_row),
        ),
        scratch_shapes=[
            pltpu.VMEM((8, D), f32),
            pltpu.VMEM((D, rb), bf),
            pltpu.VMEM((ff, D), bf),
            pltpu.VMEM(mine.shape, bf),
            pltpu.VMEM(mine.shape, bf),
            pltpu.SemaphoreType.DMA((2,)),
        ],
        compiler_params=pltpu.CompilerParams(vmem_limit_bytes=58 * 2**20),
        cost_estimate=pl.CostEstimate(
            flops=rows * D * (14 * ff + 4 * D), bytes_accessed=30 * 2**20, transcendentals=rows * ff
        ),
        name="middle",
    )(info, x, dy, mine, other, *out_w, *chunks)
    return list(outs[:groups]), outs[groups:]


def last_kernel(groups, chosen, x_ref, base_ref, gain_ref, *refs):
    count = groups * len(chosen)
    chunks = refs[:count]
    pairs = refs[count : 2 * count]
    value_refs = refs[2 * count : 3 * count]
    out_ref, dp_ref, wh_ref, g_ref = refs[-4:]
    both = groups * 2 * HD

    @pl.when(pl.program_id(0) == 0)
    def _():
        g_ref[...] = gain_ref[...].astype(f32).T[HD : HD + 8]
        for n, h in enumerate(chosen):
            side = (h & 1) * HD
            pieces = [ref[...] for ref in pairs[n * groups : (n + 1) * groups]]
            pieces += [ref[:, side : side + HD] for ref in value_refs[n * groups : (n + 1) * groups]]
            wh_ref[:, n * D : (n + 1) * D] = jnp.concatenate(pieces, axis=1)

    for n in range(len(chosen)):
        for j in range(groups):
            chunk = chunks[n * groups + j]
            start = n * D + j * 2 * HD
            dp_ref[start : start + 2 * HD, :] = chunk[: 2 * HD, :]
            start = n * D + both + j * HD
            dp_ref[start : start + HD, :] = chunk[2 * HD :, :]
    d_normed = dg(wh_ref[...], dp_ref[...], NN).T
    unit, inverse = unit_rows_of(x_ref[...].astype(f32))
    out_ref[...] = base_ref[...] + normalize_back(d_normed, unit, inverse, g_ref[:1])


def last(groups, heads, chosen, x, base, peers, chunks, after):
    rows = chunks[0].shape[1]
    rb = min(256, rows)
    by_row = lambda i: (i, 0)

    def tile(n):
        return pl.BlockSpec((D, 128), lambda i: (0, n), pipeline_mode=pl.Buffered(1))

    pairs = [tile(h) for h in chosen for _ in peers]
    value_tiles = [tile(heads + h // 2) for h in chosen for _ in peers]
    return pl.pallas_call(
        functools.partial(last_kernel, groups, chosen),
        grid=(rows // rb,),
        out_shape=jax.ShapeDtypeStruct((rows, D), f32),
        in_specs=[
            pl.BlockSpec((rb, D), by_row),
            pl.BlockSpec((rb, D), by_row),
            tile(peers[0].shape[1] // 128 - 1),
        ]
        + [pl.BlockSpec((3 * HD, rb), lambda i: (0, i))] * len(chunks)
        + pairs
        + value_tiles
        + [pl.BlockSpec(memory_space=pl.ANY)] * len(after),
        out_specs=pl.BlockSpec((rb, D), by_row),
        scratch_shapes=[
            pltpu.VMEM((len(chosen) * D, rb), bf),
            pltpu.VMEM((D, len(chosen) * D), bf),
            pltpu.VMEM((8, D), f32),
        ],
        compiler_params=pltpu.CompilerParams(vmem_limit_bytes=58 * 2**20),
        cost_estimate=pl.CostEstimate(
            flops=2 * len(chosen) * rows * D * D, bytes_accessed=12 * 2**20, transcendentals=0
        ),
        name="last",
    )(x, base, peers[0], *chunks, *(list(peers) * (2 * len(chosen))), *after)


def own_kernel(groups, heads, info_ref, w_ref, gain_ref, out_ref):
    for g in range(groups):

        @pl.when(info_ref[0] == g)
        def _():
            def piece(t, h):
                start = t * D + (g * heads + h) * HD
                return w_ref[:, start : start + HD]

            pieces = []
            for h in range(heads):
                pieces += [piece(0, h), piece(1, h)]
            pieces += [piece(2, h) for h in range(heads)] + [column(gain_ref).astype(bf)]
            missing = out_ref.shape[2] - 3 * heads * HD - 1
            pieces.append(jnp.zeros((w_ref.shape[0], missing), bf))
            own = jnp.concatenate(pieces, axis=1)
            for f in range(out_ref.shape[0]):
                out_ref[f] = own


def own_columns(groups, heads, shards, info, w, gain):
    width = (3 * heads * HD + 128) // 128 * 128
    return pl.pallas_call(
        functools.partial(own_kernel, groups, heads),
        out_shape=jax.ShapeDtypeStruct((shards, w.shape[0], width), bf),
        in_specs=[
            pl.BlockSpec(memory_space=pltpu.SMEM),
            pl.BlockSpec(memory_space=pltpu.VMEM),
            pl.BlockSpec(memory_space=pltpu.VMEM),
        ],
        out_specs=pl.BlockSpec(memory_space=pltpu.VMEM),
        name="own_columns",
    )(info, w, gain)


def tables_kernel(cos_ref, sin_ref, cos_rows_ref, sin_rows_ref, cos_t_ref, sin_t_ref):
    c, s = cos_ref[...], sin_ref[...]
    cos_t_ref[...] = jnp.concatenate([c, c], axis=0)
    sin_t_ref[...] = jnp.concatenate([s, s], axis=0)
    scale = HD**-0.5 * LOG2E
    cos_rows_ref[...] = jnp.concatenate([c * scale, c * scale, c, c], axis=0).T
    sin_rows_ref[...] = jnp.concatenate([s * -scale, s * scale, -s, s], axis=0).T


def tables(cosine, sine):
    half, S = cosine.shape
    rb = min(1024, S)
    return pl.pallas_call(
        tables_kernel,
        grid=(S // rb,),
        out_shape=(jax.ShapeDtypeStruct((S, 4 * half), f32),) * 2
        + (jax.ShapeDtypeStruct((2 * half, S), f32),) * 2,
        in_specs=[pl.BlockSpec((half, rb), lambda i: (0, i))] * 2,
        out_specs=(pl.BlockSpec((rb, 4 * half), lambda i: (i, 0)),) * 2
        + (pl.BlockSpec((2 * half, rb), lambda i: (0, i)),) * 2,
        name="tables",
    )(cosine, sine)


def grads_kernel(place_ref, second_ref, dgu_ref, mixed_ref, branch_ref, inner_ref, dy_ref, *refs):
    outs, tall_ref, held_ref = refs[:-2], refs[-2], refs[-1]
    i = pl.program_id(0)
    group = i ^ place_ref[0]
    end = pl.num_programs(0) - 1

    @pl.when(group < end)
    def _():
        held_ref[...] = dg(second_ref[...], dgu_ref[...], TN).astype(bf)

    @pl.when(group == end)
    def _():
        held_ref[...] = dg(mixed_ref[...], branch_ref[...], NN).astype(bf)

    @pl.when(i < end)
    def _():
        tall_ref[...] = dg(inner_ref[...], dy_ref[...], TN).astype(bf)

    for j in range(len(outs)):

        @pl.when(i == j)
        def _():
            outs[j][...] = held_ref[...]


def weight_grads(place, second, d_gate_up, mixed_t, branch, inner, dy):
    rows = second.shape[0]
    ff = inner.shape[1]
    steps = d_gate_up.shape[1] // D
    whole = lambda i, p: (0, 0)
    part = lambda i, p: (0, jnp.minimum(i, steps - 1))
    outs = pl.pallas_call(
        grads_kernel,
        grid_spec=pltpu.PrefetchScalarGridSpec(
            num_scalar_prefetch=1,
            grid=(steps + 1,),
            in_specs=[
                pl.BlockSpec((rows, D), whole),
                pl.BlockSpec((rows, D), lambda i, p: (0, jnp.minimum(i ^ p[0], steps - 1))),
                pl.BlockSpec((D, rows), whole),
                pl.BlockSpec((rows, D), whole),
                pl.BlockSpec((rows, ff // steps), part),
                pl.BlockSpec((rows, D), whole),
            ],
            out_specs=(pl.BlockSpec((D, D), whole),) * (steps + 1)
            + (pl.BlockSpec((ff // steps, D), lambda i, p: (jnp.minimum(i, steps - 1), 0)),),
            scratch_shapes=[pltpu.VMEM((D, D), bf)],
        ),
        out_shape=(jax.ShapeDtypeStruct((D, D), bf),) * (steps + 1)
        + (jax.ShapeDtypeStruct((ff, D), bf),),
        compiler_params=pltpu.CompilerParams(vmem_limit_bytes=58 * 2**20),
        cost_estimate=pl.CostEstimate(
            flops=2 * rows * D * (D * (steps + 1) + ff), bytes_accessed=20 * 2**20, transcendentals=0
        ),
        name="weight_grads",
    )(place, second, d_gate_up, mixed_t, branch, inner, dy)
    return list(outs[:-1]), outs[-1]


def ordered(
    kernel, arrays, after, carry, out_shape, in_specs, out_specs, name, grid=(), scratch=()
):
    first = len(arrays) + len(after)
    own = len(out_shape)
    anywhere = pl.BlockSpec(memory_space=pl.ANY)

    def call(*refs):
        outs = refs[first + len(carry) :]
        kernel(*refs[: len(arrays)], *outs[:own], *outs[own + len(carry) :])

    outs = pl.pallas_call(
        call,
        grid=grid,
        out_shape=tuple(out_shape) + tuple(jax.ShapeDtypeStruct(a.shape, a.dtype) for a in carry),
        in_specs=list(in_specs) + [anywhere] * (len(after) + len(carry)),
        out_specs=tuple(out_specs) + (anywhere,) * len(carry),
        scratch_shapes=list(scratch),
        input_output_aliases={first + n: own + n for n in range(len(carry))},
        compiler_params=pltpu.CompilerParams(vmem_limit_bytes=58 * 2**20),
        name=name,
    )(*arrays, *after, *carry)
    return list(outs[:own]), list(outs[own:])


def add_kernel(*refs):
    total = refs[0][...].astype(f32)
    for ref in refs[1:-1]:
        total = total + ref[...].astype(f32)
    refs[-1][...] = total.astype(bf)


def add_up(arrays, after, carry):
    rows, columns = arrays[0].shape
    rb = 256
    spec = pl.BlockSpec((rb, columns), lambda i: (i, 0))
    (total,), carried = ordered(
        add_kernel, arrays, after, carry, [jax.ShapeDtypeStruct((rows, columns), bf)],
        [spec] * len(arrays), [spec], "add_up", grid=(rows // rb,),
    )
    return total, carried


def up16(n):
    return -(-n // 16) * 16


def beside_kernel(first_ref, second_ref, *refs):
    out_ref = refs[-1]
    start = 0
    for ref in (first_ref, second_ref):
        total = ref[0].astype(f32)
        for f in range(1, ref.shape[0]):
            total = total + ref[f].astype(f32)
        out_ref[:, start : start + ref.shape[2]] = total.astype(bf)
        start += ref.shape[2]


def beside(first, second, after):
    vmem = pl.BlockSpec(memory_space=pltpu.VMEM)
    return pl.pallas_call(
        beside_kernel,
        out_shape=jax.ShapeDtypeStruct((first.shape[1], first.shape[2] + second.shape[2]), bf),
        in_specs=[vmem, vmem] + [pl.BlockSpec(memory_space=pl.ANY)] * len(after),
        out_specs=vmem,
        compiler_params=pltpu.CompilerParams(vmem_limit_bytes=58 * 2**20),
        name="beside",
    )(first, second, *after)


def owned_kernel(wide_ref, tall_ref, *refs):
    out_ref = refs[-1]
    start = 0
    for ref in (wide_ref, tall_ref):
        total = ref[0].astype(f32)
        for f in range(1, ref.shape[0]):
            total = total + ref[f].astype(f32)
        out_ref[start : start + ref.shape[1], :] = total.astype(bf)
        start += up16(ref.shape[1])


def owned(wide, tall, after, carry):
    vmem = pl.BlockSpec(memory_space=pltpu.VMEM)
    shape = (up16(wide.shape[1]) + up16(tall.shape[1]), D)
    (total,), carried = ordered(
        owned_kernel, [wide, tall], after, carry, [jax.ShapeDtypeStruct(shape, bf)],
        [vmem] * 2, [vmem], "owned",
    )
    return total, carried


def finish_wide_kernel(groups, info_ref, w_ref, gain_ref, *refs):
    in_ref, proj_ref, dgain_ref, out_ref, held_ref = refs[groups:]
    shard = w_ref.shape[0]
    start = up16(shard)
    tall = 0.0
    for j in range(groups):
        held_ref[info_ref[0] ^ j] = refs[j][...]
        tall = tall + refs[j][start : start + out_ref.shape[0], :].astype(f32)
    out_ref[...] = tall
    total = 0.0
    for g in range(groups - 1):
        at = slice(g * D, (g + 1) * D)
        grad = held_ref[g, :shard, :].astype(f32)
        in_ref[:, at] = grad
        total = total + jnp.sum(w_ref[:, at].astype(f32) * grad, axis=1, keepdims=True)
    proj_ref[...] = held_ref[groups - 1, :shard, :].astype(f32)
    dgain_ref[...] = row_of(total / column(gain_ref))


def finish_qkv_kernel(groups, heads, info_ref, w_ref, gain_ref, *refs):
    out_ref, dgain_ref, held_ref = refs[groups : groups + 3]
    for j in range(groups):
        held_ref[info_ref[0] ^ j] = refs[j][...]
    pieces = []
    for t in range(3):
        for g in range(groups):
            for h in range(heads):
                start = h * 256 + t * HD
                pieces.append(held_ref[g, :, start : start + HD].astype(f32))
    grad = jnp.concatenate(pieces, axis=1)
    out_ref[...] = grad
    total = jnp.sum(w_ref[...].astype(f32) * grad, axis=1, keepdims=True)
    dgain_ref[...] = row_of(total / column(gain_ref))


def finish(kernel, groups, info, w, gain, parts, shapes, name, after=(), carry=()):
    vmem = pl.BlockSpec(memory_space=pltpu.VMEM)
    return ordered(
        kernel, [info, w, gain, *parts], list(after), list(carry),
        [jax.ShapeDtypeStruct(shape, f32) for shape in shapes],
        [pl.BlockSpec(memory_space=pltpu.SMEM)] + [vmem] * (2 + groups),
        [vmem] * len(shapes), name,
        scratch=[pltpu.VMEM((groups,) + parts[0].shape, bf)],
    )


def body(
    tokens, lengths, attn_gain, qkv_weight, proj_weight, ffn_gain, in_weight, out_weight, out_grad
):
    rows = tokens.shape[1]
    groups = lax.axis_size("seq")
    shards = lax.axis_size("fsdp")
    heads = HEADS // groups
    shard = D // shards
    me = lax.axis_index("seq")

    def swap(array, j, axis="seq"):
        size = lax.axis_size(axis)
        return lax.ppermute(array, axis, [(i, i ^ j) for i in range(size)])

    def exchange(chunks):
        return [chunks[0]] + [swap(chunks[j], j) for j in range(1, groups)]

    def gather(array):
        return lax.all_gather(array, "fsdp", axis=0, tiled=True)

    place = jnp.stack([me]).astype(jnp.int32)
    x0 = tokens[0]
    across = swap(x0, 2)
    near = swap(x0, 1)
    attn_row = attn_gain[None, :]
    ffn_row = ffn_gain[None, :]
    own = own_columns(groups, heads, shards, place, qkv_weight, attn_row)
    own = lax.all_to_all(own, "fsdp", split_axis=0, concat_axis=0, tiled=True).reshape(D, -1)

    half = HD // 2
    frequency = rope_base ** (-(lax.iota(f32, half) * 2.0) / HD)
    starts = [(me ^ j) * rows for j in range(groups)]
    positions = jnp.concatenate([s + lax.iota(jnp.int32, rows) for s in starts]).astype(f32)
    angles = frequency[:, None] * positions[None, :]
    cos_rows, sin_rows, cos_t, sin_t = tables(jnp.cos(angles), jnp.sin(angles))

    def project(j, block, carried):
        info = jnp.stack([starts[j], lengths[0]]).astype(jnp.int32)
        return qkv_call(j, groups, heads, info, block, cos_rows, sin_rows, own, carried)

    diagonal = swap(across, 1)
    carried = project(2, across, None)
    carried = project(0, x0, carried)
    carried = project(1, near, carried)
    normed, k, v, qt, kt, vt = project(3, diagonal, carried)

    ff = in_weight.shape[1] // 2
    tall = out_weight.shape[0]
    packed = shards <= 8
    mine = gather(own_half(packed, place, in_weight, proj_weight, ffn_row, out_weight, [own, cos_t]))
    out_full = [] if packed else [gather(out_weight)]

    own = hold(own, [normed])
    own_near, own_across = swap(own, 1), swap(own, 2)

    kept = []
    chunks = []
    for h in range(heads):
        before = [kept[-1][2]] if kept else []
        if h == 1:
            before += [own_near, own_across]
        saved, mixed = attend(h, k, qt, vt, groups, before)
        kept.append(saved)
        if h > 0:
            early = [chunks[n] for n in range((h - 1) * groups, h * groups) if n % groups]
            extra = [mine] if h == heads - 2 else [own_across]
            _, carried = ordered(
                lambda: None, [], [saved[2]] + early, mixed[1:] + extra, [], [], [], "hold"
            )
            mixed = mixed[:1] + carried[:-1]
            if h == heads - 2:
                mine = carried[-1]
                other = swap(mine, 1)
            else:
                own_across = carried[-1]
                own_diagonal = swap(own_across, 1)
        chunks += exchange(mixed)

    dy = out_grad[0]
    d_mixed, (result, d_hidden, mixed_t, second, d_gate_up, inner, branch) = middle(
        groups, heads, shards, ff, place, x0, dy, mine, other, out_full, chunks
    )
    d_mixed = exchange(d_mixed)

    def to_owner(array):
        parts = array.reshape(shards, array.shape[0] // shards, -1)
        return lax.all_to_all(parts, "fsdp", split_axis=0, concat_axis=0, tiled=True)

    def from_peers(array):
        return [array] + [swap(array, j) for j in range(1, groups)]

    wide, tall_grad = weight_grads(place, second, d_gate_up, mixed_t, branch, inner, dy)
    _, carried = ordered(
        lambda: None, [], d_mixed[1:], wide[1:] + [tall_grad], [], [], [], "hold"
    )
    tall_grad = carried[-1]
    wide_all = exchange(wide[:1] + carried[:-1])
    tall_parts = to_owner(tall_grad)

    def back(h, grad_place, after):
        return attend_back(
            h, v, kt, qt, d_mixed, kept[h], cos_t, sin_t, normed, groups, grad_place, after
        )

    peers = [own, own_near, own_across, own_diagonal]
    sent_0, qkv_first = back(0, (512, 0, None), [tall_grad, own_diagonal])
    wide_sum, others = add_up(wide_all, [qkv_first, tall_parts], sent_0[1:])
    wide_parts = to_owner(wide_sum)
    received_0 = exchange(sent_0[:1] + others)

    sent_1, qkv_first = back(1, (512, 1, qkv_first), [wide_sum])
    both, carried = owned(wide_parts, tall_parts, received_0[1:], sent_1[1:] + [qkv_first])
    received_1 = exchange(sent_1[:1] + carried[:-1])
    both_far = [swap(both, j) for j in range(2, groups)]
    qkv_parts = to_owner(carried[-1])

    sent_2, qkv_second = back(2, (256, 0, None), [both])
    _, carried = ordered(
        lambda: None, [], received_1[1:] + both_far + [qkv_parts],
        sent_2[1:] + [qkv_second, both], [], [], [], "pass_on",
    )
    qkv_second, both = carried[-2:]
    received_2 = exchange(sent_2[:1] + carried[:-2])
    both_peers = [both, swap(both, 1)] + both_far
    (in_weight_grad, proj_weight_grad, ffn_gain_grad, out_weight_grad), carried = finish(
        functools.partial(finish_wide_kernel, groups),
        groups, place, in_weight, ffn_row, both_peers,
        ((shard, 2 * ff), (shard, D), (1, shard), (tall, D)), "finish_wide",
        carry=[qkv_second],
    )
    qkv_second_parts = to_owner(carried[0])
    base = last(
        groups, heads, (0, 1), x0, d_hidden, peers, received_0 + received_1, [carried[0]]
    )
    qkv_peers = from_peers(beside(qkv_parts, qkv_second_parts, [base] + received_2[1:]))
    tokens_grad = last(groups, heads, (2,), x0, base, peers, received_2, [])
    (qkv_weight_grad, attn_gain_grad), _ = finish(
        functools.partial(finish_qkv_kernel, groups, heads),
        groups, place, qkv_weight, attn_row, qkv_peers,
        ((shard, 3 * D), (1, shard)), "finish_qkv", [tokens_grad],
    )
    return (
        result[None],
        tokens_grad[None],
        attn_gain_grad[0],
        qkv_weight_grad,
        proj_weight_grad,
        ffn_gain_grad[0],
        in_weight_grad,
        out_weight_grad,
    )


def solution(mesh):
    in_specs = (
        P("fsdp", "seq", None),
        P("fsdp"),
        P("fsdp"),
        P("fsdp", None),
        P("fsdp", None),
        P("fsdp"),
        P("fsdp", None),
        P("fsdp", None),
        P("fsdp", "seq", None),
    )
    out_specs = (
        P("fsdp", "seq", None),
        P("fsdp", "seq", None),
        P("fsdp"),
        P("fsdp", None),
        P("fsdp", None),
        P("fsdp"),
        P("fsdp", None),
        P("fsdp", None),
    )
    return jax.shard_map(body, mesh=mesh, in_specs=in_specs, out_specs=out_specs, check_vma=False)
```

```python
import functools

import jax
import jax.numpy as jnp
from jax import lax
from jax.experimental import pallas as pl
from jax.experimental.pallas import tpu as pltpu
from jax.sharding import PartitionSpec as P

D = 768
HEADS = 12
HD = 64

epsilon = 1e-05
rope_base = 160000.0
masked_score = -1e30
LOG2E = 1.4426950408889634
LN2 = 0.6931471805599453

VMEM = 63 * 2**20

bf = jnp.bfloat16
f32 = jnp.float32
NN = ((1,), (0,))
NT = ((1,), (1,))
TN = ((0,), (0,))


def dg(a, b, dims):
    return lax.dot_general(a, b, (dims, ((), ())), preferred_element_type=f32)


def unit_rows_of(x):
    centred = x - jnp.mean(x, axis=-1, keepdims=True)
    inverse = lax.rsqrt(jnp.mean(centred * centred, axis=-1, keepdims=True) + epsilon)
    return centred * inverse, inverse


def qkv_kernel(heads, info_ref, x_ref, cos_ref, sin_ref, w_ref, *refs):
    n_ref, k_ref, v_ref, qt_ref, kt_ref, vt_ref, g_ref = refs[-7:]
    rb = x_ref.shape[0]
    value_at = heads * 128

    @pl.when(pl.program_id(0) == 0)
    def _():
        last = w_ref[:, w_ref.shape[1] - 128 :].astype(f32).T
        g_ref[...] = last[HD : HD + 8]

    unit, _ = unit_rows_of(x_ref[...].astype(f32))
    normed = (unit * g_ref[:1]).astype(bf)
    n_ref[...] = normed
    lane = lax.broadcasted_iota(jnp.int32, (rb, 128), 1)
    row = lax.broadcasted_iota(jnp.int32, (rb, 128), 0)
    position = info_ref[0] + pl.program_id(0) * rb + row
    bias = jnp.where(position < info_ref[1], 0.0, masked_score)
    key_tail = jnp.where(lane == HD, bias, 0.0)
    value_tail = jnp.where(lane < HD + 2, -1.0, 0.0)
    head_lane = lane < HD
    lower = (lane & (HD - 1)) < HD // 2
    one_row = jnp.where(lax.broadcasted_iota(jnp.int32, (HD, rb), 0) == 0, 1.0, 0.0).astype(bf)
    y = dg(normed, w_ref[...], NN)
    for h in range(heads):
        t = y[:, h * 128 : (h + 1) * 128]
        turned = jnp.where(lower, pltpu.roll(t, 128 - HD // 2, 1), pltpu.roll(t, HD // 2, 1))
        t = t * cos_ref[...] + turned * sin_ref[...]
        k_ref[h] = jnp.where(head_lane, pltpu.roll(t, HD, 1), key_tail).astype(bf)
        t = t.T.astype(bf)
        qt_ref[h, :HD] = t[:HD]
        qt_ref[h, HD:] = one_row
        kt_ref[h] = t[HD:]
    for h in range(heads):
        at = value_at + h // 2 * 128
        t = y[:, at : at + 128]
        turned = t if h % 2 == 0 else pltpu.roll(t, HD, 1)
        v_ref[h] = jnp.where(head_lane, turned, value_tail).astype(bf)
        if h % 2 == 0:
            t_rows = t.T.astype(bf)
        vt_ref[h, :HD] = t_rows[:HD] if h % 2 == 0 else t_rows[HD:]
        vt_ref[h, HD:] = one_row[:16]


def qkv_call(block, blocks, heads, info, x, cos, sin, w, carried):
    rows = x.shape[0]
    S = rows * blocks
    rb = min(512, rows)
    steps = rows // rb
    width = w.shape[1]
    at = lambda i: block * steps + i
    outs = (
        jax.ShapeDtypeStruct((S, D), bf),
        jax.ShapeDtypeStruct((heads, S, 128), bf),
        jax.ShapeDtypeStruct((heads, S, 128), bf),
        jax.ShapeDtypeStruct((heads, 128, S), bf),
        jax.ShapeDtypeStruct((heads, HD, S), bf),
        jax.ShapeDtypeStruct((heads, 80, S), bf),
    )
    in_specs = [
        pl.BlockSpec(memory_space=pltpu.SMEM),
        pl.BlockSpec((rb, D), lambda i: (i, 0)),
        pl.BlockSpec((rb, 128), lambda i: (at(i), 0)),
        pl.BlockSpec((rb, 128), lambda i: (at(i), 0)),
        pl.BlockSpec((D, width), lambda i: (0, 0)),
    ]
    aliases = {}
    if carried is not None:
        first = len(in_specs)
        in_specs += [pl.BlockSpec(memory_space=pl.ANY)] * 6
        aliases = {first + n: n for n in range(6)}
    return pl.pallas_call(
        functools.partial(qkv_kernel, heads),
        grid=(steps,),
        out_shape=outs,
        in_specs=in_specs,
        out_specs=(
            pl.BlockSpec((rb, D), lambda i: (at(i), 0)),
            pl.BlockSpec((heads, rb, 128), lambda i: (0, at(i), 0)),
            pl.BlockSpec((heads, rb, 128), lambda i: (0, at(i), 0)),
            pl.BlockSpec((heads, 128, rb), lambda i: (0, 0, at(i))),
            pl.BlockSpec((heads, HD, rb), lambda i: (0, 0, at(i))),
            pl.BlockSpec((heads, 80, rb), lambda i: (0, 0, at(i))),
        ),
        scratch_shapes=[pltpu.VMEM((8, D), f32)],
        input_output_aliases=aliases,
        compiler_params=pltpu.CompilerParams(vmem_limit_bytes=VMEM),
        cost_estimate=pl.CostEstimate(
            flops=4 * rows * D * width, bytes_accessed=rows * 8192, transcendentals=0
        ),
        name="qkv",
    )(info, x, cos, sin, w, *(carried or ()))


def attend_kernel(kc, half, count, k_ref, qa_ref, qb_ref, v_ref, *refs):
    refs = refs[count:]
    pa_ref, pb_ref, oa_ref, ob_ref, la_ref, lb_ref = refs[:6]
    chunks = refs[6 : 6 + half]
    sa_ref, sb_ref, m_ref = refs[6 + half :]
    i = pl.program_id(0)
    rows = k_ref.shape[1]
    bq = qa_ref.shape[2]

    def stage(new, old):
        if new is not None:
            q_ref, s_new, new_slot = new
            q = q_ref[0]
            m = jnp.full((8, bq), -jnp.inf, f32)
        if old is not None:
            s_old, old_slot, p_ref, o_ref, l_ref, block = old
            top = jnp.max(m_ref[old_slot], axis=0, keepdims=True)
            acc = jnp.zeros((v_ref.shape[1], bq), f32)
        for c in range(rows // kc):
            at = slice(c * kc, (c + 1) * kc)
            if new is not None:
                s = dg(k_ref[0, at, :], q, NN)
                s_new[at, :] = s
                m = jnp.maximum(m, jnp.max(s.reshape(kc // 8, 8, bq), axis=0))
            if old is not None:
                p = jnp.exp2(s_old[at, :] - top).astype(bf)
                p_ref[0, at, :] = p
                acc = acc + dg(v_ref[0, :, at], p, NN)
        if new is not None:
            m_ref[new_slot] = m
        if old is not None:
            linv = 1.0 / acc[HD : HD + 1, :]
            o = acc[:HD, :] * linv
            o_ref[...] = o
            l_ref[0] = linv
            low = o.astype(bf)
            for j in range(half):

                @pl.when(block // 2 == j)
                def _():
                    chunks[j][:, old_slot * bq : (old_slot + 1) * bq] = low

    first = (qa_ref, sa_ref, 0)
    odd = (sb_ref, 1, pb_ref, ob_ref, lb_ref, 2 * i - 1)

    @pl.when(i == 0)
    def _():
        stage(first, None)

    @pl.when((i > 0) & (i < half))
    def _():
        stage(first, odd)

    @pl.when(i == half)
    def _():
        stage(None, odd)

    @pl.when(i < half)
    def _():
        stage((qb_ref, sb_ref, 1), (sa_ref, 0, pa_ref, oa_ref, la_ref, 2 * i))


def attend(h, k, qt, vt, groups, after, kc=256):
    S = k.shape[1]
    bq = S // groups // 2
    a = lambda i: jnp.minimum(i, groups - 1)
    b = lambda i: jnp.maximum(i - 1, 0)
    outs = pl.pallas_call(
        functools.partial(attend_kernel, kc, groups, len(after)),
        grid=(groups + 1,),
        out_shape=(jax.ShapeDtypeStruct((groups, S, bq), bf),) * 2
        + (jax.ShapeDtypeStruct((HD, S // 2), f32),) * 2
        + (jax.ShapeDtypeStruct((groups, 1, bq), f32),) * 2
        + (jax.ShapeDtypeStruct((HD, 2 * bq), bf),) * groups,
        in_specs=[
            pl.BlockSpec((1, S, 128), lambda i: (h, 0, 0)),
            pl.BlockSpec((1, 128, bq), lambda i: (h, 0, 2 * a(i))),
            pl.BlockSpec((1, 128, bq), lambda i: (h, 0, 2 * a(i) + 1)),
            pl.BlockSpec((1, 80, S), lambda i: (h, 0, 0)),
        ]
        + [pl.BlockSpec(memory_space=pl.ANY)] * len(after),
        out_specs=(
            pl.BlockSpec((1, S, bq), lambda i: (a(i), 0, 0)),
            pl.BlockSpec((1, S, bq), lambda i: (b(i), 0, 0)),
            pl.BlockSpec((HD, bq), lambda i: (0, a(i))),
            pl.BlockSpec((HD, bq), lambda i: (0, b(i))),
            pl.BlockSpec((1, 1, bq), lambda i: (a(i), 0, 0)),
            pl.BlockSpec((1, 1, bq), lambda i: (b(i), 0, 0)),
        )
        + (pl.BlockSpec((HD, 2 * bq), lambda i: (0, 0)),) * groups,
        scratch_shapes=[
            pltpu.VMEM((S, bq), f32),
            pltpu.VMEM((S, bq), f32),
            pltpu.VMEM((2, 8, bq), f32),
        ],
        compiler_params=pltpu.CompilerParams(vmem_limit_bytes=VMEM),
        cost_estimate=pl.CostEstimate(
            flops=16 * HD * S * S, bytes_accessed=2 * S * S, transcendentals=S * S
        ),
        name="attend",
    )(k, qt, qt, vt, *after)
    return outs[:6], list(outs[6:])


def attend_back_kernel(kc, groups, v_ref, kt_ref, q_ref, *refs):
    oa_ref, ob_ref, la_ref, lb_ref, pa_ref, pb_ref, cos_ref, sin_ref, n_ref = refs[:9]
    do_refs = refs[9 : 9 + groups]
    outs = refs[-5 - groups : -5]
    grad_ref, acc_ref, do_ref, held_ref, sem = refs[-5:]
    i = pl.program_id(0)
    rows = v_ref.shape[1]
    width = q_ref.shape[2]
    bq = width // 2
    fetch = pltpu.make_async_copy(n_ref, held_ref, sem)

    @pl.when(i == 0)
    def _():
        fetch.start()
        acc_ref[...] = jnp.zeros_like(acc_ref)

    for j in range(groups):

        @pl.when(i == j)
        def _():
            do_ref[...] = do_refs[j][...]

    zero = jnp.zeros((HD, bq), bf)
    r = lax.broadcasted_iota(jnp.int32, (16, bq), 0)
    sides = []
    for n, (o_ref, l_ref, p_ref) in enumerate(((oa_ref, la_ref, pa_ref), (ob_ref, lb_ref, pb_ref))):
        at = slice(n * bq, (n + 1) * bq)
        dop = (do_ref[:, at].astype(f32) * l_ref[0]).astype(bf)
        delta = jnp.sum(dop.astype(f32) * o_ref[...], axis=0, keepdims=True)
        high = delta.astype(bf).astype(f32)
        tail = jnp.where(r == 0, high, jnp.where(r == 1, delta - high, 0.0)).astype(bf)
        doe = jnp.concatenate([dop, tail, jnp.zeros((128 - HD - 16, bq), bf)], axis=0)
        right_v = jnp.concatenate([dop, zero], axis=0).T
        right_k = jnp.concatenate([zero, q_ref[0, :HD, at]], axis=0).T
        sides.append((p_ref, doe, jnp.concatenate([right_v, right_k], axis=0)))
    dq = [jnp.zeros((HD, bq), f32), jnp.zeros((HD, bq), f32)]
    for n, (p_ref, doe, right) in enumerate(sides):
        for c in range(rows // kc):
            at = slice(c * kc, (c + 1) * kc)
            p = p_ref[0, at, :]
            ds = p * dg(v_ref[0, at, :], doe, NN).astype(bf)
            acc_ref[at, :] = acc_ref[at, :] + dg(jnp.concatenate([p, ds], axis=1), right, NN)
            dq[n] = dq[n] + dg(kt_ref[0, :, at], ds, NN)
    dq = jnp.concatenate(dq, axis=1) * HD**-0.5
    turned = jnp.concatenate([dq[HD // 2 :], -dq[: HD // 2]], axis=0)
    here = pl.ds(pl.multiple_of(i * width, width), width)
    dq = (dq * cos_ref[:, here] + turned * sin_ref[:, here]).astype(bf)
    for j in range(groups):

        @pl.when(i == j)
        def _():
            outs[j][:HD] = dq

    @pl.when(i == groups - 1)
    def _():
        fetch.wait()
        grad = jnp.zeros((3 * HD, D), f32)
        for j in range(groups):
            at = slice(j * width, (j + 1) * width)
            t = acc_ref[at, :].T
            dk = t[HD:] * LN2
            turned_k = jnp.concatenate([dk[HD // 2 :], -dk[: HD // 2]], axis=0)
            dk = dk * cos_ref[:, at] + turned_k * sin_ref[:, at]
            outs[j][HD : 2 * HD] = dk.astype(bf)
            outs[j][2 * HD :] = t[:HD].astype(bf)
            grad = grad + dg(outs[j][...], held_ref[at, :], NN)
        grad_ref[:, : 3 * HD] = grad.T.astype(bf)
        grad_ref[:, 3 * HD :] = jnp.zeros((D, HD), bf)


def attend_back(h, v, kt, qt, do, kept, cos, sin, normed, groups, place, after, kc=256):
    S = v.shape[1]
    width = S // groups
    bq = width // 2
    pa, pb, oa, ob, la, lb = kept
    columns, column, earlier = place
    extra = list(after) if earlier is None else [earlier] + list(after)
    whole = lambda i: (0, 0)
    by_block = lambda i: (i, 0, 0)
    outs = pl.pallas_call(
        functools.partial(attend_back_kernel, kc, groups),
        grid=(groups,),
        out_shape=(jax.ShapeDtypeStruct((3 * HD, width), bf),) * groups
        + (jax.ShapeDtypeStruct((D, columns), bf),),
        in_specs=[
            pl.BlockSpec((1, S, 128), lambda i: (h, 0, 0)),
            pl.BlockSpec((1, HD, S), lambda i: (h, 0, 0)),
            pl.BlockSpec((1, 128, width), lambda i: (h, 0, i)),
            pl.BlockSpec((HD, bq), lambda i: (0, i)),
            pl.BlockSpec((HD, bq), lambda i: (0, i)),
            pl.BlockSpec((1, 1, bq), by_block),
            pl.BlockSpec((1, 1, bq), by_block),
            pl.BlockSpec((1, S, bq), by_block),
            pl.BlockSpec((1, S, bq), by_block),
            pl.BlockSpec((HD, S), whole),
            pl.BlockSpec((HD, S), whole),
            pl.BlockSpec(memory_space=pl.ANY),
        ]
        + [pl.BlockSpec((HD, width), lambda i: (h, 0))] * groups
        + [pl.BlockSpec(memory_space=pl.ANY)] * len(extra),
        out_specs=(pl.BlockSpec((3 * HD, width), whole),) * groups
        + (pl.BlockSpec((D, 256), lambda i: (0, column)),),
        scratch_shapes=[
            pltpu.VMEM((S, 128), f32),
            pltpu.VMEM((HD, width), bf),
            pltpu.VMEM((S, D), bf),
            pltpu.SemaphoreType.DMA,
        ],
        input_output_aliases={} if earlier is None else {12 + groups: groups},
        compiler_params=pltpu.CompilerParams(vmem_limit_bytes=VMEM),
        cost_estimate=pl.CostEstimate(
            flops=24 * HD * S * S, bytes_accessed=2 * S * S, transcendentals=0
        ),
        name="attend_back",
    )(v, kt, qt, oa, ob, la, lb, pa, pb, cos, sin, normed, *do, *extra)
    return list(outs[:groups]), outs[groups]


def normalize_back(gradient, unit_rows, inverse, gain_row):
    scaled = gradient * gain_row
    return inverse * (
        scaled
        - jnp.mean(scaled, axis=-1, keepdims=True)
        - unit_rows * jnp.mean(scaled * unit_rows, axis=-1, keepdims=True)
    )


def column(row_ref):
    row = row_ref[...].astype(f32)
    return jnp.broadcast_to(row, (8, row.shape[1])).T[:, :1]


def row_of(total):
    return jnp.broadcast_to(total, (total.shape[0], 128)).T[:1]


def half_kernel(packed, info_ref, in_ref, proj_ref, gain_ref, out_w_ref, *refs):
    half_ref = refs[-1]
    side = info_ref[0] & 1

    @pl.when(side == 0)
    def _():
        half_ref[...] = in_ref[...]

    @pl.when(side == 1)
    def _():
        short = in_ref.shape[0]
        half_ref[:, :D] = proj_ref[...]
        gain = jnp.broadcast_to(column(gain_ref), (short, 128)).astype(bf)
        half_ref[:, D : D + 128] = gain
        if packed:
            one, two, three = D + 128, 2 * D + 128, 2 * D + D // 2 + 128
            tall = out_w_ref.shape[0]
            half_ref[:, one:two] = out_w_ref[:short, :]
            half_ref[: tall - short, two:three] = out_w_ref[short:, : D // 2]
            half_ref[tall - short :, two:three] = out_w_ref[short:, D // 2 :]


def own_half(packed, info, in_w, proj_w, gain, out_w, after):
    vmem = pl.BlockSpec(memory_space=pltpu.VMEM)
    return pl.pallas_call(
        functools.partial(half_kernel, packed),
        out_shape=jax.ShapeDtypeStruct(in_w.shape, bf),
        in_specs=[pl.BlockSpec(memory_space=pltpu.SMEM)]
        + [vmem] * 4
        + [pl.BlockSpec(memory_space=pl.ANY)] * len(after),
        out_specs=vmem,
        compiler_params=pltpu.CompilerParams(vmem_limit_bytes=VMEM),
        name="own_half",
    )(info, in_w, proj_w, gain, out_w, *after)


def hold(array, after):
    def kernel(*refs):
        pass

    return pl.pallas_call(
        kernel,
        out_shape=jax.ShapeDtypeStruct(array.shape, array.dtype),
        in_specs=[pl.BlockSpec(memory_space=pl.ANY)] * (1 + len(after)),
        out_specs=pl.BlockSpec(memory_space=pl.ANY),
        input_output_aliases={0: 0},
        compiler_params=pltpu.CompilerParams(vmem_limit_bytes=VMEM),
        name="hold",
    )(array, *after)


def middle_kernel(groups, heads, ff, shards, info_ref, x_ref, dy_ref, mine_ref, other_ref, *refs):
    count = groups * heads
    given = len(refs) - count - groups - 13
    out_given = refs[:given]
    chunks = refs[given : given + count]
    d_chunks = refs[given + count : given + count + groups]
    (result_ref, dh_ref, mixed_ref, second_ref, dgu_ref, inner_ref, branch_ref,
     g_ref, t_ref, out_w_ref, w_ref, rest_ref, sems) = refs[given + count + groups :]
    width = heads * HD
    me = info_ref[0]

    @pl.when(pl.program_id(0) == 0)
    def _():
        def fetch(first, second):
            copies = [
                pltpu.make_async_copy(first, w_ref, sems.at[0]),
                pltpu.make_async_copy(second, rest_ref, sems.at[1]),
            ]
            for copy in copies:
                copy.start()
            for copy in copies:
                copy.wait()

        @pl.when((me & 1) == 0)
        def _():
            fetch(mine_ref, other_ref)

        @pl.when((me & 1) == 1)
        def _():
            fetch(other_ref, mine_ref)

        g_ref[...] = rest_ref[:, D : D + 128].astype(f32).T[:8]
        if given:
            out_w_ref[...] = out_given[0][...]
        else:
            tall, short = ff // shards, D // shards
            rest = tall - short
            one, two, three = D + 128, 2 * D + 128, 2 * D + D // 2 + 128
            for f in range(shards):
                src = slice(f * short, (f + 1) * short)
                out_w_ref[f * tall : f * tall + short, :] = rest_ref[src, one:two]
                dst = slice(f * tall + short, (f + 1) * tall)
                src = slice(f * short, f * short + rest)
                out_w_ref[dst, : D // 2] = rest_ref[src, two:three]
                src = slice(f * short + rest, f * short + 2 * rest)
                out_w_ref[dst, D // 2 :] = rest_ref[src, two:three]

    for h in range(heads):
        for j in range(groups):
            start = pl.multiple_of((me ^ j) * width + h * HD, HD)
            mixed_ref[pl.ds(start, HD), :] = chunks[h * groups + j][...]
    gain = g_ref[:1]
    proj = rest_ref[:, :D]
    hidden = x_ref[...].astype(f32) + dg(mixed_ref[...], proj, TN)
    unit, inverse = unit_rows_of(hidden)
    second = (unit * gain).astype(bf)
    second_ref[...] = second
    dy = dy_ref[...]
    result = hidden
    d_second = jnp.zeros_like(hidden)
    step = 384
    for c in range(ff // step):
        a = slice(c * step, (c + 1) * step)
        b = slice(ff + c * step, ff + (c + 1) * step)
        gate = dg(second, w_ref[:, a], NN)
        up = dg(second, w_ref[:, b], NN)
        d_inner = dg(dy, out_w_ref[a, :], NT)
        bell = 0.5 + 0.5 * lax.erf(gate * 0.7071067811865476)
        gelu = gate * bell
        inner = (gelu * up).astype(bf)
        inner_ref[:, a] = inner
        result = result + dg(inner, out_w_ref[a, :], NN)
        slope = bell + gate * (jnp.exp(-0.5 * gate * gate) * 0.3989422804014327)
        d_gate = (d_inner * up * slope).astype(bf)
        d_up = (d_inner * gelu).astype(bf)
        dgu_ref[:, a] = d_gate
        dgu_ref[:, b] = d_up
        d_second = d_second + dg(d_gate, w_ref[:, a], NT) + dg(d_up, w_ref[:, b], NT)
    result_ref[...] = result.astype(bf)
    d_hidden = dy.astype(f32) + normalize_back(d_second, unit, inverse, gain)
    dh_ref[...] = d_hidden
    branch = d_hidden.astype(bf)
    branch_ref[...] = branch
    t_ref[...] = dg(proj, branch, NT).astype(bf)
    for j in range(groups):
        start = pl.multiple_of((me ^ j) * width, HD)
        d_chunks[j][...] = t_ref[pl.ds(start, width), :]


def middle(groups, heads, shards, ff, info, x, dy, mine, other, out_w, chunks):
    rows = x.shape[0]
    rb = min(256, rows)
    by_row = lambda i: (i, 0)
    by_column = lambda i: (0, i)
    whole = lambda i: (0, 0)
    outs = pl.pallas_call(
        functools.partial(middle_kernel, groups, heads, ff, shards),
        grid=(rows // rb,),
        out_shape=(jax.ShapeDtypeStruct((heads * HD, rows), bf),) * groups
        + (
            jax.ShapeDtypeStruct((rows, D), bf),
            jax.ShapeDtypeStruct((rows, D), f32),
            jax.ShapeDtypeStruct((D, rows), bf),
            jax.ShapeDtypeStruct((rows, D), bf),
            jax.ShapeDtypeStruct((rows, 2 * ff), bf),
            jax.ShapeDtypeStruct((rows, ff), bf),
            jax.ShapeDtypeStruct((rows, D), bf),
        ),
        in_specs=[
            pl.BlockSpec(memory_space=pltpu.SMEM),
            pl.BlockSpec((rb, D), by_row),
            pl.BlockSpec((rb, D), by_row),
            pl.BlockSpec(memory_space=pl.ANY),
            pl.BlockSpec(memory_space=pl.ANY),
        ]
        + [pl.BlockSpec(w.shape, whole, pipeline_mode=pl.Buffered(1)) for w in out_w]
        + [pl.BlockSpec((HD, rb), by_column)] * (groups * heads),
        out_specs=(pl.BlockSpec((heads * HD, rb), by_column),) * groups
        + (
            pl.BlockSpec((rb, D), by_row),
            pl.BlockSpec((rb, D), by_row),
            pl.BlockSpec((D, rb), by_column),
            pl.BlockSpec((rb, D), by_row),
            pl.BlockSpec((rb, 2 * ff), by_row),
            pl.BlockSpec((rb, ff), by_row),
            pl.BlockSpec((rb, D), by_row),
        ),
        scratch_shapes=[
            pltpu.VMEM((8, D), f32),
            pltpu.VMEM((D, rb), bf),
            pltpu.VMEM((ff, D), bf),
            pltpu.VMEM(mine.shape, bf),
            pltpu.VMEM(mine.shape, bf),
            pltpu.SemaphoreType.DMA((2,)),
        ],
        compiler_params=pltpu.CompilerParams(vmem_limit_bytes=VMEM),
        cost_estimate=pl.CostEstimate(
            flops=rows * D * (14 * ff + 4 * D), bytes_accessed=30 * 2**20, transcendentals=rows * ff
        ),
        name="middle",
    )(info, x, dy, mine, other, *out_w, *chunks)
    return list(outs[:groups]), outs[groups:]


def last_kernel(groups, chosen, x_ref, base_ref, gain_ref, *refs):
    count = groups * len(chosen)
    chunks = refs[:count]
    pairs = refs[count : 2 * count]
    value_refs = refs[2 * count : 3 * count]
    out_ref, dp_ref, wh_ref, g_ref = refs[-4:]
    both = groups * 2 * HD

    @pl.when(pl.program_id(0) == 0)
    def _():
        g_ref[...] = gain_ref[...].astype(f32).T[HD : HD + 8]
        for n, h in enumerate(chosen):
            side = (h & 1) * HD
            pieces = [ref[...] for ref in pairs[n * groups : (n + 1) * groups]]
            pieces += [ref[:, side : side + HD] for ref in value_refs[n * groups : (n + 1) * groups]]
            wh_ref[:, n * D : (n + 1) * D] = jnp.concatenate(pieces, axis=1)

    for n in range(len(chosen)):
        for j in range(groups):
            chunk = chunks[n * groups + j]
            start = n * D + j * 2 * HD
            dp_ref[start : start + 2 * HD, :] = chunk[: 2 * HD, :]
            start = n * D + both + j * HD
            dp_ref[start : start + HD, :] = chunk[2 * HD :, :]
    d_normed = dg(wh_ref[...], dp_ref[...], NN).T
    unit, inverse = unit_rows_of(x_ref[...].astype(f32))
    out_ref[...] = base_ref[...] + normalize_back(d_normed, unit, inverse, g_ref[:1])


def last(groups, heads, chosen, x, base, peers, chunks, after):
    rows = chunks[0].shape[1]
    rb = min(256, rows)
    by_row = lambda i: (i, 0)

    def tile(n):
        return pl.BlockSpec((D, 128), lambda i: (0, n), pipeline_mode=pl.Buffered(1))

    pairs = [tile(h) for h in chosen for _ in peers]
    value_tiles = [tile(heads + h // 2) for h in chosen for _ in peers]
    return pl.pallas_call(
        functools.partial(last_kernel, groups, chosen),
        grid=(rows // rb,),
        out_shape=jax.ShapeDtypeStruct((rows, D), f32),
        in_specs=[
            pl.BlockSpec((rb, D), by_row),
            pl.BlockSpec((rb, D), by_row),
            tile(peers[0].shape[1] // 128 - 1),
        ]
        + [pl.BlockSpec((3 * HD, rb), lambda i: (0, i))] * len(chunks)
        + pairs
        + value_tiles
        + [pl.BlockSpec(memory_space=pl.ANY)] * len(after),
        out_specs=pl.BlockSpec((rb, D), by_row),
        scratch_shapes=[
            pltpu.VMEM((len(chosen) * D, rb), bf),
            pltpu.VMEM((D, len(chosen) * D), bf),
            pltpu.VMEM((8, D), f32),
        ],
        compiler_params=pltpu.CompilerParams(vmem_limit_bytes=VMEM),
        cost_estimate=pl.CostEstimate(
            flops=2 * len(chosen) * rows * D * D, bytes_accessed=12 * 2**20, transcendentals=0
        ),
        name="last",
    )(x, base, peers[0], *chunks, *(list(peers) * (2 * len(chosen))), *after)


def own_kernel(groups, heads, info_ref, w_ref, gain_ref, out_ref):
    for g in range(groups):

        @pl.when(info_ref[0] == g)
        def _():
            def piece(t, h):
                start = t * D + (g * heads + h) * HD
                return w_ref[:, start : start + HD]

            pieces = []
            for h in range(heads):
                pieces += [piece(0, h), piece(1, h)]
            pieces += [piece(2, h) for h in range(heads)] + [column(gain_ref).astype(bf)]
            missing = out_ref.shape[2] - 3 * heads * HD - 1
            pieces.append(jnp.zeros((w_ref.shape[0], missing), bf))
            own = jnp.concatenate(pieces, axis=1)
            for f in range(out_ref.shape[0]):
                out_ref[f] = own


def own_columns(groups, heads, shards, info, w, gain):
    width = (3 * heads * HD + 128) // 128 * 128
    return pl.pallas_call(
        functools.partial(own_kernel, groups, heads),
        out_shape=jax.ShapeDtypeStruct((shards, w.shape[0], width), bf),
        in_specs=[
            pl.BlockSpec(memory_space=pltpu.SMEM),
            pl.BlockSpec(memory_space=pltpu.VMEM),
            pl.BlockSpec(memory_space=pltpu.VMEM),
        ],
        out_specs=pl.BlockSpec(memory_space=pltpu.VMEM),
        compiler_params=pltpu.CompilerParams(vmem_limit_bytes=VMEM),
        name="own_columns",
    )(info, w, gain)


def tables_kernel(cos_ref, sin_ref, cos_rows_ref, sin_rows_ref, cos_t_ref, sin_t_ref):
    c, s = cos_ref[...], sin_ref[...]
    cos_t_ref[...] = jnp.concatenate([c, c], axis=0)
    sin_t_ref[...] = jnp.concatenate([s, s], axis=0)
    scale = HD**-0.5 * LOG2E
    cos_rows_ref[...] = jnp.concatenate([c * scale, c * scale, c, c], axis=0).T
    sin_rows_ref[...] = jnp.concatenate([s * -scale, s * scale, -s, s], axis=0).T


def tables(cosine, sine):
    half, S = cosine.shape
    rb = min(1024, S)
    return pl.pallas_call(
        tables_kernel,
        grid=(S // rb,),
        out_shape=(jax.ShapeDtypeStruct((S, 4 * half), f32),) * 2
        + (jax.ShapeDtypeStruct((2 * half, S), f32),) * 2,
        in_specs=[pl.BlockSpec((half, rb), lambda i: (0, i))] * 2,
        out_specs=(pl.BlockSpec((rb, 4 * half), lambda i: (i, 0)),) * 2
        + (pl.BlockSpec((2 * half, rb), lambda i: (0, i)),) * 2,
        compiler_params=pltpu.CompilerParams(vmem_limit_bytes=VMEM),
        name="tables",
    )(cosine, sine)


def grads_kernel(place_ref, second_ref, dgu_ref, mixed_ref, branch_ref, inner_ref, dy_ref, *refs):
    outs, tall_ref, held_ref = refs[:-2], refs[-2], refs[-1]
    i = pl.program_id(0)
    group = i ^ place_ref[0]
    end = pl.num_programs(0) - 1

    @pl.when(group < end)
    def _():
        held_ref[...] = dg(second_ref[...], dgu_ref[...], TN).astype(bf)

    @pl.when(group == end)
    def _():
        held_ref[...] = dg(mixed_ref[...], branch_ref[...], NN).astype(bf)

    @pl.when(i < end)
    def _():
        tall_ref[...] = dg(inner_ref[...], dy_ref[...], TN).astype(bf)

    for j in range(len(outs)):

        @pl.when(i == j)
        def _():
            outs[j][...] = held_ref[...]


def weight_grads(place, second, d_gate_up, mixed_t, branch, inner, dy):
    rows = second.shape[0]
    ff = inner.shape[1]
    steps = d_gate_up.shape[1] // D
    whole = lambda i, p: (0, 0)
    part = lambda i, p: (0, jnp.minimum(i, steps - 1))
    outs = pl.pallas_call(
        grads_kernel,
        grid_spec=pltpu.PrefetchScalarGridSpec(
            num_scalar_prefetch=1,
            grid=(steps + 1,),
            in_specs=[
                pl.BlockSpec((rows, D), whole),
                pl.BlockSpec((rows, D), lambda i, p: (0, jnp.minimum(i ^ p[0], steps - 1))),
                pl.BlockSpec((D, rows), whole),
                pl.BlockSpec((rows, D), whole),
                pl.BlockSpec((rows, ff // steps), part),
                pl.BlockSpec((rows, D), whole),
            ],
            out_specs=(pl.BlockSpec((D, D), whole),) * (steps + 1)
            + (pl.BlockSpec((ff // steps, D), lambda i, p: (jnp.minimum(i, steps - 1), 0)),),
            scratch_shapes=[pltpu.VMEM((D, D), bf)],
        ),
        out_shape=(jax.ShapeDtypeStruct((D, D), bf),) * (steps + 1)
        + (jax.ShapeDtypeStruct((ff, D), bf),),
        compiler_params=pltpu.CompilerParams(vmem_limit_bytes=VMEM),
        cost_estimate=pl.CostEstimate(
            flops=2 * rows * D * (D * (steps + 1) + ff), bytes_accessed=20 * 2**20, transcendentals=0
        ),
        name="weight_grads",
    )(place, second, d_gate_up, mixed_t, branch, inner, dy)
    return list(outs[:-1]), outs[-1]


def ordered(
    kernel, arrays, after, carry, out_shape, in_specs, out_specs, name, grid=(), scratch=()
):
    first = len(arrays) + len(after)
    own = len(out_shape)
    anywhere = pl.BlockSpec(memory_space=pl.ANY)

    def call(*refs):
        outs = refs[first + len(carry) :]
        kernel(*refs[: len(arrays)], *outs[:own], *outs[own + len(carry) :])

    outs = pl.pallas_call(
        call,
        grid=grid,
        out_shape=tuple(out_shape) + tuple(jax.ShapeDtypeStruct(a.shape, a.dtype) for a in carry),
        in_specs=list(in_specs) + [anywhere] * (len(after) + len(carry)),
        out_specs=tuple(out_specs) + (anywhere,) * len(carry),
        scratch_shapes=list(scratch),
        input_output_aliases={first + n: own + n for n in range(len(carry))},
        compiler_params=pltpu.CompilerParams(vmem_limit_bytes=VMEM),
        name=name,
    )(*arrays, *after, *carry)
    return list(outs[:own]), list(outs[own:])


def add_kernel(*refs):
    total = refs[0][...].astype(f32)
    for ref in refs[1:-1]:
        total = total + ref[...].astype(f32)
    refs[-1][...] = total.astype(bf)


def add_up(arrays, after, carry):
    rows, columns = arrays[0].shape
    rb = 256
    spec = pl.BlockSpec((rb, columns), lambda i: (i, 0))
    (total,), carried = ordered(
        add_kernel, arrays, after, carry, [jax.ShapeDtypeStruct((rows, columns), bf)],
        [spec] * len(arrays), [spec], "add_up", grid=(rows // rb,),
    )
    return total, carried


def up16(n):
    return -(-n // 16) * 16


def beside_kernel(first_ref, second_ref, *refs):
    out_ref = refs[-1]
    start = 0
    for ref in (first_ref, second_ref):
        total = ref[0].astype(f32)
        for f in range(1, ref.shape[0]):
            total = total + ref[f].astype(f32)
        out_ref[:, start : start + ref.shape[2]] = total.astype(bf)
        start += ref.shape[2]


def beside(first, second, after):
    vmem = pl.BlockSpec(memory_space=pltpu.VMEM)
    return pl.pallas_call(
        beside_kernel,
        out_shape=jax.ShapeDtypeStruct((first.shape[1], first.shape[2] + second.shape[2]), bf),
        in_specs=[vmem, vmem] + [pl.BlockSpec(memory_space=pl.ANY)] * len(after),
        out_specs=vmem,
        compiler_params=pltpu.CompilerParams(vmem_limit_bytes=VMEM),
        name="beside",
    )(first, second, *after)


def owned_kernel(wide_ref, tall_ref, *refs):
    out_ref = refs[-1]
    start = 0
    for ref in (wide_ref, tall_ref):
        total = ref[0].astype(f32)
        for f in range(1, ref.shape[0]):
            total = total + ref[f].astype(f32)
        out_ref[start : start + ref.shape[1], :] = total.astype(bf)
        start += up16(ref.shape[1])


def owned(wide, tall, after, carry):
    vmem = pl.BlockSpec(memory_space=pltpu.VMEM)
    shape = (up16(wide.shape[1]) + up16(tall.shape[1]), D)
    (total,), carried = ordered(
        owned_kernel, [wide, tall], after, carry, [jax.ShapeDtypeStruct(shape, bf)],
        [vmem] * 2, [vmem], "owned",
    )
    return total, carried


def finish_wide_kernel(groups, info_ref, w_ref, gain_ref, *refs):
    in_ref, proj_ref, dgain_ref, out_ref, held_ref = refs[groups:]
    shard = w_ref.shape[0]
    start = up16(shard)
    tall = 0.0
    for j in range(groups):
        held_ref[info_ref[0] ^ j] = refs[j][...]
        tall = tall + refs[j][start : start + out_ref.shape[0], :].astype(f32)
    out_ref[...] = tall
    total = 0.0
    for g in range(groups - 1):
        at = slice(g * D, (g + 1) * D)
        grad = held_ref[g, :shard, :].astype(f32)
        in_ref[:, at] = grad
        total = total + jnp.sum(w_ref[:, at].astype(f32) * grad, axis=1, keepdims=True)
    proj_ref[...] = held_ref[groups - 1, :shard, :].astype(f32)
    dgain_ref[...] = row_of(total / column(gain_ref))


def finish_qkv_kernel(groups, heads, info_ref, w_ref, gain_ref, *refs):
    out_ref, dgain_ref, held_ref = refs[groups : groups + 3]
    for j in range(groups):
        held_ref[info_ref[0] ^ j] = refs[j][...]
    pieces = []
    for t in range(3):
        for g in range(groups):
            for h in range(heads):
                start = h * 256 + t * HD
                pieces.append(held_ref[g, :, start : start + HD].astype(f32))
    grad = jnp.concatenate(pieces, axis=1)
    out_ref[...] = grad
    total = jnp.sum(w_ref[...].astype(f32) * grad, axis=1, keepdims=True)
    dgain_ref[...] = row_of(total / column(gain_ref))


def finish(kernel, groups, info, w, gain, parts, shapes, name, after=(), carry=()):
    vmem = pl.BlockSpec(memory_space=pltpu.VMEM)
    return ordered(
        kernel, [info, w, gain, *parts], list(after), list(carry),
        [jax.ShapeDtypeStruct(shape, f32) for shape in shapes],
        [pl.BlockSpec(memory_space=pltpu.SMEM)] + [vmem] * (2 + groups),
        [vmem] * len(shapes), name,
        scratch=[pltpu.VMEM((groups,) + parts[0].shape, bf)],
    )


def body(
    tokens, lengths, attn_gain, qkv_weight, proj_weight, ffn_gain, in_weight, out_weight, out_grad
):
    rows = tokens.shape[1]
    groups = lax.axis_size("seq")
    shards = lax.axis_size("fsdp")
    heads = HEADS // groups
    shard = D // shards
    me = lax.axis_index("seq")

    def swap(array, j, axis="seq"):
        size = lax.axis_size(axis)
        return lax.ppermute(array, axis, [(i, i ^ j) for i in range(size)])

    def exchange(chunks):
        return [chunks[0]] + [swap(chunks[j], j) for j in range(1, groups)]

    def gather(array):
        return lax.all_gather(array, "fsdp", axis=0, tiled=True)

    place = jnp.stack([me]).astype(jnp.int32)
    x0 = tokens[0]
    across = swap(x0, 2)
    near = swap(x0, 1)
    attn_row = attn_gain[None, :]
    ffn_row = ffn_gain[None, :]
    own = own_columns(groups, heads, shards, place, qkv_weight, attn_row)
    own = lax.all_to_all(own, "fsdp", split_axis=0, concat_axis=0, tiled=True).reshape(D, -1)

    half = HD // 2
    frequency = rope_base ** (-(lax.iota(f32, half) * 2.0) / HD)
    starts = [(me ^ j) * rows for j in range(groups)]
    positions = jnp.concatenate([s + lax.iota(jnp.int32, rows) for s in starts]).astype(f32)
    angles = frequency[:, None] * positions[None, :]
    cos_rows, sin_rows, cos_t, sin_t = tables(jnp.cos(angles), jnp.sin(angles))

    def project(j, block, carried):
        info = jnp.stack([starts[j], lengths[0]]).astype(jnp.int32)
        return qkv_call(j, groups, heads, info, block, cos_rows, sin_rows, own, carried)

    diagonal = swap(across, 1)
    carried = project(2, across, None)
    carried = project(0, x0, carried)
    carried = project(1, near, carried)
    normed, k, v, qt, kt, vt = project(3, diagonal, carried)

    ff = in_weight.shape[1] // 2
    tall = out_weight.shape[0]
    packed = shards <= 8
    mine = gather(own_half(packed, place, in_weight, proj_weight, ffn_row, out_weight, [own, cos_t]))
    out_full = [] if packed else [gather(out_weight)]

    own = hold(own, [normed])
    own_near, own_across = swap(own, 1), swap(own, 2)

    kept = []
    chunks = []
    for h in range(heads):
        before = [kept[-1][2]] if kept else []
        if h == 1:
            before += [own_near, own_across]
        saved, mixed = attend(h, k, qt, vt, groups, before)
        kept.append(saved)
        if h > 0:
            early = [chunks[n] for n in range((h - 1) * groups, h * groups) if n % groups]
            extra = [mine] if h == heads - 2 else [own_across]
            _, carried = ordered(
                lambda: None, [], [saved[2]] + early, mixed[1:] + extra, [], [], [], "hold"
            )
            mixed = mixed[:1] + carried[:-1]
            if h == heads - 2:
                mine = carried[-1]
                other = swap(mine, 1)
            else:
                own_across = carried[-1]
                own_diagonal = swap(own_across, 1)
        chunks += exchange(mixed)

    dy = out_grad[0]
    d_mixed, (result, d_hidden, mixed_t, second, d_gate_up, inner, branch) = middle(
        groups, heads, shards, ff, place, x0, dy, mine, other, out_full, chunks
    )
    d_mixed = exchange(d_mixed)

    def to_owner(array):
        parts = array.reshape(shards, array.shape[0] // shards, -1)
        return lax.all_to_all(parts, "fsdp", split_axis=0, concat_axis=0, tiled=True)

    def from_peers(array):
        return [array] + [swap(array, j) for j in range(1, groups)]

    wide, tall_grad = weight_grads(place, second, d_gate_up, mixed_t, branch, inner, dy)
    _, carried = ordered(
        lambda: None, [], d_mixed[1:], wide[1:] + [tall_grad], [], [], [], "hold"
    )
    tall_grad = carried[-1]
    wide_all = exchange(wide[:1] + carried[:-1])
    tall_parts = to_owner(tall_grad)

    def back(h, grad_place, after):
        return attend_back(
            h, v, kt, qt, d_mixed, kept[h], cos_t, sin_t, normed, groups, grad_place, after
        )

    peers = [own, own_near, own_across, own_diagonal]
    sent_0, qkv_first = back(0, (512, 0, None), [tall_grad, own_diagonal])
    wide_sum, others = add_up(wide_all, [qkv_first, tall_parts], sent_0[1:])
    wide_parts = to_owner(wide_sum)
    received_0 = exchange(sent_0[:1] + others)

    sent_1, qkv_first = back(1, (512, 1, qkv_first), [wide_sum])
    both, carried = owned(wide_parts, tall_parts, received_0[1:], sent_1[1:] + [qkv_first])
    received_1 = exchange(sent_1[:1] + carried[:-1])
    both_far = [swap(both, j) for j in range(2, groups)]
    qkv_parts = to_owner(carried[-1])

    sent_2, qkv_second = back(2, (256, 0, None), [both])
    _, carried = ordered(
        lambda: None, [], received_1[1:] + both_far + [qkv_parts],
        sent_2[1:] + [qkv_second, both], [], [], [], "pass_on",
    )
    qkv_second, both = carried[-2:]
    received_2 = exchange(sent_2[:1] + carried[:-2])
    both_peers = [both, swap(both, 1)] + both_far
    (in_weight_grad, proj_weight_grad, ffn_gain_grad, out_weight_grad), carried = finish(
        functools.partial(finish_wide_kernel, groups),
        groups, place, in_weight, ffn_row, both_peers,
        ((shard, 2 * ff), (shard, D), (1, shard), (tall, D)), "finish_wide",
        carry=[qkv_second],
    )
    qkv_second_parts = to_owner(carried[0])
    base = last(
        groups, heads, (0, 1), x0, d_hidden, peers, received_0 + received_1, [carried[0]]
    )
    qkv_peers = from_peers(beside(qkv_parts, qkv_second_parts, [base] + received_2[1:]))
    tokens_grad = last(groups, heads, (2,), x0, base, peers, received_2, [])
    (qkv_weight_grad, attn_gain_grad), _ = finish(
        functools.partial(finish_qkv_kernel, groups, heads),
        groups, place, qkv_weight, attn_row, qkv_peers,
        ((shard, 3 * D), (1, shard)), "finish_qkv", [tokens_grad],
    )
    return (
        result[None],
        tokens_grad[None],
        attn_gain_grad[0],
        qkv_weight_grad,
        proj_weight_grad,
        ffn_gain_grad[0],
        in_weight_grad,
        out_weight_grad,
    )


def solution(mesh):
    in_specs = (
        P("fsdp", "seq", None),
        P("fsdp"),
        P("fsdp"),
        P("fsdp", None),
        P("fsdp", None),
        P("fsdp"),
        P("fsdp", None),
        P("fsdp", None),
        P("fsdp", "seq", None),
    )
    out_specs = (
        P("fsdp", "seq", None),
        P("fsdp", "seq", None),
        P("fsdp"),
        P("fsdp", None),
        P("fsdp", None),
        P("fsdp"),
        P("fsdp", None),
        P("fsdp", None),
    )
    return jax.shard_map(body, mesh=mesh, in_specs=in_specs, out_specs=out_specs, check_vma=False)
```

```python
import functools

import jax
import jax.numpy as jnp
from jax import lax
from jax.experimental import pallas as pl
from jax.experimental.pallas import tpu as pltpu
from jax.sharding import PartitionSpec as P

D = 768
HEADS = 12
HD = 64

epsilon = 1e-05
rope_base = 160000.0
masked_score = -1e30
LOG2E = 1.4426950408889634
LN2 = 0.6931471805599453

VMEM = 63 * 2**20
SMALL = pl.CostEstimate(flops=1024, bytes_accessed=1024, transcendentals=0)

bf = jnp.bfloat16
f32 = jnp.float32
NN = ((1,), (0,))
NT = ((1,), (1,))
TN = ((0,), (0,))


def dg(a, b, dims):
    return lax.dot_general(a, b, (dims, ((), ())), preferred_element_type=f32)


def unit_rows_of(x):
    centred = x - jnp.mean(x, axis=-1, keepdims=True)
    inverse = lax.rsqrt(jnp.mean(centred * centred, axis=-1, keepdims=True) + epsilon)
    return centred * inverse, inverse


def qkv_kernel(heads, info_ref, x_ref, cos_ref, sin_ref, w_ref, *refs):
    n_ref, k_ref, v_ref, qt_ref, kt_ref, vt_ref, g_ref = refs[-7:]
    rb = x_ref.shape[0]
    value_at = heads * 128

    @pl.when(pl.program_id(0) == 0)
    def _():
        last = w_ref[:, w_ref.shape[1] - 128 :].astype(f32).T
        g_ref[...] = last[HD : HD + 8]

    unit, _ = unit_rows_of(x_ref[...].astype(f32))
    normed = (unit * g_ref[:1]).astype(bf)
    n_ref[...] = normed
    lane = lax.broadcasted_iota(jnp.int32, (rb, 128), 1)
    row = lax.broadcasted_iota(jnp.int32, (rb, 128), 0)
    position = info_ref[0] + pl.program_id(0) * rb + row
    bias = jnp.where(position < info_ref[1], 0.0, masked_score)
    key_tail = jnp.where(lane == HD, bias, 0.0)
    value_tail = jnp.where(lane < HD + 2, -1.0, 0.0)
    head_lane = lane < HD
    lower = (lane & (HD - 1)) < HD // 2
    one_row = jnp.where(lax.broadcasted_iota(jnp.int32, (HD, rb), 0) == 0, 1.0, 0.0).astype(bf)
    y = dg(normed, w_ref[...], NN)
    for h in range(heads):
        t = y[:, h * 128 : (h + 1) * 128]
        turned = jnp.where(lower, pltpu.roll(t, 128 - HD // 2, 1), pltpu.roll(t, HD // 2, 1))
        t = t * cos_ref[...] + turned * sin_ref[...]
        k_ref[h] = jnp.where(head_lane, pltpu.roll(t, HD, 1), key_tail).astype(bf)
        t = t.T.astype(bf)
        qt_ref[h, :HD] = t[:HD]
        qt_ref[h, HD:] = one_row
        kt_ref[h] = t[HD:]
    for h in range(heads):
        at = value_at + h // 2 * 128
        t = y[:, at : at + 128]
        turned = t if h % 2 == 0 else pltpu.roll(t, HD, 1)
        v_ref[h] = jnp.where(head_lane, turned, value_tail).astype(bf)
        if h % 2 == 0:
            t_rows = t.T.astype(bf)
        vt_ref[h, :HD] = t_rows[:HD] if h % 2 == 0 else t_rows[HD:]
        vt_ref[h, HD:] = one_row[:16]


def qkv_call(block, blocks, heads, info, x, cos, sin, w, carried):
    rows = x.shape[0]
    S = rows * blocks
    rb = min(512, rows)
    steps = rows // rb
    width = w.shape[1]
    at = lambda i: block * steps + i
    outs = (
        jax.ShapeDtypeStruct((S, D), bf),
        jax.ShapeDtypeStruct((heads, S, 128), bf),
        jax.ShapeDtypeStruct((heads, S, 128), bf),
        jax.ShapeDtypeStruct((heads, 128, S), bf),
        jax.ShapeDtypeStruct((heads, HD, S), bf),
        jax.ShapeDtypeStruct((heads, 80, S), bf),
    )
    in_specs = [
        pl.BlockSpec(memory_space=pltpu.SMEM),
        pl.BlockSpec((rb, D), lambda i: (i, 0)),
        pl.BlockSpec((rb, 128), lambda i: (at(i), 0)),
        pl.BlockSpec((rb, 128), lambda i: (at(i), 0)),
        pl.BlockSpec((D, width), lambda i: (0, 0)),
    ]
    aliases = {}
    if carried is not None:
        first = len(in_specs)
        in_specs += [pl.BlockSpec(memory_space=pl.ANY)] * 6
        aliases = {first + n: n for n in range(6)}
    return pl.pallas_call(
        functools.partial(qkv_kernel, heads),
        grid=(steps,),
        out_shape=outs,
        in_specs=in_specs,
        out_specs=(
            pl.BlockSpec((rb, D), lambda i: (at(i), 0)),
            pl.BlockSpec((heads, rb, 128), lambda i: (0, at(i), 0)),
            pl.BlockSpec((heads, rb, 128), lambda i: (0, at(i), 0)),
            pl.BlockSpec((heads, 128, rb), lambda i: (0, 0, at(i))),
            pl.BlockSpec((heads, HD, rb), lambda i: (0, 0, at(i))),
            pl.BlockSpec((heads, 80, rb), lambda i: (0, 0, at(i))),
        ),
        scratch_shapes=[pltpu.VMEM((8, D), f32)],
        input_output_aliases=aliases,
        compiler_params=pltpu.CompilerParams(vmem_limit_bytes=VMEM),
        cost_estimate=SMALL,
        name="qkv",
    )(info, x, cos, sin, w, *(carried or ()))


def attend_kernel(kc, half, count, k_ref, qa_ref, qb_ref, v_ref, *refs):
    refs = refs[count:]
    pa_ref, pb_ref, oa_ref, ob_ref, la_ref, lb_ref = refs[:6]
    chunks = refs[6 : 6 + half]
    sa_ref, sb_ref, m_ref = refs[6 + half :]
    i = pl.program_id(0)
    rows = k_ref.shape[1]
    bq = qa_ref.shape[2]

    def stage(new, old):
        if new is not None:
            q_ref, s_new, new_slot = new
            q = q_ref[0]
            m = jnp.full((8, bq), -jnp.inf, f32)
        if old is not None:
            s_old, old_slot, p_ref, o_ref, l_ref, block = old
            top = jnp.max(m_ref[old_slot], axis=0, keepdims=True)
            acc = jnp.zeros((v_ref.shape[1], bq), f32)
        for c in range(rows // kc):
            at = slice(c * kc, (c + 1) * kc)
            if new is not None:
                s = dg(k_ref[0, at, :], q, NN)
                s_new[at, :] = s
                m = jnp.maximum(m, jnp.max(s.reshape(kc // 8, 8, bq), axis=0))
            if old is not None:
                p = jnp.exp2(s_old[at, :] - top).astype(bf)
                p_ref[0, at, :] = p
                acc = acc + dg(v_ref[0, :, at], p, NN)
        if new is not None:
            m_ref[new_slot] = m
        if old is not None:
            linv = 1.0 / acc[HD : HD + 1, :]
            o = acc[:HD, :] * linv
            o_ref[...] = o
            l_ref[0] = linv
            low = o.astype(bf)
            for j in range(half):

                @pl.when(block // 2 == j)
                def _():
                    chunks[j][:, old_slot * bq : (old_slot + 1) * bq] = low

    first = (qa_ref, sa_ref, 0)
    odd = (sb_ref, 1, pb_ref, ob_ref, lb_ref, 2 * i - 1)

    @pl.when(i == 0)
    def _():
        stage(first, None)

    @pl.when((i > 0) & (i < half))
    def _():
        stage(first, odd)

    @pl.when(i == half)
    def _():
        stage(None, odd)

    @pl.when(i < half)
    def _():
        stage((qb_ref, sb_ref, 1), (sa_ref, 0, pa_ref, oa_ref, la_ref, 2 * i))


def attend(h, k, qt, vt, groups, after, kc=256):
    S = k.shape[1]
    bq = S // groups // 2
    a = lambda i: jnp.minimum(i, groups - 1)
    b = lambda i: jnp.maximum(i - 1, 0)
    outs = pl.pallas_call(
        functools.partial(attend_kernel, kc, groups, len(after)),
        grid=(groups + 1,),
        out_shape=(jax.ShapeDtypeStruct((groups, S, bq), bf),) * 2
        + (jax.ShapeDtypeStruct((HD, S // 2), f32),) * 2
        + (jax.ShapeDtypeStruct((groups, 1, bq), f32),) * 2
        + (jax.ShapeDtypeStruct((HD, 2 * bq), bf),) * groups,
        in_specs=[
            pl.BlockSpec((1, S, 128), lambda i: (h, 0, 0)),
            pl.BlockSpec((1, 128, bq), lambda i: (h, 0, 2 * a(i))),
            pl.BlockSpec((1, 128, bq), lambda i: (h, 0, 2 * a(i) + 1)),
            pl.BlockSpec((1, 80, S), lambda i: (h, 0, 0)),
        ]
        + [pl.BlockSpec(memory_space=pl.ANY)] * len(after),
        out_specs=(
            pl.BlockSpec((1, S, bq), lambda i: (a(i), 0, 0)),
            pl.BlockSpec((1, S, bq), lambda i: (b(i), 0, 0)),
            pl.BlockSpec((HD, bq), lambda i: (0, a(i))),
            pl.BlockSpec((HD, bq), lambda i: (0, b(i))),
            pl.BlockSpec((1, 1, bq), lambda i: (a(i), 0, 0)),
            pl.BlockSpec((1, 1, bq), lambda i: (b(i), 0, 0)),
        )
        + (pl.BlockSpec((HD, 2 * bq), lambda i: (0, 0)),) * groups,
        scratch_shapes=[
            pltpu.VMEM((S, bq), f32),
            pltpu.VMEM((S, bq), f32),
            pltpu.VMEM((2, 8, bq), f32),
        ],
        compiler_params=pltpu.CompilerParams(vmem_limit_bytes=VMEM),
        cost_estimate=SMALL,
        name="attend",
    )(k, qt, qt, vt, *after)
    return outs[:6], list(outs[6:])


def attend_back_kernel(kc, groups, v_ref, kt_ref, q_ref, *refs):
    oa_ref, ob_ref, la_ref, lb_ref, pa_ref, pb_ref, cos_ref, sin_ref, n_ref = refs[:9]
    do_refs = refs[9 : 9 + groups]
    outs = refs[-5 - groups : -5]
    grad_ref, acc_ref, do_ref, held_ref, sem = refs[-5:]
    i = pl.program_id(0)
    rows = v_ref.shape[1]
    width = q_ref.shape[2]
    bq = width // 2
    fetch = pltpu.make_async_copy(n_ref, held_ref, sem)

    @pl.when(i == 0)
    def _():
        fetch.start()
        acc_ref[...] = jnp.zeros_like(acc_ref)

    for j in range(groups):

        @pl.when(i == j)
        def _():
            do_ref[...] = do_refs[j][...]

    zero = jnp.zeros((HD, bq), bf)
    r = lax.broadcasted_iota(jnp.int32, (16, bq), 0)
    sides = []
    for n, (o_ref, l_ref, p_ref) in enumerate(((oa_ref, la_ref, pa_ref), (ob_ref, lb_ref, pb_ref))):
        at = slice(n * bq, (n + 1) * bq)
        dop = (do_ref[:, at].astype(f32) * l_ref[0]).astype(bf)
        delta = jnp.sum(dop.astype(f32) * o_ref[...], axis=0, keepdims=True)
        high = delta.astype(bf).astype(f32)
        tail = jnp.where(r == 0, high, jnp.where(r == 1, delta - high, 0.0)).astype(bf)
        doe = jnp.concatenate([dop, tail, jnp.zeros((128 - HD - 16, bq), bf)], axis=0)
        right_v = jnp.concatenate([dop, zero], axis=0).T
        right_k = jnp.concatenate([zero, q_ref[0, :HD, at]], axis=0).T
        sides.append((p_ref, doe, jnp.concatenate([right_v, right_k], axis=0)))
    dq = [jnp.zeros((HD, bq), f32), jnp.zeros((HD, bq), f32)]
    for n, (p_ref, doe, right) in enumerate(sides):
        for c in range(rows // kc):
            at = slice(c * kc, (c + 1) * kc)
            p = p_ref[0, at, :]
            ds = p * dg(v_ref[0, at, :], doe, NN).astype(bf)
            acc_ref[at, :] = acc_ref[at, :] + dg(jnp.concatenate([p, ds], axis=1), right, NN)
            dq[n] = dq[n] + dg(kt_ref[0, :, at], ds, NN)
    dq = jnp.concatenate(dq, axis=1) * HD**-0.5
    turned = jnp.concatenate([dq[HD // 2 :], -dq[: HD // 2]], axis=0)
    here = pl.ds(pl.multiple_of(i * width, width), width)
    dq = (dq * cos_ref[:, here] + turned * sin_ref[:, here]).astype(bf)
    for j in range(groups):

        @pl.when(i == j)
        def _():
            outs[j][:HD] = dq

    @pl.when(i == groups - 1)
    def _():
        fetch.wait()
        grad = jnp.zeros((3 * HD, D), f32)
        for j in range(groups):
            at = slice(j * width, (j + 1) * width)
            t = acc_ref[at, :].T
            dk = t[HD:] * LN2
            turned_k = jnp.concatenate([dk[HD // 2 :], -dk[: HD // 2]], axis=0)
            dk = dk * cos_ref[:, at] + turned_k * sin_ref[:, at]
            outs[j][HD : 2 * HD] = dk.astype(bf)
            outs[j][2 * HD :] = t[:HD].astype(bf)
            grad = grad + dg(outs[j][...], held_ref[at, :], NN)
        grad_ref[:, : 3 * HD] = grad.T.astype(bf)
        grad_ref[:, 3 * HD :] = jnp.zeros((D, HD), bf)


def attend_back(h, v, kt, qt, do, kept, cos, sin, normed, groups, place, after, kc=256):
    S = v.shape[1]
    width = S // groups
    bq = width // 2
    pa, pb, oa, ob, la, lb = kept
    columns, column, earlier = place
    extra = list(after) if earlier is None else [earlier] + list(after)
    whole = lambda i: (0, 0)
    by_block = lambda i: (i, 0, 0)
    outs = pl.pallas_call(
        functools.partial(attend_back_kernel, kc, groups),
        grid=(groups,),
        out_shape=(jax.ShapeDtypeStruct((3 * HD, width), bf),) * groups
        + (jax.ShapeDtypeStruct((D, columns), bf),),
        in_specs=[
            pl.BlockSpec((1, S, 128), lambda i: (h, 0, 0)),
            pl.BlockSpec((1, HD, S), lambda i: (h, 0, 0)),
            pl.BlockSpec((1, 128, width), lambda i: (h, 0, i)),
            pl.BlockSpec((HD, bq), lambda i: (0, i)),
            pl.BlockSpec((HD, bq), lambda i: (0, i)),
            pl.BlockSpec((1, 1, bq), by_block),
            pl.BlockSpec((1, 1, bq), by_block),
            pl.BlockSpec((1, S, bq), by_block),
            pl.BlockSpec((1, S, bq), by_block),
            pl.BlockSpec((HD, S), whole),
            pl.BlockSpec((HD, S), whole),
            pl.BlockSpec(memory_space=pl.ANY),
        ]
        + [pl.BlockSpec((HD, width), lambda i: (h, 0))] * groups
        + [pl.BlockSpec(memory_space=pl.ANY)] * len(extra),
        out_specs=(pl.BlockSpec((3 * HD, width), whole),) * groups
        + (pl.BlockSpec((D, 256), lambda i: (0, column)),),
        scratch_shapes=[
            pltpu.VMEM((S, 128), f32),
            pltpu.VMEM((HD, width), bf),
            pltpu.VMEM((S, D), bf),
            pltpu.SemaphoreType.DMA,
        ],
        input_output_aliases={} if earlier is None else {12 + groups: groups},
        compiler_params=pltpu.CompilerParams(vmem_limit_bytes=VMEM),
        cost_estimate=SMALL,
        name="attend_back",
    )(v, kt, qt, oa, ob, la, lb, pa, pb, cos, sin, normed, *do, *extra)
    return list(outs[:groups]), outs[groups]


def normalize_back(gradient, unit_rows, inverse, gain_row):
    scaled = gradient * gain_row
    return inverse * (
        scaled
        - jnp.mean(scaled, axis=-1, keepdims=True)
        - unit_rows * jnp.mean(scaled * unit_rows, axis=-1, keepdims=True)
    )


def column(row_ref):
    row = row_ref[...].astype(f32)
    return jnp.broadcast_to(row, (8, row.shape[1])).T[:, :1]


def row_of(total):
    return jnp.broadcast_to(total, (total.shape[0], 128)).T[:1]


def half_kernel(packed, info_ref, in_ref, proj_ref, gain_ref, out_w_ref, *refs):
    half_ref = refs[-1]
    side = info_ref[0] & 1

    @pl.when(side == 0)
    def _():
        half_ref[...] = in_ref[...]

    @pl.when(side == 1)
    def _():
        short = in_ref.shape[0]
        half_ref[:, :D] = proj_ref[...]
        gain = jnp.broadcast_to(column(gain_ref), (short, 128)).astype(bf)
        half_ref[:, D : D + 128] = gain
        if packed:
            one, two, three = D + 128, 2 * D + 128, 2 * D + D // 2 + 128
            tall = out_w_ref.shape[0]
            half_ref[:, one:two] = out_w_ref[:short, :]
            half_ref[: tall - short, two:three] = out_w_ref[short:, : D // 2]
            half_ref[tall - short :, two:three] = out_w_ref[short:, D // 2 :]


def own_half(packed, info, in_w, proj_w, gain, out_w, after):
    vmem = pl.BlockSpec(memory_space=pltpu.VMEM)
    return pl.pallas_call(
        functools.partial(half_kernel, packed),
        out_shape=jax.ShapeDtypeStruct(in_w.shape, bf),
        in_specs=[pl.BlockSpec(memory_space=pltpu.SMEM)]
        + [vmem] * 4
        + [pl.BlockSpec(memory_space=pl.ANY)] * len(after),
        out_specs=vmem,
        compiler_params=pltpu.CompilerParams(vmem_limit_bytes=VMEM),
        cost_estimate=SMALL,
        name="own_half",
    )(info, in_w, proj_w, gain, out_w, *after)


def hold(array, after):
    def kernel(*refs):
        pass

    return pl.pallas_call(
        kernel,
        out_shape=jax.ShapeDtypeStruct(array.shape, array.dtype),
        in_specs=[pl.BlockSpec(memory_space=pl.ANY)] * (1 + len(after)),
        out_specs=pl.BlockSpec(memory_space=pl.ANY),
        input_output_aliases={0: 0},
        compiler_params=pltpu.CompilerParams(vmem_limit_bytes=VMEM),
        cost_estimate=SMALL,
        name="hold",
    )(array, *after)


def middle_kernel(groups, heads, ff, shards, info_ref, x_ref, dy_ref, mine_ref, other_ref, *refs):
    count = groups * heads
    given = len(refs) - count - groups - 13
    out_given = refs[:given]
    chunks = refs[given : given + count]
    d_chunks = refs[given + count : given + count + groups]
    (result_ref, dh_ref, mixed_ref, second_ref, dgu_ref, inner_ref, branch_ref,
     g_ref, t_ref, out_w_ref, w_ref, rest_ref, sems) = refs[given + count + groups :]
    width = heads * HD
    me = info_ref[0]

    @pl.when(pl.program_id(0) == 0)
    def _():
        def fetch(first, second):
            copies = [
                pltpu.make_async_copy(first, w_ref, sems.at[0]),
                pltpu.make_async_copy(second, rest_ref, sems.at[1]),
            ]
            for copy in copies:
                copy.start()
            for copy in copies:
                copy.wait()

        @pl.when((me & 1) == 0)
        def _():
            fetch(mine_ref, other_ref)

        @pl.when((me & 1) == 1)
        def _():
            fetch(other_ref, mine_ref)

        g_ref[...] = rest_ref[:, D : D + 128].astype(f32).T[:8]
        if given:
            out_w_ref[...] = out_given[0][...]
        else:
            tall, short = ff // shards, D // shards
            rest = tall - short
            one, two, three = D + 128, 2 * D + 128, 2 * D + D // 2 + 128
            for f in range(shards):
                src = slice(f * short, (f + 1) * short)
                out_w_ref[f * tall : f * tall + short, :] = rest_ref[src, one:two]
                dst = slice(f * tall + short, (f + 1) * tall)
                src = slice(f * short, f * short + rest)
                out_w_ref[dst, : D // 2] = rest_ref[src, two:three]
                src = slice(f * short + rest, f * short + 2 * rest)
                out_w_ref[dst, D // 2 :] = rest_ref[src, two:three]

    for h in range(heads):
        for j in range(groups):
            start = pl.multiple_of((me ^ j) * width + h * HD, HD)
            mixed_ref[pl.ds(start, HD), :] = chunks[h * groups + j][...]
    gain = g_ref[:1]
    proj = rest_ref[:, :D]
    hidden = x_ref[...].astype(f32) + dg(mixed_ref[...], proj, TN)
    unit, inverse = unit_rows_of(hidden)
    second = (unit * gain).astype(bf)
    second_ref[...] = second
    dy = dy_ref[...]
    result = hidden
    d_second = jnp.zeros_like(hidden)
    step = 384
    for c in range(ff // step):
        a = slice(c * step, (c + 1) * step)
        b = slice(ff + c * step, ff + (c + 1) * step)
        gate = dg(second, w_ref[:, a], NN)
        up = dg(second, w_ref[:, b], NN)
        d_inner = dg(dy, out_w_ref[a, :], NT)
        bell = 0.5 + 0.5 * lax.erf(gate * 0.7071067811865476)
        gelu = gate * bell
        inner = (gelu * up).astype(bf)
        inner_ref[:, a] = inner
        result = result + dg(inner, out_w_ref[a, :], NN)
        slope = bell + gate * (jnp.exp(-0.5 * gate * gate) * 0.3989422804014327)
        d_gate = (d_inner * up * slope).astype(bf)
        d_up = (d_inner * gelu).astype(bf)
        dgu_ref[:, a] = d_gate
        dgu_ref[:, b] = d_up
        d_second = d_second + dg(d_gate, w_ref[:, a], NT) + dg(d_up, w_ref[:, b], NT)
    result_ref[...] = result.astype(bf)
    d_hidden = dy.astype(f32) + normalize_back(d_second, unit, inverse, gain)
    dh_ref[...] = d_hidden
    branch = d_hidden.astype(bf)
    branch_ref[...] = branch
    t_ref[...] = dg(proj, branch, NT).astype(bf)
    for j in range(groups):
        start = pl.multiple_of((me ^ j) * width, HD)
        d_chunks[j][...] = t_ref[pl.ds(start, width), :]


def middle(groups, heads, shards, ff, info, x, dy, mine, other, out_w, chunks):
    rows = x.shape[0]
    rb = min(256, rows)
    by_row = lambda i: (i, 0)
    by_column = lambda i: (0, i)
    whole = lambda i: (0, 0)
    outs = pl.pallas_call(
        functools.partial(middle_kernel, groups, heads, ff, shards),
        grid=(rows // rb,),
        out_shape=(jax.ShapeDtypeStruct((heads * HD, rows), bf),) * groups
        + (
            jax.ShapeDtypeStruct((rows, D), bf),
            jax.ShapeDtypeStruct((rows, D), f32),
            jax.ShapeDtypeStruct((D, rows), bf),
            jax.ShapeDtypeStruct((rows, D), bf),
            jax.ShapeDtypeStruct((rows, 2 * ff), bf),
            jax.ShapeDtypeStruct((rows, ff), bf),
            jax.ShapeDtypeStruct((rows, D), bf),
        ),
        in_specs=[
            pl.BlockSpec(memory_space=pltpu.SMEM),
            pl.BlockSpec((rb, D), by_row),
            pl.BlockSpec((rb, D), by_row),
            pl.BlockSpec(memory_space=pl.ANY),
            pl.BlockSpec(memory_space=pl.ANY),
        ]
        + [pl.BlockSpec(w.shape, whole, pipeline_mode=pl.Buffered(1)) for w in out_w]
        + [pl.BlockSpec((HD, rb), by_column)] * (groups * heads),
        out_specs=(pl.BlockSpec((heads * HD, rb), by_column),) * groups
        + (
            pl.BlockSpec((rb, D), by_row),
            pl.BlockSpec((rb, D), by_row),
            pl.BlockSpec((D, rb), by_column),
            pl.BlockSpec((rb, D), by_row),
            pl.BlockSpec((rb, 2 * ff), by_row),
            pl.BlockSpec((rb, ff), by_row),
            pl.BlockSpec((rb, D), by_row),
        ),
        scratch_shapes=[
            pltpu.VMEM((8, D), f32),
            pltpu.VMEM((D, rb), bf),
            pltpu.VMEM((ff, D), bf),
            pltpu.VMEM(mine.shape, bf),
            pltpu.VMEM(mine.shape, bf),
            pltpu.SemaphoreType.DMA((2,)),
        ],
        compiler_params=pltpu.CompilerParams(vmem_limit_bytes=VMEM),
        cost_estimate=SMALL,
        name="middle",
    )(info, x, dy, mine, other, *out_w, *chunks)
    return list(outs[:groups]), outs[groups:]


def last_kernel(groups, chosen, x_ref, base_ref, gain_ref, *refs):
    count = groups * len(chosen)
    chunks = refs[:count]
    pairs = refs[count : 2 * count]
    value_refs = refs[2 * count : 3 * count]
    out_ref, dp_ref, wh_ref, g_ref = refs[-4:]
    both = groups * 2 * HD

    @pl.when(pl.program_id(0) == 0)
    def _():
        g_ref[...] = gain_ref[...].astype(f32).T[HD : HD + 8]
        for n, h in enumerate(chosen):
            side = (h & 1) * HD
            pieces = [ref[...] for ref in pairs[n * groups : (n + 1) * groups]]
            pieces += [ref[:, side : side + HD] for ref in value_refs[n * groups : (n + 1) * groups]]
            wh_ref[:, n * D : (n + 1) * D] = jnp.concatenate(pieces, axis=1)

    for n in range(len(chosen)):
        for j in range(groups):
            chunk = chunks[n * groups + j]
            start = n * D + j * 2 * HD
            dp_ref[start : start + 2 * HD, :] = chunk[: 2 * HD, :]
            start = n * D + both + j * HD
            dp_ref[start : start + HD, :] = chunk[2 * HD :, :]
    d_normed = dg(wh_ref[...], dp_ref[...], NN).T
    unit, inverse = unit_rows_of(x_ref[...].astype(f32))
    out_ref[...] = base_ref[...] + normalize_back(d_normed, unit, inverse, g_ref[:1])


def last(groups, heads, chosen, x, base, peers, chunks, after):
    rows = chunks[0].shape[1]
    rb = min(256, rows)
    by_row = lambda i: (i, 0)

    def tile(n):
        return pl.BlockSpec((D, 128), lambda i: (0, n), pipeline_mode=pl.Buffered(1))

    pairs = [tile(h) for h in chosen for _ in peers]
    value_tiles = [tile(heads + h // 2) for h in chosen for _ in peers]
    return pl.pallas_call(
        functools.partial(last_kernel, groups, chosen),
        grid=(rows // rb,),
        out_shape=jax.ShapeDtypeStruct((rows, D), f32),
        in_specs=[
            pl.BlockSpec((rb, D), by_row),
            pl.BlockSpec((rb, D), by_row),
            tile(peers[0].shape[1] // 128 - 1),
        ]
        + [pl.BlockSpec((3 * HD, rb), lambda i: (0, i))] * len(chunks)
        + pairs
        + value_tiles
        + [pl.BlockSpec(memory_space=pl.ANY)] * len(after),
        out_specs=pl.BlockSpec((rb, D), by_row),
        scratch_shapes=[
            pltpu.VMEM((len(chosen) * D, rb), bf),
            pltpu.VMEM((D, len(chosen) * D), bf),
            pltpu.VMEM((8, D), f32),
        ],
        compiler_params=pltpu.CompilerParams(vmem_limit_bytes=VMEM),
        cost_estimate=SMALL,
        name="last",
    )(x, base, peers[0], *chunks, *(list(peers) * (2 * len(chosen))), *after)


def own_kernel(groups, heads, info_ref, w_ref, gain_ref, out_ref):
    for g in range(groups):

        @pl.when(info_ref[0] == g)
        def _():
            def piece(t, h):
                start = t * D + (g * heads + h) * HD
                return w_ref[:, start : start + HD]

            pieces = []
            for h in range(heads):
                pieces += [piece(0, h), piece(1, h)]
            pieces += [piece(2, h) for h in range(heads)] + [column(gain_ref).astype(bf)]
            missing = out_ref.shape[2] - 3 * heads * HD - 1
            pieces.append(jnp.zeros((w_ref.shape[0], missing), bf))
            own = jnp.concatenate(pieces, axis=1)
            for f in range(out_ref.shape[0]):
                out_ref[f] = own


def own_columns(groups, heads, shards, info, w, gain):
    width = (3 * heads * HD + 128) // 128 * 128
    return pl.pallas_call(
        functools.partial(own_kernel, groups, heads),
        out_shape=jax.ShapeDtypeStruct((shards, w.shape[0], width), bf),
        in_specs=[
            pl.BlockSpec(memory_space=pltpu.SMEM),
            pl.BlockSpec(memory_space=pltpu.VMEM),
            pl.BlockSpec(memory_space=pltpu.VMEM),
        ],
        out_specs=pl.BlockSpec(memory_space=pltpu.VMEM),
        compiler_params=pltpu.CompilerParams(vmem_limit_bytes=VMEM),
        cost_estimate=SMALL,
        name="own_columns",
    )(info, w, gain)


def tables_kernel(cos_ref, sin_ref, cos_rows_ref, sin_rows_ref, cos_t_ref, sin_t_ref):
    c, s = cos_ref[...], sin_ref[...]
    cos_t_ref[...] = jnp.concatenate([c, c], axis=0)
    sin_t_ref[...] = jnp.concatenate([s, s], axis=0)
    scale = HD**-0.5 * LOG2E
    cos_rows_ref[...] = jnp.concatenate([c * scale, c * scale, c, c], axis=0).T
    sin_rows_ref[...] = jnp.concatenate([s * -scale, s * scale, -s, s], axis=0).T


def tables(cosine, sine):
    half, S = cosine.shape
    rb = min(1024, S)
    return pl.pallas_call(
        tables_kernel,
        grid=(S // rb,),
        out_shape=(jax.ShapeDtypeStruct((S, 4 * half), f32),) * 2
        + (jax.ShapeDtypeStruct((2 * half, S), f32),) * 2,
        in_specs=[pl.BlockSpec((half, rb), lambda i: (0, i))] * 2,
        out_specs=(pl.BlockSpec((rb, 4 * half), lambda i: (i, 0)),) * 2
        + (pl.BlockSpec((2 * half, rb), lambda i: (0, i)),) * 2,
        compiler_params=pltpu.CompilerParams(vmem_limit_bytes=VMEM),
        cost_estimate=SMALL,
        name="tables",
    )(cosine, sine)


def grads_kernel(place_ref, second_ref, dgu_ref, mixed_ref, branch_ref, inner_ref, dy_ref, *refs):
    outs, tall_ref, held_ref = refs[:-2], refs[-2], refs[-1]
    i = pl.program_id(0)
    group = i ^ place_ref[0]
    end = pl.num_programs(0) - 1

    @pl.when(group < end)
    def _():
        held_ref[...] = dg(second_ref[...], dgu_ref[...], TN).astype(bf)

    @pl.when(group == end)
    def _():
        held_ref[...] = dg(mixed_ref[...], branch_ref[...], NN).astype(bf)

    @pl.when(i < end)
    def _():
        tall_ref[...] = dg(inner_ref[...], dy_ref[...], TN).astype(bf)

    for j in range(len(outs)):

        @pl.when(i == j)
        def _():
            outs[j][...] = held_ref[...]


def weight_grads(place, second, d_gate_up, mixed_t, branch, inner, dy):
    rows = second.shape[0]
    ff = inner.shape[1]
    steps = d_gate_up.shape[1] // D
    whole = lambda i, p: (0, 0)
    part = lambda i, p: (0, jnp.minimum(i, steps - 1))
    outs = pl.pallas_call(
        grads_kernel,
        grid_spec=pltpu.PrefetchScalarGridSpec(
            num_scalar_prefetch=1,
            grid=(steps + 1,),
            in_specs=[
                pl.BlockSpec((rows, D), whole),
                pl.BlockSpec((rows, D), lambda i, p: (0, jnp.minimum(i ^ p[0], steps - 1))),
                pl.BlockSpec((D, rows), whole),
                pl.BlockSpec((rows, D), whole),
                pl.BlockSpec((rows, ff // steps), part),
                pl.BlockSpec((rows, D), whole),
            ],
            out_specs=(pl.BlockSpec((D, D), whole),) * (steps + 1)
            + (pl.BlockSpec((ff // steps, D), lambda i, p: (jnp.minimum(i, steps - 1), 0)),),
            scratch_shapes=[pltpu.VMEM((D, D), bf)],
        ),
        out_shape=(jax.ShapeDtypeStruct((D, D), bf),) * (steps + 1)
        + (jax.ShapeDtypeStruct((ff, D), bf),),
        compiler_params=pltpu.CompilerParams(vmem_limit_bytes=VMEM),
        cost_estimate=SMALL,
        name="weight_grads",
    )(place, second, d_gate_up, mixed_t, branch, inner, dy)
    return list(outs[:-1]), outs[-1]


def ordered(
    kernel, arrays, after, carry, out_shape, in_specs, out_specs, name, grid=(), scratch=()
):
    first = len(arrays) + len(after)
    own = len(out_shape)
    anywhere = pl.BlockSpec(memory_space=pl.ANY)

    def call(*refs):
        outs = refs[first + len(carry) :]
        kernel(*refs[: len(arrays)], *outs[:own], *outs[own + len(carry) :])

    outs = pl.pallas_call(
        call,
        grid=grid,
        out_shape=tuple(out_shape) + tuple(jax.ShapeDtypeStruct(a.shape, a.dtype) for a in carry),
        in_specs=list(in_specs) + [anywhere] * (len(after) + len(carry)),
        out_specs=tuple(out_specs) + (anywhere,) * len(carry),
        scratch_shapes=list(scratch),
        input_output_aliases={first + n: own + n for n in range(len(carry))},
        compiler_params=pltpu.CompilerParams(vmem_limit_bytes=VMEM),
        cost_estimate=SMALL,
        name=name,
    )(*arrays, *after, *carry)
    return list(outs[:own]), list(outs[own:])


def add_kernel(*refs):
    total = refs[0][...].astype(f32)
    for ref in refs[1:-1]:
        total = total + ref[...].astype(f32)
    refs[-1][...] = total.astype(bf)


def add_up(arrays, after, carry):
    rows, columns = arrays[0].shape
    rb = 256
    spec = pl.BlockSpec((rb, columns), lambda i: (i, 0))
    (total,), carried = ordered(
        add_kernel, arrays, after, carry, [jax.ShapeDtypeStruct((rows, columns), bf)],
        [spec] * len(arrays), [spec], "add_up", grid=(rows // rb,),
    )
    return total, carried


def up16(n):
    return -(-n // 16) * 16


def beside_kernel(first_ref, second_ref, *refs):
    out_ref = refs[-1]
    start = 0
    for ref in (first_ref, second_ref):
        total = ref[0].astype(f32)
        for f in range(1, ref.shape[0]):
            total = total + ref[f].astype(f32)
        out_ref[:, start : start + ref.shape[2]] = total.astype(bf)
        start += ref.shape[2]


def beside(first, second, after):
    vmem = pl.BlockSpec(memory_space=pltpu.VMEM)
    return pl.pallas_call(
        beside_kernel,
        out_shape=jax.ShapeDtypeStruct((first.shape[1], first.shape[2] + second.shape[2]), bf),
        in_specs=[vmem, vmem] + [pl.BlockSpec(memory_space=pl.ANY)] * len(after),
        out_specs=vmem,
        compiler_params=pltpu.CompilerParams(vmem_limit_bytes=VMEM),
        cost_estimate=SMALL,
        name="beside",
    )(first, second, *after)


def owned_kernel(wide_ref, tall_ref, *refs):
    out_ref = refs[-1]
    start = 0
    for ref in (wide_ref, tall_ref):
        total = ref[0].astype(f32)
        for f in range(1, ref.shape[0]):
            total = total + ref[f].astype(f32)
        out_ref[start : start + ref.shape[1], :] = total.astype(bf)
        start += up16(ref.shape[1])


def owned(wide, tall, after, carry):
    vmem = pl.BlockSpec(memory_space=pltpu.VMEM)
    shape = (up16(wide.shape[1]) + up16(tall.shape[1]), D)
    (total,), carried = ordered(
        owned_kernel, [wide, tall], after, carry, [jax.ShapeDtypeStruct(shape, bf)],
        [vmem] * 2, [vmem], "owned",
    )
    return total, carried


def finish_wide_kernel(groups, info_ref, w_ref, gain_ref, *refs):
    in_ref, proj_ref, dgain_ref, out_ref, held_ref = refs[groups:]
    shard = w_ref.shape[0]
    start = up16(shard)
    tall = 0.0
    for j in range(groups):
        held_ref[info_ref[0] ^ j] = refs[j][...]
        tall = tall + refs[j][start : start + out_ref.shape[0], :].astype(f32)
    out_ref[...] = tall
    total = 0.0
    for g in range(groups - 1):
        at = slice(g * D, (g + 1) * D)
        grad = held_ref[g, :shard, :].astype(f32)
        in_ref[:, at] = grad
        total = total + jnp.sum(w_ref[:, at].astype(f32) * grad, axis=1, keepdims=True)
    proj_ref[...] = held_ref[groups - 1, :shard, :].astype(f32)
    dgain_ref[...] = row_of(total / column(gain_ref))


def finish_qkv_kernel(groups, heads, info_ref, w_ref, gain_ref, *refs):
    out_ref, dgain_ref, held_ref = refs[groups : groups + 3]
    for j in range(groups):
        held_ref[info_ref[0] ^ j] = refs[j][...]
    pieces = []
    for t in range(3):
        for g in range(groups):
            for h in range(heads):
                start = h * 256 + t * HD
                pieces.append(held_ref[g, :, start : start + HD].astype(f32))
    grad = jnp.concatenate(pieces, axis=1)
    out_ref[...] = grad
    total = jnp.sum(w_ref[...].astype(f32) * grad, axis=1, keepdims=True)
    dgain_ref[...] = row_of(total / column(gain_ref))


def finish(kernel, groups, info, w, gain, parts, shapes, name, after=(), carry=()):
    vmem = pl.BlockSpec(memory_space=pltpu.VMEM)
    return ordered(
        kernel, [info, w, gain, *parts], list(after), list(carry),
        [jax.ShapeDtypeStruct(shape, f32) for shape in shapes],
        [pl.BlockSpec(memory_space=pltpu.SMEM)] + [vmem] * (2 + groups),
        [vmem] * len(shapes), name,
        scratch=[pltpu.VMEM((groups,) + parts[0].shape, bf)],
    )


def body(
    tokens, lengths, attn_gain, qkv_weight, proj_weight, ffn_gain, in_weight, out_weight, out_grad
):
    rows = tokens.shape[1]
    groups = lax.axis_size("seq")
    shards = lax.axis_size("fsdp")
    heads = HEADS // groups
    shard = D // shards
    me = lax.axis_index("seq")

    def swap(array, j, axis="seq"):
        size = lax.axis_size(axis)
        return lax.ppermute(array, axis, [(i, i ^ j) for i in range(size)])

    def exchange(chunks):
        return [chunks[0]] + [swap(chunks[j], j) for j in range(1, groups)]

    def gather(array):
        return lax.all_gather(array, "fsdp", axis=0, tiled=True)

    place = jnp.stack([me]).astype(jnp.int32)
    x0 = tokens[0]
    across = swap(x0, 2)
    near = swap(x0, 1)
    attn_row = attn_gain[None, :]
    ffn_row = ffn_gain[None, :]
    own = own_columns(groups, heads, shards, place, qkv_weight, attn_row)
    own = lax.all_to_all(own, "fsdp", split_axis=0, concat_axis=0, tiled=True).reshape(D, -1)

    half = HD // 2
    frequency = rope_base ** (-(lax.iota(f32, half) * 2.0) / HD)
    starts = [(me ^ j) * rows for j in range(groups)]
    positions = jnp.concatenate([s + lax.iota(jnp.int32, rows) for s in starts]).astype(f32)
    angles = frequency[:, None] * positions[None, :]
    cos_rows, sin_rows, cos_t, sin_t = tables(jnp.cos(angles), jnp.sin(angles))

    def project(j, block, carried):
        info = jnp.stack([starts[j], lengths[0]]).astype(jnp.int32)
        return qkv_call(j, groups, heads, info, block, cos_rows, sin_rows, own, carried)

    diagonal = swap(across, 1)
    carried = project(2, across, None)
    carried = project(0, x0, carried)
    carried = project(1, near, carried)
    normed, k, v, qt, kt, vt = project(3, diagonal, carried)

    ff = in_weight.shape[1] // 2
    tall = out_weight.shape[0]
    packed = shards <= 8
    mine = gather(own_half(packed, place, in_weight, proj_weight, ffn_row, out_weight, [own, cos_t]))
    out_full = [] if packed else [gather(out_weight)]

    own = hold(own, [normed])
    own_near, own_across = swap(own, 1), swap(own, 2)

    kept = []
    chunks = []
    for h in range(heads):
        before = [kept[-1][2]] if kept else []
        if h == 1:
            before += [own_near, own_across]
        saved, mixed = attend(h, k, qt, vt, groups, before)
        kept.append(saved)
        if h > 0:
            early = [chunks[n] for n in range((h - 1) * groups, h * groups) if n % groups]
            extra = [mine] if h == heads - 2 else [own_across]
            _, carried = ordered(
                lambda: None, [], [saved[2]] + early, mixed[1:] + extra, [], [], [], "hold"
            )
            mixed = mixed[:1] + carried[:-1]
            if h == heads - 2:
                mine = carried[-1]
                other = swap(mine, 1)
            else:
                own_across = carried[-1]
                own_diagonal = swap(own_across, 1)
        chunks += exchange(mixed)

    dy = out_grad[0]
    d_mixed, (result, d_hidden, mixed_t, second, d_gate_up, inner, branch) = middle(
        groups, heads, shards, ff, place, x0, dy, mine, other, out_full, chunks
    )
    d_mixed = exchange(d_mixed)

    def to_owner(array):
        parts = array.reshape(shards, array.shape[0] // shards, -1)
        return lax.all_to_all(parts, "fsdp", split_axis=0, concat_axis=0, tiled=True)

    def from_peers(array):
        return [array] + [swap(array, j) for j in range(1, groups)]

    wide, tall_grad = weight_grads(place, second, d_gate_up, mixed_t, branch, inner, dy)
    _, carried = ordered(
        lambda: None, [], d_mixed[1:], wide[1:] + [tall_grad], [], [], [], "hold"
    )
    tall_grad = carried[-1]
    wide_all = exchange(wide[:1] + carried[:-1])
    tall_parts = to_owner(tall_grad)

    def back(h, grad_place, after):
        return attend_back(
            h, v, kt, qt, d_mixed, kept[h], cos_t, sin_t, normed, groups, grad_place, after
        )

    peers = [own, own_near, own_across, own_diagonal]
    sent_0, qkv_first = back(0, (512, 0, None), [tall_grad, own_diagonal])
    wide_sum, others = add_up(wide_all, [qkv_first, tall_parts], sent_0[1:])
    wide_parts = to_owner(wide_sum)
    received_0 = exchange(sent_0[:1] + others)

    sent_1, qkv_first = back(1, (512, 1, qkv_first), [wide_sum])
    both, carried = owned(wide_parts, tall_parts, received_0[1:], sent_1[1:] + [qkv_first])
    received_1 = exchange(sent_1[:1] + carried[:-1])
    both_far = [swap(both, j) for j in range(2, groups)]
    qkv_parts = to_owner(carried[-1])

    sent_2, qkv_second = back(2, (256, 0, None), [both])
    _, carried = ordered(
        lambda: None, [], received_1[1:] + both_far + [qkv_parts],
        sent_2[1:] + [qkv_second, both], [], [], [], "pass_on",
    )
    qkv_second, both = carried[-2:]
    received_2 = exchange(sent_2[:1] + carried[:-2])
    both_peers = [both, swap(both, 1)] + both_far
    (in_weight_grad, proj_weight_grad, ffn_gain_grad, out_weight_grad), carried = finish(
        functools.partial(finish_wide_kernel, groups),
        groups, place, in_weight, ffn_row, both_peers,
        ((shard, 2 * ff), (shard, D), (1, shard), (tall, D)), "finish_wide",
        carry=[qkv_second],
    )
    qkv_second_parts = to_owner(carried[0])
    base = last(
        groups, heads, (0, 1), x0, d_hidden, peers, received_0 + received_1, [carried[0]]
    )
    qkv_peers = from_peers(beside(qkv_parts, qkv_second_parts, [base] + received_2[1:]))
    tokens_grad = last(groups, heads, (2,), x0, base, peers, received_2, [])
    (qkv_weight_grad, attn_gain_grad), _ = finish(
        functools.partial(finish_qkv_kernel, groups, heads),
        groups, place, qkv_weight, attn_row, qkv_peers,
        ((shard, 3 * D), (1, shard)), "finish_qkv", [tokens_grad],
    )
    return (
        result[None],
        tokens_grad[None],
        attn_gain_grad[0],
        qkv_weight_grad,
        proj_weight_grad,
        ffn_gain_grad[0],
        in_weight_grad,
        out_weight_grad,
    )


def solution(mesh):
    in_specs = (
        P("fsdp", "seq", None),
        P("fsdp"),
        P("fsdp"),
        P("fsdp", None),
        P("fsdp", None),
        P("fsdp"),
        P("fsdp", None),
        P("fsdp", None),
        P("fsdp", "seq", None),
    )
    out_specs = (
        P("fsdp", "seq", None),
        P("fsdp", "seq", None),
        P("fsdp"),
        P("fsdp", None),
        P("fsdp", None),
        P("fsdp"),
        P("fsdp", None),
        P("fsdp", None),
    )
    return jax.shard_map(body, mesh=mesh, in_specs=in_specs, out_specs=out_specs, check_vma=False)
```

```python
import functools

import jax
import jax.numpy as jnp
from jax import lax
from jax.experimental import pallas as pl
from jax.experimental.pallas import tpu as pltpu
from jax.sharding import PartitionSpec as P

D = 768
HEADS = 12
HD = 64

epsilon = 1e-05
rope_base = 160000.0
masked_score = -1e30
LOG2E = 1.4426950408889634
LN2 = 0.6931471805599453

VMEM = 63 * 2**20

bf = jnp.bfloat16
f32 = jnp.float32
NN = ((1,), (0,))
NT = ((1,), (1,))
TN = ((0,), (0,))


def dg(a, b, dims):
    return lax.dot_general(a, b, (dims, ((), ())), preferred_element_type=f32)


def unit_rows_of(x):
    centred = x - jnp.mean(x, axis=-1, keepdims=True)
    inverse = lax.rsqrt(jnp.mean(centred * centred, axis=-1, keepdims=True) + epsilon)
    return centred * inverse, inverse


def qkv_kernel(heads, info_ref, x_ref, cos_ref, sin_ref, w_ref, *refs):
    n_ref, k_ref, v_ref, qt_ref, kt_ref, vt_ref, g_ref = refs[-7:]
    rb = x_ref.shape[0]
    value_at = heads * 128

    @pl.when(pl.program_id(0) == 0)
    def _():
        last = w_ref[:, w_ref.shape[1] - 128 :].astype(f32).T
        g_ref[...] = last[HD : HD + 8]

    unit, _ = unit_rows_of(x_ref[...].astype(f32))
    normed = (unit * g_ref[:1]).astype(bf)
    n_ref[...] = normed
    lane = lax.broadcasted_iota(jnp.int32, (rb, 128), 1)
    row = lax.broadcasted_iota(jnp.int32, (rb, 128), 0)
    position = info_ref[0] + pl.program_id(0) * rb + row
    bias = jnp.where(position < info_ref[1], 0.0, masked_score)
    key_tail = jnp.where(lane == HD, bias, 0.0)
    value_tail = jnp.where(lane < HD + 2, -1.0, 0.0)
    head_lane = lane < HD
    lower = (lane & (HD - 1)) < HD // 2
    one_row = jnp.where(lax.broadcasted_iota(jnp.int32, (HD, rb), 0) == 0, 1.0, 0.0).astype(bf)
    y = dg(normed, w_ref[...], NN)
    for h in range(heads):
        t = y[:, h * 128 : (h + 1) * 128]
        turned = jnp.where(lower, pltpu.roll(t, 128 - HD // 2, 1), pltpu.roll(t, HD // 2, 1))
        t = t * cos_ref[...] + turned * sin_ref[...]
        k_ref[h] = jnp.where(head_lane, pltpu.roll(t, HD, 1), key_tail).astype(bf)
        t = t.T.astype(bf)
        qt_ref[h, :HD] = t[:HD]
        qt_ref[h, HD:] = one_row
        kt_ref[h] = t[HD:]
    for h in range(heads):
        at = value_at + h // 2 * 128
        t = y[:, at : at + 128]
        turned = t if h % 2 == 0 else pltpu.roll(t, HD, 1)
        v_ref[h] = jnp.where(head_lane, turned, value_tail).astype(bf)
        if h % 2 == 0:
            t_rows = t.T.astype(bf)
        vt_ref[h, :HD] = t_rows[:HD] if h % 2 == 0 else t_rows[HD:]
        vt_ref[h, HD:] = one_row[:16]


def qkv_call(block, blocks, heads, info, x, cos, sin, w, carried):
    rows = x.shape[0]
    S = rows * blocks
    rb = min(256, rows)
    steps = rows // rb
    width = w.shape[1]
    at = lambda i: block * steps + i
    outs = (
        jax.ShapeDtypeStruct((S, D), bf),
        jax.ShapeDtypeStruct((heads, S, 128), bf),
        jax.ShapeDtypeStruct((heads, S, 128), bf),
        jax.ShapeDtypeStruct((heads, 128, S), bf),
        jax.ShapeDtypeStruct((heads, HD, S), bf),
        jax.ShapeDtypeStruct((heads, 80, S), bf),
    )
    in_specs = [
        pl.BlockSpec(memory_space=pltpu.SMEM),
        pl.BlockSpec((rb, D), lambda i: (i, 0)),
        pl.BlockSpec((rb, 128), lambda i: (at(i), 0)),
        pl.BlockSpec((rb, 128), lambda i: (at(i), 0)),
        pl.BlockSpec((D, width), lambda i: (0, 0)),
    ]
    aliases = {}
    if carried is not None:
        first = len(in_specs)
        in_specs += [pl.BlockSpec(memory_space=pl.ANY)] * 6
        aliases = {first + n: n for n in range(6)}
    return pl.pallas_call(
        functools.partial(qkv_kernel, heads),
        grid=(steps,),
        out_shape=outs,
        in_specs=in_specs,
        out_specs=(
            pl.BlockSpec((rb, D), lambda i: (at(i), 0)),
            pl.BlockSpec((heads, rb, 128), lambda i: (0, at(i), 0)),
            pl.BlockSpec((heads, rb, 128), lambda i: (0, at(i), 0)),
            pl.BlockSpec((heads, 128, rb), lambda i: (0, 0, at(i))),
            pl.BlockSpec((heads, HD, rb), lambda i: (0, 0, at(i))),
            pl.BlockSpec((heads, 80, rb), lambda i: (0, 0, at(i))),
        ),
        scratch_shapes=[pltpu.VMEM((8, D), f32)],
        input_output_aliases=aliases,
        compiler_params=pltpu.CompilerParams(vmem_limit_bytes=VMEM),
        cost_estimate=pl.CostEstimate(
            flops=4 * rows * D * width, bytes_accessed=rows * 8192, transcendentals=0
        ),
        name="qkv",
    )(info, x, cos, sin, w, *(carried or ()))


def attend_kernel(kc, half, count, k_ref, qa_ref, qb_ref, v_ref, *refs):
    refs = refs[count:]
    pa_ref, pb_ref, oa_ref, ob_ref, la_ref, lb_ref = refs[:6]
    chunks = refs[6 : 6 + half]
    sa_ref, sb_ref, m_ref = refs[6 + half :]
    i = pl.program_id(0)
    rows = k_ref.shape[1]
    bq = qa_ref.shape[2]

    def stage(new, old):
        if new is not None:
            q_ref, s_new, new_slot = new
            q = q_ref[0]
            m = jnp.full((8, bq), -jnp.inf, f32)
        if old is not None:
            s_old, old_slot, p_ref, o_ref, l_ref, block = old
            top = jnp.max(m_ref[old_slot], axis=0, keepdims=True)
            acc = jnp.zeros((v_ref.shape[1], bq), f32)
        for c in range(rows // kc):
            at = slice(c * kc, (c + 1) * kc)
            if new is not None:
                s = dg(k_ref[0, at, :], q, NN)
                s_new[at, :] = s
                m = jnp.maximum(m, jnp.max(s.reshape(kc // 8, 8, bq), axis=0))
            if old is not None:
                p = jnp.exp2(s_old[at, :] - top).astype(bf)
                p_ref[0, at, :] = p
                acc = acc + dg(v_ref[0, :, at], p, NN)
        if new is not None:
            m_ref[new_slot] = m
        if old is not None:
            linv = 1.0 / acc[HD : HD + 1, :]
            o = acc[:HD, :] * linv
            o_ref[...] = o
            l_ref[0] = linv
            low = o.astype(bf)
            for j in range(half):

                @pl.when(block // 2 == j)
                def _():
                    chunks[j][:, old_slot * bq : (old_slot + 1) * bq] = low

    first = (qa_ref, sa_ref, 0)
    odd = (sb_ref, 1, pb_ref, ob_ref, lb_ref, 2 * i - 1)

    @pl.when(i == 0)
    def _():
        stage(first, None)

    @pl.when((i > 0) & (i < half))
    def _():
        stage(first, odd)

    @pl.when(i == half)
    def _():
        stage(None, odd)

    @pl.when(i < half)
    def _():
        stage((qb_ref, sb_ref, 1), (sa_ref, 0, pa_ref, oa_ref, la_ref, 2 * i))


def attend(h, k, qt, vt, groups, after, kc=256):
    S = k.shape[1]
    bq = S // groups // 2
    a = lambda i: jnp.minimum(i, groups - 1)
    b = lambda i: jnp.maximum(i - 1, 0)
    outs = pl.pallas_call(
        functools.partial(attend_kernel, kc, groups, len(after)),
        grid=(groups + 1,),
        out_shape=(jax.ShapeDtypeStruct((groups, S, bq), bf),) * 2
        + (jax.ShapeDtypeStruct((HD, S // 2), f32),) * 2
        + (jax.ShapeDtypeStruct((groups, 1, bq), f32),) * 2
        + (jax.ShapeDtypeStruct((HD, 2 * bq), bf),) * groups,
        in_specs=[
            pl.BlockSpec((1, S, 128), lambda i: (h, 0, 0)),
            pl.BlockSpec((1, 128, bq), lambda i: (h, 0, 2 * a(i))),
            pl.BlockSpec((1, 128, bq), lambda i: (h, 0, 2 * a(i) + 1)),
            pl.BlockSpec((1, 80, S), lambda i: (h, 0, 0)),
        ]
        + [pl.BlockSpec(memory_space=pl.ANY)] * len(after),
        out_specs=(
            pl.BlockSpec((1, S, bq), lambda i: (a(i), 0, 0)),
            pl.BlockSpec((1, S, bq), lambda i: (b(i), 0, 0)),
            pl.BlockSpec((HD, bq), lambda i: (0, a(i))),
            pl.BlockSpec((HD, bq), lambda i: (0, b(i))),
            pl.BlockSpec((1, 1, bq), lambda i: (a(i), 0, 0)),
            pl.BlockSpec((1, 1, bq), lambda i: (b(i), 0, 0)),
        )
        + (pl.BlockSpec((HD, 2 * bq), lambda i: (0, 0)),) * groups,
        scratch_shapes=[
            pltpu.VMEM((S, bq), f32),
            pltpu.VMEM((S, bq), f32),
            pltpu.VMEM((2, 8, bq), f32),
        ],
        compiler_params=pltpu.CompilerParams(vmem_limit_bytes=VMEM),
        cost_estimate=pl.CostEstimate(
            flops=16 * HD * S * S, bytes_accessed=2 * S * S, transcendentals=S * S
        ),
        name="attend",
    )(k, qt, qt, vt, *after)
    return outs[:6], list(outs[6:])


def attend_back_kernel(kc, groups, v_ref, kt_ref, q_ref, *refs):
    oa_ref, ob_ref, la_ref, lb_ref, pa_ref, pb_ref, cos_ref, sin_ref, n_ref = refs[:9]
    do_refs = refs[9 : 9 + groups]
    outs = refs[-5 - groups : -5]
    grad_ref, acc_ref, do_ref, held_ref, sem = refs[-5:]
    i = pl.program_id(0)
    rows = v_ref.shape[1]
    width = q_ref.shape[2]
    bq = width // 2
    fetch = pltpu.make_async_copy(n_ref, held_ref, sem)

    @pl.when(i == 0)
    def _():
        fetch.start()
        acc_ref[...] = jnp.zeros_like(acc_ref)

    for j in range(groups):

        @pl.when(i == j)
        def _():
            do_ref[...] = do_refs[j][...]

    zero = jnp.zeros((HD, bq), bf)
    r = lax.broadcasted_iota(jnp.int32, (16, bq), 0)
    sides = []
    for n, (o_ref, l_ref, p_ref) in enumerate(((oa_ref, la_ref, pa_ref), (ob_ref, lb_ref, pb_ref))):
        at = slice(n * bq, (n + 1) * bq)
        dop = (do_ref[:, at].astype(f32) * l_ref[0]).astype(bf)
        delta = jnp.sum(dop.astype(f32) * o_ref[...], axis=0, keepdims=True)
        high = delta.astype(bf).astype(f32)
        tail = jnp.where(r == 0, high, jnp.where(r == 1, delta - high, 0.0)).astype(bf)
        doe = jnp.concatenate([dop, tail, jnp.zeros((128 - HD - 16, bq), bf)], axis=0)
        right_v = jnp.concatenate([dop, zero], axis=0).T
        right_k = jnp.concatenate([zero, q_ref[0, :HD, at]], axis=0).T
        sides.append((p_ref, doe, jnp.concatenate([right_v, right_k], axis=0)))
    dq = [jnp.zeros((HD, bq), f32), jnp.zeros((HD, bq), f32)]
    for n, (p_ref, doe, right) in enumerate(sides):
        for c in range(rows // kc):
            at = slice(c * kc, (c + 1) * kc)
            p = p_ref[0, at, :]
            ds = p * dg(v_ref[0, at, :], doe, NN).astype(bf)
            acc_ref[at, :] = acc_ref[at, :] + dg(jnp.concatenate([p, ds], axis=1), right, NN)
            dq[n] = dq[n] + dg(kt_ref[0, :, at], ds, NN)
    dq = jnp.concatenate(dq, axis=1) * HD**-0.5
    turned = jnp.concatenate([dq[HD // 2 :], -dq[: HD // 2]], axis=0)
    here = pl.ds(pl.multiple_of(i * width, width), width)
    dq = (dq * cos_ref[:, here] + turned * sin_ref[:, here]).astype(bf)
    for j in range(groups):

        @pl.when(i == j)
        def _():
            outs[j][:HD] = dq

    @pl.when(i == groups - 1)
    def _():
        fetch.wait()
        grad = jnp.zeros((3 * HD, D), f32)
        for j in range(groups):
            at = slice(j * width, (j + 1) * width)
            t = acc_ref[at, :].T
            dk = t[HD:] * LN2
            turned_k = jnp.concatenate([dk[HD // 2 :], -dk[: HD // 2]], axis=0)
            dk = dk * cos_ref[:, at] + turned_k * sin_ref[:, at]
            outs[j][HD : 2 * HD] = dk.astype(bf)
            outs[j][2 * HD :] = t[:HD].astype(bf)
            grad = grad + dg(outs[j][...], held_ref[at, :], NN)
        grad_ref[:, : 3 * HD] = grad.T.astype(bf)
        grad_ref[:, 3 * HD :] = jnp.zeros((D, HD), bf)


def attend_back(h, v, kt, qt, do, kept, cos, sin, normed, groups, place, after, kc=256):
    S = v.shape[1]
    width = S // groups
    bq = width // 2
    pa, pb, oa, ob, la, lb = kept
    columns, column, earlier = place
    extra = list(after) if earlier is None else [earlier] + list(after)
    whole = lambda i: (0, 0)
    by_block = lambda i: (i, 0, 0)
    outs = pl.pallas_call(
        functools.partial(attend_back_kernel, kc, groups),
        grid=(groups,),
        out_shape=(jax.ShapeDtypeStruct((3 * HD, width), bf),) * groups
        + (jax.ShapeDtypeStruct((D, columns), bf),),
        in_specs=[
            pl.BlockSpec((1, S, 128), lambda i: (h, 0, 0)),
            pl.BlockSpec((1, HD, S), lambda i: (h, 0, 0)),
            pl.BlockSpec((1, 128, width), lambda i: (h, 0, i)),
            pl.BlockSpec((HD, bq), lambda i: (0, i)),
            pl.BlockSpec((HD, bq), lambda i: (0, i)),
            pl.BlockSpec((1, 1, bq), by_block),
            pl.BlockSpec((1, 1, bq), by_block),
            pl.BlockSpec((1, S, bq), by_block),
            pl.BlockSpec((1, S, bq), by_block),
            pl.BlockSpec((HD, S), whole),
            pl.BlockSpec((HD, S), whole),
            pl.BlockSpec(memory_space=pl.ANY),
        ]
        + [pl.BlockSpec((HD, width), lambda i: (h, 0))] * groups
        + [pl.BlockSpec(memory_space=pl.ANY)] * len(extra),
        out_specs=(pl.BlockSpec((3 * HD, width), whole),) * groups
        + (pl.BlockSpec((D, 256), lambda i: (0, column)),),
        scratch_shapes=[
            pltpu.VMEM((S, 128), f32),
            pltpu.VMEM((HD, width), bf),
            pltpu.VMEM((S, D), bf),
            pltpu.SemaphoreType.DMA,
        ],
        input_output_aliases={} if earlier is None else {12 + groups: groups},
        compiler_params=pltpu.CompilerParams(vmem_limit_bytes=VMEM),
        cost_estimate=pl.CostEstimate(
            flops=24 * HD * S * S, bytes_accessed=2 * S * S, transcendentals=0
        ),
        name="attend_back",
    )(v, kt, qt, oa, ob, la, lb, pa, pb, cos, sin, normed, *do, *extra)
    return list(outs[:groups]), outs[groups]


def normalize_back(gradient, unit_rows, inverse, gain_row):
    scaled = gradient * gain_row
    return inverse * (
        scaled
        - jnp.mean(scaled, axis=-1, keepdims=True)
        - unit_rows * jnp.mean(scaled * unit_rows, axis=-1, keepdims=True)
    )


def column(row_ref):
    row = row_ref[...].astype(f32)
    return jnp.broadcast_to(row, (8, row.shape[1])).T[:, :1]


def row_of(total):
    return jnp.broadcast_to(total, (total.shape[0], 128)).T[:1]


def half_kernel(packed, info_ref, in_ref, proj_ref, gain_ref, out_w_ref, *refs):
    half_ref = refs[-1]
    side = info_ref[0] & 1

    @pl.when(side == 0)
    def _():
        half_ref[...] = in_ref[...]

    @pl.when(side == 1)
    def _():
        short = in_ref.shape[0]
        half_ref[:, :D] = proj_ref[...]
        gain = jnp.broadcast_to(column(gain_ref), (short, 128)).astype(bf)
        half_ref[:, D : D + 128] = gain
        if packed:
            one, two, three = D + 128, 2 * D + 128, 2 * D + D // 2 + 128
            tall = out_w_ref.shape[0]
            half_ref[:, one:two] = out_w_ref[:short, :]
            half_ref[: tall - short, two:three] = out_w_ref[short:, : D // 2]
            half_ref[tall - short :, two:three] = out_w_ref[short:, D // 2 :]


def own_half(packed, info, in_w, proj_w, gain, out_w, after):
    vmem = pl.BlockSpec(memory_space=pltpu.VMEM)
    return pl.pallas_call(
        functools.partial(half_kernel, packed),
        out_shape=jax.ShapeDtypeStruct(in_w.shape, bf),
        in_specs=[pl.BlockSpec(memory_space=pltpu.SMEM)]
        + [vmem] * 4
        + [pl.BlockSpec(memory_space=pl.ANY)] * len(after),
        out_specs=vmem,
        compiler_params=pltpu.CompilerParams(vmem_limit_bytes=VMEM),
        name="own_half",
    )(info, in_w, proj_w, gain, out_w, *after)


def hold(array, after):
    def kernel(*refs):
        pass

    return pl.pallas_call(
        kernel,
        out_shape=jax.ShapeDtypeStruct(array.shape, array.dtype),
        in_specs=[pl.BlockSpec(memory_space=pl.ANY)] * (1 + len(after)),
        out_specs=pl.BlockSpec(memory_space=pl.ANY),
        input_output_aliases={0: 0},
        compiler_params=pltpu.CompilerParams(vmem_limit_bytes=VMEM),
        name="hold",
    )(array, *after)


def middle_kernel(groups, heads, ff, shards, info_ref, x_ref, dy_ref, mine_ref, other_ref, *refs):
    count = groups * heads
    given = len(refs) - count - groups - 13
    out_given = refs[:given]
    chunks = refs[given : given + count]
    d_chunks = refs[given + count : given + count + groups]
    (result_ref, dh_ref, mixed_ref, second_ref, dgu_ref, inner_ref, branch_ref,
     g_ref, t_ref, out_w_ref, w_ref, rest_ref, sems) = refs[given + count + groups :]
    width = heads * HD
    me = info_ref[0]

    @pl.when(pl.program_id(0) == 0)
    def _():
        def fetch(first, second):
            copies = [
                pltpu.make_async_copy(first, w_ref, sems.at[0]),
                pltpu.make_async_copy(second, rest_ref, sems.at[1]),
            ]
            for copy in copies:
                copy.start()
            for copy in copies:
                copy.wait()

        @pl.when((me & 1) == 0)
        def _():
            fetch(mine_ref, other_ref)

        @pl.when((me & 1) == 1)
        def _():
            fetch(other_ref, mine_ref)

        g_ref[...] = rest_ref[:, D : D + 128].astype(f32).T[:8]
        if given:
            out_w_ref[...] = out_given[0][...]
        else:
            tall, short = ff // shards, D // shards
            rest = tall - short
            one, two, three = D + 128, 2 * D + 128, 2 * D + D // 2 + 128
            for f in range(shards):
                src = slice(f * short, (f + 1) * short)
                out_w_ref[f * tall : f * tall + short, :] = rest_ref[src, one:two]
                dst = slice(f * tall + short, (f + 1) * tall)
                src = slice(f * short, f * short + rest)
                out_w_ref[dst, : D // 2] = rest_ref[src, two:three]
                src = slice(f * short + rest, f * short + 2 * rest)
                out_w_ref[dst, D // 2 :] = rest_ref[src, two:three]

    for h in range(heads):
        for j in range(groups):
            start = pl.multiple_of((me ^ j) * width + h * HD, HD)
            mixed_ref[pl.ds(start, HD), :] = chunks[h * groups + j][...]
    gain = g_ref[:1]
    proj = rest_ref[:, :D]
    hidden = x_ref[...].astype(f32) + dg(mixed_ref[...], proj, TN)
    unit, inverse = unit_rows_of(hidden)
    second = (unit * gain).astype(bf)
    second_ref[...] = second
    dy = dy_ref[...]
    result = hidden
    d_second = jnp.zeros_like(hidden)
    step = ff
    for c in range(ff // step):
        a = slice(c * step, (c + 1) * step)
        b = slice(ff + c * step, ff + (c + 1) * step)
        gate = dg(second, w_ref[:, a], NN)
        up = dg(second, w_ref[:, b], NN)
        d_inner = dg(dy, out_w_ref[a, :], NT)
        bell = 0.5 + 0.5 * lax.erf(gate * 0.7071067811865476)
        gelu = gate * bell
        inner = (gelu * up).astype(bf)
        inner_ref[:, a] = inner
        result = result + dg(inner, out_w_ref[a, :], NN)
        slope = bell + gate * (jnp.exp(-0.5 * gate * gate) * 0.3989422804014327)
        d_gate = (d_inner * up * slope).astype(bf)
        d_up = (d_inner * gelu).astype(bf)
        dgu_ref[:, a] = d_gate
        dgu_ref[:, b] = d_up
        d_second = d_second + dg(d_gate, w_ref[:, a], NT) + dg(d_up, w_ref[:, b], NT)
    result_ref[...] = result.astype(bf)
    d_hidden = dy.astype(f32) + normalize_back(d_second, unit, inverse, gain)
    dh_ref[...] = d_hidden
    branch = d_hidden.astype(bf)
    branch_ref[...] = branch
    t_ref[...] = dg(proj, branch, NT).astype(bf)
    for j in range(groups):
        start = pl.multiple_of((me ^ j) * width, HD)
        d_chunks[j][...] = t_ref[pl.ds(start, width), :]


def middle(groups, heads, shards, ff, info, x, dy, mine, other, out_w, chunks):
    rows = x.shape[0]
    rb = min(256, rows)
    by_row = lambda i: (i, 0)
    by_column = lambda i: (0, i)
    whole = lambda i: (0, 0)
    outs = pl.pallas_call(
        functools.partial(middle_kernel, groups, heads, ff, shards),
        grid=(rows // rb,),
        out_shape=(jax.ShapeDtypeStruct((heads * HD, rows), bf),) * groups
        + (
            jax.ShapeDtypeStruct((rows, D), bf),
            jax.ShapeDtypeStruct((rows, D), f32),
            jax.ShapeDtypeStruct((D, rows), bf),
            jax.ShapeDtypeStruct((rows, D), bf),
            jax.ShapeDtypeStruct((rows, 2 * ff), bf),
            jax.ShapeDtypeStruct((rows, ff), bf),
            jax.ShapeDtypeStruct((rows, D), bf),
        ),
        in_specs=[
            pl.BlockSpec(memory_space=pltpu.SMEM),
            pl.BlockSpec((rb, D), by_row),
            pl.BlockSpec((rb, D), by_row),
            pl.BlockSpec(memory_space=pl.ANY),
            pl.BlockSpec(memory_space=pl.ANY),
        ]
        + [pl.BlockSpec(w.shape, whole, pipeline_mode=pl.Buffered(1)) for w in out_w]
        + [pl.BlockSpec((HD, rb), by_column)] * (groups * heads),
        out_specs=(pl.BlockSpec((heads * HD, rb), by_column),) * groups
        + (
            pl.BlockSpec((rb, D), by_row),
            pl.BlockSpec((rb, D), by_row),
            pl.BlockSpec((D, rb), by_column),
            pl.BlockSpec((rb, D), by_row),
            pl.BlockSpec((rb, 2 * ff), by_row),
            pl.BlockSpec((rb, ff), by_row),
            pl.BlockSpec((rb, D), by_row),
        ),
        scratch_shapes=[
            pltpu.VMEM((8, D), f32),
            pltpu.VMEM((D, rb), bf),
            pltpu.VMEM((ff, D), bf),
            pltpu.VMEM(mine.shape, bf),
            pltpu.VMEM(mine.shape, bf),
            pltpu.SemaphoreType.DMA((2,)),
        ],
        compiler_params=pltpu.CompilerParams(vmem_limit_bytes=VMEM),
        cost_estimate=pl.CostEstimate(
            flops=rows * D * (14 * ff + 4 * D), bytes_accessed=30 * 2**20, transcendentals=rows * ff
        ),
        name="middle",
    )(info, x, dy, mine, other, *out_w, *chunks)
    return list(outs[:groups]), outs[groups:]


def last_kernel(groups, chosen, x_ref, base_ref, gain_ref, *refs):
    count = groups * len(chosen)
    chunks = refs[:count]
    pairs = refs[count : 2 * count]
    value_refs = refs[2 * count : 3 * count]
    out_ref, dp_ref, wh_ref, g_ref = refs[-4:]
    both = groups * 2 * HD

    @pl.when(pl.program_id(0) == 0)
    def _():
        g_ref[...] = gain_ref[...].astype(f32).T[HD : HD + 8]
        for n, h in enumerate(chosen):
            side = (h & 1) * HD
            pieces = [ref[...] for ref in pairs[n * groups : (n + 1) * groups]]
            pieces += [ref[:, side : side + HD] for ref in value_refs[n * groups : (n + 1) * groups]]
            wh_ref[:, n * D : (n + 1) * D] = jnp.concatenate(pieces, axis=1)

    for n in range(len(chosen)):
        for j in range(groups):
            chunk = chunks[n * groups + j]
            start = n * D + j * 2 * HD
            dp_ref[start : start + 2 * HD, :] = chunk[: 2 * HD, :]
            start = n * D + both + j * HD
            dp_ref[start : start + HD, :] = chunk[2 * HD :, :]
    d_normed = dg(wh_ref[...], dp_ref[...], NN).T
    unit, inverse = unit_rows_of(x_ref[...].astype(f32))
    out_ref[...] = base_ref[...] + normalize_back(d_normed, unit, inverse, g_ref[:1])


def last(groups, heads, chosen, x, base, peers, chunks, after):
    rows = chunks[0].shape[1]
    rb = min(256, rows)
    by_row = lambda i: (i, 0)

    def tile(n):
        return pl.BlockSpec((D, 128), lambda i: (0, n), pipeline_mode=pl.Buffered(1))

    pairs = [tile(h) for h in chosen for _ in peers]
    value_tiles = [tile(heads + h // 2) for h in chosen for _ in peers]
    return pl.pallas_call(
        functools.partial(last_kernel, groups, chosen),
        grid=(rows // rb,),
        out_shape=jax.ShapeDtypeStruct((rows, D), f32),
        in_specs=[
            pl.BlockSpec((rb, D), by_row),
            pl.BlockSpec((rb, D), by_row),
            tile(peers[0].shape[1] // 128 - 1),
        ]
        + [pl.BlockSpec((3 * HD, rb), lambda i: (0, i))] * len(chunks)
        + pairs
        + value_tiles
        + [pl.BlockSpec(memory_space=pl.ANY)] * len(after),
        out_specs=pl.BlockSpec((rb, D), by_row),
        scratch_shapes=[
            pltpu.VMEM((len(chosen) * D, rb), bf),
            pltpu.VMEM((D, len(chosen) * D), bf),
            pltpu.VMEM((8, D), f32),
        ],
        compiler_params=pltpu.CompilerParams(vmem_limit_bytes=VMEM),
        cost_estimate=pl.CostEstimate(
            flops=2 * len(chosen) * rows * D * D, bytes_accessed=12 * 2**20, transcendentals=0
        ),
        name="last",
    )(x, base, peers[0], *chunks, *(list(peers) * (2 * len(chosen))), *after)


def own_kernel(groups, heads, info_ref, w_ref, gain_ref, out_ref):
    for g in range(groups):

        @pl.when(info_ref[0] == g)
        def _():
            def piece(t, h):
                start = t * D + (g * heads + h) * HD
                return w_ref[:, start : start + HD]

            pieces = []
            for h in range(heads):
                pieces += [piece(0, h), piece(1, h)]
            pieces += [piece(2, h) for h in range(heads)] + [column(gain_ref).astype(bf)]
            missing = out_ref.shape[2] - 3 * heads * HD - 1
            pieces.append(jnp.zeros((w_ref.shape[0], missing), bf))
            own = jnp.concatenate(pieces, axis=1)
            for f in range(out_ref.shape[0]):
                out_ref[f] = own


def own_columns(groups, heads, shards, info, w, gain):
    width = (3 * heads * HD + 128) // 128 * 128
    return pl.pallas_call(
        functools.partial(own_kernel, groups, heads),
        out_shape=jax.ShapeDtypeStruct((shards, w.shape[0], width), bf),
        in_specs=[
            pl.BlockSpec(memory_space=pltpu.SMEM),
            pl.BlockSpec(memory_space=pltpu.VMEM),
            pl.BlockSpec(memory_space=pltpu.VMEM),
        ],
        out_specs=pl.BlockSpec(memory_space=pltpu.VMEM),
        compiler_params=pltpu.CompilerParams(vmem_limit_bytes=VMEM),
        name="own_columns",
    )(info, w, gain)


def tables_kernel(cos_ref, sin_ref, cos_rows_ref, sin_rows_ref, cos_t_ref, sin_t_ref):
    c, s = cos_ref[...], sin_ref[...]
    cos_t_ref[...] = jnp.concatenate([c, c], axis=0)
    sin_t_ref[...] = jnp.concatenate([s, s], axis=0)
    scale = HD**-0.5 * LOG2E
    cos_rows_ref[...] = jnp.concatenate([c * scale, c * scale, c, c], axis=0).T
    sin_rows_ref[...] = jnp.concatenate([s * -scale, s * scale, -s, s], axis=0).T


def tables(cosine, sine):
    half, S = cosine.shape
    rb = min(1024, S)
    return pl.pallas_call(
        tables_kernel,
        grid=(S // rb,),
        out_shape=(jax.ShapeDtypeStruct((S, 4 * half), f32),) * 2
        + (jax.ShapeDtypeStruct((2 * half, S), f32),) * 2,
        in_specs=[pl.BlockSpec((half, rb), lambda i: (0, i))] * 2,
        out_specs=(pl.BlockSpec((rb, 4 * half), lambda i: (i, 0)),) * 2
        + (pl.BlockSpec((2 * half, rb), lambda i: (0, i)),) * 2,
        compiler_params=pltpu.CompilerParams(vmem_limit_bytes=VMEM),
        name="tables",
    )(cosine, sine)


def grads_kernel(place_ref, second_ref, dgu_ref, mixed_ref, branch_ref, inner_ref, dy_ref, *refs):
    outs, tall_ref, held_ref = refs[:-2], refs[-2], refs[-1]
    i = pl.program_id(0)
    group = i ^ place_ref[0]
    end = pl.num_programs(0) - 1

    @pl.when(group < end)
    def _():
        held_ref[...] = dg(second_ref[...], dgu_ref[...], TN).astype(bf)

    @pl.when(group == end)
    def _():
        held_ref[...] = dg(mixed_ref[...], branch_ref[...], NN).astype(bf)

    @pl.when(i < end)
    def _():
        tall_ref[...] = dg(inner_ref[...], dy_ref[...], TN).astype(bf)

    for j in range(len(outs)):

        @pl.when(i == j)
        def _():
            outs[j][...] = held_ref[...]


def weight_grads(place, second, d_gate_up, mixed_t, branch, inner, dy):
    rows = second.shape[0]
    ff = inner.shape[1]
    steps = d_gate_up.shape[1] // D
    whole = lambda i, p: (0, 0)
    part = lambda i, p: (0, jnp.minimum(i, steps - 1))
    outs = pl.pallas_call(
        grads_kernel,
        grid_spec=pltpu.PrefetchScalarGridSpec(
            num_scalar_prefetch=1,
            grid=(steps + 1,),
            in_specs=[
                pl.BlockSpec((rows, D), whole),
                pl.BlockSpec((rows, D), lambda i, p: (0, jnp.minimum(i ^ p[0], steps - 1))),
                pl.BlockSpec((D, rows), whole),
                pl.BlockSpec((rows, D), whole),
                pl.BlockSpec((rows, ff // steps), part),
                pl.BlockSpec((rows, D), whole),
            ],
            out_specs=(pl.BlockSpec((D, D), whole),) * (steps + 1)
            + (pl.BlockSpec((ff // steps, D), lambda i, p: (jnp.minimum(i, steps - 1), 0)),),
            scratch_shapes=[pltpu.VMEM((D, D), bf)],
        ),
        out_shape=(jax.ShapeDtypeStruct((D, D), bf),) * (steps + 1)
        + (jax.ShapeDtypeStruct((ff, D), bf),),
        compiler_params=pltpu.CompilerParams(vmem_limit_bytes=VMEM),
        cost_estimate=pl.CostEstimate(
            flops=2 * rows * D * (D * (steps + 1) + ff), bytes_accessed=20 * 2**20, transcendentals=0
        ),
        name="weight_grads",
    )(place, second, d_gate_up, mixed_t, branch, inner, dy)
    return list(outs[:-1]), outs[-1]


def ordered(
    kernel, arrays, after, carry, out_shape, in_specs, out_specs, name, grid=(), scratch=()
):
    first = len(arrays) + len(after)
    own = len(out_shape)
    anywhere = pl.BlockSpec(memory_space=pl.ANY)

    def call(*refs):
        outs = refs[first + len(carry) :]
        kernel(*refs[: len(arrays)], *outs[:own], *outs[own + len(carry) :])

    outs = pl.pallas_call(
        call,
        grid=grid,
        out_shape=tuple(out_shape) + tuple(jax.ShapeDtypeStruct(a.shape, a.dtype) for a in carry),
        in_specs=list(in_specs) + [anywhere] * (len(after) + len(carry)),
        out_specs=tuple(out_specs) + (anywhere,) * len(carry),
        scratch_shapes=list(scratch),
        input_output_aliases={first + n: own + n for n in range(len(carry))},
        compiler_params=pltpu.CompilerParams(vmem_limit_bytes=VMEM),
        name=name,
    )(*arrays, *after, *carry)
    return list(outs[:own]), list(outs[own:])


def add_kernel(*refs):
    total = refs[0][...].astype(f32)
    for ref in refs[1:-1]:
        total = total + ref[...].astype(f32)
    refs[-1][...] = total.astype(bf)


def add_up(arrays, after, carry):
    rows, columns = arrays[0].shape
    rb = 256
    spec = pl.BlockSpec((rb, columns), lambda i: (i, 0))
    (total,), carried = ordered(
        add_kernel, arrays, after, carry, [jax.ShapeDtypeStruct((rows, columns), bf)],
        [spec] * len(arrays), [spec], "add_up", grid=(rows // rb,),
    )
    return total, carried


def up16(n):
    return -(-n // 16) * 16


def sum_kernel(parts_ref, *refs):
    total = parts_ref[0].astype(f32)
    for f in range(1, parts_ref.shape[0]):
        total = total + parts_ref[f].astype(f32)
    refs[-1][...] = total.astype(bf)


def sum_owned(parts, after):
    vmem = pl.BlockSpec(memory_space=pltpu.VMEM)
    (total,), _ = ordered(
        sum_kernel, [parts], after, [], [jax.ShapeDtypeStruct(parts.shape[1:], bf)],
        [vmem], [vmem], "sum_owned",
    )
    return total


def owned_kernel(wide_ref, tall_ref, *refs):
    out_ref = refs[-1]
    start = 0
    for ref in (wide_ref, tall_ref):
        total = ref[0].astype(f32)
        for f in range(1, ref.shape[0]):
            total = total + ref[f].astype(f32)
        out_ref[start : start + ref.shape[1], :] = total.astype(bf)
        start += up16(ref.shape[1])


def owned(wide, tall, after, carry):
    vmem = pl.BlockSpec(memory_space=pltpu.VMEM)
    shape = (up16(wide.shape[1]) + up16(tall.shape[1]), D)
    (total,), carried = ordered(
        owned_kernel, [wide, tall], after, carry, [jax.ShapeDtypeStruct(shape, bf)],
        [vmem] * 2, [vmem], "owned",
    )
    return total, carried


def finish_wide_kernel(groups, info_ref, w_ref, gain_ref, *refs):
    in_ref, proj_ref, dgain_ref, out_ref, held_ref = refs[groups:]
    shard = w_ref.shape[0]
    start = up16(shard)
    tall = 0.0
    for j in range(groups):
        held_ref[info_ref[0] ^ j] = refs[j][...]
        tall = tall + refs[j][start : start + out_ref.shape[0], :].astype(f32)
    out_ref[...] = tall
    total = 0.0
    for g in range(groups - 1):
        at = slice(g * D, (g + 1) * D)
        grad = held_ref[g, :shard, :].astype(f32)
        in_ref[:, at] = grad
        total = total + jnp.sum(w_ref[:, at].astype(f32) * grad, axis=1, keepdims=True)
    proj_ref[...] = held_ref[groups - 1, :shard, :].astype(f32)
    dgain_ref[...] = row_of(total / column(gain_ref))


def finish_qkv_kernel(groups, heads, info_ref, w_ref, gain_ref, *refs):
    out_ref, dgain_ref, held_ref = refs[groups : groups + 3]
    for j in range(groups):
        held_ref[info_ref[0] ^ j] = refs[j][...]
    pieces = []
    for t in range(3):
        for g in range(groups):
            for h in range(heads):
                start = h * 256 + t * HD
                pieces.append(held_ref[g, :, start : start + HD].astype(f32))
    grad = jnp.concatenate(pieces, axis=1)
    out_ref[...] = grad
    total = jnp.sum(w_ref[...].astype(f32) * grad, axis=1, keepdims=True)
    dgain_ref[...] = row_of(total / column(gain_ref))


def finish(kernel, groups, info, w, gain, parts, shapes, name, after=(), carry=()):
    vmem = pl.BlockSpec(memory_space=pltpu.VMEM)
    return ordered(
        kernel, [info, w, gain, *parts], list(after), list(carry),
        [jax.ShapeDtypeStruct(shape, f32) for shape in shapes],
        [pl.BlockSpec(memory_space=pltpu.SMEM)] + [vmem] * (2 + groups),
        [vmem] * len(shapes), name,
        scratch=[pltpu.VMEM((groups,) + parts[0].shape, bf)],
    )


def body(
    tokens, lengths, attn_gain, qkv_weight, proj_weight, ffn_gain, in_weight, out_weight, out_grad
):
    rows = tokens.shape[1]
    groups = lax.axis_size("seq")
    shards = lax.axis_size("fsdp")
    heads = HEADS // groups
    shard = D // shards
    me = lax.axis_index("seq")

    def swap(array, j, axis="seq"):
        size = lax.axis_size(axis)
        return lax.ppermute(array, axis, [(i, i ^ j) for i in range(size)])

    def exchange(chunks):
        return [chunks[0]] + [swap(chunks[j], j) for j in range(1, groups)]

    def gather(array):
        return lax.all_gather(array, "fsdp", axis=0, tiled=True)

    place = jnp.stack([me]).astype(jnp.int32)
    x0 = tokens[0]
    across = swap(x0, 2)
    near = swap(x0, 1)
    attn_row = attn_gain[None, :]
    ffn_row = ffn_gain[None, :]
    own = own_columns(groups, heads, shards, place, qkv_weight, attn_row)
    own = lax.all_to_all(own, "fsdp", split_axis=0, concat_axis=0, tiled=True).reshape(D, -1)

    half = HD // 2
    frequency = rope_base ** (-(lax.iota(f32, half) * 2.0) / HD)
    starts = [(me ^ j) * rows for j in range(groups)]
    positions = jnp.concatenate([s + lax.iota(jnp.int32, rows) for s in starts]).astype(f32)
    angles = frequency[:, None] * positions[None, :]
    cos_rows, sin_rows, cos_t, sin_t = tables(jnp.cos(angles), jnp.sin(angles))

    def project(j, block, carried):
        info = jnp.stack([starts[j], lengths[0]]).astype(jnp.int32)
        return qkv_call(j, groups, heads, info, block, cos_rows, sin_rows, own, carried)

    diagonal = swap(across, 1)
    carried = project(2, across, None)
    carried = project(0, x0, carried)
    carried = project(1, near, carried)
    normed, k, v, qt, kt, vt = project(3, diagonal, carried)

    ff = in_weight.shape[1] // 2
    tall = out_weight.shape[0]
    packed = shards <= 8
    mine = gather(own_half(packed, place, in_weight, proj_weight, ffn_row, out_weight, [own, cos_t]))
    out_full = [] if packed else [gather(out_weight)]

    own = hold(own, [normed])
    own_near, own_across = swap(own, 1), swap(own, 2)

    kept = []
    chunks = []
    for h in range(heads):
        before = [kept[-1][2]] if kept else []
        if h == 1:
            before += [own_near, own_across]
        saved, mixed = attend(h, k, qt, vt, groups, before)
        kept.append(saved)
        if h > 0:
            early = [chunks[n] for n in range((h - 1) * groups, h * groups) if n % groups]
            extra = [mine] if h == heads - 2 else [own_across]
            _, carried = ordered(
                lambda: None, [], [saved[2]] + early, mixed[1:] + extra, [], [], [], "hold"
            )
            mixed = mixed[:1] + carried[:-1]
            if h == heads - 2:
                mine = carried[-1]
                other = swap(mine, 1)
            else:
                own_across = carried[-1]
                own_diagonal = swap(own_across, 1)
        chunks += exchange(mixed)

    dy = out_grad[0]
    d_mixed, (result, d_hidden, mixed_t, second, d_gate_up, inner, branch) = middle(
        groups, heads, shards, ff, place, x0, dy, mine, other, out_full, chunks
    )
    d_mixed = exchange(d_mixed)

    def to_owner(array):
        parts = array.reshape(shards, array.shape[0] // shards, -1)
        return lax.all_to_all(parts, "fsdp", split_axis=0, concat_axis=0, tiled=True)

    def from_peers(array):
        return [array] + [swap(array, j) for j in range(1, groups)]

    wide, tall_grad = weight_grads(place, second, d_gate_up, mixed_t, branch, inner, dy)
    _, carried = ordered(
        lambda: None, [], d_mixed[1:], wide[1:] + [tall_grad], [], [], [], "hold"
    )
    tall_grad = carried[-1]
    wide_all = exchange(wide[:1] + carried[:-1])
    tall_parts = to_owner(tall_grad)

    def back(h, grad_place, after):
        return attend_back(
            h, v, kt, qt, d_mixed, kept[h], cos_t, sin_t, normed, groups, grad_place, after
        )

    peers = [own, own_near, own_across, own_diagonal]
    sent_0, qkv_first = back(0, (768, 0, None), [tall_grad, own_diagonal])
    wide_sum, others = add_up(wide_all, [qkv_first, tall_parts], sent_0[1:])
    wide_parts = to_owner(wide_sum)
    received_0 = exchange(sent_0[:1] + others)

    sent_1, qkv_first = back(1, (768, 1, qkv_first), [wide_sum])
    both, carried = owned(wide_parts, tall_parts, received_0[1:], sent_1[1:] + [qkv_first])
    received_1 = exchange(sent_1[:1] + carried[:-1])
    both_far = [swap(both, j) for j in range(2, groups)]

    sent_2, qkv_second = back(2, (768, 2, carried[-1]), [both])
    _, carried = ordered(
        lambda: None, [], received_1[1:] + both_far,
        sent_2[1:] + [qkv_second, both], [], [], [], "pass_on",
    )
    qkv_second, both = carried[-2:]
    received_2 = exchange(sent_2[:1] + carried[:-2])
    both_peers = [both, swap(both, 1)] + both_far
    (in_weight_grad, proj_weight_grad, ffn_gain_grad, out_weight_grad), carried = finish(
        functools.partial(finish_wide_kernel, groups),
        groups, place, in_weight, ffn_row, both_peers,
        ((shard, 2 * ff), (shard, D), (1, shard), (tall, D)), "finish_wide",
        carry=[qkv_second],
    )
    qkv_parts = to_owner(carried[0])
    base = last(
        groups, heads, (0, 1), x0, d_hidden, peers, received_0 + received_1, [carried[0]]
    )
    qkv_peers = from_peers(sum_owned(qkv_parts, [base] + received_2[1:]))
    tokens_grad = last(groups, heads, (2,), x0, base, peers, received_2, [])
    (qkv_weight_grad, attn_gain_grad), _ = finish(
        functools.partial(finish_qkv_kernel, groups, heads),
        groups, place, qkv_weight, attn_row, qkv_peers,
        ((shard, 3 * D), (1, shard)), "finish_qkv", [tokens_grad],
    )
    return (
        result[None],
        tokens_grad[None],
        attn_gain_grad[0],
        qkv_weight_grad,
        proj_weight_grad,
        ffn_gain_grad[0],
        in_weight_grad,
        out_weight_grad,
    )


def solution(mesh):
    in_specs = (
        P("fsdp", "seq", None),
        P("fsdp"),
        P("fsdp"),
        P("fsdp", None),
        P("fsdp", None),
        P("fsdp"),
        P("fsdp", None),
        P("fsdp", None),
        P("fsdp", "seq", None),
    )
    out_specs = (
        P("fsdp", "seq", None),
        P("fsdp", "seq", None),
        P("fsdp"),
        P("fsdp", None),
        P("fsdp", None),
        P("fsdp"),
        P("fsdp", None),
        P("fsdp", None),
    )
    return jax.shard_map(body, mesh=mesh, in_specs=in_specs, out_specs=out_specs, check_vma=False)
```
